32 devices in a mesh: dp: 8 (over y, x, core), mp: 4 (over z).
Axes of the slice: x: 2, y: 2, z: 4, core: 2. Of those that a mesh axis runs over, the one named last changes fastest.
Arguments:
- tokens: bfloat16 [16384, 768], P('dp'), may hold values from -6 to 6
- seg_ids: int32 [16384], P('dp'), may hold values from 0 to 64, as said below
- qkv_weight: bfloat16 [3, 768, 768], P(None, None, 'mp'), may hold values from -0.21875 to 0.21875
- qkv_bias: float32 [3, 768], P(None, 'mp'), may hold values from -3 to 3
- out_weight: bfloat16 [768, 768], P('mp'), may hold values from -0.875 to 0.875
- out_bias: float32 [768], replicated, may hold values from -2 to 2
- up_weight: bfloat16 [768, 3072], P(None, 'mp'), may hold values from -0.21875 to 0.21875
- up_bias: float32 [3072], P('mp'), may hold values from -3 to 3
- down_weight: bfloat16 [3072, 768], P('mp'), may hold values from -0.109375 to 0.109375
- down_bias: float32 [768], replicated, may hold values from -2 to 2
- norm1_gain: float32 [768], replicated, may hold values from 0.5 to 1.5
- norm1_shift: float32 [768], replicated, may hold values from -2 to 2
- query_gain: float32 [64], replicated, may hold values from 0.5 to 1.5
- query_shift: float32 [64], replicated, may hold values from -2 to 2
- key_gain: float32 [64], replicated, may hold values from 0.5 to 1.5
- norm2_gain: float32 [768], replicated, may hold values from 0.5 to 1.5
- norm2_shift: float32 [768], replicated, may hold values from -2 to 2
- cotangent: bfloat16 [16384, 768], P('dp'), may hold values from -6 to 6
Outputs:
- block_out: bfloat16 [16384, 768], P(('dp', 'mp'))
- input_grad: bfloat16 [16384, 768], P(('dp', 'mp'))
- qkv_weight_grad: float32 [3, 768, 768], P(None, None, 'mp')
- qkv_bias_grad: float32 [3, 768], P(None, 'mp')
- out_weight_grad: float32 [768, 768], P('mp')
- out_bias_grad: float32 [768], replicated
- up_weight_grad: float32 [768, 3072], P(None, 'mp')
- up_bias_grad: float32 [3072], P('mp')
- down_weight_grad: float32 [3072, 768], P('mp')
- down_bias_grad: float32 [768], replicated
- norm1_gain_grad: float32 [768], replicated
- norm1_shift_grad: float32 [768], replicated
- query_gain_grad: float32 [64], replicated
- query_shift_grad: float32 [64], replicated
- key_gain_grad: float32 [64], replicated
- norm2_gain_grad: float32 [768], replicated
- norm2_shift_grad: float32 [768], replicated
The draws below stay inside these ranges and needn't reach their ends.
Inputs may be any that keep to these rules, and one draw needn't show every extreme that they name: `seg_ids`: within each packed sequence of 1024 slots the ids run 1, 2, 3 and so on over whole images that are square patch grids of 16 or more patches laid end to end, followed by zeros for padding up to the sequence's end.
All inputs are finite; a program needn't handle non-finite values.
Results may differ from the reference program's by a relative error of at most 0.012.
Values sent between devices are 32-bit elements; how exact they have to be, the bound alone decides.
No kernel may reach another device: no remote copies, remote signals or barrier semaphores. Data moves between devices by JAX's collectives and lax.ppermute only.
A program may use at most 192 MiB of HBM per device.

```python
import math
import jax
import jax.numpy as jnp
from jax import lax

D = 768
H = 12
DH = 64
FF = 3072
SEQ_LEN = 1024
TOKENS = 16384


def draw_seg_ids(key, part):
    key = jax.random.fold_in(key, 7)
    slot_count = SEQ_LEN // 16 + 1
    top_side = min(33, math.isqrt(SEQ_LEN) + 1)
    seq_count = TOKENS // SEQ_LEN
    image_sides = jax.random.randint(key, (seq_count, slot_count), 4, top_side)
    chosen_seq = jax.random.randint(jax.random.fold_in(key, 1), (), 0, seq_count)
    seq_numbers = jnp.arange(seq_count, dtype=jnp.int32)
    image_sides = jnp.where(seq_numbers[:, None] == chosen_seq, 4, image_sides)
    image_ends = jnp.cumsum(image_sides * image_sides, axis=1)
    positions = jnp.arange(SEQ_LEN, dtype=jnp.int32)
    prior_count = jnp.sum((image_ends[:, None, :] <= positions[None, :, None]).astype(jnp.int32), axis=2)
    filled_upto = jnp.max(jnp.where(image_ends <= SEQ_LEN, image_ends, 0), axis=1)
    segment_ids = jnp.where(positions[None, :] < filled_upto[:, None], prior_count + 1, 0)
    return segment_ids.reshape(-1).astype(jnp.int32)


def level_of(own_key, shape, split, smallest, largest):
    def one(position, blocks):
        draws = jax.random.uniform(jax.random.fold_in(jax.random.fold_in(own_key, 6), position), (blocks,), jnp.float32, smallest / len(split), largest / len(split))
        return jnp.repeat(jnp.exp(draws), shape[position] // blocks).reshape((-1,) + (1,) * (len(shape) - position - 1))

    gain = one(*split[0])
    for cut in split[1:]:
        gain = gain * one(*cut)
    return gain


def centred(key, extent, deviation, reach, cuts=(), kind=jnp.bfloat16):
    entries = deviation * jax.random.normal(key, extent, jnp.float32)
    if cuts:
        entries = entries * level_of(key, extent, cuts, -0.22, 0.18)
    return jnp.clip(entries, -reach, reach).astype(kind)


def setup_inputs(seed: int = 0) -> dict:
    splits = jax.random.split(jax.random.key(seed), 19)
    tokens = centred(splits[0], (TOKENS, D), 1.0, 6.0, ((0, 8),))
    seg_ids = draw_seg_ids(jax.random.fold_in(splits[18], 71), 0)
    qkv_weight = centred(splits[2], (3, D, D), D ** -0.5, 0.21875, ((2, 4),))
    qkv_bias = centred(splits[3], (3, D), 0.5, 3.0, ((1, 4),), jnp.float32)
    out_weight = centred(splits[4], (D, D), (D // 16) ** -0.5, 0.875, ((0, 4),))
    out_bias = centred(splits[5], (D,), 0.3, 2.0, (), jnp.float32)
    up_weight = centred(splits[6], (D, FF), D ** -0.5, 0.21875, ((1, 4),))
    up_bias = centred(splits[7], (FF,), 0.5, 3.0, ((0, 4),), jnp.float32)
    down_weight = centred(splits[8], (FF, D), FF ** -0.5, 0.109375, ((0, 4),))
    down_bias = centred(splits[9], (D,), 0.3, 2.0, (), jnp.float32)
    norm1_gain = jnp.clip(1.0 + 0.1 * jax.random.normal(splits[10], (D,), jnp.float32), 0.5, 1.5)
    norm1_shift = centred(splits[11], (D,), 0.3, 2.0, (), jnp.float32)
    query_gain = jnp.clip(1.0 + 0.1 * jax.random.normal(splits[12], (DH,), jnp.float32), 0.5, 1.5)
    query_shift = centred(splits[13], (DH,), 0.3, 2.0, (), jnp.float32)
    key_gain = jnp.clip(1.0 + 0.1 * jax.random.normal(splits[14], (DH,), jnp.float32), 0.5, 1.5)
    norm2_gain = jnp.clip(1.0 + 0.1 * jax.random.normal(splits[15], (D,), jnp.float32), 0.5, 1.5)
    norm2_shift = centred(splits[16], (D,), 0.3, 2.0, (), jnp.float32)
    cotangent = centred(splits[17], (TOKENS, D), 1.0, 6.0, ((0, 8),))
    return {"tokens": tokens, "seg_ids": seg_ids, "qkv_weight": qkv_weight, "qkv_bias": qkv_bias, "out_weight": out_weight, "out_bias": out_bias, "up_weight": up_weight, "up_bias": up_bias, "down_weight": down_weight, "down_bias": down_bias, "norm1_gain": norm1_gain, "norm1_shift": norm1_shift, "query_gain": query_gain, "query_shift": query_shift, "key_gain": key_gain, "norm2_gain": norm2_gain, "norm2_shift": norm2_shift, "cotangent": cotangent}


norm_eps = 1e-06

@jax.custom_vjp
def low(v):
    return lax.optimization_barrier(v.astype(jnp.bfloat16)).astype(jnp.float32)

@jax.custom_vjp
def low_back(v):
    return v

def low_keep(v):
    return (low(v), None)

def low_pass(kept, grad):
    return (grad,)

def back_keep(v):
    return (v, None)

def back_low(kept, grad):
    return (low(grad),)
low.defvjp(low_keep, low_pass)
low_back.defvjp(back_keep, back_low)

def layer_norm(values, scale_vec, offset_vec):
    average = lax.optimization_barrier(jnp.mean(values, axis=-1, keepdims=True))
    centered = values - average
    variance = lax.optimization_barrier(jnp.mean(centered * centered, axis=-1, keepdims=True))
    return centered * lax.rsqrt(variance + norm_eps) * scale_vec + offset_vec

def forward(token_rows, seg_rows, qkv_weight, qkv_bias, out_weight, out_bias, up_weight, up_bias, down_weight, down_bias, norm1_gain, norm1_shift, query_gain, query_shift, key_gain, norm2_gain, norm2_shift):
    highest = lax.Precision.HIGHEST
    row_count = token_rows.shape[0]
    seq_count = row_count // SEQ_LEN
    normed = low(layer_norm(token_rows, norm1_gain, norm1_shift))
    project = low_back(jnp.einsum('td,sde->ste', normed, qkv_weight, precision=highest) + qkv_bias[:, None, :])
    head_view = project.reshape(3, seq_count, SEQ_LEN, H, DH)
    queries = low(layer_norm(head_view[0], query_gain, query_shift))
    key_vectors = low(layer_norm(head_view[1], key_gain, 0.0))
    value_vectors = low(head_view[2])
    scores = low_back(jnp.einsum('bqhd,bkhd->bhqk', queries, key_vectors, precision=highest) * DH ** (-0.5))
    seg_view = seg_rows.reshape(seq_count, SEQ_LEN)
    same_segment = seg_view[:, None, :, None] == seg_view[:, None, None, :]
    scores = jnp.where(same_segment, scores, -1e+30)
    row_max = lax.optimization_barrier(jnp.max(scores, axis=-1, keepdims=True))
    exponent = jnp.exp(scores - row_max)
    attn_weights = exponent / lax.optimization_barrier(jnp.sum(exponent, axis=-1, keepdims=True))
    mixture = jnp.einsum('bhqk,bkhd->bqhd', low(attn_weights), value_vectors, precision=highest)
    mixture = low(low_back(mixture.reshape(row_count, D)))
    attended = low_back(jnp.dot(mixture, out_weight, precision=highest) + out_bias)
    middle = token_rows + attended
    second = low(layer_norm(middle, norm2_gain, norm2_shift))
    hidden_pre = low_back(jnp.dot(second, up_weight, precision=highest) + up_bias)
    hidden = low(jax.nn.gelu(hidden_pre, approximate=False))
    return middle + jnp.dot(hidden, down_weight, precision=highest) + down_bias

def reference(tokens, seg_ids, qkv_weight, qkv_bias, out_weight, out_bias, up_weight, up_bias, down_weight, down_bias, norm1_gain, norm1_shift, query_gain, query_shift, key_gain, norm2_gain, norm2_shift, cotangent):
    params = tuple((member.astype(jnp.float32) for member in (qkv_weight, qkv_bias, out_weight, out_bias, up_weight, up_bias, down_weight, down_bias, norm1_gain, norm1_shift, query_gain, query_shift, key_gain, norm2_gain, norm2_shift)))
    seq_total = TOKENS // SEQ_LEN
    group_seqs = math.gcd(seq_total, max(1, 4096 // SEQ_LEN))
    group_rows = group_seqs * SEQ_LEN
    rounds = seq_total // group_seqs
    token_blocks = tokens.astype(jnp.float32).reshape(rounds, group_rows, D)
    seg_blocks = seg_ids.reshape(rounds, group_rows)
    cot_blocks = cotangent.astype(jnp.float32).reshape(rounds, group_rows, D)

    def one_group(totals, inputs_block):
        token_rows, seg_rows, cot_rows = inputs_block

        def apply_layer(rows_in, *weight_list):
            return forward(rows_in, seg_rows, *weight_list)
        result, pullback = jax.vjp(apply_layer, token_rows, *params)
        gradients = pullback(cot_rows)
        totals = jax.tree.map(lambda before_sum, added: before_sum + added, totals, tuple(gradients[1:]))
        return (totals, (result.astype(jnp.bfloat16), gradients[0].astype(jnp.bfloat16)))
    initial = tuple((jnp.zeros(member.shape, jnp.float32) for member in params))
    totals, (out_blocks, grad_blocks) = lax.scan(one_group, initial, (token_blocks, seg_blocks, cot_blocks))
    return (out_blocks.reshape(TOKENS, D), grad_blocks.reshape(TOKENS, D), totals[0], totals[1], totals[2], totals[3], totals[4], totals[5], totals[6], totals[7], totals[8], totals[9], totals[10], totals[11], totals[12], totals[13], totals[14])
```

```python
import functools
import math

import jax
import jax.numpy as jnp
from jax import lax
from jax.experimental import pallas as pl
from jax.experimental.pallas import tpu as pltpu
from jax.sharding import PartitionSpec as P

F32 = jnp.float32
BF16 = jnp.bfloat16
DH = 64
SEQ_LEN = 1024
NORM_EPS = 1e-06
PIECES = 8
SEG_COLS = 128
LOG2E = math.log2(math.e)
SCALE = DH ** (-0.5)
BITS_A = (2, 4, 1)
BITS_B = (4, 2, 1)
VMEM_LIMIT = 56 * 1024 * 1024


def mm(a, b):
    return lax.dot_general(a, b, (((1,), (0,)), ((), ())), preferred_element_type=F32)


def mm_nt(a, b):
    return lax.dot_general(a, b, (((1,), (1,)), ((), ())), preferred_element_type=F32)


def mm_tn(a, b):
    return lax.dot_general(a, b, (((0,), (0,)), ((), ())), preferred_element_type=F32)


def call(kernel, out_shape, flops=0, bytes_accessed=0, **kw):
    return pl.pallas_call(
        kernel,
        out_shape=out_shape,
        compiler_params=pltpu.CompilerParams(vmem_limit_bytes=VMEM_LIMIT),
        cost_estimate=pl.CostEstimate(
            flops=flops, bytes_accessed=bytes_accessed, transcendentals=0
        ),
        **kw,
    )


def sds(shape, dtype):
    return jax.ShapeDtypeStruct(shape, dtype)


def row_norm(x):
    mean = jnp.mean(x, axis=-1, keepdims=True)
    cen = x - mean
    rstd = lax.rsqrt(jnp.mean(cen * cen, axis=-1, keepdims=True) + NORM_EPS)
    return cen * rstd, rstd


def row_norm_back(f, n, rstd):
    mean_f = jnp.mean(f, axis=-1, keepdims=True)
    mean_fn = jnp.mean(f * n, axis=-1, keepdims=True)
    return (f - mean_f - n * mean_fn) * rstd


def col_norm(x):
    mean = jnp.mean(x, axis=0, keepdims=True)
    cen = x - mean
    rstd = lax.rsqrt(jnp.mean(cen * cen, axis=0, keepdims=True) + NORM_EPS)
    return cen * rstd, rstd


def col_norm_back(f, n, rstd):
    mean_f = jnp.mean(f, axis=0, keepdims=True)
    mean_fn = jnp.mean(f * n, axis=0, keepdims=True)
    return (f - mean_f - n * mean_fn) * rstd


def lane_fold(x):
    out = x[:, :128]
    for t in range(1, x.shape[1] // 128):
        out = out + x[:, t * 128 : (t + 1) * 128]
    return out


def norm1_kernel(blk_ref, x_ref, g_ref, s_ref, out_ref):
    n, _ = row_norm(x_ref[...].astype(F32))
    out_ref[...] = (n * g_ref[...] + s_ref[...]).astype(BF16)


def build_q_aug(q_pre, qg, qs, qaug_ref):
    n, rstd = col_norm(q_pre)
    q_low = (n * qg + qs).astype(BF16)
    scaled = q_low.astype(F32) * (SCALE * LOG2E)
    hi = scaled.astype(BF16)
    lo = (scaled - hi.astype(F32)).astype(BF16)
    qaug_ref[0:DH, :] = hi
    qaug_ref[DH : 2 * DH, :] = lo
    return n, rstd, q_low


def build_k_aug(k_pre, kg, kaug_ref):
    n, rstd = col_norm(k_pre)
    k_low = (n * kg).astype(BF16)
    kaug_ref[:, 0 : 2 * DH] = jnp.concatenate([k_low, k_low], axis=0).T
    return n, rstd, k_low


def attn_fwd_kernel(
    idx_ref, x_ref, w_ref, b_ref, qg_ref, qs_ref, kg_ref, kmask_ref, qhot_ref,
    qpre_ref, kpre_ref, vt_ref, wt_ref, mixt_ref, mix_ref, l_ref,
    qaug_ref, kaug_ref,
):
    part = 24
    e = PIECES * part
    rows = qhot_ref.shape[1]
    heads = e // DH
    for s in range(3):
        w = jnp.concatenate(
            [w_ref[idx_ref[p], s * part : (s + 1) * part, :] for p in range(PIECES)], axis=0
        ).astype(BF16)
        wt_ref[s * e : (s + 1) * e, :] = w
    qpre_ref[...] = mm_nt(wt_ref[0:e, :], x_ref[0:rows, :]) + b_ref[0:e, :]
    kpre_ref[...] = mm_nt(wt_ref[e : 2 * e, :], x_ref[...]) + b_ref[e : 2 * e, :]
    vt_ref[...] = (mm_nt(wt_ref[2 * e : 3 * e, :], x_ref[...]) + b_ref[2 * e : 3 * e, :]).astype(
        BF16
    )
    qaug_ref[2 * DH :, :] = qhot_ref[...]
    kaug_ref[:, 2 * DH :] = kmask_ref[...]
    ones = jnp.ones((16, x_ref.shape[0]), BF16)
    for h in range(heads):
        hs = slice(h * DH, (h + 1) * DH)
        build_q_aug(qpre_ref[hs, :], qg_ref[...], qs_ref[...], qaug_ref)
        build_k_aug(kpre_ref[hs, :], kg_ref[...], kaug_ref)
        prob = jnp.exp2(mm(kaug_ref[...], qaug_ref[...])).astype(BF16)
        vaug = jnp.concatenate([vt_ref[hs, :], ones], axis=0)
        o = mm(vaug, prob)
        total = o[DH : DH + 1, :]
        l_ref[h : h + 1, :] = total
        mixt_ref[hs, :] = (o[0:DH, :] / total).astype(BF16)
    mix_ref[...] = mixt_ref[...].T


def out_norm2_kernel(
    nslot, blk_ref, *refs
):
    idxs = refs[:nslot]
    x_ref = refs[nslot]
    mixes = refs[nslot + 1 : 2 * nslot + 1]
    ws = refs[2 * nslot + 1 : 3 * nslot + 1]
    ob_ref, g_ref, s_ref = refs[3 * nslot + 1 : 3 * nslot + 4]
    mid_ref, sec_ref, ow_ref = refs[3 * nslot + 4 :]
    part = 24
    acc = x_ref[...].astype(F32) + ob_ref[...]
    for k in range(nslot):
        w = jnp.concatenate(
            [ws[k][idxs[k][p], 3 * part : 4 * part, :] for p in range(PIECES)], axis=0
        ).astype(BF16)
        ow_ref[k] = w
        acc = acc + mm(mixes[k][...], w)
    mid_ref[...] = acc
    n, _ = row_norm(acc)
    sec_ref[...] = (n * g_ref[...] + s_ref[...]).astype(BF16)


def mlp_kernel(first, *refs):
    if first:
        (sec_ref, cot_ref, ua_ref, ub_ref, ba_ref, bb_ref, da_ref, db_ref) = refs[:8]
        outs = refs[8:]
    else:
        (sec_ref, cot_ref, ua_ref, ub_ref, ba_ref, bb_ref, da_ref, db_ref, acc_in, gs_in) = refs[:10]
        outs = refs[10:]
    (acc_ref, gs_ref, gua_ref, gub_ref, gda_ref, gdb_ref, gba_ref, gbb_ref) = outs
    part = ua_ref.shape[1]
    up = jnp.concatenate([ua_ref[0], ub_ref[0]], axis=0).astype(BF16)
    down = jnp.concatenate([da_ref[0], db_ref[0]], axis=0).astype(BF16)
    bias = jnp.concatenate([ba_ref[0], bb_ref[0]], axis=1)
    sec = sec_ref[...]
    cot = cot_ref[...]
    pre = mm_nt(sec, up) + bias
    cdf = 0.5 * (1.0 + lax.erf(pre * (1.0 / math.sqrt(2.0))))
    hid = (pre * cdf).astype(BF16)
    pdf = jnp.exp(-0.5 * pre * pre) * (1.0 / math.sqrt(2.0 * math.pi))
    gpre_f = mm_nt(cot, down) * (cdf + pre * pdf)
    gpre = gpre_f.astype(BF16)
    gb = jnp.sum(gpre.astype(F32), axis=0, keepdims=True)
    gba_ref[0] = gb[:, :part]
    gbb_ref[0] = gb[:, part:]
    acc_new = mm(hid, down)
    gs_new = mm(gpre, up)
    if first:
        @pl.when(pl.program_id(0) == 0)
        def _():
            acc_ref[...] = acc_new
            gs_ref[...] = gs_new

        @pl.when(pl.program_id(0) > 0)
        def _():
            acc_ref[...] += acc_new
            gs_ref[...] += gs_new
    else:
        @pl.when(pl.program_id(0) == 0)
        def _():
            acc_ref[...] = acc_in[...] + acc_new
            gs_ref[...] = gs_in[...] + gs_new

        @pl.when(pl.program_id(0) > 0)
        def _():
            acc_ref[...] += acc_new
            gs_ref[...] += gs_new
    gd = mm_tn(hid, cot)
    gda_ref[0] = gd[:part]
    gdb_ref[0] = gd[part:]
    gu = mm_tn(gpre, sec)
    gua_ref[0] = gu[:part]
    gub_ref[0] = gu[part:]


def mid_kernel(
    nslot, idx_ref, mid_ref, acc_ref, gs_ref, cot_ref, db_ref, g_ref, ow_ref, *refs
):
    mixts = refs[:nslot]
    bo_ref, gm_ref, gmt_ref, gow_ref, st_ref = refs[nslot:]
    part = 24
    mid = mid_ref[...]
    bo_ref[...] = (mid + acc_ref[...] + db_ref[...]).astype(BF16)
    n, rstd = row_norm(mid)
    e = gs_ref[...]
    cot = cot_ref[...].astype(F32)
    gm = cot + row_norm_back(e * g_ref[...], n, rstd)
    gm_ref[...] = gm
    gm_low = gm.astype(BF16)
    st_ref[0:1, :] = jnp.sum(e * n, axis=0, keepdims=True)
    st_ref[1:2, :] = jnp.sum(e, axis=0, keepdims=True)
    st_ref[2:3, :] = jnp.sum(gm_low.astype(F32), axis=0, keepdims=True)
    st_ref[3:4, :] = jnp.sum(cot, axis=0, keepdims=True)
    st_ref[4:8, :] = jnp.zeros((4, mid.shape[1]), F32)
    for k in range(nslot):
        gmt_ref[k] = mm_nt(ow_ref[k], gm_low).astype(BF16)
        g = mm(mixts[k][...], gm_low)
        for p in range(PIECES):
            gow_ref[idx_ref[p], k * part : (k + 1) * part, :] = g[p * part : (p + 1) * part, :]


def attn_bwd_kernel(
    first, idx_ref, x_ref, qpre_ref, kpre_ref, vt_ref, wt_ref, gmt_ref, mixt_ref, l_ref,
    qg_ref, qs_ref, kg_ref, kmask_ref, qhot_ref, *refs
):
    if first:
        gw_ref, gn_ref, st_ref, gb_ref, qaug_ref, kaug_ref, gpt_ref = refs
    else:
        gn_in, gw_ref, gn_ref, st_ref, gb_ref, qaug_ref, kaug_ref, gpt_ref = refs
    part = 24
    e = PIECES * part
    rows = qhot_ref.shape[1]
    full = x_ref.shape[0]
    heads = e // DH
    qaug_ref[2 * DH :, :] = qhot_ref[...]
    kaug_ref[:, 2 * DH :] = kmask_ref[...]
    qg, qs, kg = qg_ref[...], qs_ref[...], kg_ref[...]
    qg_sum = jnp.zeros((DH, 128), F32)
    qs_sum = jnp.zeros((DH, 128), F32)
    kg_sum = jnp.zeros((DH, 128), F32)
    one_rows = (lax.broadcasted_iota(jnp.int32, (DH, full), 0) < 3).astype(F32).astype(BF16)
    row_no = lax.broadcasted_iota(jnp.int32, (DH, rows), 0)
    for h in range(heads):
        hs = slice(h * DH, (h + 1) * DH)
        qn, qr, q_low = build_q_aug(qpre_ref[hs, :], qg, qs, qaug_ref)
        kn, kr, k_low = build_k_aug(kpre_ref[hs, :], kg, kaug_ref)
        inv = 1.0 / l_ref[h : h + 1, :]
        go = gmt_ref[hs, :].astype(F32) * inv
        go_low = go.astype(BF16)
        delta = -jnp.sum(go * mixt_ref[hs, :].astype(F32), axis=0, keepdims=True)
        d0 = delta.astype(BF16).astype(F32)
        d1 = (delta - d0).astype(BF16).astype(F32)
        d2 = delta - d0 - d1
        extra = jnp.where(
            row_no == 0, d0, jnp.where(row_no == 1, d1, jnp.where(row_no == 2, d2, 0.0))
        ).astype(BF16)
        goaug = jnp.concatenate([go_low, extra], axis=0)
        vaug = jnp.concatenate([vt_ref[hs, :], one_rows], axis=0).T
        prob = jnp.exp2(mm(kaug_ref[...], qaug_ref[...]))
        ds = (prob * mm(vaug, goaug)).astype(BF16)
        gv = mm_nt(go_low, prob.astype(BF16))
        gk = mm_nt(q_low, ds) * SCALE
        gq = mm(k_low, ds) * SCALE
        qg_sum += lane_fold(gq * qn)
        qs_sum += lane_fold(gq)
        kg_sum += lane_fold(gk * kn)
        gpt_ref[h * DH : (h + 1) * DH, 0:rows] = col_norm_back(gq * qg, qn, qr).astype(BF16)
        gpt_ref[e + h * DH : e + (h + 1) * DH, :] = col_norm_back(gk * kg, kn, kr).astype(BF16)
        gpt_ref[2 * e + h * DH : 2 * e + (h + 1) * DH, :] = gv.astype(BF16)
    st_ref[0] = qg_sum
    st_ref[1] = qs_sum
    st_ref[2] = kg_sum
    gpq = gpt_ref[0:e, 0:rows]
    gpkv = gpt_ref[e : 3 * e, :]
    gb_ref[0:e, :] = lane_fold(gpq.astype(F32))
    gb_ref[e : 3 * e, :] = lane_fold(gpkv.astype(F32))
    gwq = mm(gpq, x_ref[0:rows, :])
    gwkv = mm(gpkv, x_ref[...])
    for p in range(PIECES):
        at = idx_ref[p]
        gw_ref[at, 0:part, :] = gwq[p * part : (p + 1) * part, :]
        gw_ref[at, part : 2 * part, :] = gwkv[p * part : (p + 1) * part, :]
        gw_ref[at, 2 * part : 3 * part, :] = gwkv[e + p * part : e + (p + 1) * part, :]
    gnq = mm_tn(gpq, wt_ref[0:e, :])
    gnkv = mm_tn(gpkv, wt_ref[e : 3 * e, :])
    if first:
        gn_ref[0:rows, :] = gnkv[0:rows] + gnq
        gn_ref[rows:, :] = gnkv[rows:]
    else:
        gn_ref[0:rows, :] = gn_in[0:rows, :] + gnkv[0:rows] + gnq
        gn_ref[rows:, :] = gn_in[rows:, :] + gnkv[rows:]


def norm1_stats_kernel(blk_ref, x_ref, gn_ref, out_ref):
    n, _ = row_norm(x_ref[...].astype(F32))
    e = gn_ref[...]

    @pl.when(pl.program_id(0) == 0)
    def _():
        out_ref[...] = jnp.zeros_like(out_ref)

    out_ref[0:1, :] += jnp.sum(e * n, axis=0, keepdims=True)
    out_ref[1:2, :] += jnp.sum(e, axis=0, keepdims=True)


def final_kernel(blk_ref, x_ref, gn_ref, got_ref, gm_ref, g_ref, out_ref):
    n, rstd = row_norm(x_ref[...].astype(F32))
    f = (gn_ref[...] + got_ref[...]) * g_ref[...]
    out_ref[...] = (gm_ref[...] + row_norm_back(f, n, rstd)).astype(BF16)


def unpack_kernel(idx_ref, s_ref, out_ref):
    groups = out_ref.shape[0]
    part = s_ref.shape[1] // groups
    for g in range(groups):
        whole = jnp.concatenate(
            [s_ref[idx_ref[p], g * part : (g + 1) * part, :] for p in range(PIECES)], axis=0
        )
        out_ref[g] = whole.T


def unpack_rows_kernel(idx_ref, s_ref, out_ref):
    part = s_ref.shape[1]
    for p in range(PIECES):
        out_ref[p * part : (p + 1) * part, :] = s_ref[idx_ref[p]]


def from_slot(a, k, size):
    return lax.ppermute(a, "mp", [(s, (s - k) % size) for s in range(size)])


def to_slot(a, k, size):
    return lax.ppermute(a, "mp", [(s, (s + k) % size) for s in range(size)])


def swap_plane(a, bit, size):
    return lax.ppermute(a, "dp", [(d, d ^ bit) for d in range(size)])


def gather_plane(piece, bits, size):
    state = piece[None]
    for bit in bits[:-1]:
        state = jnp.concatenate([state, swap_plane(state, bit, size)], axis=0)
    return state, swap_plane(state, bits[-1], size)


def gather_whole(piece, bits, size):
    return jnp.concatenate(gather_plane(piece, bits, size), axis=0)


def reduce_plane(keep, send, bits, size):
    cur = keep + swap_plane(send, bits[2], size)
    cur = cur[:2] + swap_plane(cur[2:], bits[1], size)
    cur = cur[:1] + swap_plane(cur[1:], bits[0], size)
    return cur[0]


def storage_of(r, bits):
    return sum(jnp.where((r & bit) != 0, 1 << t, 0) for t, bit in enumerate(bits))


def offset_of(s, bits):
    return sum(bit for t, bit in enumerate(bits) if (s >> t) & 1)


def shards(
    tokens,
    seg_ids,
    qkv_weight,
    qkv_bias,
    out_weight,
    out_bias,
    up_weight,
    up_bias,
    down_weight,
    down_bias,
    norm1_gain,
    norm1_shift,
    query_gain,
    query_shift,
    key_gain,
    norm2_gain,
    norm2_shift,
    cotangent,
):
    ndp = lax.axis_size("dp")
    nmp = lax.axis_size("mp")
    dp_no = lax.axis_index("dp")
    mp_no = lax.axis_index("mp")
    me = dp_no % PIECES
    row_count, width = tokens.shape
    share = row_count // nmp
    full = SEQ_LEN
    assert full == 2 * share
    e = qkv_weight.shape[2]
    part = e // PIECES
    units = up_weight.shape[1]
    upart = units // PIECES

    vmem = pl.BlockSpec(memory_space=pltpu.VMEM)
    smem = pl.BlockSpec(memory_space=pltpu.SMEM)

    qkv_t = jnp.swapaxes(qkv_weight, 1, 2).reshape(3, PIECES, part, width)
    out_p = out_weight.reshape(1, PIECES, part, width)
    att0 = (
        jnp.concatenate([qkv_t, out_p], axis=0)
        .transpose(1, 0, 2, 3)
        .reshape(PIECES, 4 * part, width)
        .astype(F32)
    )
    up_t = up_weight.T.reshape(PIECES, upart, width)
    down_p = down_weight.reshape(PIECES, upart, width)

    def pick(a, bits, s):
        return lax.dynamic_index_in_dim(a, me ^ offset_of(s, bits), 0, keepdims=False)

    up_half = [
        jnp.stack([pick(up_t, BITS_A, s) for s in half]) for half in (range(4), range(4, 8))
    ]
    down_half = [
        jnp.stack([pick(down_p, BITS_B, s) for s in half]) for half in (range(4), range(4, 8))
    ]
    ub = up_bias.reshape(PIECES, 1, upart)
    ub0 = jnp.stack([pick(ub, BITS_A, s) for s in range(PIECES)])

    att_piece = lax.dynamic_index_in_dim(att0, me, 0, keepdims=False)
    up_piece = up_half[0][0].astype(F32)
    down_piece = down_half[0][0].astype(F32)
    bias_pack = jnp.concatenate([qkv_bias.reshape(-1), ub0.reshape(-1)])

    att_bits = [BITS_A if k % 2 else BITS_B for k in range(nmp)]
    att = [att0]
    bias = [bias_pack]
    for k in range(1, nmp):
        bias.append(from_slot(bias_pack, k, nmp))
        att.append(gather_whole(from_slot(att_piece, k, nmp), att_bits[k], ndp))
    up = [up_half]
    down = [down_half]
    for k in range(1, nmp):
        up.append(gather_plane(from_slot(up_piece, k, nmp), BITS_A, ndp))
        down.append(gather_plane(from_slot(down_piece, k, nmp), BITS_B, ndp))

    idx_a = storage_of(jnp.arange(PIECES, dtype=jnp.int32) ^ me, BITS_A).astype(jnp.int32)
    idx_b = storage_of(jnp.arange(PIECES, dtype=jnp.int32) ^ me, BITS_B).astype(jnp.int32)
    idx_of = {BITS_A: idx_a, BITS_B: idx_b}
    idx_same = jnp.arange(PIECES, dtype=jnp.int32)
    att_idx = [idx_same] + [idx_of[att_bits[k]] for k in range(1, nmp)]

    block = 256
    per = share // block
    steps = 2 * per
    tile_no = jnp.arange(steps, dtype=jnp.int32)
    blk = jnp.where(tile_no < per, mp_no * per + tile_no, (mp_no ^ 1) * per + tile_no - per).astype(
        jnp.int32
    )
    row1 = lambda v: v.reshape(1, -1)
    const2 = lambda t, b: (0, 0)
    tok_spec = pl.BlockSpec((block, width), lambda t, b: (b[t], 0))
    run_spec = pl.BlockSpec((block, width), lambda t, b: (t, 0))
    vec_spec = pl.BlockSpec((1, width), const2)

    normed = call(
        norm1_kernel,
        sds((full, width), BF16),
        flops=full * width * 10,
        bytes_accessed=full * width * 4,
        grid_spec=pltpu.PrefetchScalarGridSpec(
            num_scalar_prefetch=1,
            grid=(steps,),
            in_specs=[tok_spec, vec_spec, vec_spec],
            out_specs=run_spec,
        ),
    )(blk, tokens, row1(norm1_gain), row1(norm1_shift))

    seg_own = lax.dynamic_slice_in_dim(seg_ids, mp_no * share, share, 0)
    seg_other = lax.dynamic_slice_in_dim(seg_ids, (mp_no ^ 1) * share, share, 0)
    seg_keys = jnp.concatenate([seg_own, seg_other])
    qhot = (
        lax.broadcasted_iota(jnp.int32, (SEG_COLS, share), 0) == seg_own[None, :]
    ).astype(BF16)
    kmask = jnp.where(
        lax.broadcasted_iota(jnp.int32, (full, SEG_COLS), 1) == seg_keys[:, None], 0.0, -1e30
    ).astype(BF16)
    col = lambda v: v.reshape(-1, 1)
    qg, qs, kg = col(query_gain), col(query_shift), col(key_gain)

    heads_state = []
    for k in range(nmp):
        heads_state.append(
            call(
                attn_fwd_kernel,
                (
                    sds((e, share), F32),
                    sds((e, full), F32),
                    sds((e, full), BF16),
                    sds((3 * e, width), BF16),
                    sds((e, share), BF16),
                    sds((share, e), BF16),
                    sds((8, share), F32),
                ),
                flops=2 * (full * width * e * 5 // 2 + full * share * e * 8),
                bytes_accessed=8_000_000,
                in_specs=[smem] + [vmem] * 8,
                out_specs=(vmem,) * 7,
                scratch_shapes=[
                    pltpu.VMEM((2 * DH + SEG_COLS, share), BF16),
                    pltpu.VMEM((full, 2 * DH + SEG_COLS), BF16),
                ],
            )(
                att_idx[k],
                normed,
                att[k],
                bias[k][: 3 * e].reshape(3 * e, 1),
                qg,
                qs,
                kg,
                kmask,
                qhot,
            )
        )

    own_spec = pl.BlockSpec((share, width), lambda t, b: (b[0] // per, 0))
    whole = lambda shape: pl.BlockSpec(shape, lambda t, b: (0,) * len(shape))
    middle, second, out_full = call(
        functools.partial(out_norm2_kernel, nmp),
        (
            sds((share, width), F32),
            sds((share, width), BF16),
            sds((nmp, e, width), BF16),
        ),
        flops=2 * share * width * e * nmp,
        bytes_accessed=16_000_000,
        grid_spec=pltpu.PrefetchScalarGridSpec(
            num_scalar_prefetch=1,
            grid=(1,),
            in_specs=[smem] * nmp
            + [own_spec]
            + [whole((share, e))] * nmp
            + [whole((PIECES, 4 * part, width))] * nmp
            + [whole((1, width))] * 3,
            out_specs=(
                whole((share, width)),
                whole((share, width)),
                whole((nmp, e, width)),
            ),
        ),
    )(
        blk,
        *att_idx,
        tokens,
        *[st[5] for st in heads_state],
        *att,
        row1(out_bias),
        row1(norm2_gain),
        row1(norm2_shift),
    )

    cot_own = lax.dynamic_slice_in_dim(cotangent, mp_no * share, share, 0)
    half = PIECES // 2
    piece_spec = pl.BlockSpec((1, upart, width), lambda t: (t, 0, 0))
    swap_spec = pl.BlockSpec((1, upart, width), lambda t: ((t % 2) * 2 + t // 2, 0, 0))
    bias_spec = pl.BlockSpec((1, 1, upart), lambda t: (t, 0, 0))
    rows_spec = pl.BlockSpec((share, width), lambda t: (0, 0))
    acc = None
    up_grads, down_grads, ub_grads = [], [], []
    for k in range(nmp):
        first = k == 0
        ubk = bias[k][3 * e :].reshape(PIECES, 1, upart)
        args = [second, cot_own, up[k][0], up[k][1], ubk[:half], ubk[half:], down[k][0], down[k][1]]
        specs = [rows_spec, rows_spec, piece_spec, piece_spec, bias_spec, bias_spec, swap_spec, swap_spec]
        alias = {}
        if not first:
            args += list(acc)
            specs += [rows_spec, rows_spec]
            alias = {8: 0, 9: 1}
        res = call(
            functools.partial(mlp_kernel, first),
            (
                sds((share, width), F32),
                sds((share, width), F32),
                *[sds((half, upart, width), F32)] * 4,
                *[sds((half, 1, upart), F32)] * 2,
            ),
            flops=2 * share * width * units * 6,
            bytes_accessed=16_000_000,
            grid=(half,),
            in_specs=specs,
            out_specs=(
                rows_spec,
                rows_spec,
                piece_spec,
                piece_spec,
                swap_spec,
                swap_spec,
                bias_spec,
                bias_spec,
            ),
            input_output_aliases=alias,
        )(*args)
        acc = res[:2]
        up_grads.append(reduce_plane(res[2], res[3], BITS_A, ndp))
        down_grads.append(reduce_plane(res[4], res[5], BITS_B, ndp))
        ub_grads.append(jnp.concatenate([res[6], res[7]], axis=0)[:, 0, :])

    block_out, grad_mid, gmt, out_grads, mid_stats = call(
        functools.partial(mid_kernel, nmp),
        (
            sds((share, width), BF16),
            sds((share, width), F32),
            sds((nmp, e, share), BF16),
            sds((PIECES, nmp * part, width), F32),
            sds((8, width), F32),
        ),
        flops=2 * share * width * e * nmp * 2,
        bytes_accessed=12_000_000,
        in_specs=[smem] + [vmem] * (7 + nmp),
        out_specs=(vmem,) * 5,
    )(
        idx_a,
        middle,
        acc[0],
        acc[1],
        cot_own,
        row1(down_bias),
        row1(norm2_gain),
        out_full,
        *[st[4] for st in heads_state],
    )

    gn = None
    qkv_grads, head_stats, qkvb_grads = [], [], []
    for k in range(nmp):
        first = k == 0
        st = heads_state[k]
        args = [
            idx_of[att_bits[k]], normed, st[0], st[1], st[2], st[3], gmt[k], st[4], st[6],
            qg, qs, kg, kmask, qhot,
        ]
        alias = {}
        if not first:
            args.append(gn)
            alias = {len(args) - 1: 1}
        gw, gn, hst, gb = call(
            functools.partial(attn_bwd_kernel, first),
            (
                sds((PIECES, 3 * part, width), F32),
                sds((full, width), F32),
                sds((3, DH, 128), F32),
                sds((3 * e, 128), F32),
            ),
            flops=2 * (full * width * e * 5 + full * share * e * 20),
            bytes_accessed=14_000_000,
            in_specs=[smem] + [vmem] * (len(args) - 1),
            out_specs=(vmem,) * 4,
            scratch_shapes=[
                pltpu.VMEM((2 * DH + SEG_COLS, share), BF16),
                pltpu.VMEM((full, 2 * DH + SEG_COLS), BF16),
                pltpu.VMEM((3 * e, full), BF16),
            ],
            input_output_aliases=alias,
        )(*args)
        qkv_grads.append(reduce_plane(gw[:half], gw[half:], att_bits[k], ndp))
        head_stats.append(hst)
        qkvb_grads.append(jnp.sum(gb, axis=1))

    got = lax.ppermute(gn[share:], "mp", [(s, s ^ 1) for s in range(nmp)])
    n1_stats = call(
        norm1_stats_kernel,
        sds((8, width), F32),
        flops=full * width * 10,
        bytes_accessed=full * width * 6,
        grid_spec=pltpu.PrefetchScalarGridSpec(
            num_scalar_prefetch=1,
            grid=(steps,),
            in_specs=[tok_spec, run_spec],
            out_specs=pl.BlockSpec((8, width), const2),
        ),
    )(blk, tokens, gn)
    input_grad = call(
        final_kernel,
        sds((share, width), BF16),
        flops=share * width * 20,
        bytes_accessed=share * width * 16,
        grid_spec=pltpu.PrefetchScalarGridSpec(
            num_scalar_prefetch=1,
            grid=(per,),
            in_specs=[tok_spec, run_spec, run_spec, run_spec, vec_spec],
            out_specs=run_spec,
        ),
    )(blk, tokens, gn, got, grad_mid, row1(norm1_gain))

    def finish(pieces, bits):
        total = pieces[0]
        for k in range(1, nmp):
            total = total + to_slot(pieces[k], k, nmp)
        bit = PIECES
        while bit < ndp:
            total = total + swap_plane(total, bit, ndp)
            bit *= 2
        return gather_whole(total, bits, ndp)

    up_state = finish(up_grads, BITS_A)
    down_state = finish(down_grads, BITS_B)
    out_piece = reduce_plane(out_grads[:half], out_grads[half:], BITS_A, ndp)
    out_state = finish([out_piece[k * part : (k + 1) * part] for k in range(nmp)], BITS_A)
    qkv_state = finish(qkv_grads, BITS_B)

    def unpack(kernel, state, idx, shape):
        return call(
            kernel,
            sds(shape, F32),
            bytes_accessed=2 * 4 * math.prod(shape),
            in_specs=[smem, vmem],
            out_specs=vmem,
        )(idx, state)

    up_weight_grad = unpack(unpack_kernel, up_state, idx_a, (1, width, units))[0]
    down_weight_grad = unpack(unpack_rows_kernel, down_state, idx_b, (units, width))
    out_weight_grad = unpack(unpack_rows_kernel, out_state, idx_a, (e, width))
    qkv_weight_grad = unpack(unpack_kernel, qkv_state, idx_b, (3, width, e))

    head_sum = jnp.sum(sum(head_stats), axis=-1)
    copied = jnp.concatenate(
        [mid_stats[:4].reshape(-1), n1_stats[:2].reshape(-1), head_sum.reshape(-1)]
    )
    own_parts = [
        jnp.concatenate([qkvb_grads[k], jnp.take(ub_grads[k], idx_a, axis=0).reshape(-1)])
        for k in range(nmp)
    ]
    small = jnp.concatenate([copied] + own_parts)
    bit = 1
    while bit < ndp:
        small = small + swap_plane(small, bit, ndp)
        bit *= 2
    nc = copied.shape[0]
    no = own_parts[0].shape[0]
    small_sum = small[: nc + no]
    for k in range(1, nmp):
        sent = jnp.concatenate([small[:nc], small[nc + k * no : nc + (k + 1) * no]])
        small_sum = small_sum + to_slot(sent, k, nmp)
    rows_of = small_sum[: 6 * width].reshape(6, width)
    heads_of = small_sum[6 * width : nc].reshape(3, DH)
    qkv_bias_grad = small_sum[nc : nc + 3 * e].reshape(3, e)
    up_bias_grad = small_sum[nc + 3 * e :]
    return (
        block_out,
        input_grad,
        qkv_weight_grad,
        qkv_bias_grad,
        out_weight_grad,
        rows_of[2],
        up_weight_grad,
        up_bias_grad,
        down_weight_grad,
        rows_of[3],
        rows_of[4],
        rows_of[5],
        heads_of[0],
        heads_of[1],
        heads_of[2],
        rows_of[0],
        rows_of[1],
    )


def solution(mesh):
    in_specs = (
        P("dp", None),
        P("dp"),
        P(None, None, "mp"),
        P(None, "mp"),
        P("mp", None),
        P(),
        P(None, "mp"),
        P("mp"),
        P("mp", None),
        P(),
        P(),
        P(),
        P(),
        P(),
        P(),
        P(),
        P(),
        P("dp", None),
    )
    out_specs = (
        P(("dp", "mp"), None),
        P(("dp", "mp"), None),
        P(None, None, "mp"),
        P(None, "mp"),
        P("mp", None),
        P(),
        P(None, "mp"),
        P("mp"),
        P("mp", None),
        P(),
        P(),
        P(),
        P(),
        P(),
        P(),
        P(),
        P(),
    )
    return jax.shard_map(shards, mesh=mesh, in_specs=in_specs, out_specs=out_specs, check_vma=False)
```

```python
import functools
import math

import jax
import jax.numpy as jnp
from jax import lax
from jax.experimental import pallas as pl
from jax.experimental.pallas import tpu as pltpu
from jax.sharding import PartitionSpec as P

F32 = jnp.float32
BF16 = jnp.bfloat16
DH = 64
SEQ_LEN = 1024
NORM_EPS = 1e-06
PIECES = 8
SEG_COLS = 128
LOG2E = math.log2(math.e)
SCALE = DH ** (-0.5)
BITS_A = (2, 4, 1)
BITS_B = (4, 2, 1)
VMEM_LIMIT = 56 * 1024 * 1024


def mm(a, b):
    return lax.dot_general(a, b, (((1,), (0,)), ((), ())), preferred_element_type=F32)


def mm_nt(a, b):
    return lax.dot_general(a, b, (((1,), (1,)), ((), ())), preferred_element_type=F32)


def mm_tn(a, b):
    return lax.dot_general(a, b, (((0,), (0,)), ((), ())), preferred_element_type=F32)


def call(kernel, out_shape, flops=0, bytes_accessed=0, **kw):
    return pl.pallas_call(
        kernel,
        out_shape=out_shape,
        compiler_params=pltpu.CompilerParams(vmem_limit_bytes=VMEM_LIMIT),
        cost_estimate=pl.CostEstimate(
            flops=flops, bytes_accessed=bytes_accessed, transcendentals=0
        ),
        **kw,
    )


def sds(shape, dtype):
    return jax.ShapeDtypeStruct(shape, dtype)


def row_norm(x):
    mean = jnp.mean(x, axis=-1, keepdims=True)
    cen = x - mean
    rstd = lax.rsqrt(jnp.mean(cen * cen, axis=-1, keepdims=True) + NORM_EPS)
    return cen * rstd, rstd


def row_norm_back(f, n, rstd):
    mean_f = jnp.mean(f, axis=-1, keepdims=True)
    mean_fn = jnp.mean(f * n, axis=-1, keepdims=True)
    return (f - mean_f - n * mean_fn) * rstd


def col_norm(x):
    mean = jnp.mean(x, axis=0, keepdims=True)
    cen = x - mean
    rstd = lax.rsqrt(jnp.mean(cen * cen, axis=0, keepdims=True) + NORM_EPS)
    return cen * rstd, rstd


def col_norm_back(f, n, rstd):
    mean_f = jnp.mean(f, axis=0, keepdims=True)
    mean_fn = jnp.mean(f * n, axis=0, keepdims=True)
    return (f - mean_f - n * mean_fn) * rstd


def lane_fold(x):
    out = x[:, :128]
    for t in range(1, x.shape[1] // 128):
        out = out + x[:, t * 128 : (t + 1) * 128]
    return out


def norm1_kernel(blk_ref, x_ref, g_ref, s_ref, out_ref):
    n, _ = row_norm(x_ref[...].astype(F32))
    out_ref[...] = (n * g_ref[...] + s_ref[...]).astype(BF16)


def build_q_aug(q_pre, qg, qs, qaug_ref):
    n, rstd = col_norm(q_pre)
    q_low = (n * qg + qs).astype(BF16)
    scaled = q_low.astype(F32) * (SCALE * LOG2E)
    hi = scaled.astype(BF16)
    lo = (scaled - hi.astype(F32)).astype(BF16)
    qaug_ref[0:DH, :] = hi
    qaug_ref[DH : 2 * DH, :] = lo
    return n, rstd, q_low


def build_k_aug(k_pre, kg, kaug_ref):
    n, rstd = col_norm(k_pre)
    k_low = (n * kg).astype(BF16)
    kaug_ref[:, 0 : 2 * DH] = jnp.concatenate([k_low, k_low], axis=0).T
    return n, rstd, k_low


def attn_fwd_kernel(
    at, ia_ref, ib_ref, x_ref, wa_ref, wb_ref, b_ref, qg_ref, qs_ref, kg_ref, kmask_ref, qhot_ref,
    qpre_ref, kpre_ref, vt_ref, wt_ref, ow_ref, mixt_ref, mixf_ref, l_ref,
    qaug_ref, kaug_ref,
):
    part = 24
    e = PIECES * part
    rows = qhot_ref.shape[1]
    heads = e // DH
    for s, (w_ref, i_ref, off) in enumerate(
        ((wa_ref, ia_ref, 0), (wa_ref, ia_ref, part), (wb_ref, ib_ref, 0), (wb_ref, ib_ref, part))
    ):
        w = jnp.concatenate(
            [w_ref[i_ref[p], at, off : off + part, :] for p in range(PIECES)], axis=0
        ).astype(BF16)
        if s < 3:
            wt_ref[s * e : (s + 1) * e, :] = w
        else:
            ow_ref[...] = w
    qpre_ref[...] = mm_nt(wt_ref[0:e, :], x_ref[0:rows, :]) + b_ref[0:e, :]
    kpre_ref[...] = mm_nt(wt_ref[e : 2 * e, :], x_ref[...]) + b_ref[e : 2 * e, :]
    vt_ref[...] = (mm_nt(wt_ref[2 * e : 3 * e, :], x_ref[...]) + b_ref[2 * e : 3 * e, :]).astype(
        BF16
    )
    qaug_ref[2 * DH :, :] = qhot_ref[...]
    kaug_ref[:, 2 * DH :] = kmask_ref[...]
    ones = jnp.ones((16, x_ref.shape[0]), BF16)
    for h in range(heads):
        hs = slice(h * DH, (h + 1) * DH)
        build_q_aug(qpre_ref[hs, :], qg_ref[...], qs_ref[...], qaug_ref)
        build_k_aug(kpre_ref[hs, :], kg_ref[...], kaug_ref)
        prob = jnp.exp2(mm(kaug_ref[...], qaug_ref[...])).astype(BF16)
        vaug = jnp.concatenate([vt_ref[hs, :], ones], axis=0)
        o = mm(vaug, prob)
        total = o[DH : DH + 1, :]
        l_ref[h : h + 1, :] = total
        mix = o[0:DH, :] / total
        mixf_ref[hs, :] = mix
        mixt_ref[hs, :] = mix.astype(BF16)


def out_norm2_kernel(nslot, blk_ref, x_ref, *refs):
    mixes = refs[:nslot]
    ws = refs[nslot : 2 * nslot]
    ob_ref, g_ref, s_ref, mid_ref, sec_ref = refs[2 * nslot :]
    acc = x_ref[...].astype(F32) + ob_ref[...]
    for k in range(nslot):
        acc = acc + mm_tn(mixes[k][...], ws[k][...])
    mid_ref[...] = acc
    n, _ = row_norm(acc)
    sec_ref[...] = (n * g_ref[...] + s_ref[...]).astype(BF16)


def mlp_kernel(first, *refs):
    if first:
        (sec_ref, cot_ref, ua_ref, ub_ref, ba_ref, bb_ref, da_ref, db_ref) = refs[:8]
        outs = refs[8:]
    else:
        (sec_ref, cot_ref, ua_ref, ub_ref, ba_ref, bb_ref, da_ref, db_ref, acc_in, gs_in) = refs[:10]
        outs = refs[10:]
    (acc_ref, gs_ref, gua_ref, gub_ref, gda_ref, gdb_ref, gba_ref, gbb_ref) = outs
    part = ua_ref.shape[1]
    up = jnp.concatenate([ua_ref[0], ub_ref[0]], axis=0).astype(BF16)
    down = jnp.concatenate([da_ref[0], db_ref[0]], axis=0).astype(BF16)
    bias = jnp.concatenate([ba_ref[0], bb_ref[0]], axis=1)
    sec = sec_ref[...]
    cot = cot_ref[...]
    pre = mm_nt(sec, up) + bias
    cdf = 0.5 * (1.0 + lax.erf(pre * (1.0 / math.sqrt(2.0))))
    hid = (pre * cdf).astype(BF16)
    pdf = jnp.exp(-0.5 * pre * pre) * (1.0 / math.sqrt(2.0 * math.pi))
    gpre_f = mm_nt(cot, down) * (cdf + pre * pdf)
    gpre = gpre_f.astype(BF16)
    gb = jnp.sum(gpre.astype(F32), axis=0, keepdims=True)
    gba_ref[0] = gb[:, :part]
    gbb_ref[0] = gb[:, part:]
    acc_new = mm(hid, down)
    gs_new = mm(gpre, up)
    if first:
        @pl.when(pl.program_id(0) == 0)
        def _():
            acc_ref[...] = acc_new
            gs_ref[...] = gs_new

        @pl.when(pl.program_id(0) > 0)
        def _():
            acc_ref[...] += acc_new
            gs_ref[...] += gs_new
    else:
        @pl.when(pl.program_id(0) == 0)
        def _():
            acc_ref[...] = acc_in[...] + acc_new
            gs_ref[...] = gs_in[...] + gs_new

        @pl.when(pl.program_id(0) > 0)
        def _():
            acc_ref[...] += acc_new
            gs_ref[...] += gs_new
    gd = mm_tn(hid, cot)
    gda_ref[0] = gd[:part]
    gdb_ref[0] = gd[part:]
    gu = mm_tn(gpre, sec)
    gua_ref[0] = gu[:part]
    gub_ref[0] = gu[part:]


def mid_kernel(
    nslot, idx_ref, mid_ref, acc_ref, gs_ref, cot_ref, db_ref, g_ref, *refs
):
    ows = refs[:nslot]
    mixts = refs[nslot : 2 * nslot]
    gmts = refs[2 * nslot : 3 * nslot]
    bo_ref, gm_ref, gow_keep, gow_send, st_ref = refs[3 * nslot :]
    part = 24
    mid = mid_ref[...]
    bo_ref[...] = (mid + acc_ref[...] + db_ref[...]).astype(BF16)
    n, rstd = row_norm(mid)
    e = gs_ref[...]
    cot = cot_ref[...].astype(F32)
    gm = cot + row_norm_back(e * g_ref[...], n, rstd)
    gm_ref[...] = gm
    gm_low = gm.astype(BF16)
    st_ref[0:1, :] = jnp.sum(e * n, axis=0, keepdims=True)
    st_ref[1:2, :] = jnp.sum(e, axis=0, keepdims=True)
    st_ref[2:3, :] = jnp.sum(gm_low.astype(F32), axis=0, keepdims=True)
    st_ref[3:4, :] = jnp.sum(cot, axis=0, keepdims=True)
    st_ref[4:8, :] = jnp.zeros((4, mid.shape[1]), F32)
    for k in range(nslot):
        gmts[k][...] = mm_nt(ows[k][...], gm_low).astype(BF16)
        g = mm(mixts[k][...], gm_low)
        for p in range(PIECES):
            at = idx_ref[p]
            rows = slice(k * part, (k + 1) * part)

            @pl.when(at < PIECES // 2)
            def _():
                gow_keep[at, rows, :] = g[p * part : (p + 1) * part, :]

            @pl.when(at >= PIECES // 2)
            def _():
                gow_send[at - PIECES // 2, rows, :] = g[p * part : (p + 1) * part, :]


def attn_bwd_kernel(
    first, idx_ref, x_ref, qpre_ref, kpre_ref, vt_ref, wt_ref, gmt_ref, mixt_ref, l_ref,
    qg_ref, qs_ref, kg_ref, kmask_ref, qhot_ref, *refs
):
    if first:
        gk_ref, gs_ref, gn_ref, st_ref, gb_ref, qaug_ref, kaug_ref, gpt_ref = refs
    else:
        gn_in, gk_ref, gs_ref, gn_ref, st_ref, gb_ref, qaug_ref, kaug_ref, gpt_ref = refs
    part = 24
    e = PIECES * part
    rows = qhot_ref.shape[1]
    full = x_ref.shape[0]
    heads = e // DH
    qaug_ref[2 * DH :, :] = qhot_ref[...]
    kaug_ref[:, 2 * DH :] = kmask_ref[...]
    qg, qs, kg = qg_ref[...], qs_ref[...], kg_ref[...]
    qg_sum = jnp.zeros((DH, 128), F32)
    qs_sum = jnp.zeros((DH, 128), F32)
    kg_sum = jnp.zeros((DH, 128), F32)
    one_rows = (lax.broadcasted_iota(jnp.int32, (DH, full), 0) < 3).astype(F32).astype(BF16)
    row_no = lax.broadcasted_iota(jnp.int32, (DH, rows), 0)
    for h in range(heads):
        hs = slice(h * DH, (h + 1) * DH)
        qn, qr, q_low = build_q_aug(qpre_ref[hs, :], qg, qs, qaug_ref)
        kn, kr, k_low = build_k_aug(kpre_ref[hs, :], kg, kaug_ref)
        inv = 1.0 / l_ref[h : h + 1, :]
        go = gmt_ref[hs, :].astype(F32) * inv
        go_low = go.astype(BF16)
        delta = -jnp.sum(go_low.astype(F32) * mixt_ref[hs, :], axis=0, keepdims=True)
        d0 = delta.astype(BF16).astype(F32)
        d1 = (delta - d0).astype(BF16).astype(F32)
        d2 = delta - d0 - d1
        extra = jnp.where(
            row_no == 0, d0, jnp.where(row_no == 1, d1, jnp.where(row_no == 2, d2, 0.0))
        ).astype(BF16)
        goaug = jnp.concatenate([go_low, extra], axis=0)
        vaug = jnp.concatenate([vt_ref[hs, :], one_rows], axis=0).T
        prob = jnp.exp2(mm(kaug_ref[...], qaug_ref[...]))
        ds = (prob * mm(vaug, goaug)).astype(BF16)
        gv = mm_nt(go_low, prob.astype(BF16))
        gk = mm_nt(q_low, ds) * SCALE
        gq = mm(k_low, ds) * SCALE
        qg_sum += lane_fold(gq * qn)
        qs_sum += lane_fold(gq)
        kg_sum += lane_fold(gk * kn)
        gpt_ref[h * DH : (h + 1) * DH, 0:rows] = col_norm_back(gq * qg, qn, qr).astype(BF16)
        gpt_ref[e + h * DH : e + (h + 1) * DH, :] = col_norm_back(gk * kg, kn, kr).astype(BF16)
        gpt_ref[2 * e + h * DH : 2 * e + (h + 1) * DH, :] = gv.astype(BF16)
    st_ref[0] = qg_sum
    st_ref[1] = qs_sum
    st_ref[2] = kg_sum
    gpq = gpt_ref[0:e, 0:rows]
    gpkv = gpt_ref[e : 3 * e, :]
    gb_ref[0:e, :] = lane_fold(gpq.astype(F32))
    gb_ref[e : 3 * e, :] = lane_fold(gpkv.astype(F32))
    gwq = mm(gpq, x_ref[0:rows, :])
    gwkv = mm(gpkv, x_ref[...])

    def put(ref, at, p):
        ref[at, 0:part, :] = gwq[p * part : (p + 1) * part, :]
        ref[at, part : 2 * part, :] = gwkv[p * part : (p + 1) * part, :]
        ref[at, 2 * part : 3 * part, :] = gwkv[e + p * part : e + (p + 1) * part, :]

    for p in range(PIECES):
        at = idx_ref[p]

        @pl.when(at < PIECES // 2)
        def _():
            put(gk_ref, at, p)

        @pl.when(at >= PIECES // 2)
        def _():
            put(gs_ref, at - PIECES // 2, p)

    gnq = mm_tn(gpq, wt_ref[0:e, :])
    gnkv = mm_tn(gpkv, wt_ref[e : 3 * e, :])
    if first:
        gn_ref[0:rows, :] = gnkv[0:rows] + gnq
        gn_ref[rows:, :] = gnkv[rows:]
    else:
        gn_ref[0:rows, :] = gn_in[0:rows, :] + gnkv[0:rows] + gnq
        gn_ref[rows:, :] = gn_in[rows:, :] + gnkv[rows:]


def norm1_stats_kernel(blk_ref, x_ref, gn_ref, out_ref):
    n, _ = row_norm(x_ref[...].astype(F32))
    e = gn_ref[...]

    @pl.when(pl.program_id(0) == 0)
    def _():
        out_ref[...] = jnp.zeros_like(out_ref)

    out_ref[0:1, :] += jnp.sum(e * n, axis=0, keepdims=True)
    out_ref[1:2, :] += jnp.sum(e, axis=0, keepdims=True)


def final_kernel(blk_ref, x_ref, gn_ref, got_ref, gm_ref, g_ref, out_ref):
    n, rstd = row_norm(x_ref[...].astype(F32))
    f = (gn_ref[...] + got_ref[...]) * g_ref[...]
    out_ref[...] = (gm_ref[...] + row_norm_back(f, n, rstd)).astype(BF16)


def unpack_kernel(idx_ref, s_ref, out_ref):
    groups = out_ref.shape[0]
    part = s_ref.shape[1] // groups
    for g in range(groups):
        whole = jnp.concatenate(
            [s_ref[idx_ref[p], g * part : (g + 1) * part, :] for p in range(PIECES)], axis=0
        )
        out_ref[g] = whole.T


def unpack_rows_kernel(idx_ref, s_ref, out_ref):
    part = s_ref.shape[1]
    for p in range(PIECES):
        out_ref[p * part : (p + 1) * part, :] = s_ref[idx_ref[p]]


def unpack_att_kernel(ia_ref, ib_ref, a_ref, b_ref, qkv_ref, out_ref):
    part = a_ref.shape[1] // 2

    def whole(ref, i_ref, off):
        return jnp.concatenate(
            [ref[i_ref[p], off : off + part, :] for p in range(PIECES)], axis=0
        )

    qkv_ref[0] = whole(a_ref, ia_ref, 0).T
    qkv_ref[1] = whole(a_ref, ia_ref, part).T
    qkv_ref[2] = whole(b_ref, ib_ref, 0).T
    out_ref[...] = whole(b_ref, ib_ref, part)


def from_slot(a, k, size):
    return lax.ppermute(a, "mp", [(s, (s - k) % size) for s in range(size)])


def to_slot(a, k, size):
    return lax.ppermute(a, "mp", [(s, (s + k) % size) for s in range(size)])


def swap_plane(a, bit, size):
    return lax.ppermute(a, "dp", [(d, d ^ bit) for d in range(size)])


def storage_of(r, bits):
    return sum(jnp.where((r & bit) != 0, 1 << t, 0) for t, bit in enumerate(bits))


def offset_of(s, bits):
    return sum(bit for t, bit in enumerate(bits) if (s >> t) & 1)


class Stages:
    def __init__(self):
        self.live = {}
        self.flying = []

    def __setitem__(self, name, value):
        self.live[name] = value

    def __getitem__(self, name):
        return self.live[name]

    def pop(self, name):
        return self.live.pop(name)

    def fence(self, *still_flying):
        now = {n: a for n, a in self.live.items() if n not in still_flying}
        leaves, tree = jax.tree.flatten(now)
        self.live.update(jax.tree.unflatten(tree, lax.optimization_barrier(leaves)))


def shards(
    tokens,
    seg_ids,
    qkv_weight,
    qkv_bias,
    out_weight,
    out_bias,
    up_weight,
    up_bias,
    down_weight,
    down_bias,
    norm1_gain,
    norm1_shift,
    query_gain,
    query_shift,
    key_gain,
    norm2_gain,
    norm2_shift,
    cotangent,
):
    ndp = lax.axis_size("dp")
    nmp = lax.axis_size("mp")
    dp_no = lax.axis_index("dp")
    mp_no = lax.axis_index("mp")
    me = dp_no % PIECES
    row_count, width = tokens.shape
    share = row_count // nmp
    full = SEQ_LEN
    assert full == 2 * share and nmp == 4 and ndp % PIECES == 0
    e = qkv_weight.shape[2]
    part = e // PIECES
    units = up_weight.shape[1]
    upart = units // PIECES
    half = PIECES // 2
    core, px, py = 1, 2, 4

    vmem = pl.BlockSpec(memory_space=pltpu.VMEM)
    smem = pl.BlockSpec(memory_space=pltpu.SMEM)
    row1 = lambda v: v.reshape(1, -1)
    col = lambda v: v.reshape(-1, 1)
    swap = lambda a, bit: swap_plane(a, bit, ndp)
    get = lambda a, k: from_slot(a, k, nmp)
    put = lambda a, k: to_slot(a, k, nmp)
    v = Stages()

    qkv_t = jnp.swapaxes(qkv_weight, 1, 2).reshape(3, PIECES, part, width)
    out_p = out_weight.reshape(PIECES, part, width)
    att_a0 = jnp.concatenate([qkv_t[0], qkv_t[1]], axis=1).astype(F32)
    att_b0 = jnp.concatenate([qkv_t[2], out_p], axis=1).astype(F32)
    up_t = up_weight.T.reshape(PIECES, upart, width)
    down_p = down_weight.reshape(PIECES, upart, width)

    def pick(a, r):
        return lax.dynamic_index_in_dim(a, me ^ r, 0, keepdims=False)

    att_piece = jnp.concatenate([pick(att_a0, 0), pick(att_b0, 0)], axis=0)
    mlp_piece = jnp.concatenate([pick(up_t, 0), pick(down_p, 0)], axis=0).astype(F32)
    up_half = [
        jnp.stack([pick(up_t, offset_of(s, BITS_A)) for s in h]) for h in (range(4), range(4, 8))
    ]
    down_half = [
        jnp.stack([pick(down_p, offset_of(s, BITS_B)) for s in h])
        for h in (range(4), range(4, 8))
    ]
    ub = up_bias.reshape(PIECES, 1, upart)
    ub0 = jnp.stack([pick(ub, offset_of(s, BITS_A)) for s in range(PIECES)])
    bias_pack = jnp.concatenate([qkv_bias.reshape(-1), ub0.reshape(-1)])

    numbers = jnp.arange(PIECES, dtype=jnp.int32)
    idx_a = storage_of(numbers ^ me, BITS_A).astype(jnp.int32)
    idx_b = storage_of(numbers ^ me, BITS_B).astype(jnp.int32)

    block = 256
    per = share // block
    steps = 2 * per
    tile_no = jnp.arange(steps, dtype=jnp.int32)
    blk = jnp.where(tile_no < per, mp_no * per + tile_no, (mp_no ^ 1) * per + tile_no - per).astype(
        jnp.int32
    )
    const2 = lambda t, b: (0, 0)
    tok_spec = pl.BlockSpec((block, width), lambda t, b: (b[t], 0))
    run_spec = pl.BlockSpec((block, width), lambda t, b: (t, 0))
    vec_spec = pl.BlockSpec((1, width), const2)

    def run_norm1():
        return call(
            norm1_kernel,
            sds((full, width), BF16),
            flops=full * width * 10,
            bytes_accessed=full * width * 4,
            grid_spec=pltpu.PrefetchScalarGridSpec(
                num_scalar_prefetch=1,
                grid=(steps,),
                in_specs=[tok_spec, vec_spec, vec_spec],
                out_specs=run_spec,
            ),
        )(blk, tokens, row1(norm1_gain), row1(norm1_shift))

    seg_own = lax.dynamic_slice_in_dim(seg_ids, mp_no * share, share, 0)
    seg_other = lax.dynamic_slice_in_dim(seg_ids, (mp_no ^ 1) * share, share, 0)
    seg_keys = jnp.concatenate([seg_own, seg_other])
    qhot = (
        lax.broadcasted_iota(jnp.int32, (SEG_COLS, share), 0) == seg_own[None, :]
    ).astype(BF16)
    kmask = jnp.where(
        lax.broadcasted_iota(jnp.int32, (full, SEG_COLS), 1) == seg_keys[:, None], 0.0, -1e30
    ).astype(BF16)
    qg, qs, kg = col(query_gain), col(query_shift), col(key_gain)

    def run_attn_fwd(k, at, wa, wb, ia, ib, bias):
        names = ("qpre", "kpre", "vt", "wt", "ow", "mixt", "mixf", "l")
        outs = call(
            functools.partial(attn_fwd_kernel, at),
            (
                sds((e, share), F32),
                sds((e, full), F32),
                sds((e, full), BF16),
                sds((3 * e, width), BF16),
                sds((e, width), BF16),
                sds((e, share), BF16),
                sds((e, share), F32),
                sds((8, share), F32),
            ),
            flops=2 * (full * width * e * 5 // 2 + full * share * e * 8),
            bytes_accessed=8_000_000,
            in_specs=[smem, smem] + [vmem] * 9,
            out_specs=(vmem,) * 8,
            scratch_shapes=[
                pltpu.VMEM((2 * DH + SEG_COLS, share), BF16),
                pltpu.VMEM((full, 2 * DH + SEG_COLS), BF16),
            ],
        )(
            ia,
            ib,
            v["normed"],
            wa,
            wb,
            bias[: 3 * e].reshape(3 * e, 1),
            qg,
            qs,
            kg,
            kmask,
            qhot,
        )
        v[f"st{k}"] = dict(zip(names, outs))

    def run_out():
        own_spec = pl.BlockSpec((share, width), lambda t, b: (b[0] // per, 0))
        whole = lambda shape: pl.BlockSpec(shape, lambda t, b: (0,) * len(shape))
        v["middle"], v["second"] = call(
            functools.partial(out_norm2_kernel, nmp),
            (sds((share, width), F32), sds((share, width), BF16)),
            flops=2 * share * width * e * nmp,
            bytes_accessed=8_000_000,
            grid_spec=pltpu.PrefetchScalarGridSpec(
                num_scalar_prefetch=1,
                grid=(1,),
                in_specs=[own_spec]
                + [whole((e, share))] * nmp
                + [whole((e, width))] * nmp
                + [whole((1, width))] * 3,
                out_specs=(whole((share, width)), whole((share, width))),
            ),
        )(
            blk,
            tokens,
            *[v[f"st{k}"]["mixt"] for k in range(nmp)],
            *[v[f"st{k}"]["ow"] for k in range(nmp)],
            row1(out_bias),
            row1(norm2_gain),
            row1(norm2_shift),
        )

    piece_spec = pl.BlockSpec((1, upart, width), lambda t: (t, 0, 0))
    swap_spec = pl.BlockSpec((1, upart, width), lambda t: ((t % 2) * 2 + t // 2, 0, 0))
    bias_spec = pl.BlockSpec((1, 1, upart), lambda t: (t, 0, 0))
    rows_spec = pl.BlockSpec((share, width), lambda t: (0, 0))

    def run_mlp(k, up, down, bias, first):
        ubk = bias[3 * e :].reshape(PIECES, 1, upart)
        args = [
            v["second"], v["cot"], up[0], up[1], ubk[:half], ubk[half:], down[0], down[1],
        ]
        specs = [
            rows_spec, rows_spec, piece_spec, piece_spec, bias_spec, bias_spec, swap_spec, swap_spec,
        ]
        alias = {}
        if not first:
            args += [v["acc"], v["gs"]]
            specs += [rows_spec, rows_spec]
            alias = {8: 0, 9: 1}
        res = call(
            functools.partial(mlp_kernel, first),
            (
                sds((share, width), F32),
                sds((share, width), F32),
                *[sds((half, upart, width), F32)] * 4,
                *[sds((half, 1, upart), F32)] * 2,
            ),
            flops=2 * share * width * units * 6,
            bytes_accessed=16_000_000,
            grid=(half,),
            in_specs=specs,
            out_specs=(
                rows_spec,
                rows_spec,
                piece_spec,
                piece_spec,
                swap_spec,
                swap_spec,
                bias_spec,
                bias_spec,
            ),
            input_output_aliases=alias,
        )(*args)
        v["acc"], v["gs"] = res[0], res[1]
        v[f"u{k}"] = (res[2], res[3])
        v[f"d{k}"] = (res[4], res[5])
        v[f"ubg{k}"] = jnp.concatenate([res[6], res[7]], axis=0)[:, 0, :]

    def run_mid():
        *gmts, bo, gm, keep, send, mst = call(
            functools.partial(mid_kernel, nmp),
            (
                *[sds((e, share), BF16)] * nmp,
                sds((share, width), BF16),
                sds((share, width), F32),
                sds((half, nmp * part, width), F32),
                sds((half, nmp * part, width), F32),
                sds((8, width), F32),
            ),
            flops=2 * share * width * e * nmp * 2,
            bytes_accessed=12_000_000,
            in_specs=[smem] + [vmem] * (6 + 2 * nmp),
            out_specs=(vmem,) * (5 + nmp),
        )(
            idx_a,
            v["middle"],
            v.pop("acc"),
            v.pop("gs"),
            v["cot"],
            row1(down_bias),
            row1(norm2_gain),
            *[v[f"st{k}"]["ow"] for k in range(nmp)],
            *[v[f"st{k}"]["mixt"] for k in range(nmp)],
        )
        v["block_out"], v["gm"], v["mst"] = bo, gm, mst
        for k in range(nmp):
            v[f"gmt{k}"] = gmts[k]
        v["o"] = (keep, send)

    def run_attn_bwd(k, idx, first):
        st = v.pop(f"st{k}")
        args = [
            idx, v["normed"], st["qpre"], st["kpre"], st["vt"], st["wt"], v.pop(f"gmt{k}"), st["mixf"],
            st["l"], qg, qs, kg, kmask, qhot,
        ]
        specs = [smem] + [vmem] * 13
        alias = {}
        if not first:
            args.append(v["gn"])
            specs.append(vmem)
            alias = {len(args) - 1: 2}
        keep, send, gn, hst, gb = call(
            functools.partial(attn_bwd_kernel, first),
            (
                sds((half, 3 * part, width), F32),
                sds((half, 3 * part, width), F32),
                sds((full, width), F32),
                sds((3, DH, 128), F32),
                sds((3 * e, 128), F32),
            ),
            flops=2 * (full * width * e * 5 + full * share * e * 20),
            bytes_accessed=14_000_000,
            in_specs=specs,
            out_specs=(vmem,) * 5,
            scratch_shapes=[
                pltpu.VMEM((2 * DH + SEG_COLS, share), BF16),
                pltpu.VMEM((full, 2 * DH + SEG_COLS), BF16),
                pltpu.VMEM((3 * e, full), BF16),
            ],
            input_output_aliases=alias,
        )(*args)
        v[f"q{k}"] = (keep, send)
        v["gn"] = gn
        v[f"hst{k}"] = hst
        v[f"qbg{k}"] = jnp.sum(gb, axis=1)

    def g1(n):
        a, b = v[n + "a"], v[n + "b"]
        v[n + "a"] = (a, swap(a, px))
        v[n + "b"] = (b, swap(b, py))

    def g2(n):
        a, b = (jnp.stack(v[n + t]) for t in "ab")
        v[n + "a"] = (a, swap(a, py))
        v[n + "b"] = (b, swap(b, px))

    def g3(n):
        a, b = (jnp.concatenate(v[n + t], axis=0) for t in "ab")
        v[n + "a"] = (a, swap(a, core))
        v[n + "b"] = (b, swap(b, core))

    def r1(n):
        keep, send = v[n]
        v[n] = (keep, swap(send, core))

    def r2(n, kind):
        keep, got = v[n]
        keep_sum = keep[:2] + got[:2]
        v[n] = (keep_sum, swap(keep[2:] + got[2:], py if kind == "a" else px))

    def r3(n, kind):
        keep, got = v[n]
        v[n] = (keep[0] + got[0], swap(keep[1] + got[1], px if kind == "a" else py))

    def r4(n):
        keep, got = v[n]
        v[n] = keep + got

    v["cot"] = lax.dynamic_slice_in_dim(cotangent, mp_no * share, share, 0)
    v["att_piece"], v["mlp_piece"], v["bias"] = att_piece, mlp_piece, bias_pack
    v["t1"] = get(att_piece, 1)
    v["t3"] = get(att_piece, 3)
    for k in range(1, nmp):
        v[f"bias{k}"] = get(bias_pack, k)
    v["normed"] = run_norm1()
    run_attn_fwd(0, 0, att_a0[:, None], att_b0[:, None], numbers, numbers, bias_pack)
    v.fence()
    hp = 2 * part
    t1, t3 = v.pop("t1"), v.pop("t3")
    v["ta"] = jnp.stack([t1[:hp], t3[:hp]])
    v["tb"] = jnp.stack([t1[hp:], t3[hp:]])
    g1("t")
    v["t2"] = get(v["att_piece"], 2)
    v.fence()
    g2("t")
    v["m1"] = get(v["mlp_piece"], 1)
    v.fence()
    g3("t")
    t2 = v.pop("t2")
    v["sa"], v["sb"] = t2[:hp][None], t2[hp:][None]
    g1("s")
    m1 = v.pop("m1")
    v["m1a"], v["m1b"] = m1[:upart], m1[upart:]
    g1("m1")
    v["m3"] = get(v["mlp_piece"], 3)
    v.fence()
    wa, wb = (jnp.concatenate(v.pop("t" + t), axis=0) for t in "ab")
    wa, wb = (w.reshape(PIECES, 2, hp, width) for w in (wa, wb))
    v["wa"], v["wb"] = wa, wb
    run_attn_fwd(1, 0, wa, wb, idx_a, idx_b, v["bias1"])
    g2("s")
    g2("m1")
    v["m2"] = get(v["mlp_piece"], 2)
    v.fence("m2")
    run_attn_fwd(3, 1, v.pop("wa"), v.pop("wb"), idx_a, idx_b, v["bias3"])
    g3("s")
    g3("m1")
    m3 = v.pop("m3")
    v["m3a"], v["m3b"] = m3[:upart], m3[upart:]
    g1("m3")
    v.fence()
    wa, wb = (jnp.concatenate(v.pop("s" + t), axis=0) for t in "ab")
    wa, wb = (w.reshape(PIECES, 1, hp, width) for w in (wa, wb))
    run_attn_fwd(2, 0, wa, wb, idx_a, idx_b, v["bias2"])
    run_out()
    g2("m3")
    m2 = v.pop("m2")
    v["m2a"], v["m2b"] = m2[:upart], m2[upart:]
    g1("m2")
    v.fence()
    run_mlp(0, up_half, down_half, v["bias"], True)
    g3("m3")
    g2("m2")
    v.fence()
    run_mlp(1, v.pop("m1a"), v.pop("m1b"), v["bias1"], False)
    g3("m2")
    r1("u0")
    r1("d0")
    v.fence()
    run_mlp(3, v.pop("m3a"), v.pop("m3b"), v["bias3"], False)
    r2("u0", "a")
    r2("d0", "b")
    r1("u1")
    r1("d1")
    v.fence()
    run_mlp(2, v.pop("m2a"), v.pop("m2b"), v["bias2"], False)
    r3("u0", "a")
    r3("d0", "b")
    r2("u1", "a")
    r2("d1", "b")
    r1("u3")
    r1("d3")
    v.fence()
    run_mid()
    r4("u0")
    r4("d0")
    r3("u1", "a")
    r3("d1", "b")
    r2("u3", "a")
    r2("d3", "b")
    r1("u2")
    r1("d2")
    v.fence()

    def join(k):
        r4(f"u{k}")
        r4(f"d{k}")
        return jnp.concatenate([v.pop(f"u{k}"), v.pop(f"d{k}")], axis=0)

    run_attn_bwd(1, idx_b, True)
    r3("u3", "a")
    r3("d3", "b")
    r2("u2", "a")
    r2("d2", "b")
    v["z1"] = put(join(1), 1)
    r1("o")
    v.fence()
    run_attn_bwd(2, idx_b, False)
    r3("u2", "a")
    r3("d2", "b")
    v["z3"] = put(join(3), 3)
    r2("o", "a")
    r1("q1")
    v.fence()
    run_attn_bwd(3, idx_a, False)
    v["z2"] = put(join(2), 2)
    r3("o", "a")
    r2("q1", "b")
    r1("q2")
    v.fence()

    def high_bits(a):
        bit = PIECES
        while bit < ndp:
            a = a + swap(a, bit)
            bit *= 2
        return a

    run_attn_bwd(0, idx_b, False)
    mlp_sum = jnp.concatenate([v.pop("u0"), v.pop("d0")], axis=0)
    mlp_sum = high_bits(mlp_sum + v.pop("z1") + v.pop("z2") + v.pop("z3"))
    v["ma"], v["mb"] = mlp_sum[:upart], mlp_sum[upart:]
    g1("m")
    r4("o")
    r3("q1", "b")
    r2("q2", "b")
    r1("q3")
    v.fence()
    n1_stats = call(
        norm1_stats_kernel,
        sds((8, width), F32),
        flops=full * width * 10,
        bytes_accessed=full * width * 6,
        grid_spec=pltpu.PrefetchScalarGridSpec(
            num_scalar_prefetch=1,
            grid=(steps,),
            in_specs=[tok_spec, run_spec],
            out_specs=pl.BlockSpec((8, width), const2),
        ),
    )(blk, tokens, v["gn"])
    v["got"] = lax.ppermute(v["gn"][share:], "mp", [(s, s ^ 1) for s in range(nmp)])
    r1("q0")
    g2("m")
    r4("q1")
    r3("q2", "b")
    r2("q3", "a")
    head_sum = jnp.sum(sum(v.pop(f"hst{k}") for k in range(nmp)), axis=-1)
    copied = jnp.concatenate(
        [v.pop("mst")[:4].reshape(-1), n1_stats[:2].reshape(-1), head_sum.reshape(-1)]
    )
    own_parts = [
        jnp.concatenate([v.pop(f"qbg{k}"), jnp.take(v.pop(f"ubg{k}"), idx_a, axis=0).reshape(-1)])
        for k in range(nmp)
    ]
    nc = copied.shape[0]
    no = own_parts[0].shape[0]
    v["small"] = jnp.concatenate([copied] + own_parts)
    v.fence("got")
    o = v.pop("o")
    v["o"] = o

    def joined(k):
        return jnp.concatenate([v.pop(f"q{k}"), v["o"][k * part : (k + 1) * part]], axis=0)

    r2("q0", "b")
    v["small"] = v["small"] + swap(v["small"], core)
    r4("q2")
    r3("q3", "a")
    g3("m")
    v["y1"] = put(joined(1), 1)
    v["y2"] = put(joined(2), 2)
    v.fence("got", "y1", "y2")
    r3("q0", "b")
    v["small"] = v["small"] + swap(v["small"], px)
    r4("q3")
    v["y3"] = put(joined(3), 3)
    v.fence("got", "y1", "y2", "y3")

    def unpack(kernel, state, idx, shape):
        return call(
            kernel,
            sds(shape, F32),
            bytes_accessed=2 * 4 * math.prod(shape),
            in_specs=[smem, vmem],
            out_specs=vmem,
        )(idx, state)

    r4("q0")
    v["small"] = v["small"] + swap(v["small"], py)
    v["up_g"] = unpack(
        unpack_kernel, jnp.concatenate(v.pop("ma"), axis=0), idx_a, (1, width, units)
    )[0]
    v["down_g"] = unpack(
        unpack_rows_kernel, jnp.concatenate(v.pop("mb"), axis=0), idx_b, (units, width)
    )
    v.fence()
    att_sum = high_bits(joined(0) + v.pop("y1") + v.pop("y2") + v.pop("y3"))
    v["wa"], v["wb"] = att_sum[:hp], att_sum[hp:]
    g1("w")
    small = high_bits(v.pop("small"))
    small_sum = small[: nc + no]
    for k in range(1, nmp):
        sent = jnp.concatenate([small[:nc], small[nc + k * no : nc + (k + 1) * no]])
        small_sum = small_sum + put(sent, k)
    v["input_grad"] = call(
        final_kernel,
        sds((share, width), BF16),
        flops=share * width * 20,
        bytes_accessed=share * width * 16,
        grid_spec=pltpu.PrefetchScalarGridSpec(
            num_scalar_prefetch=1,
            grid=(per,),
            in_specs=[tok_spec, run_spec, run_spec, run_spec, vec_spec],
            out_specs=run_spec,
        ),
    )(blk, tokens, v["gn"], v["got"], v["gm"], row1(norm1_gain))
    v.fence()
    g2("w")
    v.fence()
    g3("w")
    wa, wb = (jnp.concatenate(v.pop("w" + t), axis=0) for t in "ab")
    qkv_weight_grad, out_weight_grad = call(
        unpack_att_kernel,
        (sds((3, width, e), F32), sds((e, width), F32)),
        bytes_accessed=2 * 4 * 4 * width * e,
        in_specs=[smem, smem, vmem, vmem],
        out_specs=(vmem, vmem),
    )(idx_a, idx_b, wa, wb)

    rows_of = small_sum[: 6 * width].reshape(6, width)
    heads_of = small_sum[6 * width : nc].reshape(3, DH)
    qkv_bias_grad = small_sum[nc : nc + 3 * e].reshape(3, e)
    up_bias_grad = small_sum[nc + 3 * e :]
    return (
        v["block_out"],
        v["input_grad"],
        qkv_weight_grad,
        qkv_bias_grad,
        out_weight_grad,
        rows_of[2],
        v["up_g"],
        up_bias_grad,
        v["down_g"],
        rows_of[3],
        rows_of[4],
        rows_of[5],
        heads_of[0],
        heads_of[1],
        heads_of[2],
        rows_of[0],
        rows_of[1],
    )


def solution(mesh):
    in_specs = (
        P("dp", None),
        P("dp"),
        P(None, None, "mp"),
        P(None, "mp"),
        P("mp", None),
        P(),
        P(None, "mp"),
        P("mp"),
        P("mp", None),
        P(),
        P(),
        P(),
        P(),
        P(),
        P(),
        P(),
        P(),
        P("dp", None),
    )
    out_specs = (
        P(("dp", "mp"), None),
        P(("dp", "mp"), None),
        P(None, None, "mp"),
        P(None, "mp"),
        P("mp", None),
        P(),
        P(None, "mp"),
        P("mp"),
        P("mp", None),
        P(),
        P(),
        P(),
        P(),
        P(),
        P(),
        P(),
        P(),
    )
    return jax.shard_map(shards, mesh=mesh, in_specs=in_specs, out_specs=out_specs, check_vma=False)
```

```python
import functools
import math

import jax
import jax.numpy as jnp
from jax import lax
from jax.experimental import pallas as pl
from jax.experimental.pallas import tpu as pltpu
from jax.sharding import PartitionSpec as P

F32 = jnp.float32
BF16 = jnp.bfloat16
DH = 64
SEQ_LEN = 1024
NORM_EPS = 1e-06
PIECES = 8
SEG_COLS = 128
LOG2E = math.log2(math.e)
SCALE = DH ** (-0.5)
BITS_A = (2, 4, 1)
BITS_B = (4, 2, 1)
MLP_KIND = ("a", "a", "b", "b")
VMEM_LIMIT = 56 * 1024 * 1024


def mm(a, b):
    return lax.dot_general(a, b, (((1,), (0,)), ((), ())), preferred_element_type=F32)


def mm_nt(a, b):
    return lax.dot_general(a, b, (((1,), (1,)), ((), ())), preferred_element_type=F32)


def mm_tn(a, b):
    return lax.dot_general(a, b, (((0,), (0,)), ((), ())), preferred_element_type=F32)


def call(kernel, out_shape, flops=0, bytes_accessed=0, **kw):
    return pl.pallas_call(
        kernel,
        out_shape=out_shape,
        compiler_params=pltpu.CompilerParams(vmem_limit_bytes=VMEM_LIMIT),
        cost_estimate=pl.CostEstimate(
            flops=flops, bytes_accessed=bytes_accessed, transcendentals=0
        ),
        **kw,
    )


def sds(shape, dtype):
    return jax.ShapeDtypeStruct(shape, dtype)


def row_norm(x):
    mean = jnp.mean(x, axis=-1, keepdims=True)
    cen = x - mean
    rstd = lax.rsqrt(jnp.mean(cen * cen, axis=-1, keepdims=True) + NORM_EPS)
    return cen * rstd, rstd


def row_norm_back(f, n, rstd):
    mean_f = jnp.mean(f, axis=-1, keepdims=True)
    mean_fn = jnp.mean(f * n, axis=-1, keepdims=True)
    return (f - mean_f - n * mean_fn) * rstd


def col_norm(x):
    mean = jnp.mean(x, axis=0, keepdims=True)
    cen = x - mean
    rstd = lax.rsqrt(jnp.mean(cen * cen, axis=0, keepdims=True) + NORM_EPS)
    return cen * rstd, rstd


def col_norm_back(f, n, rstd):
    mean_f = jnp.mean(f, axis=0, keepdims=True)
    mean_fn = jnp.mean(f * n, axis=0, keepdims=True)
    return (f - mean_f - n * mean_fn) * rstd


def lane_fold(x):
    out = x[:, :128]
    for t in range(1, x.shape[1] // 128):
        out = out + x[:, t * 128 : (t + 1) * 128]
    return out


def norm1_kernel(blk_ref, x_ref, g_ref, s_ref, out_ref):
    n, _ = row_norm(x_ref[...].astype(F32))
    out_ref[...] = (n * g_ref[...] + s_ref[...]).astype(BF16)


def build_q_aug(q_pre, qg, qs, qaug_ref):
    n, rstd = col_norm(q_pre)
    q_low = (n * qg + qs).astype(BF16)
    scaled = q_low.astype(F32) * (SCALE * LOG2E)
    hi = scaled.astype(BF16)
    lo = (scaled - hi.astype(F32)).astype(BF16)
    qaug_ref[0:DH, :] = hi
    qaug_ref[DH : 2 * DH, :] = lo
    return n, rstd, q_low


def build_k_aug(k_pre, kg, kaug_ref):
    n, rstd = col_norm(k_pre)
    k_low = (n * kg).astype(BF16)
    kaug_ref[:, 0 : 2 * DH] = jnp.concatenate([k_low, k_low], axis=0).T
    return n, rstd, k_low


def gather_rows(w_ref, i_ref, off, part):
    return jnp.concatenate(
        [w_ref[i_ref[p], off : off + part, :] for p in range(PIECES)], axis=0
    ).astype(BF16)


def attn_fwd_kernel(
    extra, ia_ref, ib_ref, x_ref, wa_ref, wb_ref, b_ref, qg_ref, qs_ref, kg_ref, kmask_ref,
    qhot_ref, qpre_ref, kpre_ref, vt_ref, wt_ref, mixt_ref, mixf_ref, mixs_ref, l_ref, ow_ref,
    *refs,
):
    qaug_ref, kaug_ref = refs[-2:]
    part = 24
    e = PIECES * part
    full = x_ref.shape[0]
    share = full // 2
    heads = e // DH
    wt_ref[0:e, :] = gather_rows(wa_ref, ia_ref, 0, part)
    wt_ref[e : 2 * e, :] = gather_rows(wa_ref, ia_ref, part, part)
    wt_ref[2 * e : 3 * e, :] = gather_rows(wb_ref, ib_ref, 0, part)
    ow_ref[...] = gather_rows(wb_ref, ib_ref, part, part)
    if extra:
        refs[0][...] = gather_rows(wa_ref, ia_ref, 2 * part, part)
        refs[1][...] = gather_rows(wb_ref, ib_ref, 2 * part, part)
    x = x_ref[...]
    qpre_ref[...] = mm_nt(wt_ref[0:e, :], x) + b_ref[0:e, :]
    kpre_ref[...] = mm_nt(wt_ref[e : 2 * e, :], x) + b_ref[e : 2 * e, :]
    vt_ref[...] = (mm_nt(wt_ref[2 * e : 3 * e, :], x) + b_ref[2 * e : 3 * e, :]).astype(BF16)
    qaug_ref[2 * DH :, :] = qhot_ref[...]
    kaug_ref[:, 2 * DH :] = kmask_ref[...]
    ones = jnp.ones((16, full), BF16)
    for h in range(heads):
        hs = slice(h * DH, (h + 1) * DH)
        build_q_aug(qpre_ref[hs, :], qg_ref[...], qs_ref[...], qaug_ref)
        build_k_aug(kpre_ref[hs, :], kg_ref[...], kaug_ref)
        prob = jnp.exp2(mm(kaug_ref[...], qaug_ref[...])).astype(BF16)
        vaug = jnp.concatenate([vt_ref[hs, :], ones], axis=0)
        o = mm(vaug, prob)
        total = o[DH : DH + 1, :]
        l_ref[h : h + 1, :] = total
        mix = o[0:DH, :] / total
        mixf_ref[hs, :] = mix
        mixt_ref[hs, :] = mix[:, 0:share].astype(BF16)
        mixs_ref[hs, :] = mix[:, share:]


def out_norm2_kernel(nslot, blk_ref, x_ref, *refs):
    mixes = refs[:nslot]
    ws = refs[nslot : 2 * nslot]
    ob_ref, g_ref, s_ref, mid_ref, sec_ref, secf_ref = refs[2 * nslot :]
    acc = x_ref[...].astype(F32) + ob_ref[...]
    for k in range(nslot):
        acc = acc + mm_tn(mixes[k][...].astype(BF16), ws[k][...])
    mid_ref[...] = acc
    n, _ = row_norm(acc)
    sec = (n * g_ref[...] + s_ref[...]).astype(BF16)
    sec_ref[...] = sec
    secf_ref[...] = sec.astype(F32)


def mlp_kernel(
    order, sec_ref, secp_ref, cot_ref, cotp_ref, u0_ref, u1_ref, d0_ref, d1_ref, b_ref,
    hid_ref, gp_ref, ub_ref, db_ref, keep_ref, send_ref, gb_ref,
):
    part = u0_ref.shape[1]
    share = sec_ref.shape[0]
    up = jnp.concatenate([u0_ref[0], u0_ref[1], u1_ref[0], u1_ref[1]], axis=0).astype(BF16)
    down = jnp.concatenate([d0_ref[0], d1_ref[0], d0_ref[1], d1_ref[1]], axis=0).astype(BF16)
    ub_ref[...] = up
    db_ref[...] = down
    bias = b_ref[...]
    for r, (s_ref, c_ref) in enumerate(((sec_ref, cot_ref), (secp_ref, cotp_ref))):
        rows = slice(r * share, (r + 1) * share)
        sec = s_ref[...].astype(BF16)
        cot = c_ref[...].astype(BF16)
        pre = mm_nt(sec, up) + bias
        cdf = 0.5 * (1.0 + lax.erf(pre * (1.0 / math.sqrt(2.0))))
        hid = (pre * cdf).astype(BF16)
        pdf = jnp.exp(-0.5 * pre * pre) * (1.0 / math.sqrt(2.0 * math.pi))
        gpre = (mm_nt(cot, down) * (cdf + pre * pdf)).astype(BF16)
        hid_ref[rows, :] = hid
        gp_ref[rows, :] = gpre
        gb_r = jnp.sum(gpre.astype(F32), axis=0, keepdims=True)
        gd_r = mm_tn(hid, cot)
        gu_r = mm_tn(gpre, sec)
        if r == 0:
            gb, gd, gu = gb_r, gd_r, gu_r
        else:
            gb, gd, gu = gb + gb_r, gd + gd_r, gu + gu_r
    gb_ref[...] = gb
    for i, ref, j in zip(order, (keep_ref, keep_ref, send_ref, send_ref), (0, 1, 0, 1)):
        ref[j, 0] = gu[i * part : (i + 1) * part]
        ref[j, 1] = gd[i * part : (i + 1) * part]


def down_kernel(nslot, *refs):
    hids = refs[:nslot]
    gps = refs[nslot : 2 * nslot]
    ubs = refs[2 * nslot : 3 * nslot]
    dbs = refs[3 * nslot : 4 * nslot]
    out_ref = refs[4 * nslot]
    cat = lambda refs, axis: jnp.concatenate([r[...] for r in refs], axis=axis)
    out_ref[0] = mm(cat(hids, 1), cat(dbs, 0))
    out_ref[1] = mm(cat(gps, 1), cat(ubs, 0))


def mid_kernel(nslot, idx_ref, mid_ref, own_ref, got_ref, cot_ref, db_ref, g_ref, *refs):
    ows = refs[:nslot]
    mixts = refs[nslot : 2 * nslot]
    gmts = refs[2 * nslot : 3 * nslot]
    bo_ref, gm_ref, gow_keep, gow_send, st_ref = refs[3 * nslot :]
    part = 24
    mid = mid_ref[...]
    bo_ref[...] = (mid + (own_ref[0] + got_ref[0]) + db_ref[...]).astype(BF16)
    n, rstd = row_norm(mid)
    e = own_ref[1] + got_ref[1]
    cot = cot_ref[...].astype(F32)
    gm = cot + row_norm_back(e * g_ref[...], n, rstd)
    gm_ref[...] = gm
    gm_low = gm.astype(BF16)
    st_ref[0:1, :] = jnp.sum(e * n, axis=0, keepdims=True)
    st_ref[1:2, :] = jnp.sum(e, axis=0, keepdims=True)
    st_ref[2:3, :] = jnp.sum(gm_low.astype(F32), axis=0, keepdims=True)
    st_ref[3:4, :] = jnp.sum(cot, axis=0, keepdims=True)
    st_ref[4:8, :] = jnp.zeros((4, mid.shape[1]), F32)
    for k in range(nslot):
        gmts[k][...] = mm_nt(ows[k][...], gm_low).astype(gmts[k].dtype)
        g = mm(mixts[k][...].astype(BF16), gm_low)
        for p in range(PIECES):
            at = idx_ref[p]
            rows = slice(k * part, (k + 1) * part)

            @pl.when(at < PIECES // 2)
            def _():
                gow_keep[at, rows, :] = g[p * part : (p + 1) * part, :]

            @pl.when(at >= PIECES // 2)
            def _():
                gow_send[at - PIECES // 2, rows, :] = g[p * part : (p + 1) * part, :]


def attn_bwd_kernel(
    first, idx_ref, x_ref, qpre_ref, kpre_ref, vt_ref, wt_ref, gmt_ref, gmtp_ref, mixf_ref, l_ref,
    qg_ref, qs_ref, kg_ref, kmask_ref, qhot_ref, *refs
):
    if first:
        gk_ref, gs_ref, gn_ref, st_ref, gb_ref, qaug_ref, kaug_ref, gpt_ref = refs
    else:
        gn_in, gk_ref, gs_ref, gn_ref, st_ref, gb_ref, qaug_ref, kaug_ref, gpt_ref = refs
    part = 24
    e = PIECES * part
    full = x_ref.shape[0]
    heads = e // DH
    qaug_ref[2 * DH :, :] = qhot_ref[...]
    kaug_ref[:, 2 * DH :] = kmask_ref[...]
    qg, qs, kg = qg_ref[...], qs_ref[...], kg_ref[...]
    qg_sum = jnp.zeros((DH, 128), F32)
    qs_sum = jnp.zeros((DH, 128), F32)
    kg_sum = jnp.zeros((DH, 128), F32)
    row_no = lax.broadcasted_iota(jnp.int32, (DH, full), 0)
    one_rows = (row_no < 3).astype(F32).astype(BF16)
    for h in range(heads):
        hs = slice(h * DH, (h + 1) * DH)
        qn, qr, q_low = build_q_aug(qpre_ref[hs, :], qg, qs, qaug_ref)
        kn, kr, k_low = build_k_aug(kpre_ref[hs, :], kg, kaug_ref)
        inv = 1.0 / l_ref[h : h + 1, :]
        gm = jnp.concatenate(
            [gmt_ref[hs, :].astype(F32), gmtp_ref[hs, :].astype(BF16).astype(F32)], axis=1
        )
        go_low = (gm * inv).astype(BF16)
        delta = -jnp.sum(go_low.astype(F32) * mixf_ref[hs, :], axis=0, keepdims=True)
        d0 = delta.astype(BF16).astype(F32)
        d1 = (delta - d0).astype(BF16).astype(F32)
        d2 = delta - d0 - d1
        extra = jnp.where(
            row_no == 0, d0, jnp.where(row_no == 1, d1, jnp.where(row_no == 2, d2, 0.0))
        ).astype(BF16)
        goaug = jnp.concatenate([go_low, extra], axis=0)
        vaug = jnp.concatenate([vt_ref[hs, :], one_rows], axis=0).T
        prob = jnp.exp2(mm(kaug_ref[...], qaug_ref[...]))
        ds = (prob * mm(vaug, goaug)).astype(BF16)
        gv = mm_nt(go_low, prob.astype(BF16))
        gk = mm_nt(q_low, ds) * SCALE
        gq = mm(k_low, ds) * SCALE
        qg_sum += lane_fold(gq * qn)
        qs_sum += lane_fold(gq)
        kg_sum += lane_fold(gk * kn)
        gpt_ref[h * DH : (h + 1) * DH, :] = col_norm_back(gq * qg, qn, qr).astype(BF16)
        gpt_ref[e + h * DH : e + (h + 1) * DH, :] = col_norm_back(gk * kg, kn, kr).astype(BF16)
        gpt_ref[2 * e + h * DH : 2 * e + (h + 1) * DH, :] = gv.astype(BF16)
    st_ref[0] = qg_sum
    st_ref[1] = qs_sum
    st_ref[2] = kg_sum
    gp = gpt_ref[...]
    gb_ref[...] = lane_fold(gp.astype(F32))
    gw = mm(gp, x_ref[...])

    def put(ref, at, p):
        for s in range(3):
            ref[at, s * part : (s + 1) * part, :] = gw[s * e + p * part : s * e + (p + 1) * part, :]

    for p in range(PIECES):
        at = idx_ref[p]

        @pl.when(at < PIECES // 2)
        def _():
            put(gk_ref, at, p)

        @pl.when(at >= PIECES // 2)
        def _():
            put(gs_ref, at - PIECES // 2, p)

    gn = mm_tn(gp, wt_ref[...])
    gn_ref[...] = gn if first else gn_in[...] + gn


def norm1_stats_kernel(blk_ref, x_ref, gn_ref, out_ref):
    n, _ = row_norm(x_ref[...].astype(F32))
    e = gn_ref[...]

    @pl.when(pl.program_id(0) == 0)
    def _():
        out_ref[...] = jnp.zeros_like(out_ref)

    out_ref[0:1, :] += jnp.sum(e * n, axis=0, keepdims=True)
    out_ref[1:2, :] += jnp.sum(e, axis=0, keepdims=True)


def final_kernel(blk_ref, x_ref, gn_ref, got_ref, gm_ref, g_ref, out_ref):
    n, rstd = row_norm(x_ref[...].astype(F32))
    f = (gn_ref[...] + got_ref[...]) * g_ref[...]
    out_ref[...] = (gm_ref[...] + row_norm_back(f, n, rstd)).astype(BF16)


def unpack_kernel(idx_ref, s_ref, out_ref):
    groups = out_ref.shape[0]
    part = s_ref.shape[1] // groups
    for g in range(groups):
        whole = jnp.concatenate(
            [s_ref[idx_ref[p], g * part : (g + 1) * part, :] for p in range(PIECES)], axis=0
        )
        out_ref[g] = whole.T


def unpack_rows_kernel(idx_ref, s_ref, out_ref):
    part = s_ref.shape[1]
    for p in range(PIECES):
        out_ref[p * part : (p + 1) * part, :] = s_ref[idx_ref[p]]


def unpack_att_kernel(ia_ref, ib_ref, a_ref, b_ref, qkv_ref, out_ref):
    part = a_ref.shape[1] // 2

    def whole(ref, i_ref, off):
        return jnp.concatenate(
            [ref[i_ref[p], off : off + part, :] for p in range(PIECES)], axis=0
        )

    qkv_ref[0] = whole(a_ref, ia_ref, 0).T
    qkv_ref[1] = whole(a_ref, ia_ref, part).T
    qkv_ref[2] = whole(b_ref, ib_ref, 0).T
    out_ref[...] = whole(b_ref, ib_ref, part)


def swap_mp(a, k, size):
    return lax.ppermute(a, "mp", [(s, s ^ k) for s in range(size)])


def swap_plane(a, bit, size):
    return lax.ppermute(a, "dp", [(d, d ^ bit) for d in range(size)])


def storage_of(r, bits):
    return sum(jnp.where((r & bit) != 0, 1 << t, 0) for t, bit in enumerate(bits))


def offset_of(s, bits):
    return sum(bit for t, bit in enumerate(bits) if (s >> t) & 1)


class Stages:
    def __init__(self):
        self.live = {}

    def __setitem__(self, name, value):
        self.live[name] = value

    def __getitem__(self, name):
        return self.live[name]

    def pop(self, name):
        return self.live.pop(name)

    def fence(self, *still_flying):
        now = {n: a for n, a in self.live.items() if n not in still_flying}
        leaves, tree = jax.tree.flatten(now)
        self.live.update(jax.tree.unflatten(tree, lax.optimization_barrier(leaves)))


def shards(
    tokens,
    seg_ids,
    qkv_weight,
    qkv_bias,
    out_weight,
    out_bias,
    up_weight,
    up_bias,
    down_weight,
    down_bias,
    norm1_gain,
    norm1_shift,
    query_gain,
    query_shift,
    key_gain,
    norm2_gain,
    norm2_shift,
    cotangent,
):
    ndp = lax.axis_size("dp")
    nmp = lax.axis_size("mp")
    dp_no = lax.axis_index("dp")
    mp_no = lax.axis_index("mp")
    me = dp_no % PIECES
    row_count, width = tokens.shape
    share = row_count // nmp
    full = SEQ_LEN
    assert full == 2 * share and nmp == 4 and ndp % PIECES == 0
    e = qkv_weight.shape[2]
    part = e // PIECES
    units = up_weight.shape[1]
    upart = units // PIECES
    half = PIECES // 2
    mine = half * upart
    core, px, py = 1, 2, 4

    vmem = pl.BlockSpec(memory_space=pltpu.VMEM)
    smem = pl.BlockSpec(memory_space=pltpu.SMEM)
    row1 = lambda v: v.reshape(1, -1)
    col = lambda v: v.reshape(-1, 1)
    swap = lambda a, bit: swap_plane(a, bit, ndp)
    zswap = lambda a, k: swap_mp(a, k, nmp)
    v = Stages()

    qkv_t = jnp.swapaxes(qkv_weight, 1, 2).reshape(3, PIECES, part, width)
    out_p = out_weight.reshape(PIECES, part, width)
    att_a0 = jnp.concatenate([qkv_t[0], qkv_t[1]], axis=1).astype(F32)
    att_b0 = jnp.concatenate([qkv_t[2], out_p], axis=1).astype(F32)
    up_t = up_weight.T.reshape(PIECES, upart, width)
    down_p = down_weight.reshape(PIECES, upart, width)

    def pick(a, r):
        return lax.dynamic_index_in_dim(a, me ^ r, 0, keepdims=False)

    ub = up_bias.reshape(PIECES, upart)
    ub0 = jnp.concatenate([pick(ub, offset_of(s, BITS_A)) for s in range(half)])
    bias_pack = jnp.concatenate([qkv_bias.reshape(-1), ub0])
    bias_rows = jnp.pad(bias_pack, (0, 8 * width - bias_pack.shape[0])).reshape(8, width)
    out_piece = pick(out_p, 0).astype(F32)
    att_piece = jnp.concatenate([pick(att_a0, 0), pick(att_b0, 0), bias_rows], axis=0)
    ob_piece = jnp.concatenate([out_piece, bias_rows], axis=0)
    mlp_piece = jnp.concatenate([pick(up_t, 0), pick(down_p, 0)], axis=0).astype(F32)
    up_own = [jnp.stack([pick(up_t, offset_of(s, BITS_A)) for s in h]) for h in ((0, 1), (2, 3))]
    down_own = [
        jnp.stack([pick(down_p, offset_of(s, BITS_B)) for s in h]) for h in ((0, 1), (2, 3))
    ]

    numbers = jnp.arange(PIECES, dtype=jnp.int32)
    idx_a = storage_of(numbers ^ me, BITS_A).astype(jnp.int32)
    idx_b = storage_of(numbers ^ me, BITS_B).astype(jnp.int32)

    block = 256
    per = share // block
    steps = 2 * per
    tile_no = jnp.arange(steps, dtype=jnp.int32)
    blk = jnp.where(tile_no < per, mp_no * per + tile_no, (mp_no ^ 1) * per + tile_no - per).astype(
        jnp.int32
    )
    const2 = lambda t, b: (0, 0)
    tok_spec = pl.BlockSpec((block, width), lambda t, b: (b[t], 0))
    run_spec = pl.BlockSpec((block, width), lambda t, b: (t, 0))
    vec_spec = pl.BlockSpec((1, width), const2)

    def run_norm1():
        return call(
            norm1_kernel,
            sds((full, width), BF16),
            flops=full * width * 10,
            bytes_accessed=full * width * 4,
            grid_spec=pltpu.PrefetchScalarGridSpec(
                num_scalar_prefetch=1,
                grid=(steps,),
                in_specs=[tok_spec, vec_spec, vec_spec],
                out_specs=run_spec,
            ),
        )(blk, tokens, row1(norm1_gain), row1(norm1_shift))

    seg_own = lax.dynamic_slice_in_dim(seg_ids, mp_no * share, share, 0)
    seg_other = lax.dynamic_slice_in_dim(seg_ids, (mp_no ^ 1) * share, share, 0)
    seg_keys = jnp.concatenate([seg_own, seg_other])
    qhot = (
        lax.broadcasted_iota(jnp.int32, (SEG_COLS, full), 0) == seg_keys[None, :]
    ).astype(BF16)
    kmask = jnp.where(
        lax.broadcasted_iota(jnp.int32, (full, SEG_COLS), 1) == seg_keys[:, None], 0.0, -1e30
    ).astype(BF16)
    qg, qs, kg = col(query_gain), col(query_shift), col(key_gain)
    scratch = [
        pltpu.VMEM((2 * DH + SEG_COLS, full), BF16),
        pltpu.VMEM((full, 2 * DH + SEG_COLS), BF16),
    ]

    def run_attn_fwd(k, wa, wb, ia, ib, bias, extra):
        names = ["qpre", "kpre", "vt", "wt", "mixt", "mixf", "mixs", "l", "ow"]
        shapes = [
            sds((e, full), F32),
            sds((e, full), F32),
            sds((e, full), BF16),
            sds((3 * e, width), BF16),
            sds((e, share), BF16),
            sds((e, full), F32),
            sds((e, share), F32),
            sds((8, full), F32),
        ]
        shapes += [sds((e, width), BF16)] * (3 if extra else 1)
        if extra:
            names += ["ow1", "ow3"]
        outs = call(
            functools.partial(attn_fwd_kernel, extra),
            tuple(shapes),
            flops=2 * (full * width * e * 3 + full * full * e * 8),
            bytes_accessed=10_000_000,
            in_specs=[smem, smem] + [vmem] * 9,
            out_specs=(vmem,) * len(shapes),
            scratch_shapes=scratch,
        )(
            ia, ib, v["normed"], wa, wb, bias[: 3 * e].reshape(3 * e, 1), qg, qs, kg, kmask, qhot,
        )
        v[f"st{k}"] = dict(zip(names, outs))

    def by_slot():
        st0, st2 = v["st0"], v["st2"]
        mixes = [st0["mixt"], v["mix0"], st2["mixt"], v["mix2"]]
        ows = [st0["ow"], st2["ow1"], st2["ow"], st2["ow3"]]
        return mixes, ows

    def run_out():
        own_spec = pl.BlockSpec((share, width), lambda t, b: (b[0] // per, 0))
        whole = lambda shape: pl.BlockSpec(shape, lambda t, b: (0,) * len(shape))
        mixes, ows = by_slot()
        v["middle"], v["second"], v["sec_f"] = call(
            functools.partial(out_norm2_kernel, nmp),
            (sds((share, width), F32), sds((share, width), BF16), sds((share, width), F32)),
            flops=2 * share * width * e * nmp,
            bytes_accessed=8_000_000,
            grid_spec=pltpu.PrefetchScalarGridSpec(
                num_scalar_prefetch=1,
                grid=(1,),
                in_specs=[own_spec]
                + [whole((e, share))] * nmp
                + [whole((e, width))] * nmp
                + [whole((1, width))] * 3,
                out_specs=(whole((share, width)),) * 3,
            ),
        )(blk, tokens, *mixes, *ows, row1(out_bias), row1(norm2_gain), row1(norm2_shift))

    def run_mlp(k, up, down, bias):
        order = (0, 1, 2, 3) if MLP_KIND[k] == "a" else (0, 2, 1, 3)
        res = call(
            functools.partial(mlp_kernel, order),
            (
                *[sds((full, mine), BF16)] * 2,
                *[sds((mine, width), BF16)] * 2,
                *[sds((2, 2, upart, width), F32)] * 2,
                sds((1, mine), F32),
            ),
            flops=2 * full * width * mine * 4,
            bytes_accessed=12_000_000,
            in_specs=[vmem] * 9,
            out_specs=(vmem,) * 7,
        )(
            v["second"], v["sec_p"], v["cot"], v["cot_p"], up[0], up[1], down[0], down[1],
            bias[3 * e : 3 * e + mine].reshape(1, mine),
        )
        v[f"h{k}"] = res[:4]
        v[f"w{k}"] = (res[4], res[5])
        v[f"ubg{k}"] = res[6]

    def run_down(r):
        row_spec = pl.BlockSpec((share, mine), lambda t: (r, 0))
        w_spec = pl.BlockSpec((mine, width), lambda t: (0, 0))
        return call(
            functools.partial(down_kernel, nmp),
            sds((2, share, width), F32),
            flops=4 * share * width * mine * nmp,
            bytes_accessed=11_000_000,
            grid=(1,),
            in_specs=[row_spec] * (2 * nmp) + [w_spec] * (2 * nmp),
            out_specs=pl.BlockSpec((2, share, width), lambda t: (0, 0, 0)),
        )(*[v[f"h{k}"][i] for i in range(4) for k in range(nmp)])

    def run_mid():
        mixes, ows = by_slot()
        *gmts, bo, gm, keep, send, mst = call(
            functools.partial(mid_kernel, nmp),
            (
                *[sds((e, share), F32 if k % 2 else BF16) for k in range(nmp)],
                sds((share, width), BF16),
                sds((share, width), F32),
                sds((half, nmp * part, width), F32),
                sds((half, nmp * part, width), F32),
                sds((8, width), F32),
            ),
            flops=2 * share * width * e * nmp * 2,
            bytes_accessed=12_000_000,
            in_specs=[smem] + [vmem] * (6 + 2 * nmp),
            out_specs=(vmem,) * (5 + nmp),
        )(
            idx_a,
            v["middle"],
            v.pop("acc_own"),
            v.pop("acc_got"),
            v["cot"],
            row1(down_bias),
            row1(norm2_gain),
            *ows,
            *mixes,
        )
        v["block_out"], v["gm"], v["mst"] = bo, gm, mst
        for k in range(nmp):
            v[f"gmt{k}"] = gmts[k]
        v["o"] = (keep, send)

    def run_attn_bwd(k, got, idx, first):
        st = v.pop(f"st{k}")
        args = [
            idx, v["normed"], st["qpre"], st["kpre"], st["vt"], st["wt"], v.pop(f"gmt{k}"),
            v.pop(got), st["mixf"], st["l"], qg, qs, kg, kmask, qhot,
        ]
        alias = {}
        if not first:
            args.append(v["gn"])
            alias = {len(args) - 1: 2}
        keep, send, gn, hst, gb = call(
            functools.partial(attn_bwd_kernel, first),
            (
                sds((half, 3 * part, width), F32),
                sds((half, 3 * part, width), F32),
                sds((full, width), F32),
                sds((3, DH, 128), F32),
                sds((3 * e, 128), F32),
            ),
            flops=2 * (full * width * e * 6 + full * full * e * 20),
            bytes_accessed=14_000_000,
            in_specs=[smem] + [vmem] * (len(args) - 1),
            out_specs=(vmem,) * 5,
            scratch_shapes=scratch + [pltpu.VMEM((3 * e, full), BF16)],
            input_output_aliases=alias,
        )(*args)
        v[f"q{k}"] = (keep, send)
        v["gn"] = gn
        v[f"hst{k}"] = hst
        v[f"qbg{k}"] = gb

    def g1(n):
        a, b = v[n + "a"], v[n + "b"]
        v[n + "a"] = (a, swap(a, px))
        v[n + "b"] = (b, swap(b, py))

    def g2(n):
        a, b = (jnp.stack(v[n + t]) for t in "ab")
        v[n + "a"] = (a, swap(a, py))
        v[n + "b"] = (b, swap(b, px))

    def g3(n):
        a, b = (jnp.concatenate(v[n + t], axis=0) for t in "ab")
        v[n + "a"] = (a, swap(a, core))
        v[n + "b"] = (b, swap(b, core))

    def r1(n):
        keep, send = v[n]
        v[n] = (keep, swap(send, core))

    def r2(n, kind):
        keep, got = v[n]
        keep_sum = keep[:2] + got[:2]
        v[n] = (keep_sum, swap(keep[2:] + got[2:], py if kind == "a" else px))

    def r3(n, kind):
        keep, got = v[n]
        v[n] = (keep[0] + got[0], swap(keep[1] + got[1], px if kind == "a" else py))

    def r4(n):
        keep, got = v[n]
        v[n] = keep + got

    def m1(k):
        keep, send = v[f"w{k}"]
        v[f"w{k}"] = (keep, swap(send, py if MLP_KIND[k] == "a" else px))

    def m2(k):
        r3(f"w{k}", MLP_KIND[k])

    def m3(k):
        r4(f"w{k}")
        v[f"w{k}"] = v[f"w{k}"].reshape(2 * upart, width)

    def split_mlp(k):
        m = v.pop(f"m{k}")
        v[f"m{k}a"], v[f"m{k}b"] = m[:upart], m[upart:]

    def high_bits(a):
        bit = PIECES
        while bit < ndp:
            a = a + swap(a, bit)
            bit *= 2
        return a

    v["cot"] = lax.dynamic_slice_in_dim(cotangent, mp_no * share, share, 0)
    v["mlp_piece"], v["bias0"] = mlp_piece, bias_pack
    v["t2"] = zswap(att_piece, 2)
    v["o1"] = zswap(ob_piece, 1)
    v["o3"] = zswap(ob_piece, 3)
    v["m1"] = zswap(mlp_piece, 1)
    v["normed"] = run_norm1()
    v.fence()
    hp = 2 * part
    t2, o1, o3 = v.pop("t2"), v.pop("o1"), v.pop("o3")
    v["bias1"], v["bias2"], v["bias3"] = (
        o1[part:].reshape(-1),
        t2[4 * part :].reshape(-1),
        o3[part:].reshape(-1),
    )
    v["ta"] = jnp.concatenate([t2[:hp], o1[:part]], axis=0)
    v["tb"] = jnp.concatenate([t2[hp : 2 * hp], o3[:part]], axis=0)
    g1("t")
    v["m3a"] = zswap(v["mlp_piece"][:upart], 3)
    run_attn_fwd(0, att_a0, att_b0, numbers, numbers, bias_pack, False)
    v.fence()
    g2("t")
    v["mix0"] = zswap(v["st0"].pop("mixs"), 1)
    v["m3b"] = zswap(v["mlp_piece"][upart:], 3)
    split_mlp(1)
    g1("m1")
    v.fence()
    g3("t")
    wa, wb = (jnp.concatenate(v.pop("t" + t), axis=0) for t in "ab")
    wa, wb = (w.reshape(PIECES, hp + part, width) for w in (wa, wb))
    run_attn_fwd(2, wa, wb, idx_a, idx_b, v["bias2"], True)
    g2("m1")
    v["m2a"] = zswap(v["mlp_piece"][:upart], 2)
    v.fence()
    v["mix2"] = zswap(v["st2"].pop("mixs"), 1)
    run_out()
    g1("m3")
    v["m2b"] = zswap(v["mlp_piece"][upart:], 2)
    v["cot_p"] = swap(v["cot"].astype(F32), core)
    v.fence()
    v["sec_p"] = swap(v.pop("sec_f"), core)
    run_mlp(0, up_own, down_own, v["bias0"])
    run_mlp(1, v.pop("m1a"), v.pop("m1b"), v["bias1"])
    g2("m3")
    g1("m2")
    v.fence()
    run_mlp(3, v.pop("m3a"), v.pop("m3b"), v["bias3"])
    g2("m2")
    v.fence()
    run_mlp(2, v.pop("m2a"), v.pop("m2b"), v["bias2"])
    m1(0)
    m1(3)
    v["acc_got"] = swap(run_down(1), core)
    v["acc_own"] = run_down(0)
    v.fence()
    m2(0)
    m2(3)
    m1(1)
    m1(2)
    run_mid()
    v["gp2"] = zswap(v.pop("gmt3"), 1)
    v["gp0"] = zswap(v.pop("gmt1"), 1)
    run_attn_bwd(2, "gp2", idx_b, True)
    m3(3)
    v["w3"] = zswap(v["w3"], 3)
    r1("o")
    v.fence()
    r1("q2")
    m2(1)
    m2(2)
    r2("o", "a")
    m3(0)
    run_attn_bwd(0, "gp0", idx_a, False)
    v.fence()
    v["gn_a"] = zswap(v["gn"][share : share + block], 1)
    n1_stats = call(
        norm1_stats_kernel,
        sds((8, width), F32),
        flops=full * width * 10,
        bytes_accessed=full * width * 6,
        grid_spec=pltpu.PrefetchScalarGridSpec(
            num_scalar_prefetch=1,
            grid=(steps,),
            in_specs=[tok_spec, run_spec],
            out_specs=pl.BlockSpec((8, width), const2),
        ),
    )(blk, tokens, v["gn"])
    m3(1)
    m3(2)
    r1("q0")
    r2("q2", "b")
    r3("o", "a")
    v["z2a"] = zswap(v["w2"][:upart], 2)
    head_sum = jnp.sum(v.pop("hst0") + v.pop("hst2"), axis=-1)
    copied = jnp.concatenate(
        [v.pop("mst")[:4].reshape(-1), n1_stats[:2].reshape(-1), head_sum.reshape(-1)]
    )
    own_parts = []
    for k in range(nmp):
        qb = jnp.zeros((3 * e,), F32) if k % 2 else jnp.sum(v.pop(f"qbg{k}"), axis=1)
        ubg = jnp.pad(v.pop(f"ubg{k}").reshape(half, upart), ((0, half), (0, 0)))
        own_parts.append(jnp.concatenate([qb, jnp.take(ubg, idx_a, axis=0).reshape(-1)]))
    nc = copied.shape[0]
    no = own_parts[0].shape[0]
    v["small"] = jnp.concatenate([copied] + own_parts)
    v.fence()
    v["z2b"] = zswap(v["w2"][upart:], 2)
    v["z1"] = zswap(v.pop("w1"), 1)
    r2("q0", "a")
    r3("q2", "b")
    r4("o")
    v["small"] = v["small"] + swap(v["small"], core)
    v.fence()
    o = v.pop("o")
    mlp_sum = v.pop("w0") + v.pop("w3") + v.pop("z1")
    v.pop("w2")
    mlp_sum = high_bits(
        mlp_sum + jnp.concatenate([v.pop("z2a"), v.pop("z2b")], axis=0)
    )
    v["ma"], v["mb"] = mlp_sum[:upart], mlp_sum[upart:]
    g1("m")
    r3("q0", "a")
    r4("q2")
    v["y2"] = zswap(jnp.concatenate([v.pop("q2"), o[2 * part : 3 * part]], axis=0), 2)
    v["y13"] = (
        zswap(o[part : 2 * part], 1),
        zswap(o[3 * part :], 3),
        o[:part],
    )
    v.fence()
    v["gn_b"] = zswap(v["gn"][share + block :], 1)
    g2("m")
    r4("q0")
    y1, y3, o0 = v.pop("y13")
    att_sum = jnp.concatenate([v.pop("q0"), o0 + y1 + y3], axis=0)
    att_sum = high_bits(att_sum + v.pop("y2"))
    v["wa"], v["wb"] = att_sum[:hp], att_sum[hp:]
    g1("w")
    v["small"] = v["small"] + swap(v["small"], px)
    v.fence()

    def unpack(kernel, a, b, idx, shape):
        return call(
            kernel,
            sds(shape, F32),
            bytes_accessed=2 * 4 * math.prod(shape),
            in_specs=[smem, vmem],
            out_specs=vmem,
        )(idx, jnp.concatenate([a, b], axis=0).reshape(PIECES, upart, width))

    g2("w")
    ma, mb = (jnp.concatenate(v.pop("m" + t), axis=0) for t in "ab")
    mc = (jnp.stack([ma, mb]), swap(jnp.stack([ma, mb]), core))
    v["small"] = v["small"] + swap(v["small"], py)
    v["up_g"] = unpack(unpack_kernel, mc[0][0], mc[1][0], idx_a, (1, width, units))[0]
    v["down_g"] = unpack(unpack_rows_kernel, mc[0][1], mc[1][1], idx_b, (units, width))
    v["input_grad"] = call(
        final_kernel,
        sds((share, width), BF16),
        flops=share * width * 20,
        bytes_accessed=share * width * 16,
        grid_spec=pltpu.PrefetchScalarGridSpec(
            num_scalar_prefetch=1,
            grid=(per,),
            in_specs=[tok_spec, run_spec, run_spec, run_spec, vec_spec],
            out_specs=run_spec,
        ),
    )(
        blk,
        tokens,
        v["gn"],
        jnp.concatenate([v.pop("gn_a"), v.pop("gn_b")], axis=0),
        v["gm"],
        row1(norm1_gain),
    )
    v.fence()
    v["small"] = high_bits(v["small"])
    small = v["small"]
    small_sum = small[: nc + no]
    for k in range(1, nmp):
        sent = jnp.concatenate([small[:nc], small[nc + k * no : nc + (k + 1) * no]])
        small_sum = small_sum + zswap(sent, k)
    v["small_sum"] = small_sum
    wa, wb = (jnp.concatenate(v.pop("w" + t), axis=0) for t in "ab")
    own = jnp.stack([wa, wb])
    got = swap(own, core)
    wa, wb = (
        jnp.concatenate([own[i], got[i]], axis=0).reshape(PIECES, hp, width) for i in range(2)
    )
    qkv_weight_grad, out_weight_grad = call(
        unpack_att_kernel,
        (sds((3, width, e), F32), sds((e, width), F32)),
        bytes_accessed=2 * 4 * 4 * width * e,
        in_specs=[smem, smem, vmem, vmem],
        out_specs=(vmem, vmem),
    )(idx_a, idx_b, wa, wb)

    small_sum = v["small_sum"]
    rows_of = small_sum[: 6 * width].reshape(6, width)
    heads_of = small_sum[6 * width : nc].reshape(3, DH)
    qkv_bias_grad = small_sum[nc : nc + 3 * e].reshape(3, e)
    up_bias_grad = small_sum[nc + 3 * e :]
    return (
        v["block_out"],
        v["input_grad"],
        qkv_weight_grad,
        qkv_bias_grad,
        out_weight_grad,
        rows_of[2],
        v["up_g"],
        up_bias_grad,
        v["down_g"],
        rows_of[3],
        rows_of[4],
        rows_of[5],
        heads_of[0],
        heads_of[1],
        heads_of[2],
        rows_of[0],
        rows_of[1],
    )


def solution(mesh):
    in_specs = (
        P("dp", None),
        P("dp"),
        P(None, None, "mp"),
        P(None, "mp"),
        P("mp", None),
        P(),
        P(None, "mp"),
        P("mp"),
        P("mp", None),
        P(),
        P(),
        P(),
        P(),
        P(),
        P(),
        P(),
        P(),
        P("dp", None),
    )
    out_specs = (
        P(("dp", "mp"), None),
        P(("dp", "mp"), None),
        P(None, None, "mp"),
        P(None, "mp"),
        P("mp", None),
        P(),
        P(None, "mp"),
        P("mp"),
        P("mp", None),
        P(),
        P(),
        P(),
        P(),
        P(),
        P(),
        P(),
        P(),
    )
    return jax.shard_map(shards, mesh=mesh, in_specs=in_specs, out_specs=out_specs, check_vma=False)
```

```python
import functools
import math

import jax
import jax.numpy as jnp
from jax import lax
from jax.experimental import pallas as pl
from jax.experimental.pallas import tpu as pltpu
from jax.sharding import PartitionSpec as P

F32 = jnp.float32
BF16 = jnp.bfloat16
DH = 64
SEQ_LEN = 1024
NORM_EPS = 1e-06
PIECES = 8
SEG_COLS = 128
LOG2E = math.log2(math.e)
SCALE = DH ** (-0.5)
BITS_A = (2, 4, 1)
BITS_B = (4, 2, 1)
MLP_KIND = ("a", "a", "b", "b")
VMEM_LIMIT = 56 * 1024 * 1024


def mm(a, b):
    return lax.dot_general(a, b, (((1,), (0,)), ((), ())), preferred_element_type=F32)


def mm_nt(a, b):
    return lax.dot_general(a, b, (((1,), (1,)), ((), ())), preferred_element_type=F32)


def mm_tn(a, b):
    return lax.dot_general(a, b, (((0,), (0,)), ((), ())), preferred_element_type=F32)


def call(kernel, out_shape, flops=0, bytes_accessed=0, **kw):
    return pl.pallas_call(
        kernel,
        out_shape=out_shape,
        compiler_params=pltpu.CompilerParams(vmem_limit_bytes=VMEM_LIMIT),
        cost_estimate=pl.CostEstimate(
            flops=flops, bytes_accessed=bytes_accessed, transcendentals=0
        ),
        **kw,
    )


def sds(shape, dtype):
    return jax.ShapeDtypeStruct(shape, dtype)


def row_norm(x):
    mean = jnp.mean(x, axis=-1, keepdims=True)
    cen = x - mean
    rstd = lax.rsqrt(jnp.mean(cen * cen, axis=-1, keepdims=True) + NORM_EPS)
    return cen * rstd, rstd


def row_norm_back(f, n, rstd):
    mean_f = jnp.mean(f, axis=-1, keepdims=True)
    mean_fn = jnp.mean(f * n, axis=-1, keepdims=True)
    return (f - mean_f - n * mean_fn) * rstd


def col_norm(x):
    mean = jnp.mean(x, axis=0, keepdims=True)
    cen = x - mean
    rstd = lax.rsqrt(jnp.mean(cen * cen, axis=0, keepdims=True) + NORM_EPS)
    return cen * rstd, rstd


def col_norm_back(f, n, rstd):
    mean_f = jnp.mean(f, axis=0, keepdims=True)
    mean_fn = jnp.mean(f * n, axis=0, keepdims=True)
    return (f - mean_f - n * mean_fn) * rstd


def lane_fold(x):
    out = x[:, :128]
    for t in range(1, x.shape[1] // 128):
        out = out + x[:, t * 128 : (t + 1) * 128]
    return out


def offset_of(s, bits):
    return sum(bit for t, bit in enumerate(bits) if (s >> t) & 1)


def norm1_kernel(blk_ref, x_ref, g_ref, s_ref, out_ref):
    n, _ = row_norm(x_ref[...].astype(F32))
    out_ref[...] = (n * g_ref[...] + s_ref[...]).astype(BF16)


def build_q_aug(q_pre, qg, qs, qaug_ref):
    n, rstd = col_norm(q_pre)
    q_low = (n * qg + qs).astype(BF16)
    scaled = q_low.astype(F32) * (SCALE * LOG2E)
    hi = scaled.astype(BF16)
    lo = (scaled - hi.astype(F32)).astype(BF16)
    qaug_ref[0:DH, :] = hi
    qaug_ref[DH : 2 * DH, :] = lo
    return n, rstd, q_low


def build_k_aug(k_pre, kg, kaug_ref):
    n, rstd = col_norm(k_pre)
    k_low = (n * kg).astype(BF16)
    kaug_ref[:, 0 : 2 * DH] = jnp.concatenate([k_low, k_low], axis=0).T
    return n, rstd, k_low


def bias_col(b_ref, n):
    return b_ref[...].T[0:n, 0:1]


def prep_kernel(
    me_ref, w_ref, o_ref, qb_ref, ub_ref, up_ref, dn_ref,
    att_ref, ob_ref, b_ref, p_ref, c0_ref, c1_ref, c2_ref, c3_ref, u0_ref, u1_ref, d0_ref, d1_ref,
    t_ref, wf_ref,
):
    part = 24
    e = PIECES * part
    me = me_ref[0]
    b_ref[...] = jnp.zeros(b_ref.shape, F32)
    for s in range(3):
        wf_ref[...] = w_ref[s].astype(F32)
        rows = wf_ref[pl.ds(pl.multiple_of(me * part, 8), part), :]
        att_ref[s * part : (s + 1) * part, :] = rows
        b_ref[0:1, s * e : (s + 1) * e] = qb_ref[s : s + 1, :]
    upart = ub_ref.shape[1]
    for s in range(PIECES // 2):
        b_ref[1:2, s * upart : (s + 1) * upart] = ub_ref[pl.ds(me ^ offset_of(s, BITS_A), 1), :]
    wf_ref[...] = o_ref[...].astype(F32)
    rows = wf_ref[pl.ds(pl.multiple_of(me * part, 8), part), :]
    att_ref[3 * part : 4 * part, :] = rows
    ob_ref[0:part, :] = rows
    att_ref[4 * part :, :] = b_ref[...]
    ob_ref[part:, :] = b_ref[...]

    t_ref[...] = up_ref[...].astype(F32).T

    def at_piece(r):
        return pl.ds(pl.multiple_of((me ^ r) * upart, 32), upart)

    p_ref[0:upart, :] = t_ref[at_piece(0), :]
    p_ref[upart:, :] = dn_ref[at_piece(0), :].astype(F32)
    for pair in ((c0_ref, c1_ref), (c2_ref, c3_ref)):
        n = pair[0].shape[0]
        pair[0][...] = p_ref[0:n, :]
        pair[1][...] = p_ref[n:, :]
    for i, (u_ref, d_ref) in enumerate(((u0_ref, d0_ref), (u1_ref, d1_ref))):
        for j in range(2):
            u_ref[j] = t_ref[at_piece(offset_of(2 * i + j, BITS_A)), :].astype(BF16)
            d_ref[j] = dn_ref[at_piece(offset_of(2 * i + j, BITS_B)), :]


def attend(x_ref, wt_ref, b_ref, hv_ref, kmask_ref, qhot_ref, outs, qaug_ref, kaug_ref):
    qpre_ref, kpre_ref, vt_ref, mixt_ref, mixf_ref, mixs_ref, l_ref = outs
    e = qpre_ref.shape[0]
    full = x_ref.shape[0]
    share = full // 2
    heads = e // DH
    x = x_ref[...]
    bias = bias_col(b_ref, 3 * e)
    qpre_ref[...] = mm_nt(wt_ref[0:e, :], x) + bias[0:e]
    kpre_ref[...] = mm_nt(wt_ref[e : 2 * e, :], x) + bias[e : 2 * e]
    vt_ref[...] = (mm_nt(wt_ref[2 * e : 3 * e, :], x) + bias[2 * e :]).astype(BF16)
    qaug_ref[2 * DH :, :] = qhot_ref[...]
    kaug_ref[:, 2 * DH :] = kmask_ref[...]
    ones = jnp.ones((16, full), BF16)
    for h in range(heads):
        hs = slice(h * DH, (h + 1) * DH)
        build_q_aug(qpre_ref[hs, :], hv_ref[:, 0:1], hv_ref[:, 1:2], qaug_ref)
        build_k_aug(kpre_ref[hs, :], hv_ref[:, 2:3], kaug_ref)
        prob = jnp.exp2(mm(kaug_ref[...], qaug_ref[...])).astype(BF16)
        vaug = jnp.concatenate([vt_ref[hs, :], ones], axis=0)
        o = mm(vaug, prob)
        total = o[DH : DH + 1, :]
        l_ref[h : h + 1, :] = total
        mix = o[0:DH, :] / total
        mixf_ref[hs, :] = mix
        mixt_ref[hs, :] = mix[:, 0:share].astype(BF16)
        mixs_ref[hs, :] = mix[:, share:]


def attn_fwd_own_kernel(x_ref, wt_ref, b_ref, hv_ref, kmask_ref, qhot_ref, *refs):
    attend(x_ref, wt_ref, b_ref, hv_ref, kmask_ref, qhot_ref, refs[:7], *refs[7:])


def attn_fwd_kernel(
    ia_ref, ib_ref, a0_ref, a1_ref, b0_ref, b1_ref, x_ref, b_ref, hv_ref, kmask_ref, qhot_ref,
    wt_ref, ow_ref, ow1_ref, ow3_ref, *refs,
):
    wa_ref, wb_ref = refs[-2:]
    part = 24
    e = PIECES * part
    half = PIECES // 2
    wa_ref[0:half] = a0_ref[...]
    wa_ref[half:] = a1_ref[...]
    wb_ref[0:half] = b0_ref[...]
    wb_ref[half:] = b1_ref[...]

    def rows(w_ref, i_ref, at):
        return jnp.concatenate(
            [w_ref[i_ref[p], at * part : (at + 1) * part, :] for p in range(PIECES)], axis=0
        ).astype(BF16)

    wt_ref[0:e, :] = rows(wa_ref, ia_ref, 0)
    wt_ref[e : 2 * e, :] = rows(wa_ref, ia_ref, 1)
    wt_ref[2 * e : 3 * e, :] = rows(wb_ref, ib_ref, 0)
    ow_ref[...] = rows(wb_ref, ib_ref, 1)
    ow1_ref[...] = rows(wa_ref, ia_ref, 2)
    ow3_ref[...] = rows(wb_ref, ib_ref, 2)
    attend(x_ref, wt_ref, b_ref, hv_ref, kmask_ref, qhot_ref, refs[:7], *refs[7:9])


def out_norm2_kernel(nslot, blk_ref, x_ref, *refs):
    mixes = refs[:nslot]
    ws = refs[nslot : 2 * nslot]
    ob_ref, g_ref, s_ref, mid_ref, sec_ref, secf_ref = refs[2 * nslot :]
    acc = x_ref[...].astype(F32) + ob_ref[...]
    for k in range(nslot):
        acc = acc + mm_tn(mixes[k][...].astype(BF16), ws[k][...])
    mid_ref[...] = acc
    n, _ = row_norm(acc)
    sec = (n * g_ref[...] + s_ref[...]).astype(BF16)
    sec_ref[...] = sec
    secf_ref[...] = sec.astype(F32)


def mlp_kernel(
    order, sec_ref, secp_ref, cot_ref, cotp_ref, u0_ref, u1_ref, d0_ref, d1_ref, b_ref,
    hid_ref, gp_ref, ub_ref, db_ref, k0_ref, k1_ref, s0_ref, s1_ref, gb_ref,
):
    part = u0_ref.shape[1]
    share = sec_ref.shape[0]
    up = jnp.concatenate([u0_ref[0], u0_ref[1], u1_ref[0], u1_ref[1]], axis=0).astype(BF16)
    down = jnp.concatenate([d0_ref[0], d1_ref[0], d0_ref[1], d1_ref[1]], axis=0).astype(BF16)
    ub_ref[...] = up
    db_ref[...] = down
    bias = b_ref[1:2, 0 : up.shape[0]]
    for r, (s_ref, c_ref) in enumerate(((sec_ref, cot_ref), (secp_ref, cotp_ref))):
        rows = slice(r * share, (r + 1) * share)
        sec = s_ref[...].astype(BF16)
        cot = c_ref[...].astype(BF16)
        pre = mm_nt(sec, up) + bias
        cdf = 0.5 * (1.0 + lax.erf(pre * (1.0 / math.sqrt(2.0))))
        hid = (pre * cdf).astype(BF16)
        pdf = jnp.exp(-0.5 * pre * pre) * (1.0 / math.sqrt(2.0 * math.pi))
        gpre = (mm_nt(cot, down) * (cdf + pre * pdf)).astype(BF16)
        hid_ref[rows, :] = hid
        gp_ref[rows, :] = gpre
        gb_r = jnp.sum(gpre.astype(F32), axis=0, keepdims=True)
        gd_r = mm_tn(hid, cot)
        gu_r = mm_tn(gpre, sec)
        if r == 0:
            gb, gd, gu = gb_r, gd_r, gu_r
        else:
            gb, gd, gu = gb + gb_r, gd + gd_r, gu + gu_r
    gb_ref[...] = gb
    for i, ref in zip(order, (k0_ref, k1_ref, s0_ref, s1_ref)):
        ref[0:part, :] = gu[i * part : (i + 1) * part]
        ref[part:, :] = gd[i * part : (i + 1) * part]


def down_kernel(nslot, *refs):
    hids = refs[:nslot]
    gps = refs[nslot : 2 * nslot]
    ubs = refs[2 * nslot : 3 * nslot]
    dbs = refs[3 * nslot : 4 * nslot]
    out_ref = refs[4 * nslot]
    cat = lambda refs, axis: jnp.concatenate([r[...] for r in refs], axis=axis)
    out_ref[0] = mm(cat(hids, 1), cat(dbs, 0))
    out_ref[1] = mm(cat(gps, 1), cat(ubs, 0))


def mid_kernel(nslot, idx_ref, mid_ref, own_ref, got_ref, cot_ref, db_ref, g_ref, *refs):
    ows = refs[:nslot]
    mixts = refs[nslot : 2 * nslot]
    gmts = refs[2 * nslot : 3 * nslot]
    bo_ref, gm_ref, gow_keep, gow_send, st_ref = refs[3 * nslot :]
    part = 24
    mid = mid_ref[...]
    bo_ref[...] = (mid + (own_ref[0] + got_ref[0]) + db_ref[...]).astype(BF16)
    n, rstd = row_norm(mid)
    e = own_ref[1] + got_ref[1]
    cot = cot_ref[...].astype(F32)
    gm = cot + row_norm_back(e * g_ref[...], n, rstd)
    gm_ref[...] = gm
    gm_low = gm.astype(BF16)
    st_ref[0:1, :] = jnp.sum(e * n, axis=0, keepdims=True)
    st_ref[1:2, :] = jnp.sum(e, axis=0, keepdims=True)
    st_ref[2:3, :] = jnp.sum(gm_low.astype(F32), axis=0, keepdims=True)
    st_ref[3:4, :] = jnp.sum(cot, axis=0, keepdims=True)
    st_ref[4:8, :] = jnp.zeros((4, mid.shape[1]), F32)
    for k in range(nslot):
        gmts[k][...] = mm_nt(ows[k][...], gm_low).astype(gmts[k].dtype)
        g = mm(mixts[k][...].astype(BF16), gm_low)
        for p in range(PIECES):
            at = idx_ref[p]
            rows = slice(k * part, (k + 1) * part)

            @pl.when(at < PIECES // 2)
            def _():
                gow_keep[at, rows, :] = g[p * part : (p + 1) * part, :]

            @pl.when(at >= PIECES // 2)
            def _():
                gow_send[at - PIECES // 2, rows, :] = g[p * part : (p + 1) * part, :]


def attn_bwd_kernel(
    first, idx_ref, x_ref, qpre_ref, kpre_ref, vt_ref, wt_ref, gmt_ref, gmtp_ref, mixf_ref, l_ref,
    hv_ref, kmask_ref, qhot_ref, *refs
):
    if first:
        gk_ref, gs_ref, gn_ref, st_ref, gb_ref, qaug_ref, kaug_ref, gpt_ref = refs
    else:
        gn_in, gk_ref, gs_ref, gn_ref, st_ref, gb_ref, qaug_ref, kaug_ref, gpt_ref = refs
    part = 24
    e = PIECES * part
    full = x_ref.shape[0]
    heads = e // DH
    qaug_ref[2 * DH :, :] = qhot_ref[...]
    kaug_ref[:, 2 * DH :] = kmask_ref[...]
    qg, qs, kg = hv_ref[:, 0:1], hv_ref[:, 1:2], hv_ref[:, 2:3]
    qg_sum = jnp.zeros((DH, 128), F32)
    qs_sum = jnp.zeros((DH, 128), F32)
    kg_sum = jnp.zeros((DH, 128), F32)
    row_no = lax.broadcasted_iota(jnp.int32, (DH, full), 0)
    one_rows = (row_no < 3).astype(F32).astype(BF16)
    for h in range(heads):
        hs = slice(h * DH, (h + 1) * DH)
        qn, qr, q_low = build_q_aug(qpre_ref[hs, :], qg, qs, qaug_ref)
        kn, kr, k_low = build_k_aug(kpre_ref[hs, :], kg, kaug_ref)
        inv = 1.0 / l_ref[h : h + 1, :]
        gm = jnp.concatenate(
            [gmt_ref[hs, :].astype(F32), gmtp_ref[hs, :].astype(BF16).astype(F32)], axis=1
        )
        go_low = (gm * inv).astype(BF16)
        delta = -jnp.sum(go_low.astype(F32) * mixf_ref[hs, :], axis=0, keepdims=True)
        d0 = delta.astype(BF16).astype(F32)
        d1 = (delta - d0).astype(BF16).astype(F32)
        d2 = delta - d0 - d1
        extra = jnp.where(
            row_no == 0, d0, jnp.where(row_no == 1, d1, jnp.where(row_no == 2, d2, 0.0))
        ).astype(BF16)
        goaug = jnp.concatenate([go_low, extra], axis=0)
        vaug = jnp.concatenate([vt_ref[hs, :], one_rows], axis=0).T
        prob = jnp.exp2(mm(kaug_ref[...], qaug_ref[...]))
        ds = (prob * mm(vaug, goaug)).astype(BF16)
        gv = mm_nt(go_low, prob.astype(BF16))
        gk = mm_nt(q_low, ds) * SCALE
        gq = mm(k_low, ds) * SCALE
        qg_sum += lane_fold(gq * qn)
        qs_sum += lane_fold(gq)
        kg_sum += lane_fold(gk * kn)
        gpt_ref[h * DH : (h + 1) * DH, :] = col_norm_back(gq * qg, qn, qr).astype(BF16)
        gpt_ref[e + h * DH : e + (h + 1) * DH, :] = col_norm_back(gk * kg, kn, kr).astype(BF16)
        gpt_ref[2 * e + h * DH : 2 * e + (h + 1) * DH, :] = gv.astype(BF16)
    st_ref[0] = qg_sum
    st_ref[1] = qs_sum
    st_ref[2] = kg_sum
    gp = gpt_ref[...]
    gb_ref[...] = lane_fold(gp.astype(F32))
    gw = mm(gp, x_ref[...])

    def put(ref, at, p):
        for s in range(3):
            ref[at, s * part : (s + 1) * part, :] = gw[s * e + p * part : s * e + (p + 1) * part, :]

    for p in range(PIECES):
        at = idx_ref[p]

        @pl.when(at < PIECES // 2)
        def _():
            put(gk_ref, at, p)

        @pl.when(at >= PIECES // 2)
        def _():
            put(gs_ref, at - PIECES // 2, p)

    gn = mm_tn(gp, wt_ref[...])
    gn_ref[...] = gn if first else gn_in[...] + gn


def norm1_stats_kernel(blk_ref, x_ref, gn_ref, out_ref):
    n, _ = row_norm(x_ref[...].astype(F32))
    e = gn_ref[...]

    @pl.when(pl.program_id(0) == 0)
    def _():
        out_ref[...] = jnp.zeros_like(out_ref)

    out_ref[0:1, :] += jnp.sum(e * n, axis=0, keepdims=True)
    out_ref[1:2, :] += jnp.sum(e, axis=0, keepdims=True)


def final_kernel(blk_ref, x_ref, gn_ref, got_ref, gm_ref, g_ref, out_ref):
    n, rstd = row_norm(x_ref[...].astype(F32))
    f = (gn_ref[...] + got_ref[...]) * g_ref[...]
    out_ref[...] = (gm_ref[...] + row_norm_back(f, n, rstd)).astype(BF16)


def both(refs, to_ref):
    half = PIECES // 2
    to_ref[0:half] = refs[0][...]
    to_ref[half:] = refs[1][...]


def unpack_kernel(idx_ref, a_ref, b_ref, out_ref, s_ref):
    both((a_ref, b_ref), s_ref)
    whole = jnp.concatenate([s_ref[idx_ref[p]] for p in range(PIECES)], axis=0)
    out_ref[...] = whole.T


def unpack_rows_kernel(idx_ref, a_ref, b_ref, out_ref, s_ref):
    part = s_ref.shape[1]
    both((a_ref, b_ref), s_ref)
    for p in range(PIECES):
        out_ref[p * part : (p + 1) * part, :] = s_ref[idx_ref[p]]


def unpack_att_kernel(
    ia_ref, ib_ref, a0_ref, a1_ref, b0_ref, b1_ref, qkv_ref, out_ref, a_ref, b_ref
):
    part = a_ref.shape[1] // 2
    both((a0_ref, a1_ref), a_ref)
    both((b0_ref, b1_ref), b_ref)

    def whole(ref, i_ref, off):
        return jnp.concatenate(
            [ref[i_ref[p], off : off + part, :] for p in range(PIECES)], axis=0
        )

    qkv_ref[0] = whole(a_ref, ia_ref, 0)
    qkv_ref[1] = whole(a_ref, ia_ref, part)
    qkv_ref[2] = whole(b_ref, ib_ref, 0)
    out_ref[...] = whole(b_ref, ib_ref, part)


def swap_mp(a, k, size):
    return lax.ppermute(a, "mp", [(s, s ^ k) for s in range(size)])


def swap_plane(a, bit, size):
    return lax.ppermute(a, "dp", [(d, d ^ bit) for d in range(size)])


def storage_of(r, bits):
    return sum(jnp.where((r & bit) != 0, 1 << t, 0) for t, bit in enumerate(bits))


class Stages:
    def __init__(self):
        self.live = {}

    def __setitem__(self, name, value):
        self.live[name] = value

    def __getitem__(self, name):
        return self.live[name]

    def pop(self, name):
        return self.live.pop(name)

    def fence(self, *still_flying):
        now = {n: a for n, a in self.live.items() if n not in still_flying}
        leaves, tree = jax.tree.flatten(now)
        self.live.update(jax.tree.unflatten(tree, lax.optimization_barrier(leaves)))


def shards(
    tokens,
    seg_ids,
    qkv_weight,
    qkv_bias,
    out_weight,
    out_bias,
    up_weight,
    up_bias,
    down_weight,
    down_bias,
    norm1_gain,
    norm1_shift,
    query_gain,
    query_shift,
    key_gain,
    norm2_gain,
    norm2_shift,
    cotangent,
):
    ndp = lax.axis_size("dp")
    nmp = lax.axis_size("mp")
    dp_no = lax.axis_index("dp")
    mp_no = lax.axis_index("mp")
    me = dp_no % PIECES
    row_count, width = tokens.shape
    share = row_count // nmp
    full = SEQ_LEN
    assert full == 2 * share and nmp == 4 and ndp % PIECES == 0
    e = qkv_weight.shape[2]
    part = e // PIECES
    units = up_weight.shape[1]
    upart = units // PIECES
    half = PIECES // 2
    mine = half * upart
    core, px, py = 1, 2, 4

    vmem = pl.BlockSpec(memory_space=pltpu.VMEM)
    smem = pl.BlockSpec(memory_space=pltpu.SMEM)
    row1 = lambda v: v.reshape(1, -1)
    col = lambda v: v.reshape(-1, 1)
    swap = lambda a, bit: swap_plane(a, bit, ndp)
    zswap = lambda a, k: swap_mp(a, k, nmp)
    v = Stages()

    me1 = me.astype(jnp.int32).reshape(1)
    qkv_t = jnp.swapaxes(qkv_weight, 1, 2)
    wt0 = qkv_t.reshape(3 * e, width)
    cuts = (88, 2 * upart - 88, 40, 2 * upart - 40)
    att_piece, ob_piece, bias0, mlp_piece, *mlp_cut, u0, u1, d0, d1 = call(
        prep_kernel,
        (
            sds((4 * part + 8, width), F32),
            sds((part + 8, width), F32),
            sds((8, width), F32),
            sds((2 * upart, width), F32),
            *[sds((n, width), F32) for n in cuts],
            *[sds((2, upart, width), BF16)] * 4,
        ),
        bytes_accessed=9_000_000,
        in_specs=[smem] + [vmem] * 6,
        out_specs=(vmem,) * 12,
        scratch_shapes=[pltpu.VMEM((units, width), F32), pltpu.VMEM((e, width), F32)],
    )(
        me1, qkv_t, out_weight, qkv_bias, up_bias.reshape(PIECES, upart), up_weight, down_weight
    )

    numbers = jnp.arange(PIECES, dtype=jnp.int32)
    idx_a = storage_of(numbers ^ me, BITS_A).astype(jnp.int32)
    idx_b = storage_of(numbers ^ me, BITS_B).astype(jnp.int32)

    block = 256
    per = share // block
    steps = 2 * per
    tile_no = jnp.arange(steps, dtype=jnp.int32)
    blk = jnp.where(tile_no < per, mp_no * per + tile_no, (mp_no ^ 1) * per + tile_no - per).astype(
        jnp.int32
    )
    const2 = lambda t, b: (0, 0)
    tok_spec = pl.BlockSpec((block, width), lambda t, b: (b[t], 0))
    run_spec = pl.BlockSpec((block, width), lambda t, b: (t, 0))
    vec_spec = pl.BlockSpec((1, width), const2)

    def run_norm1():
        return call(
            norm1_kernel,
            sds((full, width), BF16),
            flops=full * width * 10,
            bytes_accessed=full * width * 4,
            grid_spec=pltpu.PrefetchScalarGridSpec(
                num_scalar_prefetch=1,
                grid=(steps,),
                in_specs=[tok_spec, vec_spec, vec_spec],
                out_specs=run_spec,
            ),
        )(blk, tokens, row1(norm1_gain), row1(norm1_shift))

    seg_own = lax.dynamic_slice_in_dim(seg_ids, mp_no * share, share, 0)
    seg_other = lax.dynamic_slice_in_dim(seg_ids, (mp_no ^ 1) * share, share, 0)
    seg_keys = jnp.concatenate([seg_own, seg_other])
    qhot = (
        lax.broadcasted_iota(jnp.int32, (SEG_COLS, full), 0) == seg_keys[None, :]
    ).astype(BF16)
    kmask = jnp.where(
        lax.broadcasted_iota(jnp.int32, (full, SEG_COLS), 1) == seg_keys[:, None], 0.0, -1e30
    ).astype(BF16)
    hv = jnp.stack([query_gain, query_shift, key_gain], axis=1)
    scratch = [
        pltpu.VMEM((2 * DH + SEG_COLS, full), BF16),
        pltpu.VMEM((full, 2 * DH + SEG_COLS), BF16),
    ]

    def whole(a):
        return pl.BlockSpec(a.shape, lambda t: (0,) * len(a.shape))

    def bias_at(block_no):
        return pl.BlockSpec((8, width), lambda t: (block_no, 0))

    att_names = ["qpre", "kpre", "vt", "mixt", "mixf", "mixs", "l"]
    att_shapes = [
        sds((e, full), F32),
        sds((e, full), F32),
        sds((e, full), BF16),
        sds((e, share), BF16),
        sds((e, full), F32),
        sds((e, share), F32),
        sds((8, full), F32),
    ]

    def run_attn_own():
        outs = call(
            attn_fwd_own_kernel,
            tuple(att_shapes),
            flops=2 * (full * width * e * 3 + full * full * e * 8),
            bytes_accessed=10_000_000,
            in_specs=[vmem] * 6,
            out_specs=(vmem,) * 7,
            scratch_shapes=scratch,
        )(v["normed"], wt0, bias0, hv, kmask, qhot)
        v["st0"] = dict(zip(att_names, outs))
        v["st0"]["wt"] = wt0
        v["st0"]["ow"] = out_weight

    def run_attn_far():
        shapes = [sds((3 * e, width), BF16)] + [sds((e, width), BF16)] * 3 + att_shapes
        args = [
            *v.pop("ta"), *v.pop("tb"), v["normed"], v["t2"], hv, kmask, qhot,
        ]
        specs = [whole(a) for a in args]
        specs[5] = bias_at(4 * part // 8)
        outs = call(
            attn_fwd_kernel,
            tuple(shapes),
            flops=2 * (full * width * e * 3 + full * full * e * 8),
            bytes_accessed=10_000_000,
            grid=(1,),
            in_specs=[smem, smem] + specs,
            out_specs=tuple(whole(a) for a in shapes),
            scratch_shapes=scratch
            + [pltpu.VMEM((PIECES, 3 * part, width), F32)] * 2,
        )(idx_a, idx_b, *args)
        v["st2"] = dict(zip(["wt", "ow", "ow1", "ow3"] + att_names, outs))

    def by_slot():
        st0, st2 = v["st0"], v["st2"]
        mixes = [st0["mixt"], v["mix0"], st2["mixt"], v["mix2"]]
        ows = [st0["ow"], st2["ow1"], st2["ow"], st2["ow3"]]
        return mixes, ows

    def run_out():
        own_spec = pl.BlockSpec((share, width), lambda t, b: (b[0] // per, 0))
        whole2 = lambda shape: pl.BlockSpec(shape, lambda t, b: (0,) * len(shape))
        mixes, ows = by_slot()
        v["middle"], v["second"], v["sec_f"] = call(
            functools.partial(out_norm2_kernel, nmp),
            (sds((share, width), F32), sds((share, width), BF16), sds((share, width), F32)),
            flops=2 * share * width * e * nmp,
            bytes_accessed=8_000_000,
            grid_spec=pltpu.PrefetchScalarGridSpec(
                num_scalar_prefetch=1,
                grid=(1,),
                in_specs=[own_spec]
                + [whole2((e, share))] * nmp
                + [whole2((e, width))] * nmp
                + [whole2((1, width))] * 3,
                out_specs=(whole2((share, width)),) * 3,
            ),
        )(blk, tokens, *mixes, *ows, row1(out_bias), row1(norm2_gain), row1(norm2_shift))

    def run_mlp(k, up, down, bias, block_no):
        order = (0, 1, 2, 3) if MLP_KIND[k] == "a" else (0, 2, 1, 3)
        args = [
            v["second"], v["sec_p"], v["cot"], v["cot_p"], up[0], up[1], down[0], down[1], bias,
        ]
        specs = [whole(a) for a in args]
        specs[8] = bias_at(block_no)
        shapes = (
            *[sds((full, mine), BF16)] * 2,
            *[sds((mine, width), BF16)] * 2,
            *[sds((2 * upart, width), F32)] * 4,
            sds((1, mine), F32),
        )
        res = call(
            functools.partial(mlp_kernel, order),
            shapes,
            flops=2 * full * width * mine * 4,
            bytes_accessed=12_000_000,
            grid=(1,),
            in_specs=specs,
            out_specs=tuple(whole(a) for a in shapes),
        )(*args)
        v[f"h{k}"] = res[:4]
        v[f"w{k}"] = res[4:8]
        v[f"ubg{k}"] = res[8]

    def run_down(r):
        row_spec = pl.BlockSpec((share, mine), lambda t: (r, 0))
        w_spec = pl.BlockSpec((mine, width), lambda t: (0, 0))
        return call(
            functools.partial(down_kernel, nmp),
            sds((2, share, width), F32),
            flops=4 * share * width * mine * nmp,
            bytes_accessed=11_000_000,
            grid=(1,),
            in_specs=[row_spec] * (2 * nmp) + [w_spec] * (2 * nmp),
            out_specs=pl.BlockSpec((2, share, width), lambda t: (0, 0, 0)),
        )(*[v[f"h{k}"][i] for i in range(4) for k in range(nmp)])

    def run_mid():
        mixes, ows = by_slot()
        *gmts, bo, gm, keep, send, mst = call(
            functools.partial(mid_kernel, nmp),
            (
                *[sds((e, share), F32 if k % 2 else BF16) for k in range(nmp)],
                sds((share, width), BF16),
                sds((share, width), F32),
                sds((half, nmp * part, width), F32),
                sds((half, nmp * part, width), F32),
                sds((8, width), F32),
            ),
            flops=2 * share * width * e * nmp * 2,
            bytes_accessed=12_000_000,
            in_specs=[smem] + [vmem] * (6 + 2 * nmp),
            out_specs=(vmem,) * (5 + nmp),
        )(
            idx_a,
            v["middle"],
            v.pop("acc_own"),
            v.pop("acc_got"),
            v["cot"],
            row1(down_bias),
            row1(norm2_gain),
            *ows,
            *mixes,
        )
        v["block_out"], v["gm"], v["mst"] = bo, gm, mst
        for k in range(nmp):
            v[f"gmt{k}"] = gmts[k]
        v["o"] = (keep, send)

    def run_attn_bwd(k, got, idx, first):
        st = v.pop(f"st{k}")
        args = [
            idx, v["normed"], st["qpre"], st["kpre"], st["vt"], st["wt"], v.pop(f"gmt{k}"),
            v.pop(got), st["mixf"], st["l"], hv, kmask, qhot,
        ]
        alias = {}
        if not first:
            args.append(v["gn"])
            alias = {len(args) - 1: 2}
        keep, send, gn, hst, gb = call(
            functools.partial(attn_bwd_kernel, first),
            (
                sds((half, 3 * part, width), F32),
                sds((half, 3 * part, width), F32),
                sds((full, width), F32),
                sds((3, DH, 128), F32),
                sds((3 * e, 128), F32),
            ),
            flops=2 * (full * width * e * 6 + full * full * e * 20),
            bytes_accessed=14_000_000,
            in_specs=[smem] + [vmem] * (len(args) - 1),
            out_specs=(vmem,) * 5,
            scratch_shapes=scratch + [pltpu.VMEM((3 * e, full), BF16)],
            input_output_aliases=alias,
        )(*args)
        v[f"q{k}"] = (keep, send)
        v["gn"] = gn
        v[f"hst{k}"] = hst
        v[f"qbg{k}"] = gb

    def g1(n):
        a, b = v[n + "a"], v[n + "b"]
        v[n + "a"] = (a, swap(a, px))
        v[n + "b"] = (b, swap(b, py))

    def g2(n):
        a, b = (jnp.stack(v[n + t]) for t in "ab")
        v[n + "a"] = (a, swap(a, py))
        v[n + "b"] = (b, swap(b, px))

    def g3(n):
        a, b = (jnp.concatenate(v[n + t], axis=0) for t in "ab")
        v[n + "a"] = (a, swap(a, core))
        v[n + "b"] = (b, swap(b, core))

    def r1(n):
        keep, send = v[n]
        v[n] = (keep, swap(send, core))

    def r2(n, kind):
        keep, got = v[n]
        keep_sum = keep[:2] + got[:2]
        v[n] = (keep_sum, swap(keep[2:] + got[2:], py if kind == "a" else px))

    def r3(n, kind):
        keep, got = v[n]
        v[n] = (keep[0] + got[0], swap(keep[1] + got[1], px if kind == "a" else py))

    def r4(n):
        keep, got = v[n]
        v[n] = keep + got

    def c1(k):
        k0, k1, s0, s1 = v[f"w{k}"]
        v[f"w{k}"] = (k0, k1, s0, swap(s1, py if MLP_KIND[k] == "a" else px))

    def c0(k):
        k0, k1, s0, g1 = v[f"w{k}"]
        v[f"w{k}"] = (k0, k1 + g1, swap(s0, py if MLP_KIND[k] == "a" else px))

    def c2(k):
        k0, k1, g0 = v[f"w{k}"]
        v[f"w{k}"] = (k0 + g0, swap(k1, px if MLP_KIND[k] == "a" else py))

    def c3(k):
        k0, g = v[f"w{k}"]
        v[f"w{k}"] = k0 + g

    def split_mlp(k):
        m = v.pop(f"m{k}")
        v[f"m{k}a"], v[f"m{k}b"] = m[:upart], m[upart:]

    def join_cut(k):
        x, y = v.pop(f"m{k}x"), v.pop(f"m{k}y")
        if x.shape[0] >= upart:
            v[f"m{k}a"], v[f"m{k}b"] = x[:upart], jnp.concatenate([x[upart:], y], axis=0)
        else:
            n = upart - x.shape[0]
            v[f"m{k}a"], v[f"m{k}b"] = jnp.concatenate([x, y[:n]], axis=0), y[n:]

    def high_bits(a):
        bit = PIECES
        while bit < ndp:
            a = a + swap(a, bit)
            bit *= 2
        return a

    v["cot"] = lax.dynamic_slice_in_dim(cotangent, mp_no * share, share, 0)
    v["cuts"] = tuple(mlp_cut)
    v["t2"] = zswap(att_piece, 2)
    v["o1"] = zswap(ob_piece, 1)
    v["o3"] = zswap(ob_piece, 3)
    v["m1"] = zswap(mlp_piece, 1)
    v["cot_p"] = swap(v["cot"].astype(F32), core)
    v["normed"] = run_norm1()
    v.fence()
    hp = 2 * part
    t2, o1, o3 = v["t2"], v["o1"], v["o3"]
    v["ta"] = jnp.concatenate([t2[:hp], o1[:part]], axis=0)
    v["tb"] = jnp.concatenate([t2[hp : 2 * hp], o3[:part]], axis=0)
    g1("t")
    split_mlp(1)
    g1("m1")
    v["m3x"] = zswap(v["cuts"][0], 3)
    v.fence()
    g2("t")
    v["m3y"] = zswap(v["cuts"][1], 3)
    v["m2x"] = zswap(v["cuts"][2], 2)
    run_attn_own()
    v.fence()
    g3("t")
    run_attn_far()
    g2("m1")
    v["m2y"] = zswap(v["cuts"][3], 2)
    v["mix0"] = zswap(v["st0"].pop("mixs"), 1)
    v.fence()
    v["mix2"] = zswap(v["st2"].pop("mixs"), 1)
    run_out()
    join_cut(3)
    join_cut(2)
    g1("m3")
    g1("m2")
    v.fence()
    v["sec_p"] = swap(v.pop("sec_f"), core)
    run_mlp(1, v.pop("m1a"), v.pop("m1b"), v["o1"], part // 8)
    g2("m3")
    v.fence()
    run_mlp(3, v.pop("m3a"), v.pop("m3b"), v["o3"], part // 8)
    g2("m2")
    v.fence()
    run_mlp(0, (u0, u1), (d0, d1), bias0, 0)
    c1(1)
    c1(3)
    v.fence()
    run_mlp(2, v.pop("m2a"), v.pop("m2b"), v["t2"], 4 * part // 8)
    c0(1)
    c0(3)
    v.fence()
    c2(1)
    c2(3)
    v["send"] = run_down(1)
    v.fence()
    c3(1)
    c3(3)
    c1(0)
    c1(2)
    v["w1"] = zswap(v["w1"], 1)
    v["acc_got"] = swap(v.pop("send"), core)
    v["acc_own"] = run_down(0)
    v.fence()
    c0(0)
    c0(2)
    v["w3"] = zswap(v["w3"], 1)
    run_mid()
    v.fence()
    c2(0)
    c2(2)
    v["gp2"] = zswap(v.pop("gmt3"), 1)
    r1("o")
    v.fence()
    v["gp0"] = zswap(v.pop("gmt1"), 1)
    c3(2)
    w2 = v.pop("w2") + v.pop("w3")
    v["z2x"] = zswap(w2[:128], 2)
    v["z2s"] = w2[128:]
    c3(0)
    v["w0"] = v["w0"] + v.pop("w1")
    r2("o", "a")
    run_attn_bwd(2, "gp2", idx_b, True)
    v.fence()
    r1("q2")
    r3("o", "a")
    v["z2y"] = zswap(v.pop("z2s"), 2)
    run_attn_bwd(0, "gp0", idx_b, False)
    v.fence()
    r1("q0")
    r2("q2", "b")
    mlp_sum = high_bits(
        v.pop("w0") + jnp.concatenate([v.pop("z2x"), v.pop("z2y")], axis=0)
    )
    v["ma"], v["mb"] = mlp_sum[:upart], mlp_sum[upart:]
    g1("m")
    n_gn = (128, 256, 128)
    v["gn0"] = zswap(v["gn"][share : share + n_gn[0]], 1)
    r4("o")
    n1_stats = call(
        norm1_stats_kernel,
        sds((8, width), F32),
        flops=full * width * 10,
        bytes_accessed=full * width * 6,
        grid_spec=pltpu.PrefetchScalarGridSpec(
            num_scalar_prefetch=1,
            grid=(steps,),
            in_specs=[tok_spec, run_spec],
            out_specs=pl.BlockSpec((8, width), const2),
        ),
    )(blk, tokens, v["gn"])
    head_sum = jnp.sum(v.pop("hst0") + v.pop("hst2"), axis=-1)
    copied = jnp.concatenate(
        [v.pop("mst")[:4].reshape(-1), n1_stats[:2].reshape(-1), head_sum.reshape(-1)]
    )
    own_parts = []
    for k in range(nmp):
        qb = jnp.zeros((3 * e,), F32) if k % 2 else jnp.sum(v.pop(f"qbg{k}"), axis=1)
        ubg = jnp.pad(v.pop(f"ubg{k}").reshape(half, upart), ((0, half), (0, 0)))
        own_parts.append(jnp.concatenate([qb, jnp.take(ubg, idx_a, axis=0).reshape(-1)]))
    nc = copied.shape[0]
    no = own_parts[0].shape[0]
    v["small"] = jnp.concatenate([copied] + own_parts)
    v.fence()
    r2("q0", "b")
    r3("q2", "b")
    g2("m")
    o = v.pop("o")
    at = share + n_gn[0]
    v["gn1"] = zswap(
        jnp.concatenate([v["gn"][at : at + n_gn[1]], o[part : 2 * part], o[3 * part :]], axis=0), 1
    )
    v["o0"], v["o2"] = o[:part], o[2 * part : 3 * part]
    v["small"] = v["small"] + swap(v["small"], core)
    v.fence()
    r3("q0", "b")
    r4("q2")
    gn1 = v.pop("gn1")
    o0 = v.pop("o0") + gn1[n_gn[1] : n_gn[1] + part]
    o2 = v.pop("o2") + gn1[n_gn[1] + part :]
    v["gn1"] = gn1[: n_gn[1]]
    v["o0"] = o0
    v["y2"] = zswap(jnp.concatenate([v.pop("q2"), o2], axis=0), 2)
    v["gn2"] = zswap(v["gn"][share + n_gn[0] + n_gn[1] :], 1)
    v["small"] = v["small"] + swap(v["small"], px)
    v.fence()
    r4("q0")
    att_sum = high_bits(
        jnp.concatenate([v.pop("q0"), v.pop("o0")], axis=0) + v.pop("y2")
    )
    v["wa"], v["wb"] = att_sum[:hp], att_sum[hp:]
    g1("w")
    ma, mb = (jnp.concatenate(v.pop("m" + t), axis=0) for t in "ab")
    v["mc"] = (ma, mb, swap(ma, core), swap(mb, core))
    v["small"] = v["small"] + swap(v["small"], py)
    v["input_grad"] = call(
        final_kernel,
        sds((share, width), BF16),
        flops=share * width * 20,
        bytes_accessed=share * width * 16,
        grid_spec=pltpu.PrefetchScalarGridSpec(
            num_scalar_prefetch=1,
            grid=(per,),
            in_specs=[tok_spec, run_spec, run_spec, run_spec, vec_spec],
            out_specs=run_spec,
        ),
    )(
        blk,
        tokens,
        v["gn"],
        jnp.concatenate([v.pop("gn0"), v.pop("gn1"), v.pop("gn2")], axis=0),
        v["gm"],
        row1(norm1_gain),
    )
    v.fence()

    def unpack(kernel, a, b, idx, shape):
        return call(
            kernel,
            sds(shape, F32),
            bytes_accessed=2 * 4 * math.prod(shape),
            in_specs=[smem, vmem, vmem],
            out_specs=vmem,
            scratch_shapes=[pltpu.VMEM((PIECES, upart, width), F32)],
        )(idx, a, b)

    g2("w")
    small = high_bits(v.pop("small"))
    parts = [small[nc + k * no : nc + (k + 1) * no] for k in range(nmp)]
    sent = jnp.concatenate([small[:nc], parts[1], parts[3]])
    got = zswap(sent, 1)
    v["small"] = jnp.concatenate([small[:nc], parts[0], parts[2]]) + got
    mc = [a.reshape(half, upart, width) for a in v.pop("mc")]
    v["up_g"] = unpack(unpack_kernel, mc[0], mc[2], idx_a, (width, units))
    v["down_g"] = unpack(unpack_rows_kernel, mc[1], mc[3], idx_b, (units, width))
    v.fence()
    wa, wb = (jnp.concatenate(v.pop("w" + t), axis=0) for t in "ab")
    small = v.pop("small")
    got = zswap(jnp.concatenate([small[:nc], small[nc + no :]]), 2)
    v["small_sum"] = small[: nc + no] + got
    qkv_weight_grad, out_weight_grad = call(
        unpack_att_kernel,
        (sds((3, e, width), F32), sds((e, width), F32)),
        bytes_accessed=2 * 4 * 4 * width * e,
        in_specs=[smem, smem] + [vmem] * 4,
        out_specs=(vmem, vmem),
        scratch_shapes=[pltpu.VMEM((PIECES, hp, width), F32)] * 2,
    )(idx_a, idx_b, wa, swap(wa, core), wb, swap(wb, core))
    qkv_weight_grad = jnp.swapaxes(qkv_weight_grad, 1, 2)

    small_sum = v["small_sum"]
    rows_of = small_sum[: 6 * width].reshape(6, width)
    heads_of = small_sum[6 * width : nc].reshape(3, DH)
    qkv_bias_grad = small_sum[nc : nc + 3 * e].reshape(3, e)
    up_bias_grad = small_sum[nc + 3 * e :]
    return (
        v["block_out"],
        v["input_grad"],
        qkv_weight_grad,
        qkv_bias_grad,
        out_weight_grad,
        rows_of[2],
        v["up_g"],
        up_bias_grad,
        v["down_g"],
        rows_of[3],
        rows_of[4],
        rows_of[5],
        heads_of[0],
        heads_of[1],
        heads_of[2],
        rows_of[0],
        rows_of[1],
    )


def solution(mesh):
    in_specs = (
        P("dp", None),
        P("dp"),
        P(None, None, "mp"),
        P(None, "mp"),
        P("mp", None),
        P(),
        P(None, "mp"),
        P("mp"),
        P("mp", None),
        P(),
        P(),
        P(),
        P(),
        P(),
        P(),
        P(),
        P(),
        P("dp", None),
    )
    out_specs = (
        P(("dp", "mp"), None),
        P(("dp", "mp"), None),
        P(None, None, "mp"),
        P(None, "mp"),
        P("mp", None),
        P(),
        P(None, "mp"),
        P("mp"),
        P("mp", None),
        P(),
        P(),
        P(),
        P(),
        P(),
        P(),
        P(),
        P(),
    )
    return jax.shard_map(shards, mesh=mesh, in_specs=in_specs, out_specs=out_specs, check_vma=False)
```

```python
import functools
import math

import jax
import jax.numpy as jnp
from jax import lax
from jax.experimental import pallas as pl
from jax.experimental.pallas import tpu as pltpu
from jax.sharding import PartitionSpec as P

F32 = jnp.float32
BF16 = jnp.bfloat16
DH = 64
SEQ_LEN = 1024
NORM_EPS = 1e-06
PIECES = 8
SEG_COLS = 128
LOG2E = math.log2(math.e)
SCALE = DH ** (-0.5)
BITS_A = (2, 4, 1)
BITS_B = (4, 2, 1)
MLP_KIND = ("a", "a", "b", "b")
VMEM_LIMIT = 56 * 1024 * 1024


def mm(a, b):
    return lax.dot_general(a, b, (((1,), (0,)), ((), ())), preferred_element_type=F32)


def mm_nt(a, b):
    return lax.dot_general(a, b, (((1,), (1,)), ((), ())), preferred_element_type=F32)


def mm_tn(a, b):
    return lax.dot_general(a, b, (((0,), (0,)), ((), ())), preferred_element_type=F32)


def call(kernel, out_shape, flops=0, bytes_accessed=0, **kw):
    return pl.pallas_call(
        kernel,
        out_shape=out_shape,
        compiler_params=pltpu.CompilerParams(vmem_limit_bytes=VMEM_LIMIT),
        cost_estimate=pl.CostEstimate(
            flops=flops, bytes_accessed=bytes_accessed, transcendentals=0
        ),
        **kw,
    )


def sds(shape, dtype):
    return jax.ShapeDtypeStruct(shape, dtype)


def row_norm(x):
    mean = jnp.mean(x, axis=-1, keepdims=True)
    cen = x - mean
    rstd = lax.rsqrt(jnp.mean(cen * cen, axis=-1, keepdims=True) + NORM_EPS)
    return cen * rstd, rstd


def row_norm_back(f, n, rstd):
    mean_f = jnp.mean(f, axis=-1, keepdims=True)
    mean_fn = jnp.mean(f * n, axis=-1, keepdims=True)
    return (f - mean_f - n * mean_fn) * rstd


def col_norm(x):
    mean = jnp.mean(x, axis=0, keepdims=True)
    cen = x - mean
    rstd = lax.rsqrt(jnp.mean(cen * cen, axis=0, keepdims=True) + NORM_EPS)
    return cen * rstd, rstd


def col_norm_back(f, n, rstd):
    mean_f = jnp.mean(f, axis=0, keepdims=True)
    mean_fn = jnp.mean(f * n, axis=0, keepdims=True)
    return (f - mean_f - n * mean_fn) * rstd


def lane_fold(x):
    out = x[:, :128]
    for t in range(1, x.shape[1] // 128):
        out = out + x[:, t * 128 : (t + 1) * 128]
    return out


def offset_of(s, bits):
    return sum(bit for t, bit in enumerate(bits) if (s >> t) & 1)


def norm1_kernel(blk_ref, x_ref, g_ref, s_ref, out_ref):
    n, _ = row_norm(x_ref[...].astype(F32))
    out_ref[...] = (n * g_ref[...] + s_ref[...]).astype(BF16)


def build_q_aug(q_pre, qg, qs, qaug_ref):
    n, rstd = col_norm(q_pre)
    q_low = (n * qg + qs).astype(BF16)
    scaled = q_low.astype(F32) * (SCALE * LOG2E)
    hi = scaled.astype(BF16)
    lo = (scaled - hi.astype(F32)).astype(BF16)
    qaug_ref[0:DH, :] = hi
    qaug_ref[DH : 2 * DH, :] = lo
    return n, rstd, q_low


def build_k_aug(k_pre, kg, kaug_ref):
    n, rstd = col_norm(k_pre)
    k_low = (n * kg).astype(BF16)
    kaug_ref[:, 0 : 2 * DH] = jnp.concatenate([k_low, k_low], axis=0).T
    return n, rstd, k_low


def bias_col(b_ref, n):
    return b_ref[...].T[0:n, 0:1]


def prep_kernel(
    me_ref, w_ref, o_ref, qb_ref, ub_ref, up_ref, dn_ref,
    att_ref, ob_ref, b_ref, p_ref, u0_ref, u1_ref, d0_ref, d1_ref,
    t_ref, wf_ref,
):
    part = 24
    e = PIECES * part
    me = me_ref[0]
    b_ref[...] = jnp.zeros(b_ref.shape, F32)
    for s in range(3):
        wf_ref[...] = w_ref[s].astype(F32)
        rows = wf_ref[pl.ds(pl.multiple_of(me * part, 8), part), :]
        att_ref[s * part : (s + 1) * part, :] = rows
        b_ref[0:1, s * e : (s + 1) * e] = qb_ref[s : s + 1, :]
    upart = ub_ref.shape[1]
    for s in range(PIECES // 2):
        b_ref[1:2, s * upart : (s + 1) * upart] = ub_ref[pl.ds(me ^ offset_of(s, BITS_A), 1), :]
    wf_ref[...] = o_ref[...].astype(F32)
    rows = wf_ref[pl.ds(pl.multiple_of(me * part, 8), part), :]
    att_ref[3 * part : 4 * part, :] = rows
    ob_ref[0:part, :] = rows
    att_ref[4 * part :, :] = b_ref[...]
    ob_ref[part:, :] = b_ref[...]

    t_ref[...] = up_ref[...].astype(F32).T

    def at_piece(r):
        return pl.ds(pl.multiple_of((me ^ r) * upart, 32), upart)

    p_ref[0:upart, :] = t_ref[at_piece(0), :]
    p_ref[upart:, :] = dn_ref[at_piece(0), :].astype(F32)
    for i, (u_ref, d_ref) in enumerate(((u0_ref, d0_ref), (u1_ref, d1_ref))):
        for j in range(2):
            u_ref[j] = t_ref[at_piece(offset_of(2 * i + j, BITS_A)), :].astype(BF16)
            d_ref[j] = dn_ref[at_piece(offset_of(2 * i + j, BITS_B)), :]


def attend(x_ref, wt_ref, b_ref, hv_ref, kmask_ref, qhot_ref, outs, qaug_ref, kaug_ref):
    qpre_ref, kpre_ref, vt_ref, mixt_ref, mixf_ref, mixs_ref, l_ref = outs
    e = qpre_ref.shape[0]
    full = x_ref.shape[0]
    share = full // 2
    heads = e // DH
    x = x_ref[...]
    bias = bias_col(b_ref, 3 * e)
    qpre_ref[...] = mm_nt(wt_ref[0:e, :], x) + bias[0:e]
    kpre_ref[...] = mm_nt(wt_ref[e : 2 * e, :], x) + bias[e : 2 * e]
    vt_ref[...] = (mm_nt(wt_ref[2 * e : 3 * e, :], x) + bias[2 * e :]).astype(BF16)
    qaug_ref[2 * DH :, :] = qhot_ref[...]
    kaug_ref[:, 2 * DH :] = kmask_ref[...]
    ones = jnp.ones((16, full), BF16)
    for h in range(heads):
        hs = slice(h * DH, (h + 1) * DH)
        build_q_aug(qpre_ref[hs, :], hv_ref[:, 0:1], hv_ref[:, 1:2], qaug_ref)
        build_k_aug(kpre_ref[hs, :], hv_ref[:, 2:3], kaug_ref)
        prob = jnp.exp2(mm(kaug_ref[...], qaug_ref[...])).astype(BF16)
        vaug = jnp.concatenate([vt_ref[hs, :], ones], axis=0)
        o = mm(vaug, prob)
        total = o[DH : DH + 1, :]
        l_ref[h : h + 1, :] = total
        mix = o[0:DH, :] / total
        mixf_ref[hs, :] = mix
        mixt_ref[hs, :] = mix[:, 0:share].astype(BF16)
        at = h * share
        for c in range(0, share, 256):
            block_no, lane = divmod(at + c, x.shape[1])
            mixs_ref[block_no * DH : (block_no + 1) * DH, lane : lane + 256] = mix[
                :, share + c : share + c + 256
            ]


def attn_fwd_own_kernel(x_ref, wt_ref, b_ref, hv_ref, kmask_ref, qhot_ref, *refs):
    attend(x_ref, wt_ref, b_ref, hv_ref, kmask_ref, qhot_ref, refs[:7], *refs[7:])


def attn_fwd_kernel(
    ia_ref, ib_ref, a0_ref, a1_ref, b0_ref, b1_ref, x_ref, b_ref, hv_ref, kmask_ref, qhot_ref,
    wt_ref, ow_ref, ow1_ref, ow3_ref, *refs,
):
    wa_ref, wb_ref = refs[-2:]
    part = 24
    e = PIECES * part
    half = PIECES // 2
    wa_ref[0:half] = a0_ref[...]
    wa_ref[half:] = a1_ref[...]
    wb_ref[0:half] = b0_ref[...]
    wb_ref[half:] = b1_ref[...]

    def rows(w_ref, i_ref, at):
        return jnp.concatenate(
            [w_ref[i_ref[p], at * part : (at + 1) * part, :] for p in range(PIECES)], axis=0
        ).astype(BF16)

    wt_ref[0:e, :] = rows(wa_ref, ia_ref, 0)
    wt_ref[e : 2 * e, :] = rows(wa_ref, ia_ref, 1)
    wt_ref[2 * e : 3 * e, :] = rows(wb_ref, ib_ref, 0)
    ow_ref[...] = rows(wb_ref, ib_ref, 1)
    ow1_ref[...] = rows(wa_ref, ia_ref, 2)
    ow3_ref[...] = rows(wb_ref, ib_ref, 2)
    attend(x_ref, wt_ref, b_ref, hv_ref, kmask_ref, qhot_ref, refs[:7], *refs[7:9])


def unmix(ref, heads, share):
    width = ref.shape[1]
    rows = []
    for h in range(heads):
        cols = []
        for c in range(0, share, 256):
            block_no, lane = divmod(h * share + c, width)
            cols.append(ref[block_no * DH : (block_no + 1) * DH, lane : lane + 256])
        rows.append(jnp.concatenate(cols, axis=1))
    return jnp.concatenate(rows, axis=0).astype(BF16)


def mix_of(ref, share):
    if ref.dtype == BF16:
        return ref[...]
    return unmix(ref, ref.shape[0] * ref.shape[1] // (DH * share), share)


def out_norm2_kernel(nslot, blk_ref, x_ref, *refs):
    mixes = refs[:nslot]
    ws = refs[nslot : 2 * nslot]
    ob_ref, g_ref, s_ref, mid_ref, sec_ref, secf_ref = refs[2 * nslot :]
    acc = x_ref[...].astype(F32) + ob_ref[...]
    for k in range(nslot):
        acc = acc + mm_tn(mix_of(mixes[k], x_ref.shape[0]), ws[k][...])
    mid_ref[...] = acc
    n, _ = row_norm(acc)
    sec = (n * g_ref[...] + s_ref[...]).astype(BF16)
    sec_ref[...] = sec
    secf_ref[...] = sec.astype(F32)


def mlp_kernel(
    kind, keeps, sec_ref, secp_ref, cot_ref, cotp_ref, u0_ref, u1_ref, d0_ref, d1_ref, b_ref, *refs
):
    if keeps:
        p_ref, hid_ref, gp_ref, ub_ref, db_ref, k0_ref, k1_ref, s0_ref, s1_ref, gb_ref = refs
    else:
        hid_ref, gp_ref, ub_ref, db_ref, up_ref, uq_ref, k0_ref, k1_ref, sd_ref, gb_ref = refs
    part = u0_ref.shape[1]
    share = sec_ref.shape[0]
    up = jnp.concatenate([u0_ref[0], u0_ref[1], u1_ref[0], u1_ref[1]], axis=0).astype(BF16)
    down = jnp.concatenate([d0_ref[0], d1_ref[0], d0_ref[1], d1_ref[1]], axis=0).astype(BF16)
    ub_ref[...] = up
    db_ref[...] = down
    bias = b_ref[1:2, 0 : up.shape[0]]
    for r, (s_ref, c_ref) in enumerate(((sec_ref, cot_ref), (secp_ref, cotp_ref))):
        rows = slice(r * share, (r + 1) * share)
        sec = s_ref[...].astype(BF16)
        cot = c_ref[...].astype(BF16)
        pre = mm_nt(sec, up) + bias
        cdf = 0.5 * (1.0 + lax.erf(pre * (1.0 / math.sqrt(2.0))))
        hid = (pre * cdf).astype(BF16)
        pdf = jnp.exp(-0.5 * pre * pre) * (1.0 / math.sqrt(2.0 * math.pi))
        gpre = (mm_nt(cot, down) * (cdf + pre * pdf)).astype(BF16)
        hid_ref[rows, :] = hid
        gp_ref[rows, :] = gpre
        gb_r = jnp.sum(gpre.astype(F32), axis=0, keepdims=True)
        gd_r = mm_tn(hid, cot)
        gu_r = mm_tn(gpre, sec)
        if r == 0:
            gb, gd, gu = gb_r, gd_r, gu_r
        else:
            gb, gd, gu = gb + gb_r, gd + gd_r, gu + gu_r
    gb_ref[...] = gb
    order = (0, 1, 2, 3) if kind == "a" else (0, 2, 1, 3)
    gu_at = [gu[i * part : (i + 1) * part] for i in order]
    gd_at = [gd[i * part : (i + 1) * part] for i in order]
    if keeps:
        gu_at[3] = gu_at[3] + p_ref[0:part, :]
        gu_at[2] = gu_at[2] + p_ref[part:, :]
        for i, ref in enumerate((k0_ref, k1_ref, s0_ref, s1_ref)):
            ref[0:part, :] = gu_at[i]
            ref[part:, :] = gd_at[i]
    else:
        up_ref[0:part, :] = gu_at[3]
        up_ref[part:, :] = gu_at[2]
        uq_ref[0:part, :] = gu_at[0]
        uq_ref[part:, :] = gu_at[1]
        k0_ref[...] = gd_at[0]
        k1_ref[...] = gd_at[1]
        sd_ref[0:part, :] = gd_at[3]
        sd_ref[part:, :] = gd_at[2]


def down_kernel(nslot, *refs):
    hids = refs[:nslot]
    gps = refs[nslot : 2 * nslot]
    ubs = refs[2 * nslot : 3 * nslot]
    dbs = refs[3 * nslot : 4 * nslot]
    out_ref = refs[4 * nslot]
    cat = lambda refs, axis: jnp.concatenate([r[...] for r in refs], axis=axis)
    out_ref[0] = mm(cat(hids, 1), cat(dbs, 0))
    out_ref[1] = mm(cat(gps, 1), cat(ubs, 0))


def mid_kernel(nslot, idx_ref, mid_ref, own_ref, got_ref, cot_ref, db_ref, g_ref, *refs):
    ows = refs[:nslot]
    mixts = refs[nslot : 2 * nslot]
    gmts = refs[2 * nslot : 3 * nslot]
    bo_ref, gm_ref, gow_keep, gow_send, st_ref = refs[3 * nslot :]
    part = 24
    mid = mid_ref[...]
    bo_ref[...] = (mid + (own_ref[0] + got_ref[0]) + db_ref[...]).astype(BF16)
    n, rstd = row_norm(mid)
    e = own_ref[1] + got_ref[1]
    cot = cot_ref[...].astype(F32)
    gm = cot + row_norm_back(e * g_ref[...], n, rstd)
    gm_ref[...] = gm
    gm_low = gm.astype(BF16)
    st_ref[0:1, :] = jnp.sum(e * n, axis=0, keepdims=True)
    st_ref[1:2, :] = jnp.sum(e, axis=0, keepdims=True)
    st_ref[2:3, :] = jnp.sum(gm_low.astype(F32), axis=0, keepdims=True)
    st_ref[3:4, :] = jnp.sum(cot, axis=0, keepdims=True)
    st_ref[4:8, :] = jnp.zeros((4, mid.shape[1]), F32)
    for k in range(nslot):
        gmts[k][...] = mm_nt(ows[k][...], gm_low).astype(gmts[k].dtype)
        g = mm(mix_of(mixts[k], mid.shape[0]), gm_low)
        for p in range(PIECES):
            at = idx_ref[p]
            rows = slice(k * part, (k + 1) * part)

            @pl.when(at < PIECES // 2)
            def _():
                gow_keep[at, rows, :] = g[p * part : (p + 1) * part, :]

            @pl.when(at >= PIECES // 2)
            def _():
                gow_send[at - PIECES // 2, rows, :] = g[p * part : (p + 1) * part, :]


def attn_bwd_kernel(
    first, idx_ref, x_ref, qpre_ref, kpre_ref, vt_ref, wt_ref, gmt_ref, gmtp_ref, mixf_ref, l_ref,
    hv_ref, kmask_ref, qhot_ref, *refs
):
    if first:
        gk_ref, gs_ref, gn_ref, st_ref, gb_ref, qaug_ref, kaug_ref, gpt_ref = refs
    else:
        gn_in, gk_ref, gs_ref, gn_ref, st_ref, gb_ref, qaug_ref, kaug_ref, gpt_ref = refs
    part = 24
    e = PIECES * part
    full = x_ref.shape[0]
    heads = e // DH
    qaug_ref[2 * DH :, :] = qhot_ref[...]
    kaug_ref[:, 2 * DH :] = kmask_ref[...]
    qg, qs, kg = hv_ref[:, 0:1], hv_ref[:, 1:2], hv_ref[:, 2:3]
    qg_sum = jnp.zeros((DH, 128), F32)
    qs_sum = jnp.zeros((DH, 128), F32)
    kg_sum = jnp.zeros((DH, 128), F32)
    row_no = lax.broadcasted_iota(jnp.int32, (DH, full), 0)
    one_rows = (row_no < 3).astype(F32).astype(BF16)
    for h in range(heads):
        hs = slice(h * DH, (h + 1) * DH)
        qn, qr, q_low = build_q_aug(qpre_ref[hs, :], qg, qs, qaug_ref)
        kn, kr, k_low = build_k_aug(kpre_ref[hs, :], kg, kaug_ref)
        inv = 1.0 / l_ref[h : h + 1, :]
        gm = jnp.concatenate(
            [gmt_ref[hs, :].astype(F32), gmtp_ref[hs, :].astype(BF16).astype(F32)], axis=1
        )
        go_low = (gm * inv).astype(BF16)
        delta = -jnp.sum(go_low.astype(F32) * mixf_ref[hs, :], axis=0, keepdims=True)
        d0 = delta.astype(BF16).astype(F32)
        d1 = (delta - d0).astype(BF16).astype(F32)
        d2 = delta - d0 - d1
        extra = jnp.where(
            row_no == 0, d0, jnp.where(row_no == 1, d1, jnp.where(row_no == 2, d2, 0.0))
        ).astype(BF16)
        goaug = jnp.concatenate([go_low, extra], axis=0)
        vaug = jnp.concatenate([vt_ref[hs, :], one_rows], axis=0).T
        prob = jnp.exp2(mm(kaug_ref[...], qaug_ref[...]))
        ds = (prob * mm(vaug, goaug)).astype(BF16)
        gv = mm_nt(go_low, prob.astype(BF16))
        gk = mm_nt(q_low, ds) * SCALE
        gq = mm(k_low, ds) * SCALE
        qg_sum += lane_fold(gq * qn)
        qs_sum += lane_fold(gq)
        kg_sum += lane_fold(gk * kn)
        gpt_ref[h * DH : (h + 1) * DH, :] = col_norm_back(gq * qg, qn, qr).astype(BF16)
        gpt_ref[e + h * DH : e + (h + 1) * DH, :] = col_norm_back(gk * kg, kn, kr).astype(BF16)
        gpt_ref[2 * e + h * DH : 2 * e + (h + 1) * DH, :] = gv.astype(BF16)
    st_ref[0] = qg_sum
    st_ref[1] = qs_sum
    st_ref[2] = kg_sum
    gp = gpt_ref[...]
    gb_ref[...] = lane_fold(gp.astype(F32))
    gw = mm(gp, x_ref[...])

    def put(ref, at, p):
        for s in range(3):
            ref[at, s * part : (s + 1) * part, :] = gw[s * e + p * part : s * e + (p + 1) * part, :]

    for p in range(PIECES):
        at = idx_ref[p]

        @pl.when(at < PIECES // 2)
        def _():
            put(gk_ref, at, p)

        @pl.when(at >= PIECES // 2)
        def _():
            put(gs_ref, at - PIECES // 2, p)

    gn = mm_tn(gp, wt_ref[...])
    gn_ref[...] = gn if first else gn_in[...] + gn


def norm1_stats_kernel(blk_ref, x_ref, gn_ref, out_ref):
    n, _ = row_norm(x_ref[...].astype(F32))
    e = gn_ref[...]

    @pl.when(pl.program_id(0) == 0)
    def _():
        out_ref[...] = jnp.zeros_like(out_ref)

    out_ref[0:1, :] += jnp.sum(e * n, axis=0, keepdims=True)
    out_ref[1:2, :] += jnp.sum(e, axis=0, keepdims=True)


def final_kernel(blk_ref, x_ref, gn_ref, got_ref, gm_ref, g_ref, out_ref):
    n, rstd = row_norm(x_ref[...].astype(F32))
    f = (gn_ref[...] + got_ref[...]) * g_ref[...]
    out_ref[...] = (gm_ref[...] + row_norm_back(f, n, rstd)).astype(BF16)


def both(refs, to_ref):
    half = PIECES // 2
    to_ref[0:half] = refs[0][...]
    to_ref[half:] = refs[1][...]


def lay_out(refs, to_ref):
    part = to_ref.shape[1]
    for i, ref in enumerate(refs):
        for j in range(2):
            to_ref[2 * i + j] = ref[j * part : (j + 1) * part, :]


def unpack_kernel(idx_ref, a_ref, b_ref, c_ref, d_ref, out_ref, s_ref):
    lay_out((a_ref, b_ref, c_ref, d_ref), s_ref)
    whole = jnp.concatenate([s_ref[idx_ref[p]] for p in range(PIECES)], axis=0)
    out_ref[...] = whole.T


def unpack_rows_kernel(idx_ref, a_ref, b_ref, c_ref, d_ref, out_ref, s_ref):
    part = s_ref.shape[1]
    lay_out((a_ref, b_ref, c_ref, d_ref), s_ref)
    for p in range(PIECES):
        out_ref[p * part : (p + 1) * part, :] = s_ref[idx_ref[p]]


def unpack_att_kernel(
    ia_ref, ib_ref, a0_ref, a1_ref, b0_ref, b1_ref, qkv_ref, out_ref, a_ref, b_ref
):
    part = a_ref.shape[1] // 2
    both((a0_ref, a1_ref), a_ref)
    both((b0_ref, b1_ref), b_ref)

    def whole(ref, i_ref, off):
        return jnp.concatenate(
            [ref[i_ref[p], off : off + part, :] for p in range(PIECES)], axis=0
        )

    qkv_ref[0] = whole(a_ref, ia_ref, 0)
    qkv_ref[1] = whole(a_ref, ia_ref, part)
    qkv_ref[2] = whole(b_ref, ib_ref, 0)
    out_ref[...] = whole(b_ref, ib_ref, part)


def swap_mp(a, k, size):
    return lax.ppermute(a, "mp", [(s, s ^ k) for s in range(size)])


def swap_plane(a, bit, size):
    return lax.ppermute(a, "dp", [(d, d ^ bit) for d in range(size)])


def storage_of(r, bits):
    return sum(jnp.where((r & bit) != 0, 1 << t, 0) for t, bit in enumerate(bits))


class Stages:
    def __init__(self):
        self.live = {}

    def __setitem__(self, name, value):
        self.live[name] = value

    def __getitem__(self, name):
        return self.live[name]

    def pop(self, name):
        return self.live.pop(name)

    def fence(self, *still_flying):
        now = {n: a for n, a in self.live.items() if n not in still_flying}
        leaves, tree = jax.tree.flatten(now)
        self.live.update(jax.tree.unflatten(tree, lax.optimization_barrier(leaves)))


def shards(
    tokens,
    seg_ids,
    qkv_weight,
    qkv_bias,
    out_weight,
    out_bias,
    up_weight,
    up_bias,
    down_weight,
    down_bias,
    norm1_gain,
    norm1_shift,
    query_gain,
    query_shift,
    key_gain,
    norm2_gain,
    norm2_shift,
    cotangent,
):
    ndp = lax.axis_size("dp")
    nmp = lax.axis_size("mp")
    dp_no = lax.axis_index("dp")
    mp_no = lax.axis_index("mp")
    me = dp_no % PIECES
    row_count, width = tokens.shape
    share = row_count // nmp
    full = SEQ_LEN
    assert full == 2 * share and nmp == 4 and ndp % PIECES == 0
    e = qkv_weight.shape[2]
    part = e // PIECES
    units = up_weight.shape[1]
    upart = units // PIECES
    half = PIECES // 2
    mine = half * upart
    core, px, py = 1, 2, 4

    vmem = pl.BlockSpec(memory_space=pltpu.VMEM)
    smem = pl.BlockSpec(memory_space=pltpu.SMEM)
    row1 = lambda v: v.reshape(1, -1)
    col = lambda v: v.reshape(-1, 1)
    swap = lambda a, bit: swap_plane(a, bit, ndp)
    zswap = lambda a, k: swap_mp(a, k, nmp)
    v = Stages()

    me1 = me.astype(jnp.int32).reshape(1)
    qkv_t = jnp.swapaxes(qkv_weight, 1, 2)
    wt0 = qkv_t.reshape(3 * e, width)
    att_piece, ob_piece, bias0, mlp_piece, u0, u1, d0, d1 = call(
        prep_kernel,
        (
            sds((4 * part + 8, width), F32),
            sds((part + 8, width), F32),
            sds((8, width), F32),
            sds((2 * upart, width), F32),
            *[sds((2, upart, width), BF16)] * 4,
        ),
        bytes_accessed=9_000_000,
        in_specs=[smem] + [vmem] * 6,
        out_specs=(vmem,) * 8,
        scratch_shapes=[pltpu.VMEM((units, width), F32), pltpu.VMEM((e, width), F32)],
    )(
        me1, qkv_t, out_weight, qkv_bias, up_bias.reshape(PIECES, upart), up_weight, down_weight
    )

    n_gn = (256, 136, 120)
    n_z2 = 56
    numbers = jnp.arange(PIECES, dtype=jnp.int32)
    idx_a = storage_of(numbers ^ me, BITS_A).astype(jnp.int32)
    idx_b = storage_of(numbers ^ me, BITS_B).astype(jnp.int32)

    block = 256
    per = share // block
    steps = 2 * per
    tile_no = jnp.arange(steps, dtype=jnp.int32)
    blk = jnp.where(tile_no < per, mp_no * per + tile_no, (mp_no ^ 1) * per + tile_no - per).astype(
        jnp.int32
    )
    const2 = lambda t, b: (0, 0)
    tok_spec = pl.BlockSpec((block, width), lambda t, b: (b[t], 0))
    run_spec = pl.BlockSpec((block, width), lambda t, b: (t, 0))
    vec_spec = pl.BlockSpec((1, width), const2)

    def run_norm1():
        return call(
            norm1_kernel,
            sds((full, width), BF16),
            flops=full * width * 10,
            bytes_accessed=full * width * 4,
            grid_spec=pltpu.PrefetchScalarGridSpec(
                num_scalar_prefetch=1,
                grid=(steps,),
                in_specs=[tok_spec, vec_spec, vec_spec],
                out_specs=run_spec,
            ),
        )(blk, tokens, row1(norm1_gain), row1(norm1_shift))

    seg_own = lax.dynamic_slice_in_dim(seg_ids, mp_no * share, share, 0)
    seg_other = lax.dynamic_slice_in_dim(seg_ids, (mp_no ^ 1) * share, share, 0)
    seg_keys = jnp.concatenate([seg_own, seg_other])
    qhot = (
        lax.broadcasted_iota(jnp.int32, (SEG_COLS, full), 0) == seg_keys[None, :]
    ).astype(BF16)
    kmask = jnp.where(
        lax.broadcasted_iota(jnp.int32, (full, SEG_COLS), 1) == seg_keys[:, None], 0.0, -1e30
    ).astype(BF16)
    hv = jnp.stack([query_gain, query_shift, key_gain], axis=1)
    scratch = [
        pltpu.VMEM((2 * DH + SEG_COLS, full), BF16),
        pltpu.VMEM((full, 2 * DH + SEG_COLS), BF16),
    ]

    def whole(a):
        return pl.BlockSpec(a.shape, lambda t: (0,) * len(a.shape))

    def bias_at(block_no):
        return pl.BlockSpec((8, width), lambda t: (block_no, 0))

    att_names = ["qpre", "kpre", "vt", "mixt", "mixf", "mixs", "l"]
    att_shapes = [
        sds((e, full), F32),
        sds((e, full), F32),
        sds((e, full), BF16),
        sds((e, share), BF16),
        sds((e, full), F32),
        sds((e * share // width, width), F32),
        sds((8, full), F32),
    ]
    mix_rows = e * share // width

    def run_attn_own():
        outs = call(
            attn_fwd_own_kernel,
            tuple(att_shapes),
            flops=2 * (full * width * e * 3 + full * full * e * 8),
            bytes_accessed=10_000_000,
            in_specs=[vmem] * 6,
            out_specs=(vmem,) * 7,
            scratch_shapes=scratch,
        )(v["normed"], wt0, bias0, hv, kmask, qhot)
        v["st0"] = dict(zip(att_names, outs))
        v["st0"]["wt"] = wt0
        v["st0"]["ow"] = out_weight

    def run_attn_far():
        shapes = [sds((3 * e, width), BF16)] + [sds((e, width), BF16)] * 3 + att_shapes
        args = [
            *v.pop("ta"), *v.pop("tb"), v["normed"], v["t2"], hv, kmask, qhot,
        ]
        specs = [whole(a) for a in args]
        specs[5] = bias_at(4 * part // 8)
        outs = call(
            attn_fwd_kernel,
            tuple(shapes),
            flops=2 * (full * width * e * 3 + full * full * e * 8),
            bytes_accessed=10_000_000,
            grid=(1,),
            in_specs=[smem, smem] + specs,
            out_specs=tuple(whole(a) for a in shapes),
            scratch_shapes=scratch
            + [pltpu.VMEM((PIECES, 3 * part, width), F32)] * 2,
        )(idx_a, idx_b, *args)
        v["st2"] = dict(zip(["wt", "ow", "ow1", "ow3"] + att_names, outs))

    def by_slot():
        st0, st2 = v["st0"], v["st2"]
        mixes = [st0["mixt"], v["mix0"], st2["mixt"], v["mix2"]]
        ows = [st0["ow"], st2["ow1"], st2["ow"], st2["ow3"]]
        return mixes, ows

    def run_out():
        own_spec = pl.BlockSpec((share, width), lambda t, b: (b[0] // per, 0))
        whole2 = lambda shape: pl.BlockSpec(shape, lambda t, b: (0,) * len(shape))
        mixes, ows = by_slot()
        v["middle"], v["second"], v["sec_f"] = call(
            functools.partial(out_norm2_kernel, nmp),
            (sds((share, width), F32), sds((share, width), BF16), sds((share, width), F32)),
            flops=2 * share * width * e * nmp,
            bytes_accessed=8_000_000,
            grid_spec=pltpu.PrefetchScalarGridSpec(
                num_scalar_prefetch=1,
                grid=(1,),
                in_specs=[own_spec]
                + [whole2((e, share)), whole2((mix_rows, width))] * 2
                + [whole2((e, width))] * nmp
                + [whole2((1, width))] * 3,
                out_specs=(whole2((share, width)),) * 3,
            ),
        )(blk, tokens, *mixes, *ows, row1(out_bias), row1(norm2_gain), row1(norm2_shift))

    def run_mlp(k, up, down, bias, block_no):
        keeps = k % 2 == 0
        args = [
            v["second"], v["sec_p"], v["cot"], v["cot_p"], up[0], up[1], down[0], down[1], bias,
        ]
        if keeps:
            args.append(v.pop(f"p{k + 1}"))
        specs = [whole(a) for a in args]
        specs[8] = bias_at(block_no)
        piece = lambda n: sds((n * upart, width), F32)
        shapes = (
            *[sds((full, mine), BF16)] * 2,
            *[sds((mine, width), BF16)] * 2,
            *([piece(2)] * 4 if keeps else [piece(2), piece(2), piece(1), piece(1), piece(2)]),
            sds((1, mine), F32),
        )
        res = call(
            functools.partial(mlp_kernel, MLP_KIND[k], keeps),
            shapes,
            flops=2 * full * width * mine * 4,
            bytes_accessed=12_000_000,
            grid=(1,),
            in_specs=specs,
            out_specs=tuple(whole(a) for a in shapes),
        )(*args)
        v[f"h{k}"] = res[:4]
        v[f"ubg{k}"] = res[-1]
        if keeps:
            v[f"w{k}"] = res[4:8]
        else:
            v[f"p{k}"], v[f"q{k}u"] = res[4], res[5]
            v[f"w{k}"] = res[6:9]

    def run_down(r):
        row_spec = pl.BlockSpec((share, mine), lambda t: (r, 0))
        w_spec = pl.BlockSpec((mine, width), lambda t: (0, 0))
        return call(
            functools.partial(down_kernel, nmp),
            sds((2, share, width), F32),
            flops=4 * share * width * mine * nmp,
            bytes_accessed=11_000_000,
            grid=(1,),
            in_specs=[row_spec] * (2 * nmp) + [w_spec] * (2 * nmp),
            out_specs=pl.BlockSpec((2, share, width), lambda t: (0, 0, 0)),
        )(*[v[f"h{k}"][i] for i in range(4) for k in range(nmp)])

    def run_mid():
        mixes, ows = by_slot()
        shapes = (
            *[sds((e, share), F32 if k % 2 else BF16) for k in range(nmp)],
            sds((share, width), BF16),
            sds((share, width), F32),
            sds((half, nmp * part, width), F32),
            sds((half, nmp * part, width), F32),
            sds((8, width), F32),
        )
        args = [
            v["middle"], v.pop("acc_own"), v.pop("acc_got"), v["cot"], row1(down_bias),
            row1(norm2_gain), *ows, *mixes,
        ]
        specs = [whole(a) for a in args]
        for k in (1, 3):
            specs[6 + nmp + k] = pl.BlockSpec((mix_rows, width), lambda t: (0, 0))
        *gmts, bo, gm, keep, send, mst = call(
            functools.partial(mid_kernel, nmp),
            shapes,
            flops=2 * share * width * e * nmp * 2,
            bytes_accessed=12_000_000,
            grid=(1,),
            in_specs=[smem] + specs,
            out_specs=tuple(whole(a) for a in shapes),
        )(idx_b, *args)
        v["block_out"], v["gm"], v["mst"] = bo, gm, mst
        for k in range(nmp):
            v[f"gmt{k}"] = gmts[k]
        v["o"] = (keep, send)

    def run_attn_bwd(k, got, idx, first):
        st = v.pop(f"st{k}")
        args = [
            idx, v["normed"], st["qpre"], st["kpre"], st["vt"], st["wt"], v.pop(f"gmt{k}"),
            v.pop(got), st["mixf"], st["l"], hv, kmask, qhot,
        ]
        alias = {}
        if not first:
            args.append(v["gn"])
            alias = {len(args) - 1: 2}
        keep, send, gn, hst, gb = call(
            functools.partial(attn_bwd_kernel, first),
            (
                sds((half, 3 * part, width), F32),
                sds((half, 3 * part, width), F32),
                sds((full, width), F32),
                sds((3, DH, 128), F32),
                sds((3 * e, 128), F32),
            ),
            flops=2 * (full * width * e * 6 + full * full * e * 20),
            bytes_accessed=14_000_000,
            in_specs=[smem] + [vmem] * (len(args) - 1),
            out_specs=(vmem,) * 5,
            scratch_shapes=scratch + [pltpu.VMEM((3 * e, full), BF16)],
            input_output_aliases=alias,
        )(*args)
        v[f"q{k}"] = (keep, send)
        v["gn"] = gn
        v[f"hst{k}"] = hst
        v[f"qbg{k}"] = gb

    def g1(n):
        a, b = v[n + "a"], v[n + "b"]
        v[n + "a"] = (a, swap(a, px))
        v[n + "b"] = (b, swap(b, py))

    def g2(n):
        a, b = (jnp.stack(v[n + t]) for t in "ab")
        v[n + "a"] = (a, swap(a, py))
        v[n + "b"] = (b, swap(b, px))

    def g3(n):
        a, b = (jnp.concatenate(v[n + t], axis=0) for t in "ab")
        v[n + "a"] = (a, swap(a, core))
        v[n + "b"] = (b, swap(b, core))

    def r1(n):
        keep, send = v[n]
        v[n] = (keep, swap(send, core))

    def r2(n, kind):
        keep, got = v[n]
        keep_sum = keep[:2] + got[:2]
        v[n] = (keep_sum, swap(keep[2:] + got[2:], py if kind == "a" else px))

    def r3(n, kind):
        keep, got = v[n]
        v[n] = (keep[0] + got[0], swap(keep[1] + got[1], px if kind == "a" else py))

    def r4(n):
        keep, got = v[n]
        v[n] = keep + got

    def first_link(k):
        return py if MLP_KIND[k] == "a" else px

    def second_link(k):
        return px if MLP_KIND[k] == "a" else py

    def c1(k):
        k0, k1, s0, s1 = v[f"w{k}"]
        v[f"w{k}"] = (k0, k1, s0, swap(s1, first_link(k)))

    def c0(k):
        k0, k1, s0, g1 = v[f"w{k}"]
        v[f"w{k}"] = (k0, k1, g1, swap(s0, first_link(k)))

    def c2(k):
        k0, k1, g1, g0 = v[f"w{k}"]
        q = v.pop(f"q{k + 1}u")
        k1 = jnp.concatenate([k1[:upart] + q[upart:], k1[upart:]], axis=0) + g1
        v[f"w{k}"] = (k0, g0, q[:upart], swap(k1, second_link(k)))

    def c3(k):
        k0, g0, q, g = v[f"w{k}"]
        d = v.pop(f"d{k + 1}")
        total = k0 + g0 + g
        v[f"w{k}"] = jnp.concatenate([total[:upart] + q, total[upart:] + d], axis=0)

    def e1(k):
        k0, k1, s = v[f"w{k}"]
        v[f"w{k}"] = (k0, k1, swap(s, first_link(k)))

    def e2(k):
        k0, k1, g = v[f"w{k}"]
        v[f"w{k}"] = (k0 + g[upart:], swap(k1 + g[:upart], second_link(k)))

    def e3(k):
        k0, g = v[f"w{k}"]
        v[f"w{k}"] = k0 + g

    inner = (mp_no == 1) | (mp_no == 2)

    def middle_swap(a):
        return lax.ppermute(a, "mp", [(1, 2), (2, 1)])

    def pass_out(a):
        return lax.ppermute(a, "mp", [(1, 0), (2, 3)])

    def high_bits(a):
        bit = PIECES
        while bit < ndp:
            a = a + swap(a, bit)
            bit *= 2
        return a

    v["cot"] = lax.dynamic_slice_in_dim(cotangent, mp_no * share, share, 0)
    v["piece"] = mlp_piece
    v["o3"] = zswap(ob_piece, 3)
    v["o1"] = zswap(ob_piece, 1)
    v["t2"] = zswap(att_piece, 2)
    v["cot_p"] = swap(v["cot"].astype(F32), core)
    v["normed"] = run_norm1()
    v.fence()
    hp = 2 * part
    t2, o1, o3 = v["t2"], v["o1"], v["o3"]
    v["ta"] = jnp.concatenate([t2[:hp], o1[:part]], axis=0)
    v["tb"] = jnp.concatenate([t2[hp : 2 * hp], o3[:part]], axis=0)
    g1("t")
    v["m1"] = zswap(v["piece"], 1)
    v["mid_a"] = middle_swap(v.pop("piece"))
    v.fence()
    m1 = v["m1"]
    to_y = jnp.concatenate([*v["ta"], m1[upart:]], axis=0)
    to_x = jnp.concatenate([*v["tb"], m1[:upart]], axis=0)
    v["ta"] = (to_y, swap(to_y, py))
    v["tb"] = (to_x, swap(to_x, px))
    v["mid_b"] = middle_swap(v.pop("m1"))
    v["end_a"] = pass_out(v["mid_a"])
    run_attn_own()
    v.fence()
    nt = 2 * 3 * part
    ya, yb = v.pop("ta")
    xa, xb = v.pop("tb")
    v["m1a"], v["m1b"] = (xa[nt:], xb[nt:]), (ya[nt:], yb[nt:])
    v["ta"], v["tb"] = (
        tuple(
            a.reshape(half, 3 * part, width) for a in (both_, swap(both_, core))
        )
        for both_ in (
            jnp.concatenate([ya[:nt], yb[:nt]], axis=0),
            jnp.concatenate([xa[:nt], xb[:nt]], axis=0),
        )
    )
    run_attn_far()
    g2("m1")
    v["mix0"] = zswap(jnp.concatenate([v["st0"].pop("mixs"), v["mid_b"]], axis=0), 1)
    v.fence()
    v["mix2"] = zswap(v["st2"].pop("mixs"), 1)
    run_out()
    m3 = jnp.where(inner, v.pop("mid_a"), v["mix0"][mix_rows:])
    m2 = jnp.where(inner, v.pop("mid_b"), v.pop("end_a"))
    to_x = jnp.concatenate([m3[:upart], m2[:upart]], axis=0)
    to_y = jnp.concatenate([m3[upart:], m2[upart:]], axis=0)
    v["ma"], v["mb"] = (to_x, swap(to_x, px)), (to_y, swap(to_y, py))
    v.fence()
    for t in "ab":
        own, got = v.pop(f"m{t}")
        v[f"m3{t}"] = (own[:upart], got[:upart])
        v[f"m2{t}"] = (own[upart:], got[upart:])
    v["sec_p"] = swap(v.pop("sec_f"), core)
    run_mlp(1, v.pop("m1a"), v.pop("m1b"), v["o1"], part // 8)
    g2("m3")
    v.fence()
    v["p1"] = zswap(v["p1"], 1)
    run_mlp(3, v.pop("m3a"), v.pop("m3b"), v["o3"], part // 8)
    g2("m2")
    v.fence()
    v["p3"] = zswap(v["p3"], 1)
    run_mlp(0, (u0, u1), (d0, d1), bias0, 0)
    e1(1)
    e1(3)
    v.fence()
    run_mlp(2, v.pop("m2a"), v.pop("m2b"), v["t2"], 4 * part // 8)
    e2(1)
    e2(3)
    v["q1u"] = zswap(v["q1u"], 1)
    v.fence()
    e3(1)
    e3(3)
    v["d13"] = jnp.concatenate([v.pop("w1"), v.pop("w3")], axis=0)
    v["q3u"] = zswap(v["q3u"], 1)
    c1(0)
    c1(2)
    v["send"] = run_down(1)
    v.fence()
    c0(0)
    c0(2)
    v["d13"] = zswap(v["d13"], 1)
    v["acc_got"] = swap(v.pop("send"), core)
    v["acc_own"] = run_down(0)
    v.fence()
    d13 = v.pop("d13")
    v["d1"], v["d3"] = d13[:upart], d13[upart:]
    c2(0)
    c2(2)
    run_mid()
    v.fence()
    c3(0)
    c3(2)
    w2 = v.pop("w2")
    v["z2x"] = zswap(w2[:n_z2], 2)
    v["z2s"] = w2[n_z2:]
    v["gp2"] = zswap(v.pop("gmt3"), 1)
    r1("o")
    v.fence()
    v["gp0"] = zswap(v.pop("gmt1"), 1)
    v["z2y"] = zswap(v.pop("z2s"), 2)
    r2("o", "b")
    run_attn_bwd(2, "gp2", idx_b, True)
    v.fence()
    r1("q2")
    v.fence()
    mlp_sum = high_bits(
        v.pop("w0") + jnp.concatenate([v.pop("z2x"), v.pop("z2y")], axis=0)
    )
    ma, mb = mlp_sum[:upart], mlp_sum[upart:]
    keep, got = v["q2"]
    to_x = jnp.concatenate([(keep[2:] + got[2:]).reshape(-1, width), ma], axis=0)
    v["q2"] = keep[:2] + got[:2]
    keep, got = v["o"]
    to_y = jnp.concatenate([keep[1] + got[1], mb], axis=0)
    v["o"] = keep[0] + got[0]
    v["gx"], v["gy"] = (to_x, swap(to_x, px)), (to_y, swap(to_y, py))
    run_attn_bwd(0, "gp0", idx_b, False)
    v.fence()
    nq = 2 * 3 * part
    (xa, xb), (ya, yb) = v.pop("gx"), v.pop("gy")
    r1("q0")
    q2 = v["q2"] + xb[:nq].reshape(2, 3 * part, width)
    v["q2"] = q2[0]
    to_y = jnp.concatenate([xa[nq:], xb[nq:], q2[1]], axis=0)
    to_x = jnp.concatenate([ya[nmp * part :], yb[nmp * part :]], axis=0)
    v["gx"], v["gy"] = (to_x, swap(to_x, px)), (to_y, swap(to_y, py))
    o = v.pop("o") + yb[: nmp * part]
    v["gn0"] = zswap(
        jnp.concatenate([v["gn"][share : share + n_gn[0]], o[part : 2 * part], o[3 * part :]], axis=0), 1
    )
    v["o0"], v["o2"] = o[:part], o[2 * part : 3 * part]
    n1_stats = call(
        norm1_stats_kernel,
        sds((8, width), F32),
        flops=full * width * 10,
        bytes_accessed=full * width * 6,
        grid_spec=pltpu.PrefetchScalarGridSpec(
            num_scalar_prefetch=1,
            grid=(steps,),
            in_specs=[tok_spec, run_spec],
            out_specs=pl.BlockSpec((8, width), const2),
        ),
    )(blk, tokens, v["gn"])
    head_sum = jnp.sum(v.pop("hst0") + v.pop("hst2"), axis=-1)
    copied = jnp.concatenate(
        [v.pop("mst")[:4].reshape(-1), n1_stats[:2].reshape(-1), head_sum.reshape(-1)]
    )
    own_parts = []
    for k in range(nmp):
        qb = jnp.zeros((3 * e,), F32) if k % 2 else jnp.sum(v.pop(f"qbg{k}"), axis=1)
        ubg = jnp.pad(v.pop(f"ubg{k}").reshape(half, upart), ((0, half), (0, 0)))
        own_parts.append(jnp.concatenate([qb, jnp.take(ubg, idx_a, axis=0).reshape(-1)]))
    nc = copied.shape[0]
    no = own_parts[0].shape[0]
    v["small"] = jnp.concatenate([copied] + own_parts)
    v.fence()
    r2("q0", "b")
    (xa, xb), (ya, yb) = v["gx"], v["gy"]
    gn0 = v.pop("gn0")
    v["gn0"] = gn0[: n_gn[0]]
    v["o0"] = v["o0"] + gn0[n_gn[0] : n_gn[0] + part]
    o2 = v.pop("o2") + gn0[n_gn[0] + part :]
    q2 = v.pop("q2") + yb[2 * upart :]
    v["y2"] = zswap(jnp.concatenate([q2, o2], axis=0), 2)
    at = share + n_gn[0]
    v["gn1"] = zswap(v["gn"][at : at + n_gn[1]], 1)
    v["small"] = v["small"] + swap(v["small"], core)
    v.fence()
    r3("q0", "b")
    v["gn2"] = zswap(v["gn"][share + n_gn[0] + n_gn[1] :], 1)
    v["small"] = v["small"] + swap(v["small"], px)
    ya, yb = v.pop("gy")
    v["gu"] = (ya, yb, swap(ya, core), swap(yb, core))
    v.fence()
    r4("q0")
    att_sum = high_bits(
        jnp.concatenate([v.pop("q0"), v.pop("o0")], axis=0) + v.pop("y2")
    )
    v["wa"], v["wb"] = att_sum[:hp], att_sum[hp:]
    g1("w")
    xa, xb = v.pop("gx")
    v["gd"] = (xa, xb, swap(xa, core), swap(xb, core))
    v["small"] = v["small"] + swap(v["small"], py)
    v["input_grad"] = call(
        final_kernel,
        sds((share, width), BF16),
        flops=share * width * 20,
        bytes_accessed=share * width * 16,
        grid_spec=pltpu.PrefetchScalarGridSpec(
            num_scalar_prefetch=1,
            grid=(per,),
            in_specs=[tok_spec, run_spec, run_spec, run_spec, vec_spec],
            out_specs=run_spec,
        ),
    )(
        blk,
        tokens,
        v["gn"],
        jnp.concatenate([v.pop("gn0"), v.pop("gn1"), v.pop("gn2")], axis=0),
        v["gm"],
        row1(norm1_gain),
    )
    v.fence()

    def unpack(kernel, arrays, idx, shape):
        pieces_spec = pl.BlockSpec((2 * upart, width), lambda t: (0, 0))
        return call(
            kernel,
            sds(shape, F32),
            bytes_accessed=2 * 4 * math.prod(shape),
            grid=(1,),
            in_specs=[smem] + [pieces_spec] * 4,
            out_specs=pl.BlockSpec(shape, lambda t: (0, 0)),
            scratch_shapes=[pltpu.VMEM((PIECES, upart, width), F32)],
        )(idx, *arrays)

    g2("w")
    small = high_bits(v.pop("small"))
    parts = [small[nc + k * no : nc + (k + 1) * no] for k in range(nmp)]
    sent = jnp.concatenate([small[:nc], parts[1], parts[3]])
    got = zswap(sent, 1)
    v["small"] = jnp.concatenate([small[:nc], parts[0], parts[2]]) + got
    v["up_g"] = unpack(unpack_kernel, v.pop("gu"), idx_a, (width, units))
    v["down_g"] = unpack(unpack_rows_kernel, v.pop("gd"), idx_b, (units, width))
    v.fence()
    wa, wb = (jnp.concatenate(v.pop("w" + t), axis=0) for t in "ab")
    small = v.pop("small")
    got = zswap(jnp.concatenate([small[:nc], small[nc + no :]]), 2)
    v["small_sum"] = small[: nc + no] + got
    qkv_weight_grad, out_weight_grad = call(
        unpack_att_kernel,
        (sds((3, e, width), F32), sds((e, width), F32)),
        bytes_accessed=2 * 4 * 4 * width * e,
        in_specs=[smem, smem] + [vmem] * 4,
        out_specs=(vmem, vmem),
        scratch_shapes=[pltpu.VMEM((PIECES, hp, width), F32)] * 2,
    )(idx_a, idx_b, wa, swap(wa, core), wb, swap(wb, core))
    qkv_weight_grad = jnp.swapaxes(qkv_weight_grad, 1, 2)

    small_sum = v["small_sum"]
    rows_of = small_sum[: 6 * width].reshape(6, width)
    heads_of = small_sum[6 * width : nc].reshape(3, DH)
    qkv_bias_grad = small_sum[nc : nc + 3 * e].reshape(3, e)
    up_bias_grad = small_sum[nc + 3 * e :]
    return (
        v["block_out"],
        v["input_grad"],
        qkv_weight_grad,
        qkv_bias_grad,
        out_weight_grad,
        rows_of[2],
        v["up_g"],
        up_bias_grad,
        v["down_g"],
        rows_of[3],
        rows_of[4],
        rows_of[5],
        heads_of[0],
        heads_of[1],
        heads_of[2],
        rows_of[0],
        rows_of[1],
    )


def solution(mesh):
    in_specs = (
        P("dp", None),
        P("dp"),
        P(None, None, "mp"),
        P(None, "mp"),
        P("mp", None),
        P(),
        P(None, "mp"),
        P("mp"),
        P("mp", None),
        P(),
        P(),
        P(),
        P(),
        P(),
        P(),
        P(),
        P(),
        P("dp", None),
    )
    out_specs = (
        P(("dp", "mp"), None),
        P(("dp", "mp"), None),
        P(None, None, "mp"),
        P(None, "mp"),
        P("mp", None),
        P(),
        P(None, "mp"),
        P("mp"),
        P("mp", None),
        P(),
        P(),
        P(),
        P(),
        P(),
        P(),
        P(),
        P(),
    )
    return jax.shard_map(shards, mesh=mesh, in_specs=in_specs, out_specs=out_specs, check_vma=False)
```

```python
import functools
import math

import jax
import jax.numpy as jnp
from jax import lax
from jax.experimental import pallas as pl
from jax.experimental.pallas import tpu as pltpu
from jax.sharding import PartitionSpec as P

F32 = jnp.float32
BF16 = jnp.bfloat16
DH = 64
SEQ_LEN = 1024
NORM_EPS = 1e-06
PIECES = 8
SEG_COLS = 128
LOG2E = math.log2(math.e)
SCALE = DH ** (-0.5)
BITS_A = (2, 4, 1)
BITS_B = (4, 2, 1)
MLP_KIND = ("a", "a", "b", "b")
VMEM_LIMIT = 56 * 1024 * 1024


def mm(a, b):
    return lax.dot_general(a, b, (((1,), (0,)), ((), ())), preferred_element_type=F32)


def mm_nt(a, b):
    return lax.dot_general(a, b, (((1,), (1,)), ((), ())), preferred_element_type=F32)


def mm_tn(a, b):
    return lax.dot_general(a, b, (((0,), (0,)), ((), ())), preferred_element_type=F32)


def call(kernel, out_shape, flops=0, bytes_accessed=0, **kw):
    return pl.pallas_call(
        kernel,
        out_shape=out_shape,
        compiler_params=pltpu.CompilerParams(vmem_limit_bytes=VMEM_LIMIT),
        cost_estimate=pl.CostEstimate(
            flops=flops, bytes_accessed=bytes_accessed, transcendentals=0
        ),
        **kw,
    )


def sds(shape, dtype):
    return jax.ShapeDtypeStruct(shape, dtype)


def row_norm(x):
    mean = jnp.mean(x, axis=-1, keepdims=True)
    cen = x - mean
    rstd = lax.rsqrt(jnp.mean(cen * cen, axis=-1, keepdims=True) + NORM_EPS)
    return cen * rstd, rstd


def row_norm_back(f, n, rstd):
    mean_f = jnp.mean(f, axis=-1, keepdims=True)
    mean_fn = jnp.mean(f * n, axis=-1, keepdims=True)
    return (f - mean_f - n * mean_fn) * rstd


def col_norm(x):
    mean = jnp.mean(x, axis=0, keepdims=True)
    cen = x - mean
    rstd = lax.rsqrt(jnp.mean(cen * cen, axis=0, keepdims=True) + NORM_EPS)
    return cen * rstd, rstd


def col_norm_back(f, n, rstd):
    mean_f = jnp.mean(f, axis=0, keepdims=True)
    mean_fn = jnp.mean(f * n, axis=0, keepdims=True)
    return (f - mean_f - n * mean_fn) * rstd


def lane_fold(x):
    out = x[:, :128]
    for t in range(1, x.shape[1] // 128):
        out = out + x[:, t * 128 : (t + 1) * 128]
    return out


def offset_of(s, bits):
    return sum(bit for t, bit in enumerate(bits) if (s >> t) & 1)


def norm1_kernel(blk_ref, x_ref, g_ref, s_ref, out_ref):
    n, _ = row_norm(x_ref[...].astype(F32))
    out_ref[...] = (n * g_ref[...] + s_ref[...]).astype(BF16)


def build_q_aug(q_pre, qg, qs, qaug_ref):
    n, rstd = col_norm(q_pre)
    q_low = (n * qg + qs).astype(BF16)
    scaled = q_low.astype(F32) * (SCALE * LOG2E)
    hi = scaled.astype(BF16)
    lo = (scaled - hi.astype(F32)).astype(BF16)
    qaug_ref[0:DH, :] = hi
    qaug_ref[DH : 2 * DH, :] = lo
    return n, rstd, q_low


def build_k_aug(k_pre, kg, kaug_ref):
    n, rstd = col_norm(k_pre)
    k_low = (n * kg).astype(BF16)
    kaug_ref[:, 0 : 2 * DH] = jnp.concatenate([k_low, k_low], axis=0).T
    return n, rstd, k_low


def bias_col(b_ref, n):
    return b_ref[...].T[0:n, 0:1]


def prep_kernel(
    me_ref, w_ref, o_ref, qb_ref, ub_ref, up_ref, dn_ref,
    att_ref, ob_ref, b_ref, p_ref, u0_ref, u1_ref, d0_ref, d1_ref,
    t_ref, wf_ref,
):
    part = 24
    e = PIECES * part
    me = me_ref[0]
    b_ref[...] = jnp.zeros(b_ref.shape, F32)
    for s in range(3):
        wf_ref[...] = w_ref[s].astype(F32)
        rows = wf_ref[pl.ds(pl.multiple_of(me * part, 8), part), :]
        att_ref[s * part : (s + 1) * part, :] = rows
        b_ref[0:1, s * e : (s + 1) * e] = qb_ref[s : s + 1, :]
    upart = up_ref.shape[1] // PIECES
    ub = ub_ref[...].reshape(1, PIECES * upart)
    for s in range(PIECES // 2):
        piece = jnp.zeros((1, upart), F32)
        for p in range(PIECES):
            here = (me ^ offset_of(s, BITS_A)) == p
            piece = piece + jnp.where(here, ub[:, p * upart : (p + 1) * upart], 0.0)
        b_ref[1:2, s * upart : (s + 1) * upart] = piece
    wf_ref[...] = o_ref[...].astype(F32)
    rows = wf_ref[pl.ds(pl.multiple_of(me * part, 8), part), :]
    att_ref[3 * part : 4 * part, :] = rows
    ob_ref[0:part, :] = rows
    att_ref[4 * part :, :] = b_ref[...]
    ob_ref[part:, :] = b_ref[...]

    t_ref[...] = up_ref[...].astype(F32).T

    def at_piece(r):
        return pl.ds(pl.multiple_of((me ^ r) * upart, 32), upart)

    p_ref[0:upart, :] = t_ref[at_piece(0), :]
    p_ref[upart:, :] = dn_ref[at_piece(0), :].astype(F32)
    for i, (u_ref, d_ref) in enumerate(((u0_ref, d0_ref), (u1_ref, d1_ref))):
        for j in range(2):
            u_ref[j] = t_ref[at_piece(offset_of(2 * i + j, BITS_A)), :].astype(BF16)
            d_ref[j] = dn_ref[at_piece(offset_of(2 * i + j, BITS_B)), :]


def attend(x_ref, wt_ref, b_ref, hv_ref, kmask_ref, qhot_ref, outs, qaug_ref, kaug_ref):
    qpre_ref, kpre_ref, vt_ref, mixt_ref, mixf_ref, mixs_ref, l_ref = outs
    e = qpre_ref.shape[0]
    full = x_ref.shape[0]
    share = full // 2
    heads = e // DH
    x = x_ref[...]
    bias = bias_col(b_ref, 3 * e)
    qpre_ref[...] = mm_nt(wt_ref[0:e, :], x) + bias[0:e]
    kpre_ref[...] = mm_nt(wt_ref[e : 2 * e, :], x) + bias[e : 2 * e]
    vt_ref[...] = (mm_nt(wt_ref[2 * e : 3 * e, :], x) + bias[2 * e :]).astype(BF16)
    qaug_ref[2 * DH :, :] = qhot_ref[...]
    kaug_ref[:, 2 * DH :] = kmask_ref[...]
    ones = jnp.ones((16, full), BF16)
    for h in range(heads):
        hs = slice(h * DH, (h + 1) * DH)
        build_q_aug(qpre_ref[hs, :], hv_ref[:, 0:1], hv_ref[:, 1:2], qaug_ref)
        build_k_aug(kpre_ref[hs, :], hv_ref[:, 2:3], kaug_ref)
        prob = jnp.exp2(mm(kaug_ref[...], qaug_ref[...])).astype(BF16)
        vaug = jnp.concatenate([vt_ref[hs, :], ones], axis=0)
        o = mm(vaug, prob)
        total = o[DH : DH + 1, :]
        l_ref[h : h + 1, :] = total
        mix = o[0:DH, :] / total
        mixf_ref[hs, :] = mix
        mixt_ref[hs, :] = mix[:, 0:share].astype(BF16)
        at = h * share
        for c in range(0, share, 256):
            block_no, lane = divmod(at + c, x.shape[1])
            mixs_ref[block_no * DH : (block_no + 1) * DH, lane : lane + 256] = mix[
                :, share + c : share + c + 256
            ]


def attn_fwd_own_kernel(x_ref, wt_ref, b_ref, hv_ref, kmask_ref, qhot_ref, *refs):
    attend(x_ref, wt_ref, b_ref, hv_ref, kmask_ref, qhot_ref, refs[:7], *refs[7:])


def attn_fwd_kernel(
    ia_ref, ib_ref, a0_ref, a1_ref, b0_ref, b1_ref, x_ref, b_ref, hv_ref, kmask_ref, qhot_ref,
    wt_ref, ow_ref, ow1_ref, ow3_ref, *refs,
):
    wa_ref, wb_ref = refs[-2:]
    part = 24
    e = PIECES * part
    half = PIECES // 2
    wa_ref[0:half] = a0_ref[...]
    wa_ref[half:] = a1_ref[...]
    wb_ref[0:half] = b0_ref[...]
    wb_ref[half:] = b1_ref[...]

    def rows(w_ref, i_ref, at):
        return jnp.concatenate(
            [w_ref[i_ref[p], at * part : (at + 1) * part, :] for p in range(PIECES)], axis=0
        ).astype(BF16)

    wt_ref[0:e, :] = rows(wa_ref, ia_ref, 0)
    wt_ref[e : 2 * e, :] = rows(wa_ref, ia_ref, 1)
    wt_ref[2 * e : 3 * e, :] = rows(wb_ref, ib_ref, 0)
    ow_ref[...] = rows(wb_ref, ib_ref, 1)
    ow1_ref[...] = rows(wa_ref, ia_ref, 2)
    ow3_ref[...] = rows(wb_ref, ib_ref, 2)
    attend(x_ref, wt_ref, b_ref, hv_ref, kmask_ref, qhot_ref, refs[:7], *refs[7:9])


def unmix(ref, heads, share):
    width = ref.shape[1]
    rows = []
    for h in range(heads):
        cols = []
        for c in range(0, share, 256):
            block_no, lane = divmod(h * share + c, width)
            cols.append(ref[block_no * DH : (block_no + 1) * DH, lane : lane + 256])
        rows.append(jnp.concatenate(cols, axis=1))
    return jnp.concatenate(rows, axis=0).astype(BF16)


def mix_of(ref, share):
    if ref.dtype == BF16:
        return ref[...]
    return unmix(ref, ref.shape[0] * ref.shape[1] // (DH * share), share)


def out_norm2_kernel(nslot, blk_ref, x_ref, *refs):
    mixes = refs[:nslot]
    ws = refs[nslot : 2 * nslot]
    ob_ref, g_ref, s_ref, mid_ref, sec_ref, secf_ref = refs[2 * nslot :]
    acc = x_ref[...].astype(F32) + ob_ref[...]
    for k in range(nslot):
        acc = acc + mm_tn(mix_of(mixes[k], x_ref.shape[0]), ws[k][...])
    mid_ref[...] = acc
    n, _ = row_norm(acc)
    sec = (n * g_ref[...] + s_ref[...]).astype(BF16)
    sec_ref[...] = sec
    secf_ref[...] = sec.astype(F32)


def mlp_kernel(
    kind, keeps, sec_ref, secp_ref, cot_ref, cotp_ref, u0_ref, u1_ref, d0_ref, d1_ref, b_ref, *refs
):
    if keeps:
        p_ref, hid_ref, gp_ref, ub_ref, db_ref, k0_ref, k1_ref, s0_ref, s1_ref, gb_ref = refs
    else:
        hid_ref, gp_ref, ub_ref, db_ref, up_ref, uq_ref, k0_ref, k1_ref, sd_ref, gb_ref = refs
    part = u0_ref.shape[1]
    share = sec_ref.shape[0]
    up = jnp.concatenate([u0_ref[0], u0_ref[1], u1_ref[0], u1_ref[1]], axis=0).astype(BF16)
    down = jnp.concatenate([d0_ref[0], d1_ref[0], d0_ref[1], d1_ref[1]], axis=0).astype(BF16)
    ub_ref[...] = up
    db_ref[...] = down
    bias = b_ref[1:2, 0 : up.shape[0]]
    for r, (s_ref, c_ref) in enumerate(((sec_ref, cot_ref), (secp_ref, cotp_ref))):
        rows = slice(r * share, (r + 1) * share)
        sec = s_ref[...].astype(BF16)
        cot = c_ref[...].astype(BF16)
        pre = mm_nt(sec, up) + bias
        cdf = 0.5 * (1.0 + lax.erf(pre * (1.0 / math.sqrt(2.0))))
        hid = (pre * cdf).astype(BF16)
        pdf = jnp.exp(-0.5 * pre * pre) * (1.0 / math.sqrt(2.0 * math.pi))
        gpre = (mm_nt(cot, down) * (cdf + pre * pdf)).astype(BF16)
        hid_ref[rows, :] = hid
        gp_ref[rows, :] = gpre
        gb_r = jnp.sum(gpre.astype(F32), axis=0, keepdims=True)
        gd_r = mm_tn(hid, cot)
        gu_r = mm_tn(gpre, sec)
        if r == 0:
            gb, gd, gu = gb_r, gd_r, gu_r
        else:
            gb, gd, gu = gb + gb_r, gd + gd_r, gu + gu_r
    gb_ref[...] = gb
    order = (0, 1, 2, 3) if kind == "a" else (0, 2, 1, 3)
    gu_at = [gu[i * part : (i + 1) * part] for i in order]
    gd_at = [gd[i * part : (i + 1) * part] for i in order]
    if keeps:
        gu_at[3] = gu_at[3] + p_ref[0:part, :]
        gu_at[2] = gu_at[2] + p_ref[part:, :]
        for i, ref in enumerate((k0_ref, k1_ref, s0_ref, s1_ref)):
            ref[0:part, :] = gu_at[i]
            ref[part:, :] = gd_at[i]
    else:
        up_ref[0:part, :] = gu_at[3]
        up_ref[part:, :] = gu_at[2]
        uq_ref[0:part, :] = gu_at[0]
        uq_ref[part:, :] = gu_at[1]
        k0_ref[...] = gd_at[0]
        k1_ref[...] = gd_at[1]
        sd_ref[0:part, :] = gd_at[3]
        sd_ref[part:, :] = gd_at[2]


def down_kernel(nslot, *refs):
    hids = refs[:nslot]
    gps = refs[nslot : 2 * nslot]
    ubs = refs[2 * nslot : 3 * nslot]
    dbs = refs[3 * nslot : 4 * nslot]
    out_ref = refs[4 * nslot]
    cat = lambda refs, axis: jnp.concatenate([r[...] for r in refs], axis=axis)
    out_ref[0] = mm(cat(hids, 1), cat(dbs, 0))
    out_ref[1] = mm(cat(gps, 1), cat(ubs, 0))


def mid_kernel(nslot, mid_ref, own_ref, got_ref, cot_ref, db_ref, g_ref, *refs):
    ows = refs[:nslot]
    gmts = refs[nslot : 2 * nslot]
    bo_ref, gm_ref, low_ref, st_ref = refs[2 * nslot :]
    mid = mid_ref[...]
    n, rstd = row_norm(mid)
    e = own_ref[1] + got_ref[1]
    cot = cot_ref[...].astype(F32)
    gm = cot + row_norm_back(e * g_ref[...], n, rstd)
    gm_ref[...] = gm
    gm_low = gm.astype(BF16)
    low_ref[...] = gm_low
    for k in range(nslot):
        gmts[k][...] = mm_nt(ows[k][...], gm_low).astype(gmts[k].dtype)
    bo_ref[...] = (mid + (own_ref[0] + got_ref[0]) + db_ref[...]).astype(BF16)
    st_ref[0:1, :] = jnp.sum(e * n, axis=0, keepdims=True)
    st_ref[1:2, :] = jnp.sum(e, axis=0, keepdims=True)
    st_ref[2:3, :] = jnp.sum(gm_low.astype(F32), axis=0, keepdims=True)
    st_ref[3:4, :] = jnp.sum(cot, axis=0, keepdims=True)
    st_ref[4:8, :] = jnp.zeros((4, mid.shape[1]), F32)


def out_grad_kernel(nslot, idx_ref, low_ref, *refs):
    mixts = refs[:nslot]
    gow_keep, gow_send = refs[nslot:]
    part = 24
    gm_low = low_ref[...]
    for k in range(nslot):
        g = mm(mix_of(mixts[k], gm_low.shape[0]), gm_low)
        for p in range(PIECES):
            at = idx_ref[p]
            rows = slice(k * part, (k + 1) * part)

            @pl.when(at < PIECES // 2)
            def _():
                gow_keep[at, rows, :] = g[p * part : (p + 1) * part, :]

            @pl.when(at >= PIECES // 2)
            def _():
                gow_send[at - PIECES // 2, rows, :] = g[p * part : (p + 1) * part, :]


def attn_bwd_kernel(
    first, idx_ref, x_ref, qpre_ref, kpre_ref, vt_ref, wt_ref, gmt_ref, gmtp_ref, mixf_ref, l_ref,
    hv_ref, kmask_ref, qhot_ref, *refs
):
    if first:
        gk_ref, gs_ref, gn_ref, st_ref, gb_ref, qaug_ref, kaug_ref, gpt_ref = refs
    else:
        gn_in, gk_ref, gs_ref, gn_ref, st_ref, gb_ref, qaug_ref, kaug_ref, gpt_ref = refs
    part = 24
    e = PIECES * part
    full = x_ref.shape[0]
    heads = e // DH
    qaug_ref[2 * DH :, :] = qhot_ref[...]
    kaug_ref[:, 2 * DH :] = kmask_ref[...]
    qg, qs, kg = hv_ref[:, 0:1], hv_ref[:, 1:2], hv_ref[:, 2:3]
    qg_sum = jnp.zeros((DH, 128), F32)
    qs_sum = jnp.zeros((DH, 128), F32)
    kg_sum = jnp.zeros((DH, 128), F32)
    row_no = lax.broadcasted_iota(jnp.int32, (DH, full), 0)
    one_rows = (row_no < 3).astype(F32).astype(BF16)
    for h in range(heads):
        hs = slice(h * DH, (h + 1) * DH)
        qn, qr, q_low = build_q_aug(qpre_ref[hs, :], qg, qs, qaug_ref)
        kn, kr, k_low = build_k_aug(kpre_ref[hs, :], kg, kaug_ref)
        inv = 1.0 / l_ref[h : h + 1, :]
        gm = jnp.concatenate(
            [gmt_ref[hs, :].astype(F32), gmtp_ref[hs, :].astype(BF16).astype(F32)], axis=1
        )
        go_low = (gm * inv).astype(BF16)
        delta = -jnp.sum(go_low.astype(F32) * mixf_ref[hs, :], axis=0, keepdims=True)
        d0 = delta.astype(BF16).astype(F32)
        d1 = (delta - d0).astype(BF16).astype(F32)
        d2 = delta - d0 - d1
        extra = jnp.where(
            row_no == 0, d0, jnp.where(row_no == 1, d1, jnp.where(row_no == 2, d2, 0.0))
        ).astype(BF16)
        goaug = jnp.concatenate([go_low, extra], axis=0)
        vaug = jnp.concatenate([vt_ref[hs, :], one_rows], axis=0).T
        prob = jnp.exp2(mm(kaug_ref[...], qaug_ref[...]))
        ds = (prob * mm(vaug, goaug)).astype(BF16)
        gv = mm_nt(go_low, prob.astype(BF16))
        gk = mm_nt(q_low, ds) * SCALE
        gq = mm(k_low, ds) * SCALE
        qg_sum += lane_fold(gq * qn)
        qs_sum += lane_fold(gq)
        kg_sum += lane_fold(gk * kn)
        gpt_ref[h * DH : (h + 1) * DH, :] = col_norm_back(gq * qg, qn, qr).astype(BF16)
        gpt_ref[e + h * DH : e + (h + 1) * DH, :] = col_norm_back(gk * kg, kn, kr).astype(BF16)
        gpt_ref[2 * e + h * DH : 2 * e + (h + 1) * DH, :] = gv.astype(BF16)
    st_ref[0] = qg_sum
    st_ref[1] = qs_sum
    st_ref[2] = kg_sum
    gp = gpt_ref[...]
    gb_ref[...] = lane_fold(gp.astype(F32))
    gw = mm(gp, x_ref[...])

    def put(ref, at, p):
        for s in range(3):
            ref[at, s * part : (s + 1) * part, :] = gw[s * e + p * part : s * e + (p + 1) * part, :]

    for p in range(PIECES):
        at = idx_ref[p]

        @pl.when(at < PIECES // 2)
        def _():
            put(gk_ref, at, p)

        @pl.when(at >= PIECES // 2)
        def _():
            put(gs_ref, at - PIECES // 2, p)

    gn = mm_tn(gp, wt_ref[...])
    gn_ref[...] = gn if first else gn_in[...] + gn


def sums_kernel(
    nslot, blk_ref, me_ref, x_ref, gn_ref, mst_ref, h0_ref, h2_ref, b0_ref, b2_ref, *refs
):
    ubs = refs[:nslot]
    out_ref = refs[nslot]
    n, _ = row_norm(x_ref[...].astype(F32))
    e = gn_ref[...]

    @pl.when(pl.program_id(0) == 0)
    def _():
        out_ref[...] = jnp.zeros_like(out_ref)
        out_ref[0:4, :] = mst_ref[0:4, :]
        heads = jnp.concatenate([h0_ref[i] + h2_ref[i] for i in range(3)], axis=0).T
        out_ref[6:7, 0 : heads.shape[1]] = jnp.sum(heads, axis=0, keepdims=True)
        me = me_ref[0]
        upart = out_ref.shape[1] // PIECES
        for row, k in zip((8, 10, 12, 14), (0, 2, 1, 3)):
            if k % 2 == 0:
                cols = (b0_ref if k == 0 else b2_ref)[...].T
                out_ref[row : row + 1, 0 : cols.shape[1]] = jnp.sum(cols, axis=0, keepdims=True)
            mine = ubs[k][...]
            for p in range(PIECES):
                piece = jnp.zeros((1, upart), F32)
                for t in range(PIECES // 2):
                    here = (me ^ offset_of(t, BITS_A)) == p
                    piece = piece + jnp.where(here, mine[:, t * upart : (t + 1) * upart], 0.0)
                out_ref[row + 1 : row + 2, p * upart : (p + 1) * upart] = piece

    out_ref[4:5, :] += jnp.sum(e * n, axis=0, keepdims=True)
    out_ref[5:6, :] += jnp.sum(e, axis=0, keepdims=True)


def small_out_kernel(a_ref, b_ref, qb_ref, h0_ref, h1_ref, h2_ref, *rows):
    total = a_ref[...] + b_ref[...]
    for row, ref in zip((0, 1, 2, 3, 4, 5, 9), rows):
        ref[...] = total[row]
    for i, ref in enumerate((h0_ref, h1_ref, h2_ref)):
        ref[...] = total[6, i * DH : (i + 1) * DH]
        n = qb_ref.shape[1]
        qb_ref[i : i + 1, :] = total[8:9, i * n : (i + 1) * n]


def final_kernel(blk_ref, x_ref, gn_ref, *refs):
    gots = refs[:-3]
    gm_ref, g_ref, out_ref = refs[-3:]
    at = 0
    for ref in gots:
        rows = slice(at, at + ref.shape[0])
        n, rstd = row_norm(x_ref[rows, :].astype(F32))
        f = (gn_ref[rows, :] + ref[...]) * g_ref[...]
        out_ref[rows, :] = (gm_ref[rows, :] + row_norm_back(f, n, rstd)).astype(BF16)
        at += ref.shape[0]


def lay_out(refs, to_ref):
    part = to_ref.shape[1]
    for i, ref in enumerate(refs):
        for j in range(2):
            to_ref[2 * i + j] = ref[j * part : (j + 1) * part, :]


def unpack_kernel(idx_ref, a_ref, b_ref, c_ref, d_ref, out_ref, s_ref):
    lay_out((a_ref, b_ref, c_ref, d_ref), s_ref)
    whole = jnp.concatenate([s_ref[idx_ref[p]] for p in range(PIECES)], axis=0)
    out_ref[...] = whole.T


def unpack_rows_kernel(idx_ref, a_ref, b_ref, c_ref, d_ref, out_ref, s_ref):
    part = s_ref.shape[1]
    lay_out((a_ref, b_ref, c_ref, d_ref), s_ref)
    for p in range(PIECES):
        out_ref[p * part : (p + 1) * part, :] = s_ref[idx_ref[p]]


def unpack_att_kernel(i_ref, a_ref, b_ref, qkv_ref, out_ref, s_ref):
    rows = s_ref.shape[1]
    part = rows // 4
    half = PIECES // 2
    for j in range(half):
        s_ref[j] = a_ref[j * rows : (j + 1) * rows, :]
        s_ref[half + j] = b_ref[j * rows : (j + 1) * rows, :]
    for s, ref in enumerate((qkv_ref.at[0], qkv_ref.at[1], qkv_ref.at[2], out_ref)):
        for p in range(PIECES):
            ref[p * part : (p + 1) * part, :] = s_ref[i_ref[p], s * part : (s + 1) * part, :]


def swap_mp(a, k, size):
    return lax.ppermute(a, "mp", [(s, s ^ k) for s in range(size)])


def swap_plane(a, bit, size):
    return lax.ppermute(a, "dp", [(d, d ^ bit) for d in range(size)])


def storage_of(r, bits):
    return sum(jnp.where((r & bit) != 0, 1 << t, 0) for t, bit in enumerate(bits))


class Stages:
    def __init__(self):
        self.live = {}

    def __setitem__(self, name, value):
        self.live[name] = value

    def __getitem__(self, name):
        return self.live[name]

    def pop(self, name):
        return self.live.pop(name)

    def fence(self, *still_flying):
        now = {n: a for n, a in self.live.items() if n not in still_flying}
        leaves, tree = jax.tree.flatten(now)
        self.live.update(jax.tree.unflatten(tree, lax.optimization_barrier(leaves)))


def shards(
    tokens,
    seg_ids,
    qkv_weight,
    qkv_bias,
    out_weight,
    out_bias,
    up_weight,
    up_bias,
    down_weight,
    down_bias,
    norm1_gain,
    norm1_shift,
    query_gain,
    query_shift,
    key_gain,
    norm2_gain,
    norm2_shift,
    cotangent,
):
    ndp = lax.axis_size("dp")
    nmp = lax.axis_size("mp")
    dp_no = lax.axis_index("dp")
    mp_no = lax.axis_index("mp")
    me = dp_no % PIECES
    row_count, width = tokens.shape
    share = row_count // nmp
    full = SEQ_LEN
    assert full == 2 * share and nmp == 4 and ndp % PIECES == 0
    e = qkv_weight.shape[2]
    part = e // PIECES
    units = up_weight.shape[1]
    upart = units // PIECES
    half = PIECES // 2
    mine = half * upart
    core, px, py = 1, 2, 4

    vmem = pl.BlockSpec(memory_space=pltpu.VMEM)
    smem = pl.BlockSpec(memory_space=pltpu.SMEM)
    row1 = lambda v: v.reshape(1, -1)
    col = lambda v: v.reshape(-1, 1)
    swap = lambda a, bit: swap_plane(a, bit, ndp)
    zswap = lambda a, k: swap_mp(a, k, nmp)
    v = Stages()

    me1 = me.astype(jnp.int32).reshape(1)
    qkv_t = jnp.swapaxes(qkv_weight, 1, 2)
    wt0 = qkv_t.reshape(3 * e, width)
    att_piece, ob_piece, bias0, mlp_piece, u0, u1, d0, d1 = call(
        prep_kernel,
        (
            sds((4 * part + 8, width), F32),
            sds((part + 8, width), F32),
            sds((8, width), F32),
            sds((2 * upart, width), F32),
            *[sds((2, upart, width), BF16)] * 4,
        ),
        bytes_accessed=9_000_000,
        in_specs=[smem] + [vmem] * 6,
        out_specs=(vmem,) * 8,
        scratch_shapes=[pltpu.VMEM((units, width), F32), pltpu.VMEM((e, width), F32)],
    )(
        me1, qkv_t, out_weight, qkv_bias, up_bias, up_weight, down_weight
    )

    n_gn = (256, 88, 80, 88)
    n_z2 = 64
    numbers = jnp.arange(PIECES, dtype=jnp.int32)
    idx_a = storage_of(numbers ^ me, BITS_A).astype(jnp.int32)
    idx_b = storage_of(numbers ^ me, BITS_B).astype(jnp.int32)

    block = 256
    per = share // block
    steps = 2 * per
    tile_no = jnp.arange(steps, dtype=jnp.int32)
    blk = jnp.where(tile_no < per, mp_no * per + tile_no, (mp_no ^ 1) * per + tile_no - per).astype(
        jnp.int32
    )
    const2 = lambda t, b: (0, 0)
    tok_spec = pl.BlockSpec((block, width), lambda t, b: (b[t], 0))
    run_spec = pl.BlockSpec((block, width), lambda t, b: (t, 0))
    vec_spec = pl.BlockSpec((1, width), const2)

    def run_norm1():
        return call(
            norm1_kernel,
            sds((full, width), BF16),
            flops=full * width * 10,
            bytes_accessed=full * width * 4,
            grid_spec=pltpu.PrefetchScalarGridSpec(
                num_scalar_prefetch=1,
                grid=(steps,),
                in_specs=[tok_spec, vec_spec, vec_spec],
                out_specs=run_spec,
            ),
        )(blk, tokens, row1(norm1_gain), row1(norm1_shift))

    seg_own = lax.dynamic_slice_in_dim(seg_ids, mp_no * share, share, 0)
    seg_other = lax.dynamic_slice_in_dim(seg_ids, (mp_no ^ 1) * share, share, 0)
    seg_keys = jnp.concatenate([seg_own, seg_other])
    qhot = (
        lax.broadcasted_iota(jnp.int32, (SEG_COLS, full), 0) == seg_keys[None, :]
    ).astype(BF16)
    kmask = jnp.where(
        lax.broadcasted_iota(jnp.int32, (full, SEG_COLS), 1) == seg_keys[:, None], 0.0, -1e30
    ).astype(BF16)
    hv = jnp.stack([query_gain, query_shift, key_gain], axis=1)
    scratch = [
        pltpu.VMEM((2 * DH + SEG_COLS, full), BF16),
        pltpu.VMEM((full, 2 * DH + SEG_COLS), BF16),
    ]

    def whole(a):
        return pl.BlockSpec(a.shape, lambda t: (0,) * len(a.shape))

    def bias_at(block_no):
        return pl.BlockSpec((8, width), lambda t: (block_no, 0))

    att_names = ["qpre", "kpre", "vt", "mixt", "mixf", "mixs", "l"]
    att_shapes = [
        sds((e, full), F32),
        sds((e, full), F32),
        sds((e, full), BF16),
        sds((e, share), BF16),
        sds((e, full), F32),
        sds((e * share // width, width), F32),
        sds((8, full), F32),
    ]
    mix_rows = e * share // width

    def run_attn_own():
        outs = call(
            attn_fwd_own_kernel,
            tuple(att_shapes),
            flops=2 * (full * width * e * 3 + full * full * e * 8),
            bytes_accessed=10_000_000,
            in_specs=[vmem] * 6,
            out_specs=(vmem,) * 7,
            scratch_shapes=scratch,
        )(v["normed"], wt0, bias0, hv, kmask, qhot)
        v["st0"] = dict(zip(att_names, outs))
        v["st0"]["wt"] = wt0
        v["st0"]["ow"] = out_weight

    def run_attn_far():
        shapes = [sds((3 * e, width), BF16)] + [sds((e, width), BF16)] * 3 + att_shapes
        args = [
            *v.pop("ta"), *v.pop("tb"), v["normed"], v["t2"], hv, kmask, qhot,
        ]
        specs = [whole(a) for a in args]
        specs[5] = bias_at(4 * part // 8)
        outs = call(
            attn_fwd_kernel,
            tuple(shapes),
            flops=2 * (full * width * e * 3 + full * full * e * 8),
            bytes_accessed=10_000_000,
            grid=(1,),
            in_specs=[smem, smem] + specs,
            out_specs=tuple(whole(a) for a in shapes),
            scratch_shapes=scratch
            + [pltpu.VMEM((PIECES, 3 * part, width), F32)] * 2,
        )(idx_a, idx_b, *args)
        v["st2"] = dict(zip(["wt", "ow", "ow1", "ow3"] + att_names, outs))

    def by_slot():
        st0, st2 = v["st0"], v["st2"]
        mixes = [st0["mixt"], v["mix0"], st2["mixt"], v["mix2"]]
        ows = [st0["ow"], st2["ow1"], st2["ow"], st2["ow3"]]
        return mixes, ows

    def run_out():
        own_spec = pl.BlockSpec((share, width), lambda t, b: (b[0] // per, 0))
        whole2 = lambda shape: pl.BlockSpec(shape, lambda t, b: (0,) * len(shape))
        mixes, ows = by_slot()
        v["middle"], v["second"], v["sec_f"] = call(
            functools.partial(out_norm2_kernel, nmp),
            (sds((share, width), F32), sds((share, width), BF16), sds((share, width), F32)),
            flops=2 * share * width * e * nmp,
            bytes_accessed=8_000_000,
            grid_spec=pltpu.PrefetchScalarGridSpec(
                num_scalar_prefetch=1,
                grid=(1,),
                in_specs=[own_spec]
                + [whole2((e, share)), whole2((mix_rows, width))] * 2
                + [whole2((e, width))] * nmp
                + [whole2((1, width))] * 3,
                out_specs=(whole2((share, width)),) * 3,
            ),
        )(blk, tokens, *mixes, *ows, row1(out_bias), row1(norm2_gain), row1(norm2_shift))

    def run_mlp(k, up, down, bias, block_no):
        keeps = k % 2 == 0
        args = [
            v["second"], v["sec_p"], v["cot"], v["cot_p"], up[0], up[1], down[0], down[1], bias,
        ]
        if keeps:
            args.append(v.pop(f"p{k + 1}"))
        specs = [whole(a) for a in args]
        specs[8] = bias_at(block_no)
        piece = lambda n: sds((n * upart, width), F32)
        shapes = (
            *[sds((full, mine), BF16)] * 2,
            *[sds((mine, width), BF16)] * 2,
            *([piece(2)] * 4 if keeps else [piece(2), piece(2), piece(1), piece(1), piece(2)]),
            sds((1, mine), F32),
        )
        res = call(
            functools.partial(mlp_kernel, MLP_KIND[k], keeps),
            shapes,
            flops=2 * full * width * mine * 4,
            bytes_accessed=12_000_000,
            grid=(1,),
            in_specs=specs,
            out_specs=tuple(whole(a) for a in shapes),
        )(*args)
        v[f"h{k}"] = res[:4]
        v[f"ubg{k}"] = res[-1]
        if keeps:
            v[f"w{k}"] = res[4:8]
        else:
            v[f"p{k}"], v[f"q{k}u"] = res[4], res[5]
            v[f"w{k}"] = res[6:9]

    def run_down(r):
        row_spec = pl.BlockSpec((share, mine), lambda t: (r, 0))
        w_spec = pl.BlockSpec((mine, width), lambda t: (0, 0))
        return call(
            functools.partial(down_kernel, nmp),
            sds((2, share, width), F32),
            flops=4 * share * width * mine * nmp,
            bytes_accessed=11_000_000,
            grid=(1,),
            in_specs=[row_spec] * (2 * nmp) + [w_spec] * (2 * nmp),
            out_specs=pl.BlockSpec((2, share, width), lambda t: (0, 0, 0)),
        )(*[v[f"h{k}"][i] for i in range(4) for k in range(nmp)])

    def run_mid():
        mixes, ows = by_slot()
        shapes = (
            *[sds((e, share), F32 if k % 2 else BF16) for k in range(nmp)],
            sds((share, width), BF16),
            sds((share, width), F32),
            sds((share, width), BF16),
            sds((8, width), F32),
        )
        *gmts, bo, gm, low, mst = call(
            functools.partial(mid_kernel, nmp),
            shapes,
            flops=2 * share * width * e * nmp,
            bytes_accessed=12_000_000,
            in_specs=[vmem] * (6 + nmp),
            out_specs=(vmem,) * (4 + nmp),
        )(
            v["middle"], v.pop("acc_own"), v.pop("acc_got"), v["cot"], row1(down_bias),
            row1(norm2_gain), *ows,
        )
        v["block_out"], v["gm"], v["mst"] = bo, gm, mst
        for k in range(nmp):
            v[f"gmt{k}"] = gmts[k]
        return low

    def run_out_grad(low):
        mixes, ows = by_slot()
        args = [low, *mixes]
        specs = [whole(a) for a in args]
        for k in (1, 3):
            specs[1 + k] = pl.BlockSpec((mix_rows, width), lambda t: (0, 0))
        shapes = (sds((half, nmp * part, width), F32),) * 2
        v["o"] = call(
            functools.partial(out_grad_kernel, nmp),
            shapes,
            flops=2 * share * width * e * nmp,
            bytes_accessed=5_000_000,
            grid=(1,),
            in_specs=[smem] + specs,
            out_specs=tuple(whole(a) for a in shapes),
        )(idx_b, *args)

    def run_attn_bwd(k, got, idx, first):
        st = v.pop(f"st{k}")
        args = [
            idx, v["normed"], st["qpre"], st["kpre"], st["vt"], st["wt"], v.pop(f"gmt{k}"),
            v.pop(got), st["mixf"], st["l"], hv, kmask, qhot,
        ]
        alias = {}
        if not first:
            args.append(v["gn"])
            alias = {len(args) - 1: 2}
        keep, send, gn, hst, gb = call(
            functools.partial(attn_bwd_kernel, first),
            (
                sds((half, 3 * part, width), F32),
                sds((half, 3 * part, width), F32),
                sds((full, width), F32),
                sds((3, DH, 128), F32),
                sds((3 * e, 128), F32),
            ),
            flops=2 * (full * width * e * 6 + full * full * e * 20),
            bytes_accessed=14_000_000,
            in_specs=[smem] + [vmem] * (len(args) - 1),
            out_specs=(vmem,) * 5,
            scratch_shapes=scratch + [pltpu.VMEM((3 * e, full), BF16)],
            input_output_aliases=alias,
        )(*args)
        v[f"q{k}"] = (keep, send)
        v["gn"] = gn
        v[f"hst{k}"] = hst
        v[f"qbg{k}"] = gb

    def g1(n):
        a, b = v[n + "a"], v[n + "b"]
        v[n + "a"] = (a, swap(a, px))
        v[n + "b"] = (b, swap(b, py))

    def g2(n):
        a, b = (jnp.stack(v[n + t]) for t in "ab")
        v[n + "a"] = (a, swap(a, py))
        v[n + "b"] = (b, swap(b, px))

    def g3(n):
        a, b = (jnp.concatenate(v[n + t], axis=0) for t in "ab")
        v[n + "a"] = (a, swap(a, core))
        v[n + "b"] = (b, swap(b, core))

    def r1(n):
        keep, send = v[n]
        v[n] = (keep, swap(send, core))

    def r2(n, kind):
        keep, got = v[n]
        keep_sum = keep[:2] + got[:2]
        v[n] = (keep_sum, swap(keep[2:] + got[2:], py if kind == "a" else px))

    def r3(n, kind):
        keep, got = v[n]
        v[n] = (keep[0] + got[0], swap(keep[1] + got[1], px if kind == "a" else py))

    def r4(n):
        keep, got = v[n]
        v[n] = keep + got

    def first_link(k):
        return py if MLP_KIND[k] == "a" else px

    def second_link(k):
        return px if MLP_KIND[k] == "a" else py

    def c1(k):
        k0, k1, s0, s1 = v[f"w{k}"]
        v[f"w{k}"] = (k0, k1, s0, swap(s1, first_link(k)))

    def c0(k):
        k0, k1, s0, g1 = v[f"w{k}"]
        v[f"w{k}"] = (k0, k1, g1, swap(s0, first_link(k)))

    def c2u(k):
        k0, k1, g1, g0 = v[f"w{k}"]
        q = v.pop(f"q{k + 1}u")
        sent = k1[:upart] + q[upart:] + g1[:upart]
        v[f"w{k}"] = (k0, k1, g1, g0, q, swap(sent, second_link(k)))

    def c2d(k):
        k0, k1, g1, g0, q, gu = v[f"w{k}"]
        up_sum = k0[:upart] + g0[:upart] + q[:upart] + gu
        sent = k1[upart:] + g1[upart:]
        v[f"w{k}"] = (up_sum, k0[upart:], g0[upart:], swap(sent, second_link(k)))

    def c3(k):
        up_sum, kd, g0, gd = v[f"w{k}"]
        v[f"w{k}"] = (up_sum, kd + g0 + gd + v.pop(f"d{k + 1}"))

    def e1(k):
        k0, k1, s = v[f"w{k}"]
        v[f"w{k}"] = (k0, k1, swap(s, first_link(k)))

    def e2(k):
        k0, k1, g = v[f"w{k}"]
        v[f"w{k}"] = (k0 + g[upart:], swap(k1 + g[:upart], second_link(k)))

    def e3(k):
        k0, g = v[f"w{k}"]
        v[f"w{k}"] = k0 + g

    inner = (mp_no == 1) | (mp_no == 2)

    def middle_swap(a):
        return lax.ppermute(a, "mp", [(1, 2), (2, 1)])

    def pass_out(a):
        return lax.ppermute(a, "mp", [(1, 0), (2, 3)])

    def high_bits(a):
        bit = PIECES
        while bit < ndp:
            a = a + swap(a, bit)
            bit *= 2
        return a

    cot_all, att_piece, ob_piece, mlp_piece = lax.optimization_barrier(
        (cotangent, att_piece, ob_piece, mlp_piece)
    )
    v["cot"] = lax.dynamic_slice_in_dim(cot_all, mp_no * share, share, 0)
    v["cot_f"] = v["cot"].astype(F32)
    v["piece"] = mlp_piece
    v["o3"] = zswap(ob_piece, 3)
    v["o1"] = zswap(ob_piece, 1)
    v["t2"] = zswap(att_piece, 2)
    v["normed"] = run_norm1()
    v.fence()
    hp = 2 * part
    t2, o1, o3 = v["t2"], v["o1"], v["o3"]
    v["ta"] = jnp.concatenate([t2[:hp], o1[:part]], axis=0)
    v["tb"] = jnp.concatenate([t2[hp : 2 * hp], o3[:part]], axis=0)
    g1("t")
    v["cot_p"] = swap(v.pop("cot_f"), core)
    v["m1"] = zswap(v["piece"], 1)
    v["mid_a"] = middle_swap(v.pop("piece"))
    v.fence()
    m1 = v["m1"]
    to_y = jnp.concatenate([*v["ta"], m1[upart:]], axis=0)
    to_x = jnp.concatenate([*v["tb"], m1[:upart]], axis=0)
    v["ta"] = (to_y, swap(to_y, py))
    v["tb"] = (to_x, swap(to_x, px))
    v["mid_b"] = middle_swap(v.pop("m1"))
    v["end_a"] = pass_out(v["mid_a"])
    run_attn_own()
    v.fence()
    nt = 2 * 3 * part
    ya, yb = v.pop("ta")
    xa, xb = v.pop("tb")
    v["m1a"], v["m1b"] = (xa[nt:], xb[nt:]), (ya[nt:], yb[nt:])
    v["ta"], v["tb"] = (
        tuple(
            a.reshape(half, 3 * part, width) for a in (both_, swap(both_, core))
        )
        for both_ in (
            jnp.concatenate([ya[:nt], yb[:nt]], axis=0),
            jnp.concatenate([xa[:nt], xb[:nt]], axis=0),
        )
    )
    run_attn_far()
    g2("m1")
    v["mix0"] = zswap(jnp.concatenate([v["st0"].pop("mixs"), v["mid_b"]], axis=0), 1)
    v.fence()
    v["mix2"] = zswap(v["st2"].pop("mixs"), 1)
    run_out()
    m3 = jnp.where(inner, v.pop("mid_a"), v["mix0"][mix_rows:])
    m2 = jnp.where(inner, v.pop("mid_b"), v.pop("end_a"))
    to_x = jnp.concatenate([m3[:upart], m2[:upart]], axis=0)
    to_y = jnp.concatenate([m3[upart:], m2[upart:]], axis=0)
    v["ma"], v["mb"] = (to_x, swap(to_x, px)), (to_y, swap(to_y, py))
    v.fence()
    for t in "ab":
        own, got = v.pop(f"m{t}")
        v[f"m3{t}"] = (own[:upart], got[:upart])
        v[f"m2{t}"] = (own[upart:], got[upart:])
    v["sec_p"] = swap(v.pop("sec_f"), core)
    run_mlp(1, v.pop("m1a"), v.pop("m1b"), v["o1"], part // 8)
    g2("m3")
    v.fence()
    v["p1"] = zswap(v["p1"], 1)
    run_mlp(3, v.pop("m3a"), v.pop("m3b"), v["o3"], part // 8)
    g2("m2")
    v.fence()
    v["p3"] = zswap(v["p3"], 1)
    run_mlp(0, (u0, u1), (d0, d1), bias0, 0)
    e1(1)
    e1(3)
    v.fence()
    run_mlp(2, v.pop("m2a"), v.pop("m2b"), v["t2"], 4 * part // 8)
    e2(1)
    e2(3)
    v["q1u"] = zswap(v["q1u"], 1)
    v.fence()
    e3(1)
    e3(3)
    v["d13"] = jnp.concatenate([v.pop("w1"), v.pop("w3")], axis=0)
    v["q3u"] = zswap(v["q3u"], 1)
    c1(0)
    c1(2)
    v["send"] = run_down(1)
    v.fence()
    c0(0)
    c0(2)
    v["d13"] = zswap(v["d13"], 1)
    v["acc_got"] = swap(v.pop("send"), core)
    v["acc_own"] = run_down(0)
    v.fence()
    d13 = v.pop("d13")
    v["d1"], v["d3"] = d13[:upart], d13[upart:]
    c2u(0)
    c2u(2)
    v["low"] = run_mid()
    v.fence()
    c2d(0)
    c2d(2)
    v["gp2"] = zswap(v.pop("gmt3"), 1)
    v["z2x"] = zswap(v["w2"][0][:n_z2], 2)
    run_out_grad(v.pop("low"))
    v.fence()
    c3(0)
    c3(2)
    up_sum, down_sum = v.pop("w2")
    v["z2y"] = zswap(jnp.concatenate([up_sum[n_z2:], down_sum], axis=0), 2)
    v["gp0"] = zswap(v.pop("gmt1"), 1)
    r1("o")
    r2("o", "b")
    run_attn_bwd(2, "gp2", idx_b, True)
    v.fence()
    r1("q2")
    v.fence()
    mlp_sum = high_bits(
        jnp.concatenate(v.pop("w0"), axis=0)
        + jnp.concatenate([v.pop("z2x"), v.pop("z2y")], axis=0)
    )
    ma, mb = mlp_sum[:upart], mlp_sum[upart:]
    keep, got = v["q2"]
    to_x = jnp.concatenate([(keep[2:] + got[2:]).reshape(-1, width), ma], axis=0)
    v["q2"] = keep[:2] + got[:2]
    keep, got = v["o"]
    to_y = jnp.concatenate([keep[1] + got[1], mb], axis=0)
    v["o"] = keep[0] + got[0]
    v["gx"], v["gy"] = (to_x, swap(to_x, px)), (to_y, swap(to_y, py))
    run_attn_bwd(0, "gp0", idx_b, False)
    v.fence()
    nq = 2 * 3 * part
    (xa, xb), (ya, yb) = v.pop("gx"), v.pop("gy")
    r1("q0")
    q2 = v["q2"] + xb[:nq].reshape(2, 3 * part, width)
    v["q2"] = q2[0]
    to_y = jnp.concatenate([xa[nq:], xb[nq:], q2[1]], axis=0)
    to_x = jnp.concatenate([ya[nmp * part :], yb[nmp * part :]], axis=0)
    v["gx"], v["gy"] = (to_x, swap(to_x, px)), (to_y, swap(to_y, py))
    o = v.pop("o") + yb[: nmp * part]
    v["gn0"] = zswap(
        jnp.concatenate([v["gn"][share : share + n_gn[0]], o[part : 2 * part], o[3 * part :]], axis=0), 1
    )
    v["o0"], v["o2"] = o[:part], o[2 * part : 3 * part]
    v["small"] = call(
        functools.partial(sums_kernel, nmp),
        sds((16, width), F32),
        flops=full * width * 10,
        bytes_accessed=full * width * 6,
        grid_spec=pltpu.PrefetchScalarGridSpec(
            num_scalar_prefetch=2,
            grid=(steps,),
            in_specs=[
                pl.BlockSpec((block, width), lambda t, b, m: (b[t], 0)),
                pl.BlockSpec((block, width), lambda t, b, m: (t, 0)),
                pl.BlockSpec((8, width), lambda t, b, m: (0, 0)),
                *[pl.BlockSpec((3, DH, 128), lambda t, b, m: (0, 0, 0))] * 2,
                *[pl.BlockSpec((3 * e, 128), lambda t, b, m: (0, 0))] * 2,
                *[pl.BlockSpec((1, mine), lambda t, b, m: (0, 0))] * nmp,
            ],
            out_specs=pl.BlockSpec((16, width), lambda t, b, m: (0, 0)),
        ),
    )(
        blk, me1, tokens, v["gn"], v.pop("mst"), v.pop("hst0"), v.pop("hst2"), v.pop("qbg0"),
        v.pop("qbg2"), *[v.pop(f"ubg{k}") for k in range(nmp)],
    )
    v.fence()
    r2("q0", "b")
    (xa, xb), (ya, yb) = v["gx"], v["gy"]
    gn0 = v.pop("gn0")
    v["gn0"] = gn0
    v["o0"] = v["o0"] + gn0[n_gn[0] : n_gn[0] + part]
    o2 = v.pop("o2") + gn0[n_gn[0] + part :]
    q2 = v.pop("q2") + yb[2 * upart :]
    v["y2"] = zswap(jnp.concatenate([q2, o2], axis=0), 2)
    at = share + n_gn[0]
    v["gn1"] = zswap(v["gn"][at : at + n_gn[1]], 1)
    small = v["small"] + swap(v["small"], core)
    v["small"] = small + swap(small, px)
    v.fence()
    r3("q0", "b")
    at = share + n_gn[0] + n_gn[1]
    v["gn2"] = zswap(v["gn"][at : at + n_gn[2]], 1)
    v["small"] = v["small"] + swap(v["small"], py)
    ya, yb = v.pop("gy")
    v["gu"] = (ya, yb, swap(ya, core), swap(yb, core))
    v.fence()
    r4("q0")
    att_sum = high_bits(
        jnp.concatenate([v.pop("q0"), v.pop("o0")], axis=0) + v.pop("y2")
    )
    v["w"] = (att_sum, swap(att_sum, px), swap(att_sum, py), swap(att_sum, px | py))
    xa, xb = v.pop("gx")
    gd = (xa, xb, swap(xa, core), swap(xb, core))
    small = high_bits(v.pop("small"))
    got = zswap(jnp.concatenate([small[:8], small[12:]], axis=0), 1)
    v["small"] = small[:12] + got

    def unpack(kernel, arrays, idx, shape):
        pieces_spec = pl.BlockSpec((2 * upart, width), lambda t: (0, 0))
        return call(
            kernel,
            sds(shape, F32),
            bytes_accessed=2 * 4 * math.prod(shape),
            grid=(1,),
            in_specs=[smem] + [pieces_spec] * 4,
            out_specs=pl.BlockSpec(shape, lambda t: (0, 0)),
            scratch_shapes=[pltpu.VMEM((PIECES, upart, width), F32)],
        )(idx, *arrays)

    v["up_g"] = unpack(unpack_kernel, v.pop("gu"), idx_a, (width, units))
    v["down_g"] = unpack(unpack_rows_kernel, gd, idx_b, (units, width))
    v["gn3"] = zswap(v["gn"][full - n_gn[3] :], 1)
    v.fence()
    input_grad = call(
        final_kernel,
        sds((share, width), BF16),
        flops=share * width * 20,
        bytes_accessed=share * width * 16,
        grid_spec=pltpu.PrefetchScalarGridSpec(
            num_scalar_prefetch=1,
            grid=(1,),
            in_specs=[
                pl.BlockSpec((share, width), lambda t, b: (b[0] // per, 0)),
                pl.BlockSpec((share, width), const2),
                *[pl.BlockSpec((n, width), const2) for n in n_gn],
                pl.BlockSpec((share, width), const2),
                vec_spec,
            ],
            out_specs=pl.BlockSpec((share, width), const2),
        ),
    )(blk, tokens, v["gn"], *[v[f"gn{i}"] for i in range(4)], v["gm"], row1(norm1_gain))
    w = jnp.concatenate(v.pop("w"), axis=0)
    small = v.pop("small")
    small_got = zswap(jnp.concatenate([small[:8], small[10:]], axis=0), 2)
    qkv_weight_grad, out_weight_grad = call(
        unpack_att_kernel,
        (sds((3, e, width), F32), sds((e, width), F32)),
        bytes_accessed=2 * 4 * 4 * width * e,
        in_specs=[smem] + [vmem] * 2,
        out_specs=(vmem, vmem),
        scratch_shapes=[pltpu.VMEM((PIECES, 4 * part, width), F32)],
    )(idx_a, w, swap(w, core))
    qkv_weight_grad = jnp.swapaxes(qkv_weight_grad, 1, 2)
    qkv_bias_grad, *rows_of = call(
        small_out_kernel,
        (sds((3, e), F32), *[sds((DH,), F32)] * 3, *[sds((width,), F32)] * 7),
        bytes_accessed=100_000,
        in_specs=[vmem, vmem],
        out_specs=(vmem,) * 11,
    )(small[:10], small_got)
    heads_of, rows_of = rows_of[:3], rows_of[3:]
    return (
        v["block_out"],
        input_grad,
        qkv_weight_grad,
        qkv_bias_grad,
        out_weight_grad,
        rows_of[2],
        v["up_g"],
        rows_of[6],
        v["down_g"],
        rows_of[3],
        rows_of[4],
        rows_of[5],
        heads_of[0],
        heads_of[1],
        heads_of[2],
        rows_of[0],
        rows_of[1],
    )


def solution(mesh):
    in_specs = (
        P("dp", None),
        P("dp"),
        P(None, None, "mp"),
        P(None, "mp"),
        P("mp", None),
        P(),
        P(None, "mp"),
        P("mp"),
        P("mp", None),
        P(),
        P(),
        P(),
        P(),
        P(),
        P(),
        P(),
        P(),
        P("dp", None),
    )
    out_specs = (
        P(("dp", "mp"), None),
        P(("dp", "mp"), None),
        P(None, None, "mp"),
        P(None, "mp"),
        P("mp", None),
        P(),
        P(None, "mp"),
        P("mp"),
        P("mp", None),
        P(),
        P(),
        P(),
        P(),
        P(),
        P(),
        P(),
        P(),
    )
    return jax.shard_map(shards, mesh=mesh, in_specs=in_specs, out_specs=out_specs, check_vma=False)
```

```python
import functools
import math

import jax
import jax.numpy as jnp
from jax import lax
from jax.experimental import pallas as pl
from jax.experimental.pallas import tpu as pltpu
from jax.sharding import PartitionSpec as P

F32 = jnp.float32
BF16 = jnp.bfloat16
DH = 64
SEQ_LEN = 1024
NORM_EPS = 1e-06
PIECES = 8
SEG_COLS = 128
LOG2E = math.log2(math.e)
SCALE = DH ** (-0.5)
BITS_A = (2, 4, 1)
BITS_B = (4, 2, 1)
MLP_KIND = ("a", "a", "b", "b")
VMEM_LIMIT = 26 * 1024 * 1024
VMEM_LARGE = 56 * 1024 * 1024


def mm(a, b):
    return lax.dot_general(a, b, (((1,), (0,)), ((), ())), preferred_element_type=F32)


def mm_nt(a, b):
    return lax.dot_general(a, b, (((1,), (1,)), ((), ())), preferred_element_type=F32)


def mm_tn(a, b):
    return lax.dot_general(a, b, (((0,), (0,)), ((), ())), preferred_element_type=F32)


def call(kernel, out_shape, flops=0, bytes_accessed=0, vmem_limit=VMEM_LIMIT, **kw):
    return pl.pallas_call(
        kernel,
        out_shape=out_shape,
        compiler_params=pltpu.CompilerParams(vmem_limit_bytes=vmem_limit),
        cost_estimate=pl.CostEstimate(
            flops=flops, bytes_accessed=bytes_accessed, transcendentals=0
        ),
        **kw,
    )


def sds(shape, dtype):
    return jax.ShapeDtypeStruct(shape, dtype)


def row_norm(x):
    mean = jnp.mean(x, axis=-1, keepdims=True)
    cen = x - mean
    rstd = lax.rsqrt(jnp.mean(cen * cen, axis=-1, keepdims=True) + NORM_EPS)
    return cen * rstd, rstd


def row_norm_back(f, n, rstd):
    mean_f = jnp.mean(f, axis=-1, keepdims=True)
    mean_fn = jnp.mean(f * n, axis=-1, keepdims=True)
    return (f - mean_f - n * mean_fn) * rstd


def col_norm(x):
    mean = jnp.mean(x, axis=0, keepdims=True)
    cen = x - mean
    rstd = lax.rsqrt(jnp.mean(cen * cen, axis=0, keepdims=True) + NORM_EPS)
    return cen * rstd, rstd


def col_norm_back(f, n, rstd):
    mean_f = jnp.mean(f, axis=0, keepdims=True)
    mean_fn = jnp.mean(f * n, axis=0, keepdims=True)
    return (f - mean_f - n * mean_fn) * rstd


def lane_fold(x):
    out = x[:, :128]
    for t in range(1, x.shape[1] // 128):
        out = out + x[:, t * 128 : (t + 1) * 128]
    return out


def offset_of(s, bits):
    return sum(bit for t, bit in enumerate(bits) if (s >> t) & 1)


def norm1_kernel(blk_ref, x_ref, g_ref, s_ref, out_ref):
    n, _ = row_norm(x_ref[...].astype(F32))
    out_ref[...] = (n * g_ref[...] + s_ref[...]).astype(BF16)


def build_q_aug(q_pre, qg, qs, qaug_ref):
    n, rstd = col_norm(q_pre)
    q_low = (n * qg + qs).astype(BF16)
    scaled = q_low.astype(F32) * (SCALE * LOG2E)
    hi = scaled.astype(BF16)
    lo = (scaled - hi.astype(F32)).astype(BF16)
    qaug_ref[0:DH, :] = hi
    qaug_ref[DH : 2 * DH, :] = lo
    return n, rstd, q_low


def build_k_aug(k_pre, kg, kaug_ref):
    n, rstd = col_norm(k_pre)
    k_low = (n * kg).astype(BF16)
    kaug_ref[:, 0 : 2 * DH] = jnp.concatenate([k_low, k_low], axis=0).T
    return n, rstd, k_low


def bias_col(b_ref, n):
    return b_ref[...].T[0:n, 0:1]


def prep_kernel(
    me_ref, w_ref, o_ref, qb_ref, ub_ref, up_ref, dn_ref,
    att_ref, ob_ref, b_ref, p_ref, u0_ref, u1_ref, d0_ref, d1_ref,
    t_ref, wf_ref,
):
    part = 24
    e = PIECES * part
    me = me_ref[0]
    b_ref[...] = jnp.zeros(b_ref.shape, F32)
    for s in range(3):
        wf_ref[...] = w_ref[s].astype(F32)
        rows = wf_ref[pl.ds(pl.multiple_of(me * part, 8), part), :]
        att_ref[s * part : (s + 1) * part, :] = rows
        b_ref[0:1, s * e : (s + 1) * e] = qb_ref[s : s + 1, :]
    upart = up_ref.shape[1] // PIECES
    ub = ub_ref[...].reshape(1, PIECES * upart)
    for s in range(PIECES // 2):
        piece = jnp.zeros((1, upart), F32)
        for p in range(PIECES):
            here = (me ^ offset_of(s, BITS_A)) == p
            piece = piece + jnp.where(here, ub[:, p * upart : (p + 1) * upart], 0.0)
        b_ref[1:2, s * upart : (s + 1) * upart] = piece
    wf_ref[...] = o_ref[...].astype(F32)
    rows = wf_ref[pl.ds(pl.multiple_of(me * part, 8), part), :]
    att_ref[3 * part : 4 * part, :] = rows
    ob_ref[0:part, :] = rows
    att_ref[4 * part :, :] = b_ref[...]
    ob_ref[part:, :] = b_ref[...]

    t_ref[...] = up_ref[...].astype(F32).T

    def at_piece(r):
        return pl.ds(pl.multiple_of((me ^ r) * upart, 32), upart)

    p_ref[0:upart, :] = t_ref[at_piece(0), :]
    p_ref[upart:, :] = dn_ref[at_piece(0), :].astype(F32)
    for i, (u_ref, d_ref) in enumerate(((u0_ref, d0_ref), (u1_ref, d1_ref))):
        for j in range(2):
            u_ref[j] = t_ref[at_piece(offset_of(2 * i + j, BITS_A)), :].astype(BF16)
            d_ref[j] = dn_ref[at_piece(offset_of(2 * i + j, BITS_B)), :]


def attend(x_ref, wt_ref, b_ref, hv_ref, kmask_ref, qhot_ref, outs, qaug_ref, kaug_ref):
    qpre_ref, kpre_ref, vt_ref, mixt_ref, mixf_ref, mixs_ref, l_ref = outs
    e = qpre_ref.shape[0]
    full = x_ref.shape[0]
    share = full // 2
    heads = e // DH
    x = x_ref[...]
    bias = bias_col(b_ref, 3 * e)
    qpre_ref[...] = mm_nt(wt_ref[0:e, :], x) + bias[0:e]
    kpre_ref[...] = mm_nt(wt_ref[e : 2 * e, :], x) + bias[e : 2 * e]
    vt_ref[...] = (mm_nt(wt_ref[2 * e : 3 * e, :], x) + bias[2 * e :]).astype(BF16)
    qaug_ref[2 * DH :, :] = qhot_ref[...]
    kaug_ref[:, 2 * DH :] = kmask_ref[...]
    ones = jnp.ones((16, full), BF16)
    for h in range(heads):
        hs = slice(h * DH, (h + 1) * DH)
        build_q_aug(qpre_ref[hs, :], hv_ref[:, 0:1], hv_ref[:, 1:2], qaug_ref)
        build_k_aug(kpre_ref[hs, :], hv_ref[:, 2:3], kaug_ref)
        prob = jnp.exp2(mm(kaug_ref[...], qaug_ref[...])).astype(BF16)
        vaug = jnp.concatenate([vt_ref[hs, :], ones], axis=0)
        o = mm(vaug, prob)
        total = o[DH : DH + 1, :]
        l_ref[h : h + 1, :] = total
        mix = o[0:DH, :] / total
        mixf_ref[hs, :] = mix
        mixt_ref[hs, :] = mix[:, 0:share].astype(BF16)
        at = h * share
        for c in range(0, share, 256):
            block_no, lane = divmod(at + c, x.shape[1])
            mixs_ref[block_no * DH : (block_no + 1) * DH, lane : lane + 256] = mix[
                :, share + c : share + c + 256
            ]


def attn_fwd_own_kernel(x_ref, wt_ref, b_ref, hv_ref, kmask_ref, qhot_ref, *refs):
    attend(x_ref, wt_ref, b_ref, hv_ref, kmask_ref, qhot_ref, refs[:7], *refs[7:])


def attn_fwd_kernel(
    ia_ref, ib_ref, a0_ref, a1_ref, b0_ref, b1_ref, x_ref, b_ref, hv_ref, kmask_ref, qhot_ref,
    wt_ref, ow_ref, ow1_ref, ow3_ref, *refs,
):
    wa_ref, wb_ref = refs[-2:]
    part = 24
    e = PIECES * part
    half = PIECES // 2
    wa_ref[0:half] = a0_ref[...]
    wa_ref[half:] = a1_ref[...]
    wb_ref[0:half] = b0_ref[...]
    wb_ref[half:] = b1_ref[...]

    def rows(w_ref, i_ref, at):
        return jnp.concatenate(
            [w_ref[i_ref[p], at * part : (at + 1) * part, :] for p in range(PIECES)], axis=0
        ).astype(BF16)

    wt_ref[0:e, :] = rows(wa_ref, ia_ref, 0)
    wt_ref[e : 2 * e, :] = rows(wa_ref, ia_ref, 1)
    wt_ref[2 * e : 3 * e, :] = rows(wb_ref, ib_ref, 0)
    ow_ref[...] = rows(wb_ref, ib_ref, 1)
    ow1_ref[...] = rows(wa_ref, ia_ref, 2)
    ow3_ref[...] = rows(wb_ref, ib_ref, 2)
    attend(x_ref, wt_ref, b_ref, hv_ref, kmask_ref, qhot_ref, refs[:7], *refs[7:9])


def unmix(ref, heads, share):
    width = ref.shape[1]
    rows = []
    for h in range(heads):
        cols = []
        for c in range(0, share, 256):
            block_no, lane = divmod(h * share + c, width)
            cols.append(ref[block_no * DH : (block_no + 1) * DH, lane : lane + 256])
        rows.append(jnp.concatenate(cols, axis=1))
    return jnp.concatenate(rows, axis=0).astype(BF16)


def mix_of(ref, share):
    if ref.dtype == BF16:
        return ref[...]
    return unmix(ref, ref.shape[0] * ref.shape[1] // (DH * share), share)


def out_norm2_kernel(nslot, blk_ref, x_ref, *refs):
    mixes = refs[:nslot]
    ws = refs[nslot : 2 * nslot]
    ob_ref, g_ref, s_ref, mid_ref, sec_ref, secf_ref = refs[2 * nslot :]
    acc = x_ref[...].astype(F32) + ob_ref[...]
    for k in range(nslot):
        acc = acc + mm_tn(mix_of(mixes[k], x_ref.shape[0]), ws[k][...])
    mid_ref[...] = acc
    n, _ = row_norm(acc)
    sec = (n * g_ref[...] + s_ref[...]).astype(BF16)
    sec_ref[...] = sec
    secf_ref[...] = sec.astype(F32)


def mlp_kernel(
    kind, keeps, sec_ref, secp_ref, cot_ref, cotp_ref, u0_ref, u1_ref, d0_ref, d1_ref, b_ref, *refs
):
    if keeps:
        p_ref, hid_ref, gp_ref, ub_ref, db_ref, k0_ref, k1_ref, s0_ref, s1_ref, gb_ref = refs
    else:
        hid_ref, gp_ref, ub_ref, db_ref, up_ref, uq_ref, k0_ref, k1_ref, sd_ref, gb_ref = refs
    part = u0_ref.shape[1]
    share = sec_ref.shape[0]
    up = jnp.concatenate([u0_ref[0], u0_ref[1], u1_ref[0], u1_ref[1]], axis=0).astype(BF16)
    down = jnp.concatenate([d0_ref[0], d1_ref[0], d0_ref[1], d1_ref[1]], axis=0).astype(BF16)
    ub_ref[...] = up
    db_ref[...] = down
    bias = b_ref[1:2, 0 : up.shape[0]]
    for r, (s_ref, c_ref) in enumerate(((sec_ref, cot_ref), (secp_ref, cotp_ref))):
        rows = slice(r * share, (r + 1) * share)
        sec = s_ref[...].astype(BF16)
        cot = c_ref[...].astype(BF16)
        pre = mm_nt(sec, up) + bias
        cdf = 0.5 * (1.0 + lax.erf(pre * (1.0 / math.sqrt(2.0))))
        hid = (pre * cdf).astype(BF16)
        pdf = jnp.exp(-0.5 * pre * pre) * (1.0 / math.sqrt(2.0 * math.pi))
        gpre = (mm_nt(cot, down) * (cdf + pre * pdf)).astype(BF16)
        hid_ref[rows, :] = hid
        gp_ref[rows, :] = gpre
        gb_r = jnp.sum(gpre.astype(F32), axis=0, keepdims=True)
        gd_r = mm_tn(hid, cot)
        gu_r = mm_tn(gpre, sec)
        if r == 0:
            gb, gd, gu = gb_r, gd_r, gu_r
        else:
            gb, gd, gu = gb + gb_r, gd + gd_r, gu + gu_r
    gb_ref[...] = gb
    order = (0, 1, 2, 3) if kind == "a" else (0, 2, 1, 3)
    gu_at = [gu[i * part : (i + 1) * part] for i in order]
    gd_at = [gd[i * part : (i + 1) * part] for i in order]
    if keeps:
        gu_at[3] = gu_at[3] + p_ref[0:part, :]
        gu_at[2] = gu_at[2] + p_ref[part:, :]
        for i, ref in enumerate((k0_ref, k1_ref, s0_ref, s1_ref)):
            ref[0:part, :] = gu_at[i]
            ref[part:, :] = gd_at[i]
    else:
        up_ref[0:part, :] = gu_at[3]
        up_ref[part:, :] = gu_at[2]
        uq_ref[0:part, :] = gu_at[0]
        uq_ref[part:, :] = gu_at[1]
        k0_ref[...] = gd_at[0]
        k1_ref[...] = gd_at[1]
        sd_ref[0:part, :] = gd_at[3]
        sd_ref[part:, :] = gd_at[2]


def down_kernel(nslot, *refs):
    hids = refs[:nslot]
    gps = refs[nslot : 2 * nslot]
    ubs = refs[2 * nslot : 3 * nslot]
    dbs = refs[3 * nslot : 4 * nslot]
    out_ref = refs[4 * nslot]
    cat = lambda refs, axis: jnp.concatenate([r[...] for r in refs], axis=axis)
    out_ref[0] = mm(cat(hids, 1), cat(dbs, 0))
    out_ref[1] = mm(cat(gps, 1), cat(ubs, 0))


def mid_kernel(nslot, mid_ref, own_ref, got_ref, cot_ref, db_ref, g_ref, *refs):
    ows = refs[:nslot]
    gmts = refs[nslot : 2 * nslot]
    bo_ref, gm_ref, low_ref, st_ref = refs[2 * nslot :]
    mid = mid_ref[...]
    n, rstd = row_norm(mid)
    e = own_ref[1] + got_ref[1]
    cot = cot_ref[...].astype(F32)
    gm = cot + row_norm_back(e * g_ref[...], n, rstd)
    gm_ref[...] = gm
    gm_low = gm.astype(BF16)
    low_ref[...] = gm_low
    for k in range(nslot):
        gmts[k][...] = mm_nt(ows[k][...], gm_low).astype(gmts[k].dtype)
    bo_ref[...] = (mid + (own_ref[0] + got_ref[0]) + db_ref[...]).astype(BF16)
    st_ref[0:1, :] = jnp.sum(e * n, axis=0, keepdims=True)
    st_ref[1:2, :] = jnp.sum(e, axis=0, keepdims=True)
    st_ref[2:3, :] = jnp.sum(gm_low.astype(F32), axis=0, keepdims=True)
    st_ref[3:4, :] = jnp.sum(cot, axis=0, keepdims=True)
    st_ref[4:8, :] = jnp.zeros((4, mid.shape[1]), F32)


def out_grad_kernel(nslot, idx_ref, low_ref, *refs):
    mixts = refs[:nslot]
    gow_keep, gow_send = refs[nslot:]
    part = 24
    gm_low = low_ref[...]
    for k in range(nslot):
        g = mm(mix_of(mixts[k], gm_low.shape[0]), gm_low)
        for p in range(PIECES):
            at = idx_ref[p]
            rows = slice(k * part, (k + 1) * part)

            @pl.when(at < PIECES // 2)
            def _():
                gow_keep[at, rows, :] = g[p * part : (p + 1) * part, :]

            @pl.when(at >= PIECES // 2)
            def _():
                gow_send[at - PIECES // 2, rows, :] = g[p * part : (p + 1) * part, :]


def attn_bwd_kernel(
    ncuts, idx_ref, x_ref, qpre_ref, kpre_ref, vt_ref, wt_ref, gmt_ref, gmtp_ref, mixf_ref, l_ref,
    hv_ref, kmask_ref, qhot_ref, *refs
):
    if ncuts:
        gn_in, gk_ref, gs_ref, *gn_refs = refs[: 3 + ncuts]
    else:
        gk_ref, gs_ref, gn_ref = refs[:3]
    st_ref, gb_ref, qaug_ref, kaug_ref, gpt_ref = refs[-5:]
    part = 24
    e = PIECES * part
    full = x_ref.shape[0]
    heads = e // DH
    qaug_ref[2 * DH :, :] = qhot_ref[...]
    kaug_ref[:, 2 * DH :] = kmask_ref[...]
    qg, qs, kg = hv_ref[:, 0:1], hv_ref[:, 1:2], hv_ref[:, 2:3]
    qg_sum = jnp.zeros((DH, 128), F32)
    qs_sum = jnp.zeros((DH, 128), F32)
    kg_sum = jnp.zeros((DH, 128), F32)
    row_no = lax.broadcasted_iota(jnp.int32, (DH, full), 0)
    one_rows = (row_no < 3).astype(F32).astype(BF16)
    for h in range(heads):
        hs = slice(h * DH, (h + 1) * DH)
        qn, qr, q_low = build_q_aug(qpre_ref[hs, :], qg, qs, qaug_ref)
        kn, kr, k_low = build_k_aug(kpre_ref[hs, :], kg, kaug_ref)
        inv = 1.0 / l_ref[h : h + 1, :]
        gm = jnp.concatenate(
            [gmt_ref[hs, :].astype(F32), gmtp_ref[hs, :].astype(BF16).astype(F32)], axis=1
        )
        go_low = (gm * inv).astype(BF16)
        delta = -jnp.sum(go_low.astype(F32) * mixf_ref[hs, :], axis=0, keepdims=True)
        d0 = delta.astype(BF16).astype(F32)
        d1 = (delta - d0).astype(BF16).astype(F32)
        d2 = delta - d0 - d1
        extra = jnp.where(
            row_no == 0, d0, jnp.where(row_no == 1, d1, jnp.where(row_no == 2, d2, 0.0))
        ).astype(BF16)
        goaug = jnp.concatenate([go_low, extra], axis=0)
        vaug = jnp.concatenate([vt_ref[hs, :], one_rows], axis=0).T
        prob = jnp.exp2(mm(kaug_ref[...], qaug_ref[...]))
        ds = (prob * mm(vaug, goaug)).astype(BF16)
        gv = mm_nt(go_low, prob.astype(BF16))
        gk = mm_nt(q_low, ds) * SCALE
        gq = mm(k_low, ds) * SCALE
        qg_sum += lane_fold(gq * qn)
        qs_sum += lane_fold(gq)
        kg_sum += lane_fold(gk * kn)
        gpt_ref[h * DH : (h + 1) * DH, :] = col_norm_back(gq * qg, qn, qr).astype(BF16)
        gpt_ref[e + h * DH : e + (h + 1) * DH, :] = col_norm_back(gk * kg, kn, kr).astype(BF16)
        gpt_ref[2 * e + h * DH : 2 * e + (h + 1) * DH, :] = gv.astype(BF16)
    st_ref[0] = qg_sum
    st_ref[1] = qs_sum
    st_ref[2] = kg_sum
    gp = gpt_ref[...]
    gb_ref[...] = lane_fold(gp.astype(F32))
    gw = mm(gp, x_ref[...])

    def put(ref, at, p):
        for s in range(3):
            ref[at, s * part : (s + 1) * part, :] = gw[s * e + p * part : s * e + (p + 1) * part, :]

    for p in range(PIECES):
        at = idx_ref[p]

        @pl.when(at < PIECES // 2)
        def _():
            put(gk_ref, at, p)

        @pl.when(at >= PIECES // 2)
        def _():
            put(gs_ref, at - PIECES // 2, p)

    gn = mm_tn(gp, wt_ref[...])
    if not ncuts:
        gn_ref[...] = gn
    else:
        at = 0
        for ref in gn_refs:
            rows = slice(at, at + ref.shape[0])
            ref[...] = gn_in[rows, :] + gn[rows]
            at += ref.shape[0]


def sums_kernel(
    nslot, blk_ref, me_ref, x_ref, xf_ref, gn_ref, mst_ref, h0_ref, h2_ref, b0_ref, b2_ref, *refs
):
    ubs = refs[:nslot]
    fars = refs[nslot:-1]
    out_ref = refs[-1]

    def fill():
        out_ref[...] = jnp.zeros_like(out_ref)
        out_ref[0:4, :] = mst_ref[0:4, :]
        heads = jnp.concatenate([h0_ref[i] + h2_ref[i] for i in range(3)], axis=0).T
        out_ref[6:7, 0 : heads.shape[1]] = jnp.sum(heads, axis=0, keepdims=True)
        me = me_ref[0]
        upart = out_ref.shape[1] // PIECES
        for row, k in zip((8, 10, 12, 14), (0, 2, 1, 3)):
            if k % 2 == 0:
                cols = (b0_ref if k == 0 else b2_ref)[...].T
                out_ref[row : row + 1, 0 : cols.shape[1]] = jnp.sum(cols, axis=0, keepdims=True)
            mine = ubs[k][...]
            for p in range(PIECES):
                piece = jnp.zeros((1, upart), F32)
                for t in range(PIECES // 2):
                    here = (me ^ offset_of(t, BITS_A)) == p
                    piece = piece + jnp.where(here, mine[:, t * upart : (t + 1) * upart], 0.0)
                out_ref[row + 1 : row + 2, p * upart : (p + 1) * upart] = piece

    fill()

    def add(x, e):
        n, _ = row_norm(x.astype(F32))
        out_ref[4:5, :] += jnp.sum(e * n, axis=0, keepdims=True)
        out_ref[5:6, :] += jnp.sum(e, axis=0, keepdims=True)

    add(x_ref[...], gn_ref[...])
    at = 0
    for ref in fars:
        add(xf_ref[at : at + ref.shape[0], :], ref[...])
        at += ref.shape[0]


def small_out_kernel(a_ref, b_ref, qb_ref, h0_ref, h1_ref, h2_ref, *rows):
    total = a_ref[...] + b_ref[...]
    for row, ref in zip((0, 1, 2, 3, 4, 5, 9), rows):
        ref[...] = total[row]
    for i, ref in enumerate((h0_ref, h1_ref, h2_ref)):
        ref[...] = total[6, i * DH : (i + 1) * DH]
        n = qb_ref.shape[1]
        qb_ref[i : i + 1, :] = total[8:9, i * n : (i + 1) * n]


def final_kernel(blk_ref, x_ref, gn_ref, *refs):
    gots = refs[:-3]
    gm_ref, g_ref, out_ref = refs[-3:]
    at = 0
    for ref in gots:
        rows = slice(at, at + ref.shape[0])
        n, rstd = row_norm(x_ref[rows, :].astype(F32))
        f = (gn_ref[rows, :] + ref[...]) * g_ref[...]
        out_ref[rows, :] = (gm_ref[rows, :] + row_norm_back(f, n, rstd)).astype(BF16)
        at += ref.shape[0]


def lay_out(refs, to_ref):
    part = to_ref.shape[1]
    for i, ref in enumerate(refs):
        for j in range(2):
            to_ref[2 * i + j] = ref[j * part : (j + 1) * part, :]


def unpack_kernel(idx_ref, a_ref, b_ref, c_ref, d_ref, out_ref, s_ref):
    lay_out((a_ref, b_ref, c_ref, d_ref), s_ref)
    whole = jnp.concatenate([s_ref[idx_ref[p]] for p in range(PIECES)], axis=0)
    out_ref[...] = whole.T


def unpack_rows_kernel(idx_ref, a_ref, b_ref, c_ref, d_ref, out_ref, s_ref):
    part = s_ref.shape[1]
    lay_out((a_ref, b_ref, c_ref, d_ref), s_ref)
    for p in range(PIECES):
        out_ref[p * part : (p + 1) * part, :] = s_ref[idx_ref[p]]


def unpack_att_kernel(i_ref, a_ref, b_ref, qkv_ref, out_ref, s_ref):
    rows = s_ref.shape[1]
    part = rows // 4
    half = PIECES // 2
    for j in range(half):
        s_ref[j] = a_ref[j * rows : (j + 1) * rows, :]
        s_ref[half + j] = b_ref[j * rows : (j + 1) * rows, :]
    for s, ref in enumerate((qkv_ref.at[0], qkv_ref.at[1], qkv_ref.at[2], out_ref)):
        for p in range(PIECES):
            ref[p * part : (p + 1) * part, :] = s_ref[i_ref[p], s * part : (s + 1) * part, :]


def swap_mp(a, k, size):
    return lax.ppermute(a, "mp", [(s, s ^ k) for s in range(size)])


def swap_plane(a, bit, size):
    return lax.ppermute(a, "dp", [(d, d ^ bit) for d in range(size)])


def storage_of(r, bits):
    return sum(jnp.where((r & bit) != 0, 1 << t, 0) for t, bit in enumerate(bits))


class Stages:
    def __init__(self):
        self.live = {}

    def __setitem__(self, name, value):
        self.live[name] = value

    def __getitem__(self, name):
        return self.live[name]

    def pop(self, name):
        return self.live.pop(name)

    def fence(self, *still_flying):
        now = {n: a for n, a in self.live.items() if n not in still_flying}
        leaves, tree = jax.tree.flatten(now)
        self.live.update(jax.tree.unflatten(tree, lax.optimization_barrier(leaves)))


def shards(
    tokens,
    seg_ids,
    qkv_weight,
    qkv_bias,
    out_weight,
    out_bias,
    up_weight,
    up_bias,
    down_weight,
    down_bias,
    norm1_gain,
    norm1_shift,
    query_gain,
    query_shift,
    key_gain,
    norm2_gain,
    norm2_shift,
    cotangent,
):
    ndp = lax.axis_size("dp")
    nmp = lax.axis_size("mp")
    dp_no = lax.axis_index("dp")
    mp_no = lax.axis_index("mp")
    me = dp_no % PIECES
    row_count, width = tokens.shape
    share = row_count // nmp
    full = SEQ_LEN
    assert full == 2 * share and nmp == 4 and ndp % PIECES == 0
    e = qkv_weight.shape[2]
    part = e // PIECES
    units = up_weight.shape[1]
    upart = units // PIECES
    half = PIECES // 2
    mine = half * upart
    core, px, py = 1, 2, 4

    vmem = pl.BlockSpec(memory_space=pltpu.VMEM)
    smem = pl.BlockSpec(memory_space=pltpu.SMEM)
    row1 = lambda v: v.reshape(1, -1)
    col = lambda v: v.reshape(-1, 1)
    swap = lambda a, bit: swap_plane(a, bit, ndp)
    zswap = lambda a, k: swap_mp(a, k, nmp)
    v = Stages()

    me1 = me.astype(jnp.int32).reshape(1)
    qkv_t = jnp.swapaxes(qkv_weight, 1, 2)
    wt0 = qkv_t.reshape(3 * e, width)
    att_piece, ob_piece, bias0, mlp_piece, u0, u1, d0, d1 = call(
        prep_kernel,
        (
            sds((4 * part + 8, width), F32),
            sds((part + 8, width), F32),
            sds((8, width), F32),
            sds((2 * upart, width), F32),
            *[sds((2, upart, width), BF16)] * 4,
        ),
        bytes_accessed=9_000_000,
        vmem_limit=VMEM_LARGE,
        in_specs=[smem] + [vmem] * 6,
        out_specs=(vmem,) * 8,
        scratch_shapes=[pltpu.VMEM((units, width), F32), pltpu.VMEM((e, width), F32)],
    )(
        me1, qkv_t, out_weight, qkv_bias, up_bias, up_weight, down_weight
    )

    n_gn = (256, 112, 144)
    n_z2 = 64
    numbers = jnp.arange(PIECES, dtype=jnp.int32)
    idx_a = storage_of(numbers ^ me, BITS_A).astype(jnp.int32)
    idx_b = storage_of(numbers ^ me, BITS_B).astype(jnp.int32)

    block = 256
    per = share // block
    steps = 2 * per
    tile_no = jnp.arange(steps, dtype=jnp.int32)
    blk = jnp.where(tile_no < per, mp_no * per + tile_no, (mp_no ^ 1) * per + tile_no - per).astype(
        jnp.int32
    )
    const2 = lambda t, b: (0, 0)
    tok_spec = pl.BlockSpec((block, width), lambda t, b: (b[t], 0))
    run_spec = pl.BlockSpec((block, width), lambda t, b: (t, 0))
    vec_spec = pl.BlockSpec((1, width), const2)

    def run_norm1():
        return call(
            norm1_kernel,
            sds((full, width), BF16),
            flops=full * width * 10,
            bytes_accessed=full * width * 4,
            grid_spec=pltpu.PrefetchScalarGridSpec(
                num_scalar_prefetch=1,
                grid=(steps,),
                in_specs=[tok_spec, vec_spec, vec_spec],
                out_specs=run_spec,
            ),
        )(blk, tokens, row1(norm1_gain), row1(norm1_shift))

    seg_own = lax.dynamic_slice_in_dim(seg_ids, mp_no * share, share, 0)
    seg_other = lax.dynamic_slice_in_dim(seg_ids, (mp_no ^ 1) * share, share, 0)
    seg_keys = jnp.concatenate([seg_own, seg_other])
    qhot = (
        lax.broadcasted_iota(jnp.int32, (SEG_COLS, full), 0) == seg_keys[None, :]
    ).astype(BF16)
    kmask = jnp.where(
        lax.broadcasted_iota(jnp.int32, (full, SEG_COLS), 1) == seg_keys[:, None], 0.0, -1e30
    ).astype(BF16)
    hv = jnp.stack([query_gain, query_shift, key_gain], axis=1)
    scratch = [
        pltpu.VMEM((2 * DH + SEG_COLS, full), BF16),
        pltpu.VMEM((full, 2 * DH + SEG_COLS), BF16),
    ]

    def whole(a):
        return pl.BlockSpec(a.shape, lambda t: (0,) * len(a.shape))

    def bias_at(block_no):
        return pl.BlockSpec((8, width), lambda t: (block_no, 0))

    att_names = ["qpre", "kpre", "vt", "mixt", "mixf", "mixs", "l"]
    att_shapes = [
        sds((e, full), F32),
        sds((e, full), F32),
        sds((e, full), BF16),
        sds((e, share), BF16),
        sds((e, full), F32),
        sds((e * share // width, width), F32),
        sds((8, full), F32),
    ]
    mix_rows = e * share // width

    def run_attn_own():
        outs = call(
            attn_fwd_own_kernel,
            tuple(att_shapes),
            flops=2 * (full * width * e * 3 + full * full * e * 8),
            bytes_accessed=10_000_000,
            in_specs=[vmem] * 6,
            out_specs=(vmem,) * 7,
            scratch_shapes=scratch,
        )(v["normed"], wt0, bias0, hv, kmask, qhot)
        v["st0"] = dict(zip(att_names, outs))
        v["st0"]["wt"] = wt0
        v["st0"]["ow"] = out_weight

    def run_attn_far():
        shapes = [sds((3 * e, width), BF16)] + [sds((e, width), BF16)] * 3 + att_shapes
        args = [
            *v.pop("ta"), *v.pop("tb"), v["normed"], v["t2"], hv, kmask, qhot,
        ]
        specs = [whole(a) for a in args]
        specs[5] = bias_at(4 * part // 8)
        outs = call(
            attn_fwd_kernel,
            tuple(shapes),
            flops=2 * (full * width * e * 3 + full * full * e * 8),
            bytes_accessed=10_000_000,
            grid=(1,),
            in_specs=[smem, smem] + specs,
            out_specs=tuple(whole(a) for a in shapes),
            scratch_shapes=scratch
            + [pltpu.VMEM((PIECES, 3 * part, width), F32)] * 2,
        )(idx_a, idx_b, *args)
        v["st2"] = dict(zip(["wt", "ow", "ow1", "ow3"] + att_names, outs))

    def by_slot():
        st0, st2 = v["st0"], v["st2"]
        mixes = [st0["mixt"], v["mix0"], st2["mixt"], v["mix2"]]
        ows = [st0["ow"], st2["ow1"], st2["ow"], st2["ow3"]]
        return mixes, ows

    def run_out():
        own_spec = pl.BlockSpec((share, width), lambda t, b: (b[0] // per, 0))
        whole2 = lambda shape: pl.BlockSpec(shape, lambda t, b: (0,) * len(shape))
        mixes, ows = by_slot()
        v["middle"], v["second"], v["sec_f"] = call(
            functools.partial(out_norm2_kernel, nmp),
            (sds((share, width), F32), sds((share, width), BF16), sds((share, width), F32)),
            flops=2 * share * width * e * nmp,
            bytes_accessed=8_000_000,
            grid_spec=pltpu.PrefetchScalarGridSpec(
                num_scalar_prefetch=1,
                grid=(1,),
                in_specs=[own_spec]
                + [whole2((e, share)), whole2((mix_rows, width))] * 2
                + [whole2((e, width))] * nmp
                + [whole2((1, width))] * 3,
                out_specs=(whole2((share, width)),) * 3,
            ),
        )(blk, tokens, *mixes, *ows, row1(out_bias), row1(norm2_gain), row1(norm2_shift))

    def run_mlp(k, up, down, bias, block_no):
        keeps = k % 2 == 0
        args = [
            v["second"], v["sec_p"], v["cot"], v["cot_p"], up[0], up[1], down[0], down[1], bias,
        ]
        if keeps:
            args.append(v.pop(f"p{k + 1}"))
        specs = [whole(a) for a in args]
        specs[8] = bias_at(block_no)
        piece = lambda n: sds((n * upart, width), F32)
        shapes = (
            *[sds((full, mine), BF16)] * 2,
            *[sds((mine, width), BF16)] * 2,
            *([piece(2)] * 4 if keeps else [piece(2), piece(2), piece(1), piece(1), piece(2)]),
            sds((1, mine), F32),
        )
        res = call(
            functools.partial(mlp_kernel, MLP_KIND[k], keeps),
            shapes,
            flops=2 * full * width * mine * 4,
            bytes_accessed=12_000_000,
            grid=(1,),
            in_specs=specs,
            out_specs=tuple(whole(a) for a in shapes),
        )(*args)
        v[f"h{k}"] = res[:4]
        v[f"ubg{k}"] = res[-1]
        if keeps:
            v[f"w{k}"] = res[4:8]
        else:
            v[f"p{k}"], v[f"q{k}u"] = res[4], res[5]
            v[f"w{k}"] = res[6:9]

    def run_down(r):
        row_spec = pl.BlockSpec((share, mine), lambda t: (r, 0))
        w_spec = pl.BlockSpec((mine, width), lambda t: (0, 0))
        return call(
            functools.partial(down_kernel, nmp),
            sds((2, share, width), F32),
            flops=4 * share * width * mine * nmp,
            bytes_accessed=11_000_000,
            grid=(1,),
            in_specs=[row_spec] * (2 * nmp) + [w_spec] * (2 * nmp),
            out_specs=pl.BlockSpec((2, share, width), lambda t: (0, 0, 0)),
        )(*[v[f"h{k}"][i] for i in range(4) for k in range(nmp)])

    def run_mid():
        mixes, ows = by_slot()
        shapes = (
            *[sds((e, share), F32 if k % 2 else BF16) for k in range(nmp)],
            sds((share, width), BF16),
            sds((share, width), F32),
            sds((share, width), BF16),
            sds((8, width), F32),
        )
        *gmts, bo, gm, low, mst = call(
            functools.partial(mid_kernel, nmp),
            shapes,
            flops=2 * share * width * e * nmp,
            bytes_accessed=12_000_000,
            in_specs=[vmem] * (6 + nmp),
            out_specs=(vmem,) * (4 + nmp),
        )(
            v["middle"], v.pop("acc_own"), v.pop("acc_got"), v["cot"], row1(down_bias),
            row1(norm2_gain), *ows,
        )
        v["block_out"], v["gm"], v["mst"] = bo, gm, mst
        for k in range(nmp):
            v[f"gmt{k}"] = gmts[k]
        return low

    def run_out_grad(low):
        mixes, ows = by_slot()
        args = [low, *mixes]
        specs = [whole(a) for a in args]
        for k in (1, 3):
            specs[1 + k] = pl.BlockSpec((mix_rows, width), lambda t: (0, 0))
        shapes = (sds((half, nmp * part, width), F32),) * 2
        v["o"] = call(
            functools.partial(out_grad_kernel, nmp),
            shapes,
            flops=2 * share * width * e * nmp,
            bytes_accessed=5_000_000,
            grid=(1,),
            in_specs=[smem] + specs,
            out_specs=tuple(whole(a) for a in shapes),
        )(idx_b, *args)

    def run_attn_bwd(k, got, idx, first):
        st = v.pop(f"st{k}")
        args = [
            idx, v["normed"], st["qpre"], st["kpre"], st["vt"], st["wt"], v.pop(f"gmt{k}"),
            v.pop(got), st["mixf"], st["l"], hv, kmask, qhot,
        ]
        cuts_now = (full,) if first else (share, *n_gn)
        if not first:
            args.append(v.pop("gn"))
        keep, send, *gn, hst, gb = call(
            functools.partial(attn_bwd_kernel, 0 if first else len(cuts_now)),
            (
                sds((half, 3 * part, width), F32),
                sds((half, 3 * part, width), F32),
                *[sds((n, width), F32) for n in cuts_now],
                sds((3, DH, 128), F32),
                sds((3 * e, 128), F32),
            ),
            flops=2 * (full * width * e * 6 + full * full * e * 20),
            bytes_accessed=14_000_000,
            in_specs=[smem] + [vmem] * (len(args) - 1),
            out_specs=(vmem,) * (4 + len(cuts_now)),
            scratch_shapes=scratch + [pltpu.VMEM((3 * e, full), BF16)],
        )(*args)
        v[f"q{k}"] = (keep, send)
        if first:
            v["gn"] = gn[0]
        else:
            v["gn_own"], v["gn_far"] = gn[0], tuple(gn[1:])
        v[f"hst{k}"] = hst
        v[f"qbg{k}"] = gb

    def g1(n):
        a, b = v[n + "a"], v[n + "b"]
        v[n + "a"] = (a, swap(a, px))
        v[n + "b"] = (b, swap(b, py))

    def g2(n):
        a, b = (jnp.stack(v[n + t]) for t in "ab")
        v[n + "a"] = (a, swap(a, py))
        v[n + "b"] = (b, swap(b, px))

    def g3(n):
        a, b = (jnp.concatenate(v[n + t], axis=0) for t in "ab")
        v[n + "a"] = (a, swap(a, core))
        v[n + "b"] = (b, swap(b, core))

    def r1(n):
        keep, send = v[n]
        v[n] = (keep, swap(send, core))

    def r2(n, kind):
        keep, got = v[n]
        keep_sum = keep[:2] + got[:2]
        v[n] = (keep_sum, swap(keep[2:] + got[2:], py if kind == "a" else px))

    def r3(n, kind):
        keep, got = v[n]
        v[n] = (keep[0] + got[0], swap(keep[1] + got[1], px if kind == "a" else py))

    def r4(n):
        keep, got = v[n]
        v[n] = keep + got

    def first_link(k):
        return py if MLP_KIND[k] == "a" else px

    def second_link(k):
        return px if MLP_KIND[k] == "a" else py

    def c1(k):
        k0, k1, s0, s1 = v[f"w{k}"]
        v[f"w{k}"] = (k0, k1, s0, swap(s1, first_link(k)))

    def c0(k):
        k0, k1, s0, g1 = v[f"w{k}"]
        v[f"w{k}"] = (k0, k1, g1, swap(s0, first_link(k)))

    def c2u(k):
        k0, k1, g1, g0 = v[f"w{k}"]
        q = v.pop(f"q{k + 1}u")
        sent = k1[:upart] + q[upart:] + g1[:upart]
        v[f"w{k}"] = (k0, k1, g1, g0, q, swap(sent, second_link(k)))

    def c2d(k):
        k0, k1, g1, g0, q, gu = v[f"w{k}"]
        up_sum = k0[:upart] + g0[:upart] + q[:upart] + gu
        sent = k1[upart:] + g1[upart:]
        v[f"w{k}"] = (up_sum, k0[upart:], g0[upart:], swap(sent, second_link(k)))

    def c3(k):
        up_sum, kd, g0, gd = v[f"w{k}"]
        v[f"w{k}"] = (up_sum, kd + g0 + gd + v.pop(f"d{k + 1}"))

    def e1(k):
        k0, k1, s = v[f"w{k}"]
        v[f"w{k}"] = (k0, k1, swap(s, first_link(k)))

    def e2(k):
        k0, k1, g = v[f"w{k}"]
        v[f"w{k}"] = (k0 + g[upart:], swap(k1 + g[:upart], second_link(k)))

    def e3(k):
        k0, g = v[f"w{k}"]
        v[f"w{k}"] = k0 + g

    inner = (mp_no == 1) | (mp_no == 2)

    def middle_swap(a):
        return lax.ppermute(a, "mp", [(1, 2), (2, 1)])

    def pass_out(a):
        return lax.ppermute(a, "mp", [(1, 0), (2, 3)])

    def high_bits(a):
        bit = PIECES
        while bit < ndp:
            a = a + swap(a, bit)
            bit *= 2
        return a

    cot_all, att_piece, ob_piece, mlp_piece = lax.optimization_barrier(
        (cotangent, att_piece, ob_piece, mlp_piece)
    )
    v["cot"] = lax.dynamic_slice_in_dim(cot_all, mp_no * share, share, 0)
    v["cot_f"] = v["cot"].astype(F32)
    v["piece"] = mlp_piece
    v["o3"] = zswap(ob_piece, 3)
    v["o1"] = zswap(ob_piece, 1)
    v["t2"] = zswap(att_piece, 2)
    v["normed"] = run_norm1()
    v.fence()
    hp = 2 * part
    t2, o1, o3 = v["t2"], v["o1"], v["o3"]
    v["ta"] = jnp.concatenate([t2[:hp], o1[:part]], axis=0)
    v["tb"] = jnp.concatenate([t2[hp : 2 * hp], o3[:part]], axis=0)
    g1("t")
    v["cot_p"] = swap(v.pop("cot_f"), core)
    v["m1"] = zswap(v["piece"], 1)
    v["mid_a"] = middle_swap(v.pop("piece"))
    v.fence()
    m1 = v["m1"]
    to_y = jnp.concatenate([*v["ta"], m1[upart:]], axis=0)
    to_x = jnp.concatenate([*v["tb"], m1[:upart]], axis=0)
    v["ta"] = (to_y, swap(to_y, py))
    v["tb"] = (to_x, swap(to_x, px))
    v["mid_b"] = middle_swap(v.pop("m1"))
    v["end_a"] = pass_out(v["mid_a"])
    run_attn_own()
    v.fence()
    nt = 2 * 3 * part
    ya, yb = v.pop("ta")
    xa, xb = v.pop("tb")
    v["m1a"], v["m1b"] = (xa[nt:], xb[nt:]), (ya[nt:], yb[nt:])
    v["ta"], v["tb"] = (
        tuple(
            a.reshape(half, 3 * part, width) for a in (both_, swap(both_, core))
        )
        for both_ in (
            jnp.concatenate([ya[:nt], yb[:nt]], axis=0),
            jnp.concatenate([xa[:nt], xb[:nt]], axis=0),
        )
    )
    run_attn_far()
    g2("m1")
    v["mix0"] = zswap(jnp.concatenate([v["st0"].pop("mixs"), v["mid_b"]], axis=0), 1)
    v.fence()
    v["mix2"] = zswap(v["st2"].pop("mixs"), 1)
    run_out()
    m3 = jnp.where(inner, v.pop("mid_a"), v["mix0"][mix_rows:])
    m2 = jnp.where(inner, v.pop("mid_b"), v.pop("end_a"))
    to_x = jnp.concatenate([m3[:upart], m2[:upart]], axis=0)
    to_y = jnp.concatenate([m3[upart:], m2[upart:]], axis=0)
    v["ma"], v["mb"] = (to_x, swap(to_x, px)), (to_y, swap(to_y, py))
    v.fence()
    for t in "ab":
        own, got = v.pop(f"m{t}")
        v[f"m3{t}"] = (own[:upart], got[:upart])
        v[f"m2{t}"] = (own[upart:], got[upart:])
    v["sec_p"] = swap(v.pop("sec_f"), core)
    run_mlp(1, v.pop("m1a"), v.pop("m1b"), v["o1"], part // 8)
    g2("m3")
    v.fence()
    v["p1"] = zswap(v["p1"], 1)
    run_mlp(3, v.pop("m3a"), v.pop("m3b"), v["o3"], part // 8)
    g2("m2")
    v.fence()
    v["p3"] = zswap(v["p3"], 1)
    run_mlp(0, (u0, u1), (d0, d1), bias0, 0)
    e1(1)
    e1(3)
    v.fence()
    run_mlp(2, v.pop("m2a"), v.pop("m2b"), v["t2"], 4 * part // 8)
    e2(1)
    e2(3)
    v["q1u"] = zswap(v["q1u"], 1)
    v.fence()
    e3(1)
    e3(3)
    v["d13"] = jnp.concatenate([v.pop("w1"), v.pop("w3")], axis=0)
    v["q3u"] = zswap(v["q3u"], 1)
    c1(0)
    c1(2)
    v["send"] = run_down(1)
    v.fence()
    c0(0)
    c0(2)
    v["d13"] = zswap(v["d13"], 1)
    v["acc_got"] = swap(v.pop("send"), core)
    v["acc_own"] = run_down(0)
    v.fence()
    d13 = v.pop("d13")
    v["d1"], v["d3"] = d13[:upart], d13[upart:]
    c2u(0)
    c2u(2)
    v["low"] = run_mid()
    v.fence()
    c2d(0)
    c2d(2)
    v["gp2"] = zswap(v.pop("gmt3"), 1)
    v["z2x"] = zswap(v["w2"][0][:n_z2], 2)
    run_out_grad(v.pop("low"))
    v.fence()
    c3(0)
    c3(2)
    up_sum, down_sum = v.pop("w2")
    v["z2y"] = zswap(jnp.concatenate([up_sum[n_z2:], down_sum], axis=0), 2)
    v["gp0"] = zswap(v.pop("gmt1"), 1)
    r1("o")
    r2("o", "b")
    run_attn_bwd(2, "gp2", idx_b, True)
    v.fence()
    r1("q2")
    v.fence()
    mlp_sum = high_bits(
        jnp.concatenate(v.pop("w0"), axis=0)
        + jnp.concatenate([v.pop("z2x"), v.pop("z2y")], axis=0)
    )
    ma, mb = mlp_sum[:upart], mlp_sum[upart:]
    keep, got = v["q2"]
    to_x = jnp.concatenate([(keep[2:] + got[2:]).reshape(-1, width), ma], axis=0)
    v["q2"] = keep[:2] + got[:2]
    keep, got = v["o"]
    to_y = jnp.concatenate([keep[1] + got[1], mb], axis=0)
    v["o"] = keep[0] + got[0]
    v["gx"], v["gy"] = (to_x, swap(to_x, px)), (to_y, swap(to_y, py))
    run_attn_bwd(0, "gp0", idx_b, False)
    v.fence()
    nq = 2 * 3 * part
    (xa, xb), (ya, yb) = v.pop("gx"), v.pop("gy")
    r1("q0")
    q2 = v["q2"] + xb[:nq].reshape(2, 3 * part, width)
    v["q2"] = q2[0]
    to_y = jnp.concatenate([xa[nq:], xb[nq:], q2[1]], axis=0)
    to_x = jnp.concatenate([ya[nmp * part :], yb[nmp * part :]], axis=0)
    v["gx"], v["gy"] = (to_x, swap(to_x, px)), (to_y, swap(to_y, py))
    o = v.pop("o") + yb[: nmp * part]
    v["gn0"] = zswap(v["gn_far"][0], 1)
    v["oz"] = zswap(jnp.concatenate([o[part : 2 * part], o[3 * part :]], axis=0), 1)
    v["o0"], v["o2"] = o[:part], o[2 * part : 3 * part]
    v["small"] = call(
        functools.partial(sums_kernel, nmp),
        sds((16, width), F32),
        flops=full * width * 10,
        bytes_accessed=full * width * 6,
        grid_spec=pltpu.PrefetchScalarGridSpec(
            num_scalar_prefetch=2,
            grid=(1,),
            in_specs=[
                pl.BlockSpec((share, width), lambda t, b, m: (b[0] // per, 0)),
                pl.BlockSpec((share, width), lambda t, b, m: (b[per] // per, 0)),
                pl.BlockSpec((share, width), lambda t, b, m: (0, 0)),
                pl.BlockSpec((8, width), lambda t, b, m: (0, 0)),
                *[pl.BlockSpec((3, DH, 128), lambda t, b, m: (0, 0, 0))] * 2,
                *[pl.BlockSpec((3 * e, 128), lambda t, b, m: (0, 0))] * 2,
                *[pl.BlockSpec((1, mine), lambda t, b, m: (0, 0))] * nmp,
                *[pl.BlockSpec((n, width), lambda t, b, m: (0, 0)) for n in n_gn],
            ],
            out_specs=pl.BlockSpec((16, width), lambda t, b, m: (0, 0)),
        ),
    )(
        blk, me1, tokens, tokens, v["gn_own"], v.pop("mst"), v.pop("hst0"), v.pop("hst2"),
        v.pop("qbg0"), v.pop("qbg2"), *[v.pop(f"ubg{k}") for k in range(nmp)], *v["gn_far"],
    )
    v["small"] = v["small"] + swap(v["small"], core)
    v.fence()
    r2("q0", "b")
    (xa, xb), (ya, yb) = v["gx"], v["gy"]
    oz = v.pop("oz")
    v["o0"] = v["o0"] + oz[:part]
    q2 = v.pop("q2") + yb[2 * upart :]
    v["y2"] = zswap(jnp.concatenate([q2, v.pop("o2") + oz[part:]], axis=0), 2)
    v["gn1"] = zswap(v["gn_far"][1], 1)
    v["gu"] = (ya, yb, swap(ya, core), swap(yb, core))
    v.pop("gy")
    v.fence()
    r3("q0", "b")
    v["gn2"] = zswap(v.pop("gn_far")[2], 1)
    small = v["small"] + swap(v["small"], px)
    v["small"] = small + swap(small, py)
    xa, xb = v.pop("gx")
    v["gd"] = (xa, xb, swap(xa, core), swap(xb, core))
    def unpack(kernel, arrays, idx, shape):
        pieces_spec = pl.BlockSpec((2 * upart, width), lambda t: (0, 0))
        return call(
            kernel,
            sds(shape, F32),
            bytes_accessed=2 * 4 * math.prod(shape),
            grid=(1,),
            in_specs=[smem] + [pieces_spec] * 4,
            out_specs=pl.BlockSpec(shape, lambda t: (0, 0)),
            scratch_shapes=[pltpu.VMEM((PIECES, upart, width), F32)],
        )(idx, *arrays)

    v["up_g"] = unpack(unpack_kernel, v.pop("gu"), idx_a, (width, units))
    v.fence()
    r4("q0")
    att_sum = high_bits(
        jnp.concatenate([v.pop("q0"), v.pop("o0")], axis=0) + v.pop("y2")
    )
    v["w"] = (att_sum, swap(att_sum, px), swap(att_sum, py), swap(att_sum, px | py))
    small = high_bits(v.pop("small"))
    got = zswap(jnp.concatenate([small[:8], small[12:]], axis=0), 1)
    v["small"] = small[:12] + got

    v["down_g"] = unpack(unpack_rows_kernel, v.pop("gd"), idx_b, (units, width))
    v["input_grad"] = call(
        final_kernel,
        sds((share, width), BF16),
        flops=share * width * 20,
        bytes_accessed=share * width * 16,
        grid_spec=pltpu.PrefetchScalarGridSpec(
            num_scalar_prefetch=1,
            grid=(1,),
            in_specs=[
                pl.BlockSpec((share, width), lambda t, b: (b[0] // per, 0)),
                pl.BlockSpec((share, width), const2),
                *[pl.BlockSpec((n, width), const2) for n in n_gn],
                pl.BlockSpec((share, width), const2),
                vec_spec,
            ],
            out_specs=pl.BlockSpec((share, width), const2),
        ),
    )(blk, tokens, v["gn_own"], *[v[f"gn{i}"] for i in range(3)], v["gm"], row1(norm1_gain))
    v.fence()
    w = jnp.concatenate(v.pop("w"), axis=0)
    small = v.pop("small")
    small_got = zswap(jnp.concatenate([small[:8], small[10:]], axis=0), 2)
    qkv_weight_grad, out_weight_grad = call(
        unpack_att_kernel,
        (sds((3, e, width), F32), sds((e, width), F32)),
        bytes_accessed=2 * 4 * 4 * width * e,
        in_specs=[smem] + [vmem] * 2,
        out_specs=(vmem, vmem),
        scratch_shapes=[pltpu.VMEM((PIECES, 4 * part, width), F32)],
    )(idx_a, w, swap(w, core))
    qkv_weight_grad = jnp.swapaxes(qkv_weight_grad, 1, 2)
    qkv_bias_grad, *rows_of = call(
        small_out_kernel,
        (sds((3, e), F32), *[sds((DH,), F32)] * 3, *[sds((width,), F32)] * 7),
        bytes_accessed=100_000,
        in_specs=[vmem, vmem],
        out_specs=(vmem,) * 11,
    )(small[:10], small_got)
    heads_of, rows_of = rows_of[:3], rows_of[3:]
    return (
        v["block_out"],
        v["input_grad"],
        qkv_weight_grad,
        qkv_bias_grad,
        out_weight_grad,
        rows_of[2],
        v["up_g"],
        rows_of[6],
        v["down_g"],
        rows_of[3],
        rows_of[4],
        rows_of[5],
        heads_of[0],
        heads_of[1],
        heads_of[2],
        rows_of[0],
        rows_of[1],
    )


def solution(mesh):
    in_specs = (
        P("dp", None),
        P("dp"),
        P(None, None, "mp"),
        P(None, "mp"),
        P("mp", None),
        P(),
        P(None, "mp"),
        P("mp"),
        P("mp", None),
        P(),
        P(),
        P(),
        P(),
        P(),
        P(),
        P(),
        P(),
        P("dp", None),
    )
    out_specs = (
        P(("dp", "mp"), None),
        P(("dp", "mp"), None),
        P(None, None, "mp"),
        P(None, "mp"),
        P("mp", None),
        P(),
        P(None, "mp"),
        P("mp"),
        P("mp", None),
        P(),
        P(),
        P(),
        P(),
        P(),
        P(),
        P(),
        P(),
    )
    return jax.shard_map(shards, mesh=mesh, in_specs=in_specs, out_specs=out_specs, check_vma=False)
```

```python
import functools
import math

import jax
import jax.numpy as jnp
from jax import lax
from jax.experimental import pallas as pl
from jax.experimental.pallas import tpu as pltpu
from jax.sharding import PartitionSpec as P

F32 = jnp.float32
BF16 = jnp.bfloat16
DH = 64
SEQ_LEN = 1024
NORM_EPS = 1e-06
PIECES = 8
SEG_COLS = 128
LOG2E = math.log2(math.e)
SCALE = DH ** (-0.5)
BITS_A = (2, 4, 1)
BITS_B = (4, 2, 1)
MLP_KIND = ("a", "a", "b", "b")
VMEM_LIMIT = 26 * 1024 * 1024
VMEM_LARGE = 56 * 1024 * 1024


def mm(a, b):
    return lax.dot_general(a, b, (((1,), (0,)), ((), ())), preferred_element_type=F32)


def mm_nt(a, b):
    return lax.dot_general(a, b, (((1,), (1,)), ((), ())), preferred_element_type=F32)


def mm_tn(a, b):
    return lax.dot_general(a, b, (((0,), (0,)), ((), ())), preferred_element_type=F32)


def call(kernel, out_shape, flops=0, bytes_accessed=0, vmem_limit=VMEM_LIMIT, **kw):
    return pl.pallas_call(
        kernel,
        out_shape=out_shape,
        compiler_params=pltpu.CompilerParams(vmem_limit_bytes=vmem_limit),
        cost_estimate=pl.CostEstimate(
            flops=flops, bytes_accessed=bytes_accessed, transcendentals=0
        ),
        **kw,
    )


def sds(shape, dtype):
    return jax.ShapeDtypeStruct(shape, dtype)


def row_norm(x):
    mean = jnp.mean(x, axis=-1, keepdims=True)
    cen = x - mean
    rstd = lax.rsqrt(jnp.mean(cen * cen, axis=-1, keepdims=True) + NORM_EPS)
    return cen * rstd, rstd


def row_norm_back(f, n, rstd):
    mean_f = jnp.mean(f, axis=-1, keepdims=True)
    mean_fn = jnp.mean(f * n, axis=-1, keepdims=True)
    return (f - mean_f - n * mean_fn) * rstd


def col_norm(x):
    mean = jnp.mean(x, axis=0, keepdims=True)
    cen = x - mean
    rstd = lax.rsqrt(jnp.mean(cen * cen, axis=0, keepdims=True) + NORM_EPS)
    return cen * rstd, rstd


def col_norm_back(f, n, rstd):
    mean_f = jnp.mean(f, axis=0, keepdims=True)
    mean_fn = jnp.mean(f * n, axis=0, keepdims=True)
    return (f - mean_f - n * mean_fn) * rstd


def lane_fold(x):
    out = x[:, :128]
    for t in range(1, x.shape[1] // 128):
        out = out + x[:, t * 128 : (t + 1) * 128]
    return out


def offset_of(s, bits):
    return sum(bit for t, bit in enumerate(bits) if (s >> t) & 1)


def norm1_kernel(blk_ref, x_ref, g_ref, s_ref, out_ref):
    n, _ = row_norm(x_ref[...].astype(F32))
    out_ref[...] = (n * g_ref[...] + s_ref[...]).astype(BF16)


def build_q_aug(q_pre, qg, qs, qaug_ref):
    n, rstd = col_norm(q_pre)
    q_low = (n * qg + qs).astype(BF16)
    scaled = q_low.astype(F32) * (SCALE * LOG2E)
    hi = scaled.astype(BF16)
    lo = (scaled - hi.astype(F32)).astype(BF16)
    qaug_ref[0:DH, :] = hi
    qaug_ref[DH : 2 * DH, :] = lo
    return n, rstd, q_low


def build_k_aug(k_pre, kg, kaug_ref):
    n, rstd = col_norm(k_pre)
    k_low = (n * kg).astype(BF16)
    kaug_ref[:, 0 : 2 * DH] = jnp.concatenate([k_low, k_low], axis=0).T
    return n, rstd, k_low


def bias_col(b_ref, n):
    return b_ref[...].T[0:n, 0:1]


def prep_kernel(
    me_ref, w_ref, o_ref, qb_ref, ub_ref, up_ref, dn_ref,
    att_ref, ob_ref, b_ref, p_ref, u0_ref, u1_ref, d0_ref, d1_ref,
    t_ref, wf_ref,
):
    part = 24
    e = PIECES * part
    me = me_ref[0]
    b_ref[...] = jnp.zeros(b_ref.shape, F32)
    for s in range(3):
        wf_ref[...] = w_ref[s].astype(F32)
        rows = wf_ref[pl.ds(pl.multiple_of(me * part, 8), part), :]
        att_ref[s * part : (s + 1) * part, :] = rows
        b_ref[0:1, s * e : (s + 1) * e] = qb_ref[s : s + 1, :]
    upart = up_ref.shape[1] // PIECES
    ub = ub_ref[...].reshape(1, PIECES * upart)
    for s in range(PIECES // 2):
        piece = jnp.zeros((1, upart), F32)
        for p in range(PIECES):
            here = (me ^ offset_of(s, BITS_A)) == p
            piece = piece + jnp.where(here, ub[:, p * upart : (p + 1) * upart], 0.0)
        b_ref[1:2, s * upart : (s + 1) * upart] = piece
    wf_ref[...] = o_ref[...].astype(F32)
    rows = wf_ref[pl.ds(pl.multiple_of(me * part, 8), part), :]
    att_ref[3 * part : 4 * part, :] = rows
    ob_ref[0:part, :] = rows
    att_ref[4 * part :, :] = b_ref[...]
    ob_ref[part:, :] = b_ref[...]

    t_ref[...] = up_ref[...].astype(F32).T

    def at_piece(r):
        return pl.ds(pl.multiple_of((me ^ r) * upart, 32), upart)

    p_ref[0:upart, :] = t_ref[at_piece(0), :]
    p_ref[upart:, :] = dn_ref[at_piece(0), :].astype(F32)
    for i, (u_ref, d_ref) in enumerate(((u0_ref, d0_ref), (u1_ref, d1_ref))):
        for j in range(2):
            u_ref[j] = t_ref[at_piece(offset_of(2 * i + j, BITS_A)), :].astype(BF16)
            d_ref[j] = dn_ref[at_piece(offset_of(2 * i + j, BITS_B)), :]


def attend(x_ref, wt_ref, b_ref, hv_ref, kmask_ref, qhot_ref, outs, qaug_ref, kaug_ref):
    qpre_ref, kpre_ref, vt_ref, mixt_ref, mixf_ref, mixs_ref, l_ref = outs
    e = qpre_ref.shape[0]
    full = x_ref.shape[0]
    share = full // 2
    heads = e // DH
    x = x_ref[...]
    bias = bias_col(b_ref, 3 * e)
    qpre_ref[...] = mm_nt(wt_ref[0:e, :], x) + bias[0:e]
    kpre_ref[...] = mm_nt(wt_ref[e : 2 * e, :], x) + bias[e : 2 * e]
    vt_ref[...] = (mm_nt(wt_ref[2 * e : 3 * e, :], x) + bias[2 * e :]).astype(BF16)
    qaug_ref[2 * DH :, :] = qhot_ref[...]
    kaug_ref[:, 2 * DH :] = kmask_ref[...]
    ones = jnp.ones((16, full), BF16)
    for h in range(heads):
        hs = slice(h * DH, (h + 1) * DH)
        build_q_aug(qpre_ref[hs, :], hv_ref[:, 0:1], hv_ref[:, 1:2], qaug_ref)
        build_k_aug(kpre_ref[hs, :], hv_ref[:, 2:3], kaug_ref)
        prob = jnp.exp2(mm(kaug_ref[...], qaug_ref[...])).astype(BF16)
        vaug = jnp.concatenate([vt_ref[hs, :], ones], axis=0)
        o = mm(vaug, prob)
        total = o[DH : DH + 1, :]
        l_ref[h : h + 1, :] = total
        mix = o[0:DH, :] / total
        mixf_ref[hs, :] = mix
        mixt_ref[hs, :] = mix[:, 0:share].astype(BF16)
        at = h * share
        for c in range(0, share, 256):
            block_no, lane = divmod(at + c, x.shape[1])
            mixs_ref[block_no * DH : (block_no + 1) * DH, lane : lane + 256] = mix[
                :, share + c : share + c + 256
            ]


def attn_fwd_own_kernel(x_ref, wt_ref, b_ref, hv_ref, kmask_ref, qhot_ref, *refs):
    attend(x_ref, wt_ref, b_ref, hv_ref, kmask_ref, qhot_ref, refs[:7], *refs[7:])


def attn_fwd_kernel(
    ia_ref, ib_ref, a0_ref, a1_ref, b0_ref, b1_ref, x_ref, b_ref, hv_ref, kmask_ref, qhot_ref,
    wt_ref, ow_ref, ow1_ref, ow3_ref, *refs,
):
    wa_ref, wb_ref = refs[-2:]
    part = 24
    e = PIECES * part
    half = PIECES // 2
    wa_ref[0:half] = a0_ref[...]
    wa_ref[half:] = a1_ref[...]
    wb_ref[0:half] = b0_ref[...]
    wb_ref[half:] = b1_ref[...]

    def rows(w_ref, i_ref, at):
        return jnp.concatenate(
            [w_ref[i_ref[p], at * part : (at + 1) * part, :] for p in range(PIECES)], axis=0
        ).astype(BF16)

    wt_ref[0:e, :] = rows(wa_ref, ia_ref, 0)
    wt_ref[e : 2 * e, :] = rows(wa_ref, ia_ref, 1)
    wt_ref[2 * e : 3 * e, :] = rows(wb_ref, ib_ref, 0)
    ow_ref[...] = rows(wb_ref, ib_ref, 1)
    ow1_ref[...] = rows(wa_ref, ia_ref, 2)
    ow3_ref[...] = rows(wb_ref, ib_ref, 2)
    attend(x_ref, wt_ref, b_ref, hv_ref, kmask_ref, qhot_ref, refs[:7], *refs[7:9])


def unmix(ref, heads, share):
    width = ref.shape[1]
    rows = []
    for h in range(heads):
        cols = []
        for c in range(0, share, 256):
            block_no, lane = divmod(h * share + c, width)
            cols.append(ref[block_no * DH : (block_no + 1) * DH, lane : lane + 256])
        rows.append(jnp.concatenate(cols, axis=1))
    return jnp.concatenate(rows, axis=0).astype(BF16)


def mix_of(ref, share):
    if ref.dtype == BF16:
        return ref[...]
    return unmix(ref, ref.shape[0] * ref.shape[1] // (DH * share), share)


def out_norm2_kernel(nslot, blk_ref, x_ref, *refs):
    mixes = refs[:nslot]
    ws = refs[nslot : 2 * nslot]
    ob_ref, g_ref, s_ref, mid_ref, sec_ref, secf_ref = refs[2 * nslot :]
    acc = x_ref[...].astype(F32) + ob_ref[...]
    for k in range(nslot):
        acc = acc + mm_tn(mix_of(mixes[k], x_ref.shape[0]), ws[k][...])
    mid_ref[...] = acc
    n, _ = row_norm(acc)
    sec = (n * g_ref[...] + s_ref[...]).astype(BF16)
    sec_ref[...] = sec
    secf_ref[...] = sec.astype(F32)


def mlp_kernel(
    kind, keeps, sec_ref, secp_ref, cot_ref, cotp_ref, u0_ref, u1_ref, d0_ref, d1_ref, b_ref, *refs
):
    if keeps:
        p_ref, hid_ref, gp_ref, ub_ref, db_ref, k0_ref, k1_ref, s0_ref, s1_ref, gb_ref = refs
    else:
        hid_ref, gp_ref, ub_ref, db_ref, up_ref, uq_ref, k0_ref, k1_ref, sd_ref, gb_ref = refs
    part = u0_ref.shape[1]
    share = sec_ref.shape[0]
    up = jnp.concatenate([u0_ref[0], u0_ref[1], u1_ref[0], u1_ref[1]], axis=0).astype(BF16)
    down = jnp.concatenate([d0_ref[0], d1_ref[0], d0_ref[1], d1_ref[1]], axis=0).astype(BF16)
    ub_ref[...] = up
    db_ref[...] = down
    bias = b_ref[1:2, 0 : up.shape[0]]
    for r, (s_ref, c_ref) in enumerate(((sec_ref, cot_ref), (secp_ref, cotp_ref))):
        rows = slice(r * share, (r + 1) * share)
        sec = s_ref[...].astype(BF16)
        cot = c_ref[...].astype(BF16)
        pre = mm_nt(sec, up) + bias
        cdf = 0.5 * (1.0 + lax.erf(pre * (1.0 / math.sqrt(2.0))))
        hid = (pre * cdf).astype(BF16)
        pdf = jnp.exp(-0.5 * pre * pre) * (1.0 / math.sqrt(2.0 * math.pi))
        gpre = (mm_nt(cot, down) * (cdf + pre * pdf)).astype(BF16)
        hid_ref[rows, :] = hid
        gp_ref[rows, :] = gpre
        gb_r = jnp.sum(gpre.astype(F32), axis=0, keepdims=True)
        gd_r = mm_tn(hid, cot)
        gu_r = mm_tn(gpre, sec)
        if r == 0:
            gb, gd, gu = gb_r, gd_r, gu_r
        else:
            gb, gd, gu = gb + gb_r, gd + gd_r, gu + gu_r
    gb_ref[...] = gb
    order = (0, 1, 2, 3) if kind == "a" else (0, 2, 1, 3)
    gu_at = [gu[i * part : (i + 1) * part] for i in order]
    gd_at = [gd[i * part : (i + 1) * part] for i in order]
    if keeps:
        gu_at[3] = gu_at[3] + p_ref[0:part, :]
        gu_at[2] = gu_at[2] + p_ref[part:, :]
        for i, ref in enumerate((k0_ref, k1_ref, s0_ref, s1_ref)):
            ref[0:part, :] = gu_at[i]
            ref[part:, :] = gd_at[i]
    else:
        up_ref[0:part, :] = gu_at[3]
        up_ref[part:, :] = gu_at[2]
        uq_ref[0:part, :] = gu_at[0]
        uq_ref[part:, :] = gu_at[1]
        k0_ref[...] = gd_at[0]
        k1_ref[...] = gd_at[1]
        sd_ref[0:part, :] = gd_at[3]
        sd_ref[part:, :] = gd_at[2]


def down_kernel(nslot, *refs):
    hids = refs[:nslot]
    gps = refs[nslot : 2 * nslot]
    ubs = refs[2 * nslot : 3 * nslot]
    dbs = refs[3 * nslot : 4 * nslot]
    outs = refs[4 * nslot :]
    cat = lambda refs, axis: jnp.concatenate([r[...] for r in refs], axis=axis)
    share = outs[0].shape[1]
    for i, (rows_of, w_of) in enumerate(((hids, dbs), (gps, ubs))):
        w = cat(w_of, 0)
        for r, out_ref in enumerate(outs):
            rows = slice(r * share, (r + 1) * share)
            out_ref[i] = mm(jnp.concatenate([a[rows, :] for a in rows_of], axis=1), w)


def mid_kernel(nslot, mid_ref, own_ref, got_ref, cot_ref, db_ref, g_ref, *refs):
    ows = refs[:nslot]
    gmts = refs[nslot : 2 * nslot]
    bo_ref, gm_ref, low_ref, st_ref = refs[2 * nslot :]
    mid = mid_ref[...]
    n, rstd = row_norm(mid)
    e = own_ref[1] + got_ref[1]
    cot = cot_ref[...].astype(F32)
    gm = cot + row_norm_back(e * g_ref[...], n, rstd)
    gm_ref[...] = gm
    gm_low = gm.astype(BF16)
    low_ref[...] = gm_low
    for k in range(nslot):
        gmts[k][...] = mm_nt(ows[k][...], gm_low).astype(gmts[k].dtype)
    bo_ref[...] = (mid + (own_ref[0] + got_ref[0]) + db_ref[...]).astype(BF16)
    st_ref[0:1, :] = jnp.sum(e * n, axis=0, keepdims=True)
    st_ref[1:2, :] = jnp.sum(e, axis=0, keepdims=True)
    st_ref[2:3, :] = jnp.sum(gm_low.astype(F32), axis=0, keepdims=True)
    st_ref[3:4, :] = jnp.sum(cot, axis=0, keepdims=True)
    st_ref[4:8, :] = jnp.zeros((4, mid.shape[1]), F32)


def out_grad_kernel(nslot, idx_ref, low_ref, *refs):
    mixts = refs[:nslot]
    gow_keep, gow_send = refs[nslot:]
    part = 24
    gm_low = low_ref[...]
    for k in range(nslot):
        g = mm(mix_of(mixts[k], gm_low.shape[0]), gm_low)
        for p in range(PIECES):
            at = idx_ref[p]
            rows = slice(k * part, (k + 1) * part)

            @pl.when(at < PIECES // 2)
            def _():
                gow_keep[at, rows, :] = g[p * part : (p + 1) * part, :]

            @pl.when(at >= PIECES // 2)
            def _():
                gow_send[at - PIECES // 2, rows, :] = g[p * part : (p + 1) * part, :]


def attn_bwd_kernel(
    ncuts, idx_ref, x_ref, qpre_ref, kpre_ref, vt_ref, wt_ref, gmt_ref, gmtp_ref, mixf_ref, l_ref,
    hv_ref, kmask_ref, qhot_ref, *refs
):
    if ncuts:
        gn_in, gk_ref, gs_ref, *gn_refs = refs[: 3 + ncuts]
    else:
        gk_ref, gs_ref, gn_ref = refs[:3]
    st_ref, gb_ref, qaug_ref, kaug_ref, gpt_ref = refs[-5:]
    part = 24
    e = PIECES * part
    full = x_ref.shape[0]
    heads = e // DH
    qaug_ref[2 * DH :, :] = qhot_ref[...]
    kaug_ref[:, 2 * DH :] = kmask_ref[...]
    qg, qs, kg = hv_ref[:, 0:1], hv_ref[:, 1:2], hv_ref[:, 2:3]
    qg_sum = jnp.zeros((DH, 128), F32)
    qs_sum = jnp.zeros((DH, 128), F32)
    kg_sum = jnp.zeros((DH, 128), F32)
    row_no = lax.broadcasted_iota(jnp.int32, (DH, full), 0)
    one_rows = (row_no < 3).astype(F32).astype(BF16)
    for h in range(heads):
        hs = slice(h * DH, (h + 1) * DH)
        qn, qr, q_low = build_q_aug(qpre_ref[hs, :], qg, qs, qaug_ref)
        kn, kr, k_low = build_k_aug(kpre_ref[hs, :], kg, kaug_ref)
        inv = 1.0 / l_ref[h : h + 1, :]
        gm = jnp.concatenate(
            [gmt_ref[hs, :].astype(F32), gmtp_ref[hs, :].astype(BF16).astype(F32)], axis=1
        )
        go_low = (gm * inv).astype(BF16)
        delta = -jnp.sum(go_low.astype(F32) * mixf_ref[hs, :], axis=0, keepdims=True)
        d0 = delta.astype(BF16).astype(F32)
        d1 = (delta - d0).astype(BF16).astype(F32)
        d2 = delta - d0 - d1
        extra = jnp.where(
            row_no == 0, d0, jnp.where(row_no == 1, d1, jnp.where(row_no == 2, d2, 0.0))
        ).astype(BF16)
        goaug = jnp.concatenate([go_low, extra], axis=0)
        vaug = jnp.concatenate([vt_ref[hs, :], one_rows], axis=0).T
        prob = jnp.exp2(mm(kaug_ref[...], qaug_ref[...]))
        ds = (prob * mm(vaug, goaug)).astype(BF16)
        gv = mm_nt(go_low, prob.astype(BF16))
        gk = mm_nt(q_low, ds) * SCALE
        gq = mm(k_low, ds) * SCALE
        qg_sum += lane_fold(gq * qn)
        qs_sum += lane_fold(gq)
        kg_sum += lane_fold(gk * kn)
        gpt_ref[h * DH : (h + 1) * DH, :] = col_norm_back(gq * qg, qn, qr).astype(BF16)
        gpt_ref[e + h * DH : e + (h + 1) * DH, :] = col_norm_back(gk * kg, kn, kr).astype(BF16)
        gpt_ref[2 * e + h * DH : 2 * e + (h + 1) * DH, :] = gv.astype(BF16)
    st_ref[0] = qg_sum
    st_ref[1] = qs_sum
    st_ref[2] = kg_sum
    gp = gpt_ref[...]
    gb_ref[...] = lane_fold(gp.astype(F32))
    gw = mm(gp, x_ref[...])

    def put(ref, at, p):
        for s in range(3):
            ref[at, s * part : (s + 1) * part, :] = gw[s * e + p * part : s * e + (p + 1) * part, :]

    for p in range(PIECES):
        at = idx_ref[p]

        @pl.when(at < PIECES // 2)
        def _():
            put(gk_ref, at, p)

        @pl.when(at >= PIECES // 2)
        def _():
            put(gs_ref, at - PIECES // 2, p)

    gn = mm_tn(gp, wt_ref[...])
    if not ncuts:
        gn_ref[...] = gn
    else:
        at = 0
        for ref in gn_refs:
            rows = slice(at, at + ref.shape[0])
            ref[...] = gn_in[rows, :] + gn[rows]
            at += ref.shape[0]


def sums_kernel(
    nslot, blk_ref, me_ref, x_ref, xf_ref, gn_ref, mst_ref, h0_ref, h2_ref, b0_ref, b2_ref, *refs
):
    ubs = refs[:nslot]
    fars = refs[nslot:-1]
    out_ref = refs[-1]

    def fill():
        out_ref[...] = jnp.zeros_like(out_ref)
        out_ref[0:4, :] = mst_ref[0:4, :]
        heads = jnp.concatenate([h0_ref[i] + h2_ref[i] for i in range(3)], axis=0).T
        out_ref[6:7, 0 : heads.shape[1]] = jnp.sum(heads, axis=0, keepdims=True)
        me = me_ref[0]
        upart = out_ref.shape[1] // PIECES
        for row, k in zip((8, 10, 12, 14), (0, 2, 1, 3)):
            if k % 2 == 0:
                cols = (b0_ref if k == 0 else b2_ref)[...].T
                out_ref[row : row + 1, 0 : cols.shape[1]] = jnp.sum(cols, axis=0, keepdims=True)
            mine = ubs[k][...]
            for p in range(PIECES):
                piece = jnp.zeros((1, upart), F32)
                for t in range(PIECES // 2):
                    here = (me ^ offset_of(t, BITS_A)) == p
                    piece = piece + jnp.where(here, mine[:, t * upart : (t + 1) * upart], 0.0)
                out_ref[row + 1 : row + 2, p * upart : (p + 1) * upart] = piece

    fill()

    def add(x, e):
        n, _ = row_norm(x.astype(F32))
        out_ref[4:5, :] += jnp.sum(e * n, axis=0, keepdims=True)
        out_ref[5:6, :] += jnp.sum(e, axis=0, keepdims=True)

    add(x_ref[...], gn_ref[...])
    at = 0
    for ref in fars:
        add(xf_ref[at : at + ref.shape[0], :], ref[...])
        at += ref.shape[0]


def small_out_kernel(a_ref, b_ref, qb_ref, h0_ref, h1_ref, h2_ref, *rows):
    total = a_ref[...] + b_ref[...]
    for row, ref in zip((0, 1, 2, 3, 4, 5, 9), rows):
        ref[...] = total[row]
    for i, ref in enumerate((h0_ref, h1_ref, h2_ref)):
        ref[...] = total[6, i * DH : (i + 1) * DH]
        n = qb_ref.shape[1]
        qb_ref[i : i + 1, :] = total[8:9, i * n : (i + 1) * n]


def final_kernel(blk_ref, x_ref, gn_ref, *refs):
    gots = refs[:-3]
    gm_ref, g_ref, out_ref = refs[-3:]
    at = 0
    for ref in gots:
        rows = slice(at, at + ref.shape[0])
        n, rstd = row_norm(x_ref[rows, :].astype(F32))
        f = (gn_ref[rows, :] + ref[...]) * g_ref[...]
        out_ref[rows, :] = (gm_ref[rows, :] + row_norm_back(f, n, rstd)).astype(BF16)
        at += ref.shape[0]


def unpack_mlp_kernel(ia_ref, ib_ref, a_ref, b_ref, up_ref, down_ref, s_ref):
    part = s_ref.shape[2]
    half = PIECES // 2
    for w in range(2):
        for j in range(half):
            rows = slice((w * half + j) * part, (w * half + j + 1) * part)
            s_ref[w, j] = a_ref[rows, :]
            s_ref[w, half + j] = b_ref[rows, :]
    up_ref[...] = jnp.concatenate([s_ref[0, ia_ref[p]] for p in range(PIECES)], axis=0).T
    for p in range(PIECES):
        down_ref[p * part : (p + 1) * part, :] = s_ref[1, ib_ref[p]]


def unpack_att_kernel(i_ref, a_ref, b_ref, qkv_ref, out_ref, s_ref):
    rows = s_ref.shape[1]
    part = rows // 4
    half = PIECES // 2
    for j in range(half):
        s_ref[j] = a_ref[j * rows : (j + 1) * rows, :]
        s_ref[half + j] = b_ref[j * rows : (j + 1) * rows, :]
    for s, ref in enumerate((qkv_ref.at[0], qkv_ref.at[1], qkv_ref.at[2], out_ref)):
        for p in range(PIECES):
            ref[p * part : (p + 1) * part, :] = s_ref[i_ref[p], s * part : (s + 1) * part, :]


def swap_mp(a, k, size):
    return lax.ppermute(a, "mp", [(s, s ^ k) for s in range(size)])


def swap_plane(a, bit, size):
    return lax.ppermute(a, "dp", [(d, d ^ bit) for d in range(size)])


def storage_of(r, bits):
    return sum(jnp.where((r & bit) != 0, 1 << t, 0) for t, bit in enumerate(bits))


class Stages:
    def __init__(self):
        self.live = {}

    def __setitem__(self, name, value):
        self.live[name] = value

    def __getitem__(self, name):
        return self.live[name]

    def pop(self, name):
        return self.live.pop(name)

    def fence(self, *still_flying):
        now = {n: a for n, a in self.live.items() if n not in still_flying}
        leaves, tree = jax.tree.flatten(now)
        self.live.update(jax.tree.unflatten(tree, lax.optimization_barrier(leaves)))


def shards(
    tokens,
    seg_ids,
    qkv_weight,
    qkv_bias,
    out_weight,
    out_bias,
    up_weight,
    up_bias,
    down_weight,
    down_bias,
    norm1_gain,
    norm1_shift,
    query_gain,
    query_shift,
    key_gain,
    norm2_gain,
    norm2_shift,
    cotangent,
):
    ndp = lax.axis_size("dp")
    nmp = lax.axis_size("mp")
    dp_no = lax.axis_index("dp")
    mp_no = lax.axis_index("mp")
    me = dp_no % PIECES
    row_count, width = tokens.shape
    share = row_count // nmp
    full = SEQ_LEN
    assert full == 2 * share and nmp == 4 and ndp % PIECES == 0
    e = qkv_weight.shape[2]
    part = e // PIECES
    units = up_weight.shape[1]
    upart = units // PIECES
    half = PIECES // 2
    mine = half * upart
    core, px, py = 1, 2, 4

    vmem = pl.BlockSpec(memory_space=pltpu.VMEM)
    smem = pl.BlockSpec(memory_space=pltpu.SMEM)
    row1 = lambda v: v.reshape(1, -1)
    col = lambda v: v.reshape(-1, 1)
    swap = lambda a, bit: swap_plane(a, bit, ndp)
    zswap = lambda a, k: swap_mp(a, k, nmp)
    v = Stages()

    me1 = me.astype(jnp.int32).reshape(1)
    qkv_t = jnp.swapaxes(qkv_weight, 1, 2)
    wt0 = qkv_t.reshape(3 * e, width)
    att_piece, ob_piece, bias0, mlp_piece, u0, u1, d0, d1 = call(
        prep_kernel,
        (
            sds((4 * part + 8, width), F32),
            sds((part + 8, width), F32),
            sds((8, width), F32),
            sds((2 * upart, width), F32),
            *[sds((2, upart, width), BF16)] * 4,
        ),
        bytes_accessed=9_000_000,
        vmem_limit=VMEM_LARGE,
        in_specs=[smem] + [vmem] * 6,
        out_specs=(vmem,) * 8,
        scratch_shapes=[pltpu.VMEM((units, width), F32), pltpu.VMEM((e, width), F32)],
    )(
        me1, qkv_t, out_weight, qkv_bias, up_bias, up_weight, down_weight
    )

    n_gn = (224, 208, 80)
    n_q0 = 40
    numbers = jnp.arange(PIECES, dtype=jnp.int32)
    idx_a = storage_of(numbers ^ me, BITS_A).astype(jnp.int32)
    idx_b = storage_of(numbers ^ me, BITS_B).astype(jnp.int32)

    block = 256
    per = share // block
    steps = 2 * per
    tile_no = jnp.arange(steps, dtype=jnp.int32)
    blk = jnp.where(tile_no < per, mp_no * per + tile_no, (mp_no ^ 1) * per + tile_no - per).astype(
        jnp.int32
    )
    const2 = lambda t, b: (0, 0)
    tok_spec = pl.BlockSpec((block, width), lambda t, b: (b[t], 0))
    run_spec = pl.BlockSpec((block, width), lambda t, b: (t, 0))
    vec_spec = pl.BlockSpec((1, width), const2)

    def run_norm1():
        return call(
            norm1_kernel,
            sds((full, width), BF16),
            flops=full * width * 10,
            bytes_accessed=full * width * 4,
            grid_spec=pltpu.PrefetchScalarGridSpec(
                num_scalar_prefetch=1,
                grid=(steps,),
                in_specs=[tok_spec, vec_spec, vec_spec],
                out_specs=run_spec,
            ),
        )(blk, tokens, row1(norm1_gain), row1(norm1_shift))

    seg_own = lax.dynamic_slice_in_dim(seg_ids, mp_no * share, share, 0)
    seg_other = lax.dynamic_slice_in_dim(seg_ids, (mp_no ^ 1) * share, share, 0)
    seg_keys = jnp.concatenate([seg_own, seg_other])
    qhot = (
        lax.broadcasted_iota(jnp.int32, (SEG_COLS, full), 0) == seg_keys[None, :]
    ).astype(BF16)
    kmask = jnp.where(
        lax.broadcasted_iota(jnp.int32, (full, SEG_COLS), 1) == seg_keys[:, None], 0.0, -1e30
    ).astype(BF16)
    hv = jnp.stack([query_gain, query_shift, key_gain], axis=1)
    scratch = [
        pltpu.VMEM((2 * DH + SEG_COLS, full), BF16),
        pltpu.VMEM((full, 2 * DH + SEG_COLS), BF16),
    ]

    def whole(a):
        return pl.BlockSpec(a.shape, lambda t: (0,) * len(a.shape))

    def bias_at(block_no):
        return pl.BlockSpec((8, width), lambda t: (block_no, 0))

    att_names = ["qpre", "kpre", "vt", "mixt", "mixf", "mixs", "l"]
    att_shapes = [
        sds((e, full), F32),
        sds((e, full), F32),
        sds((e, full), BF16),
        sds((e, share), BF16),
        sds((e, full), F32),
        sds((e * share // width, width), F32),
        sds((8, full), F32),
    ]
    mix_rows = e * share // width

    def run_attn_own():
        outs = call(
            attn_fwd_own_kernel,
            tuple(att_shapes),
            flops=2 * (full * width * e * 3 + full * full * e * 8),
            bytes_accessed=10_000_000,
            in_specs=[vmem] * 6,
            out_specs=(vmem,) * 7,
            scratch_shapes=scratch,
        )(v["normed"], wt0, bias0, hv, kmask, qhot)
        v["st0"] = dict(zip(att_names, outs))
        v["st0"]["wt"] = wt0
        v["st0"]["ow"] = out_weight

    def run_attn_far():
        shapes = [sds((3 * e, width), BF16)] + [sds((e, width), BF16)] * 3 + att_shapes
        args = [
            *v.pop("ta"), *v.pop("tb"), v["normed"], v["t2"], hv, kmask, qhot,
        ]
        specs = [whole(a) for a in args]
        specs[5] = bias_at(4 * part // 8)
        outs = call(
            attn_fwd_kernel,
            tuple(shapes),
            flops=2 * (full * width * e * 3 + full * full * e * 8),
            bytes_accessed=10_000_000,
            grid=(1,),
            in_specs=[smem, smem] + specs,
            out_specs=tuple(whole(a) for a in shapes),
            scratch_shapes=scratch
            + [pltpu.VMEM((PIECES, 3 * part, width), F32)] * 2,
        )(idx_a, idx_b, *args)
        v["st2"] = dict(zip(["wt", "ow", "ow1", "ow3"] + att_names, outs))

    def by_slot():
        st0, st2 = v["st0"], v["st2"]
        mixes = [st0["mixt"], v["mix0"], st2["mixt"], v["mix2"]]
        ows = [st0["ow"], st2["ow1"], st2["ow"], st2["ow3"]]
        return mixes, ows

    def run_out():
        own_spec = pl.BlockSpec((share, width), lambda t, b: (b[0] // per, 0))
        whole2 = lambda shape: pl.BlockSpec(shape, lambda t, b: (0,) * len(shape))
        mixes, ows = by_slot()
        v["middle"], v["second"], v["sec_f"] = call(
            functools.partial(out_norm2_kernel, nmp),
            (sds((share, width), F32), sds((share, width), BF16), sds((share, width), F32)),
            flops=2 * share * width * e * nmp,
            bytes_accessed=8_000_000,
            grid_spec=pltpu.PrefetchScalarGridSpec(
                num_scalar_prefetch=1,
                grid=(1,),
                in_specs=[own_spec]
                + [whole2((e, share)), whole2((mix_rows, width))] * 2
                + [whole2((e, width))] * nmp
                + [whole2((1, width))] * 3,
                out_specs=(whole2((share, width)),) * 3,
            ),
        )(blk, tokens, *mixes, *ows, row1(out_bias), row1(norm2_gain), row1(norm2_shift))

    def run_mlp(k, up, down, bias, block_no):
        keeps = k % 2 == 0
        args = [
            v["second"], v["sec_p"], v["cot"], v["cot_p"], up[0], up[1], down[0], down[1], bias,
        ]
        if keeps:
            args.append(v.pop(f"p{k + 1}"))
        specs = [whole(a) for a in args]
        specs[8] = bias_at(block_no)
        piece = lambda n: sds((n * upart, width), F32)
        shapes = (
            *[sds((full, mine), BF16)] * 2,
            *[sds((mine, width), BF16)] * 2,
            *([piece(2)] * 4 if keeps else [piece(2), piece(2), piece(1), piece(1), piece(2)]),
            sds((1, mine), F32),
        )
        res = call(
            functools.partial(mlp_kernel, MLP_KIND[k], keeps),
            shapes,
            flops=2 * full * width * mine * 4,
            bytes_accessed=12_000_000,
            grid=(1,),
            in_specs=specs,
            out_specs=tuple(whole(a) for a in shapes),
        )(*args)
        v[f"h{k}"] = res[:4]
        v[f"ubg{k}"] = res[-1]
        if keeps:
            v[f"w{k}"] = res[4:8]
        else:
            v[f"p{k}"], v[f"q{k}u"] = res[4], res[5]
            v[f"w{k}"] = res[6:9]

    def run_down():
        return call(
            functools.partial(down_kernel, nmp),
            (sds((2, share, width), F32),) * 2,
            flops=4 * full * width * mine * nmp,
            bytes_accessed=17_000_000,
            vmem_limit=40 * 1024 * 1024,
            in_specs=[vmem] * (4 * nmp),
            out_specs=(vmem,) * 2,
        )(*[v[f"h{k}"][i] for i in range(4) for k in range(nmp)])

    def run_mid():
        mixes, ows = by_slot()
        shapes = (
            *[sds((e, share), F32 if k % 2 else BF16) for k in range(nmp)],
            sds((share, width), BF16),
            sds((share, width), F32),
            sds((share, width), BF16),
            sds((8, width), F32),
        )
        *gmts, bo, gm, low, mst = call(
            functools.partial(mid_kernel, nmp),
            shapes,
            flops=2 * share * width * e * nmp,
            bytes_accessed=12_000_000,
            in_specs=[vmem] * (6 + nmp),
            out_specs=(vmem,) * (4 + nmp),
        )(
            v["middle"], v.pop("acc_own"), v.pop("acc_got"), v["cot"], row1(down_bias),
            row1(norm2_gain), *ows,
        )
        v["block_out"], v["gm"], v["mst"] = bo, gm, mst
        for k in range(nmp):
            v[f"gmt{k}"] = gmts[k]
        return low

    def run_out_grad(low):
        mixes, ows = by_slot()
        args = [low, *mixes]
        specs = [whole(a) for a in args]
        for k in (1, 3):
            specs[1 + k] = pl.BlockSpec((mix_rows, width), lambda t: (0, 0))
        shapes = (sds((half, nmp * part, width), F32),) * 2
        v["o"] = call(
            functools.partial(out_grad_kernel, nmp),
            shapes,
            flops=2 * share * width * e * nmp,
            bytes_accessed=5_000_000,
            grid=(1,),
            in_specs=[smem] + specs,
            out_specs=tuple(whole(a) for a in shapes),
        )(idx_a, *args)

    def run_attn_bwd(k, got, idx, first):
        st = v.pop(f"st{k}")
        args = [
            idx, v["normed"], st["qpre"], st["kpre"], st["vt"], st["wt"], v.pop(f"gmt{k}"),
            v.pop(got), st["mixf"], st["l"], hv, kmask, qhot,
        ]
        cuts_now = (full,) if first else (share, *n_gn)
        if not first:
            args.append(v.pop("gn"))
        keep, send, *gn, hst, gb = call(
            functools.partial(attn_bwd_kernel, 0 if first else len(cuts_now)),
            (
                sds((half, 3 * part, width), F32),
                sds((half, 3 * part, width), F32),
                *[sds((n, width), F32) for n in cuts_now],
                sds((3, DH, 128), F32),
                sds((3 * e, 128), F32),
            ),
            flops=2 * (full * width * e * 6 + full * full * e * 20),
            bytes_accessed=14_000_000,
            in_specs=[smem] + [vmem] * (len(args) - 1),
            out_specs=(vmem,) * (4 + len(cuts_now)),
            scratch_shapes=scratch + [pltpu.VMEM((3 * e, full), BF16)],
        )(*args)
        v[f"q{k}"] = (keep, send)
        if first:
            v["gn"] = gn[0]
        else:
            v["gn_own"], v["gn_far"] = gn[0], tuple(gn[1:])
        v[f"hst{k}"] = hst
        v[f"qbg{k}"] = gb

    def g1(n):
        a, b = v[n + "a"], v[n + "b"]
        v[n + "a"] = (a, swap(a, px))
        v[n + "b"] = (b, swap(b, py))

    def g2(n):
        a, b = (jnp.stack(v[n + t]) for t in "ab")
        v[n + "a"] = (a, swap(a, py))
        v[n + "b"] = (b, swap(b, px))

    def g3(n):
        a, b = (jnp.concatenate(v[n + t], axis=0) for t in "ab")
        v[n + "a"] = (a, swap(a, core))
        v[n + "b"] = (b, swap(b, core))

    def r1(n):
        keep, send = v[n]
        v[n] = (keep, swap(send, core))

    def r2(n, kind):
        keep, got = v[n]
        keep_sum = keep[:2] + got[:2]
        v[n] = (keep_sum, swap(keep[2:] + got[2:], py if kind == "a" else px))

    def r3(n, kind):
        keep, got = v[n]
        v[n] = (keep[0] + got[0], swap(keep[1] + got[1], px if kind == "a" else py))

    def r4(n):
        keep, got = v[n]
        v[n] = keep + got

    def first_link(k):
        return py if MLP_KIND[k] == "a" else px

    def second_link(k):
        return px if MLP_KIND[k] == "a" else py

    def c1(k):
        k0, k1, s0, s1 = v[f"w{k}"]
        v[f"w{k}"] = (k0, k1, s0, swap(s1, first_link(k)))

    def c0(k):
        k0, k1, s0, g1 = v[f"w{k}"]
        v[f"w{k}"] = (k0, k1, g1, swap(s0, first_link(k)))

    def c2u(k):
        k0, k1, g1, g0 = v[f"w{k}"]
        q = v.pop(f"q{k + 1}u")
        sent = k1[:upart] + q[upart:] + g1[:upart]
        v[f"w{k}"] = (k0, k1, g1, g0, q, swap(sent, second_link(k)))

    def c2d(k):
        k0, k1, g1, g0, q, gu = v[f"w{k}"]
        up_sum = k0[:upart] + g0[:upart] + q[:upart] + gu
        sent = k1[upart:] + g1[upart:]
        v[f"w{k}"] = (up_sum, k0[upart:], g0[upart:], swap(sent, second_link(k)))

    def c3(k):
        up_sum, kd, g0, gd = v[f"w{k}"]
        v[f"w{k}"] = (up_sum, kd + g0 + gd + v.pop(f"d{k + 1}"))

    def e1(k):
        k0, k1, s = v[f"w{k}"]
        v[f"w{k}"] = (k0, k1, swap(s, first_link(k)))

    def e2(k):
        k0, k1, g = v[f"w{k}"]
        v[f"w{k}"] = (k0 + g[upart:], swap(k1 + g[:upart], second_link(k)))

    def e3(k):
        k0, g = v[f"w{k}"]
        v[f"w{k}"] = k0 + g

    inner = (mp_no == 1) | (mp_no == 2)

    def middle_swap(a):
        return lax.ppermute(a, "mp", [(1, 2), (2, 1)])

    def pass_out(a):
        return lax.ppermute(a, "mp", [(1, 0), (2, 3)])

    def high_bits(a):
        bit = PIECES
        while bit < ndp:
            a = a + swap(a, bit)
            bit *= 2
        return a

    cot_all, att_piece, ob_piece, mlp_piece = lax.optimization_barrier(
        (cotangent, att_piece, ob_piece, mlp_piece)
    )
    v["cot"] = lax.dynamic_slice_in_dim(cot_all, mp_no * share, share, 0)
    v["cot_f"] = v["cot"].astype(F32)
    v["piece"] = mlp_piece
    v["o3"] = zswap(ob_piece, 3)
    v["o1"] = zswap(ob_piece, 1)
    v["t2"] = zswap(att_piece, 2)
    v["normed"] = run_norm1()
    v.fence()
    hp = 2 * part
    t2, o1, o3 = v["t2"], v["o1"], v["o3"]
    v["ta"] = jnp.concatenate([t2[:hp], o1[:part]], axis=0)
    v["tb"] = jnp.concatenate([t2[hp : 2 * hp], o3[:part]], axis=0)
    g1("t")
    v["cot_p"] = swap(v.pop("cot_f"), core)
    v["m1"] = zswap(v["piece"], 1)
    v["mid_a"] = middle_swap(v.pop("piece"))
    v.fence()
    m1 = v["m1"]
    to_y = jnp.concatenate([*v["ta"], m1[upart:]], axis=0)
    to_x = jnp.concatenate([*v["tb"], m1[:upart]], axis=0)
    v["ta"] = (to_y, swap(to_y, py))
    v["tb"] = (to_x, swap(to_x, px))
    v["mid_b"] = middle_swap(v.pop("m1"))
    v["end_a"] = pass_out(v["mid_a"])
    run_attn_own()
    v.fence()
    nt = 2 * 3 * part
    ya, yb = v.pop("ta")
    xa, xb = v.pop("tb")
    v["m1a"], v["m1b"] = (xa[nt:], xb[nt:]), (ya[nt:], yb[nt:])
    v["ta"], v["tb"] = (
        tuple(
            a.reshape(half, 3 * part, width) for a in (both_, swap(both_, core))
        )
        for both_ in (
            jnp.concatenate([ya[:nt], yb[:nt]], axis=0),
            jnp.concatenate([xa[:nt], xb[:nt]], axis=0),
        )
    )
    run_attn_far()
    g2("m1")
    v["mix0"] = zswap(jnp.concatenate([v["st0"].pop("mixs"), v["mid_b"]], axis=0), 1)
    v.fence()
    v["mix2"] = zswap(v["st2"].pop("mixs"), 1)
    run_out()
    m3 = jnp.where(inner, v.pop("mid_a"), v["mix0"][mix_rows:])
    m2 = jnp.where(inner, v.pop("mid_b"), v.pop("end_a"))
    to_x = jnp.concatenate([m3[:upart], m2[:upart]], axis=0)
    to_y = jnp.concatenate([m3[upart:], m2[upart:]], axis=0)
    v["ma"], v["mb"] = (to_x, swap(to_x, px)), (to_y, swap(to_y, py))
    v.fence()
    for t in "ab":
        own, got = v.pop(f"m{t}")
        v[f"m3{t}"] = (own[:upart], got[:upart])
        v[f"m2{t}"] = (own[upart:], got[upart:])
    v["sec_p"] = swap(v.pop("sec_f"), core)
    run_mlp(1, v.pop("m1a"), v.pop("m1b"), v["o1"], part // 8)
    g2("m3")
    v.fence()
    v["p1"] = zswap(v["p1"], 1)
    run_mlp(3, v.pop("m3a"), v.pop("m3b"), v["o3"], part // 8)
    g2("m2")
    v.fence()
    v["p3"] = zswap(v["p3"], 1)
    run_mlp(0, (u0, u1), (d0, d1), bias0, 0)
    e1(1)
    e1(3)
    v.fence()
    run_mlp(2, v.pop("m2a"), v.pop("m2b"), v["t2"], 4 * part // 8)
    e2(1)
    e2(3)
    v["q1u"] = zswap(v["q1u"], 1)
    v.fence()
    e3(1)
    e3(3)
    v["d13"] = jnp.concatenate([v.pop("w1"), v.pop("w3")], axis=0)
    v["q3u"] = zswap(v["q3u"], 1)
    c1(0)
    c1(2)
    v["acc_own"], v["acc_far"] = run_down()
    v.fence()
    c0(0)
    c0(2)
    v["d13"] = zswap(v["d13"], 1)
    v["acc_got"] = swap(v.pop("acc_far"), core)
    v["low"] = run_mid()
    v.fence()
    d13 = v.pop("d13")
    v["d1"], v["d3"] = d13[:upart], d13[upart:]
    c2u(0)
    c2u(2)
    v["gp2"] = zswap(v.pop("gmt3"), 1)
    run_out_grad(v.pop("low"))
    v.fence()
    c2d(0)
    c2d(2)
    v["gp0"] = zswap(v.pop("gmt1"), 1)
    v["z2x"] = zswap(v["w2"][0], 2)
    run_attn_bwd(2, "gp2", idx_b, True)
    v.fence()
    r1("q2")
    r1("o")
    v.fence()
    c3(0)
    c3(2)
    v["z2y"] = zswap(v.pop("w2")[1], 2)
    r2("q2", "b")
    r2("o", "a")
    run_attn_bwd(0, "gp0", idx_b, False)
    v.fence()
    up_sum, down_sum = v.pop("w0")
    ma = high_bits(up_sum + v.pop("z2x"))
    mb = high_bits(down_sum + v.pop("z2y"))
    r1("q0")
    keep, got = v["o"]
    to_x = jnp.concatenate([ma, keep[1] + got[1]], axis=0)
    v["o"] = keep[0] + got[0]
    keep, got = v["q2"]
    to_y = jnp.concatenate([mb, keep[1] + got[1]], axis=0)
    v["q2"] = keep[0] + got[0]
    v["gx"], v["gy"] = (to_x, swap(to_x, px)), (to_y, swap(to_y, py))
    v["gn0"] = zswap(v["gn_far"][0], 1)
    v["small"] = call(
        functools.partial(sums_kernel, nmp),
        sds((16, width), F32),
        flops=full * width * 10,
        bytes_accessed=full * width * 6,
        grid_spec=pltpu.PrefetchScalarGridSpec(
            num_scalar_prefetch=2,
            grid=(1,),
            in_specs=[
                pl.BlockSpec((share, width), lambda t, b, m: (b[0] // per, 0)),
                pl.BlockSpec((share, width), lambda t, b, m: (b[per] // per, 0)),
                pl.BlockSpec((share, width), lambda t, b, m: (0, 0)),
                pl.BlockSpec((8, width), lambda t, b, m: (0, 0)),
                *[pl.BlockSpec((3, DH, 128), lambda t, b, m: (0, 0, 0))] * 2,
                *[pl.BlockSpec((3 * e, 128), lambda t, b, m: (0, 0))] * 2,
                *[pl.BlockSpec((1, mine), lambda t, b, m: (0, 0))] * nmp,
                *[pl.BlockSpec((n, width), lambda t, b, m: (0, 0)) for n in n_gn],
            ],
            out_specs=pl.BlockSpec((16, width), lambda t, b, m: (0, 0)),
        ),
    )(
        blk, me1, tokens, tokens, v["gn_own"], v.pop("mst"), v.pop("hst0"), v.pop("hst2"),
        v.pop("qbg0"), v.pop("qbg2"), *[v.pop(f"ubg{k}") for k in range(nmp)], *v["gn_far"],
    )
    v["small"] = v["small"] + swap(v["small"], core)
    v.fence()
    (xa, xb), (ya, yb) = v.pop("gx"), v.pop("gy")
    o = v.pop("o") + xb[upart:]
    v["q2"] = v["q2"] + yb[upart:]
    keep, got = v.pop("q0")
    q0 = keep + got
    v["q0b"], v["q0a"] = q0[:2, :n_q0], (q0[0, n_q0:], q0[2, n_q0:])
    to_y = jnp.concatenate([xa[:upart], xb[:upart], q0[1, n_q0:], q0[3, n_q0:]], axis=0)
    to_x = jnp.concatenate([ya[:upart], yb[:upart], q0[2, :n_q0], q0[3, :n_q0]], axis=0)
    v["gx"], v["gy"] = (to_x, swap(to_x, px)), (to_y, swap(to_y, py))
    v["oz"] = zswap(jnp.concatenate([o[part : 2 * part], o[3 * part :]], axis=0), 1)
    v["o0"], v["o2"] = o[:part], o[2 * part : 3 * part]
    v["gn1"] = zswap(v["gn_far"][1], 1)
    v["small"] = v["small"] + swap(v["small"], px)
    v.fence()
    (xa, xb), (ya, yb) = v.pop("gx"), v.pop("gy")
    q0b = v.pop("q0b") + xb[2 * upart :].reshape(2, n_q0, width)
    n_rest = 3 * part - n_q0
    q0a = [
        a + yb[2 * upart + i * n_rest : 2 * upart + (i + 1) * n_rest]
        for i, a in enumerate(v.pop("q0a"))
    ]
    v["q0b"] = (q0b[0], swap(q0b[1], py))
    v["q0a"] = (q0a[0], swap(q0a[1], px))
    oz = v.pop("oz")
    v["o0"] = v["o0"] + oz[:part]
    v["y2"] = zswap(jnp.concatenate([v.pop("q2"), v.pop("o2") + oz[part:]], axis=0), 2)
    v["gn2"] = zswap(v.pop("gn_far")[2], 1)
    v["small"] = v["small"] + swap(v["small"], py)
    n2 = 2 * upart
    v["mlp"] = jnp.concatenate([ya[:n2], yb[:n2], xa[:n2], xb[:n2]], axis=0)
    v.fence()
    q0 = jnp.concatenate([a + b for a, b in (v.pop("q0b"), v.pop("q0a"))], axis=0)
    att_sum = high_bits(jnp.concatenate([q0, v.pop("o0")], axis=0) + v.pop("y2"))
    v["w"] = (att_sum, swap(att_sum, px), swap(att_sum, py), swap(att_sum, px | py))
    small = high_bits(v.pop("small"))
    got = zswap(jnp.concatenate([small[:8], small[12:]], axis=0), 1)
    v["small"] = small[:12] + got

    mlp = v.pop("mlp")
    v["up_g"], v["down_g"] = call(
        unpack_mlp_kernel,
        (sds((width, units), F32), sds((units, width), F32)),
        bytes_accessed=10_000_000,
        in_specs=[smem, smem] + [vmem] * 2,
        out_specs=(vmem,) * 2,
        scratch_shapes=[pltpu.VMEM((2, PIECES, upart, width), F32)],
    )(idx_a, idx_b, mlp, swap(mlp, core))
    v["input_grad"] = call(
        final_kernel,
        sds((share, width), BF16),
        flops=share * width * 20,
        bytes_accessed=share * width * 16,
        grid_spec=pltpu.PrefetchScalarGridSpec(
            num_scalar_prefetch=1,
            grid=(1,),
            in_specs=[
                pl.BlockSpec((share, width), lambda t, b: (b[0] // per, 0)),
                pl.BlockSpec((share, width), const2),
                *[pl.BlockSpec((n, width), const2) for n in n_gn],
                pl.BlockSpec((share, width), const2),
                vec_spec,
            ],
            out_specs=pl.BlockSpec((share, width), const2),
        ),
    )(blk, tokens, v["gn_own"], *[v[f"gn{i}"] for i in range(3)], v["gm"], row1(norm1_gain))
    v.fence()
    w = jnp.concatenate(v.pop("w"), axis=0)
    small = v.pop("small")
    small_got = zswap(jnp.concatenate([small[:8], small[10:]], axis=0), 2)
    qkv_weight_grad, out_weight_grad = call(
        unpack_att_kernel,
        (sds((3, e, width), F32), sds((e, width), F32)),
        bytes_accessed=2 * 4 * 4 * width * e,
        in_specs=[smem] + [vmem] * 2,
        out_specs=(vmem, vmem),
        scratch_shapes=[pltpu.VMEM((PIECES, 4 * part, width), F32)],
    )(idx_a, w, swap(w, core))
    qkv_weight_grad = jnp.swapaxes(qkv_weight_grad, 1, 2)
    qkv_weight_grad, out_weight_grad, small, small_got = lax.optimization_barrier(
        (qkv_weight_grad, out_weight_grad, small, small_got)
    )
    qkv_bias_grad, *rows_of = call(
        small_out_kernel,
        (sds((3, e), F32), *[sds((DH,), F32)] * 3, *[sds((width,), F32)] * 7),
        bytes_accessed=100_000,
        in_specs=[vmem, vmem],
        out_specs=(vmem,) * 11,
    )(small[:10], small_got)
    heads_of, rows_of = rows_of[:3], rows_of[3:]
    return (
        v["block_out"],
        v["input_grad"],
        qkv_weight_grad,
        qkv_bias_grad,
        out_weight_grad,
        rows_of[2],
        v["up_g"],
        rows_of[6],
        v["down_g"],
        rows_of[3],
        rows_of[4],
        rows_of[5],
        heads_of[0],
        heads_of[1],
        heads_of[2],
        rows_of[0],
        rows_of[1],
    )


def solution(mesh):
    in_specs = (
        P("dp", None),
        P("dp"),
        P(None, None, "mp"),
        P(None, "mp"),
        P("mp", None),
        P(),
        P(None, "mp"),
        P("mp"),
        P("mp", None),
        P(),
        P(),
        P(),
        P(),
        P(),
        P(),
        P(),
        P(),
        P("dp", None),
    )
    out_specs = (
        P(("dp", "mp"), None),
        P(("dp", "mp"), None),
        P(None, None, "mp"),
        P(None, "mp"),
        P("mp", None),
        P(),
        P(None, "mp"),
        P("mp"),
        P("mp", None),
        P(),
        P(),
        P(),
        P(),
        P(),
        P(),
        P(),
        P(),
    )
    return jax.shard_map(shards, mesh=mesh, in_specs=in_specs, out_specs=out_specs, check_vma=False)
```

```python
import functools
import math

import jax
import jax.numpy as jnp
from jax import lax
from jax.experimental import pallas as pl
from jax.experimental.pallas import tpu as pltpu
from jax.sharding import PartitionSpec as P

F32 = jnp.float32
BF16 = jnp.bfloat16
DH = 64
SEQ_LEN = 1024
NORM_EPS = 1e-06
PIECES = 8
SEG_COLS = 128
LOG2E = math.log2(math.e)
SCALE = DH ** (-0.5)
BITS_A = (2, 4, 1)
BITS_B = (4, 2, 1)
MLP_KIND = ("a", "a", "b", "b")
VMEM_LIMIT = 26 * 1024 * 1024
VMEM_LARGE = 56 * 1024 * 1024


def mm(a, b):
    return lax.dot_general(a, b, (((1,), (0,)), ((), ())), preferred_element_type=F32)


def mm_nt(a, b):
    return lax.dot_general(a, b, (((1,), (1,)), ((), ())), preferred_element_type=F32)


def mm_tn(a, b):
    return lax.dot_general(a, b, (((0,), (0,)), ((), ())), preferred_element_type=F32)


def call(kernel, out_shape, flops=0, bytes_accessed=0, vmem_limit=VMEM_LIMIT, **kw):
    return pl.pallas_call(
        kernel,
        out_shape=out_shape,
        compiler_params=pltpu.CompilerParams(vmem_limit_bytes=vmem_limit),
        cost_estimate=pl.CostEstimate(
            flops=flops, bytes_accessed=bytes_accessed, transcendentals=0
        ),
        **kw,
    )


def sds(shape, dtype):
    return jax.ShapeDtypeStruct(shape, dtype)


def row_norm(x):
    mean = jnp.mean(x, axis=-1, keepdims=True)
    cen = x - mean
    rstd = lax.rsqrt(jnp.mean(cen * cen, axis=-1, keepdims=True) + NORM_EPS)
    return cen * rstd, rstd


def row_norm_back(f, n, rstd):
    mean_f = jnp.mean(f, axis=-1, keepdims=True)
    mean_fn = jnp.mean(f * n, axis=-1, keepdims=True)
    return (f - mean_f - n * mean_fn) * rstd


def col_norm(x):
    mean = jnp.mean(x, axis=0, keepdims=True)
    cen = x - mean
    rstd = lax.rsqrt(jnp.mean(cen * cen, axis=0, keepdims=True) + NORM_EPS)
    return cen * rstd, rstd


def col_norm_back(f, n, rstd):
    mean_f = jnp.mean(f, axis=0, keepdims=True)
    mean_fn = jnp.mean(f * n, axis=0, keepdims=True)
    return (f - mean_f - n * mean_fn) * rstd


def lane_fold(x):
    out = x[:, :128]
    for t in range(1, x.shape[1] // 128):
        out = out + x[:, t * 128 : (t + 1) * 128]
    return out


def offset_of(s, bits):
    return sum(bit for t, bit in enumerate(bits) if (s >> t) & 1)


def norm1_kernel(blk_ref, x_ref, g_ref, s_ref, out_ref):
    n, _ = row_norm(x_ref[...].astype(F32))
    out_ref[...] = (n * g_ref[...] + s_ref[...]).astype(BF16)


def build_q_aug(q_pre, qg, qs, qaug_ref):
    n, rstd = col_norm(q_pre)
    q_low = (n * qg + qs).astype(BF16)
    scaled = q_low.astype(F32) * (SCALE * LOG2E)
    hi = scaled.astype(BF16)
    lo = (scaled - hi.astype(F32)).astype(BF16)
    qaug_ref[0:DH, :] = hi
    qaug_ref[DH : 2 * DH, :] = lo
    return n, rstd, q_low


def build_k_aug(k_pre, kg, kaug_ref):
    n, rstd = col_norm(k_pre)
    k_low = (n * kg).astype(BF16)
    kaug_ref[:, 0 : 2 * DH] = jnp.concatenate([k_low, k_low], axis=0).T
    return n, rstd, k_low


def bias_col(b_ref, n):
    return b_ref[...].T[0:n, 0:1]


def prep_kernel(
    me_ref, w_ref, o_ref, qb_ref, ub_ref, up_ref, dn_ref,
    att_ref, ob_ref, b_ref, p_ref, u0_ref, u1_ref, d0_ref, d1_ref,
    t_ref, wf_ref,
):
    part = 24
    e = PIECES * part
    me = me_ref[0]
    b_ref[...] = jnp.zeros(b_ref.shape, F32)
    for s in range(3):
        wf_ref[...] = w_ref[s].astype(F32)
        rows = wf_ref[pl.ds(pl.multiple_of(me * part, 8), part), :]
        att_ref[s * part : (s + 1) * part, :] = rows
        b_ref[0:1, s * e : (s + 1) * e] = qb_ref[s : s + 1, :]
    upart = up_ref.shape[1] // PIECES
    ub = ub_ref[...].reshape(1, PIECES * upart)
    for s in range(PIECES // 2):
        piece = jnp.zeros((1, upart), F32)
        for p in range(PIECES):
            here = (me ^ offset_of(s, BITS_A)) == p
            piece = piece + jnp.where(here, ub[:, p * upart : (p + 1) * upart], 0.0)
        b_ref[1:2, s * upart : (s + 1) * upart] = piece
    wf_ref[...] = o_ref[...].astype(F32)
    rows = wf_ref[pl.ds(pl.multiple_of(me * part, 8), part), :]
    att_ref[3 * part : 4 * part, :] = rows
    ob_ref[0:part, :] = rows
    att_ref[4 * part :, :] = b_ref[...]
    ob_ref[part:, :] = b_ref[...]

    t_ref[...] = up_ref[...].astype(F32).T

    def at_piece(r):
        return pl.ds(pl.multiple_of((me ^ r) * upart, 32), upart)

    p_ref[0:upart, :] = t_ref[at_piece(0), :]
    p_ref[upart:, :] = dn_ref[at_piece(0), :].astype(F32)
    for i, (u_ref, d_ref) in enumerate(((u0_ref, d0_ref), (u1_ref, d1_ref))):
        for j in range(2):
            u_ref[j] = t_ref[at_piece(offset_of(2 * i + j, BITS_A)), :].astype(BF16)
            d_ref[j] = dn_ref[at_piece(offset_of(2 * i + j, BITS_B)), :]


def attend(x_ref, wt_ref, b_ref, hv_ref, kmask_ref, qhot_ref, outs, qaug_ref, kaug_ref):
    qpre_ref, kpre_ref, vt_ref, mixt_ref, mixf_ref, mixs_ref, l_ref = outs
    e = qpre_ref.shape[0]
    full = x_ref.shape[0]
    share = full // 2
    heads = e // DH
    x = x_ref[...]
    bias = bias_col(b_ref, 3 * e)
    qpre_ref[...] = mm_nt(wt_ref[0:e, :], x) + bias[0:e]
    kpre_ref[...] = mm_nt(wt_ref[e : 2 * e, :], x) + bias[e : 2 * e]
    vt_ref[...] = (mm_nt(wt_ref[2 * e : 3 * e, :], x) + bias[2 * e :]).astype(BF16)
    qaug_ref[2 * DH :, :] = qhot_ref[...]
    kaug_ref[:, 2 * DH :] = kmask_ref[...]
    ones = jnp.ones((16, full), BF16)
    for h in range(heads):
        hs = slice(h * DH, (h + 1) * DH)
        build_q_aug(qpre_ref[hs, :], hv_ref[:, 0:1], hv_ref[:, 1:2], qaug_ref)
        build_k_aug(kpre_ref[hs, :], hv_ref[:, 2:3], kaug_ref)
        prob = jnp.exp2(mm(kaug_ref[...], qaug_ref[...])).astype(BF16)
        vaug = jnp.concatenate([vt_ref[hs, :], ones], axis=0)
        o = mm(vaug, prob)
        total = o[DH : DH + 1, :]
        l_ref[h : h + 1, :] = total
        mix = o[0:DH, :] / total
        mixf_ref[hs, :] = mix
        mixt_ref[hs, :] = mix[:, 0:share].astype(BF16)
        at = h * share
        for c in range(0, share, 256):
            block_no, lane = divmod(at + c, x.shape[1])
            mixs_ref[block_no * DH : (block_no + 1) * DH, lane : lane + 256] = mix[
                :, share + c : share + c + 256
            ]


def attn_fwd_own_kernel(x_ref, wt_ref, b_ref, hv_ref, kmask_ref, qhot_ref, *refs):
    attend(x_ref, wt_ref, b_ref, hv_ref, kmask_ref, qhot_ref, refs[:7], *refs[7:])


def attn_fwd_kernel(
    ia_ref, ib_ref, a0_ref, a1_ref, b0_ref, b1_ref, x_ref, b_ref, hv_ref, kmask_ref, qhot_ref,
    wt_ref, ow_ref, ow1_ref, ow3_ref, *refs,
):
    wa_ref, wb_ref = refs[-2:]
    part = 24
    e = PIECES * part
    half = PIECES // 2
    wa_ref[0:half] = a0_ref[...]
    wa_ref[half:] = a1_ref[...]
    wb_ref[0:half] = b0_ref[...]
    wb_ref[half:] = b1_ref[...]

    def rows(w_ref, i_ref, at):
        return jnp.concatenate(
            [w_ref[i_ref[p], at * part : (at + 1) * part, :] for p in range(PIECES)], axis=0
        ).astype(BF16)

    wt_ref[0:e, :] = rows(wa_ref, ia_ref, 0)
    wt_ref[e : 2 * e, :] = rows(wa_ref, ia_ref, 1)
    wt_ref[2 * e : 3 * e, :] = rows(wb_ref, ib_ref, 0)
    ow_ref[...] = rows(wb_ref, ib_ref, 1)
    ow1_ref[...] = rows(wa_ref, ia_ref, 2)
    ow3_ref[...] = rows(wb_ref, ib_ref, 2)
    attend(x_ref, wt_ref, b_ref, hv_ref, kmask_ref, qhot_ref, refs[:7], *refs[7:9])


def unmix(ref, heads, share):
    width = ref.shape[1]
    rows = []
    for h in range(heads):
        cols = []
        for c in range(0, share, 256):
            block_no, lane = divmod(h * share + c, width)
            cols.append(ref[block_no * DH : (block_no + 1) * DH, lane : lane + 256])
        rows.append(jnp.concatenate(cols, axis=1))
    return jnp.concatenate(rows, axis=0).astype(BF16)


def mix_of(ref, share):
    if ref.dtype == BF16:
        return ref[...]
    return unmix(ref, ref.shape[0] * ref.shape[1] // (DH * share), share)


def out_norm2_kernel(nslot, blk_ref, x_ref, *refs):
    mixes = refs[:nslot]
    ws = refs[nslot : 2 * nslot]
    ob_ref, g_ref, s_ref, mid_ref, sec_ref, secf_ref = refs[2 * nslot :]
    acc = x_ref[...].astype(F32) + ob_ref[...]
    for k in range(nslot):
        acc = acc + mm_tn(mix_of(mixes[k], x_ref.shape[0]), ws[k][...])
    mid_ref[...] = acc
    n, _ = row_norm(acc)
    sec = (n * g_ref[...] + s_ref[...]).astype(BF16)
    sec_ref[...] = sec
    secf_ref[...] = sec.astype(F32)


def mlp_kernel(
    kind, keeps, sec_ref, secp_ref, cot_ref, cotp_ref, u0_ref, u1_ref, d0_ref, d1_ref, b_ref, *refs
):
    if keeps:
        p_ref, hid_ref, gp_ref, ub_ref, db_ref, k0_ref, k1_ref, s0_ref, s1_ref, gb_ref = refs
    else:
        hid_ref, gp_ref, ub_ref, db_ref, up_ref, uq_ref, k0_ref, k1_ref, sd_ref, gb_ref = refs
    part = u0_ref.shape[1]
    share = sec_ref.shape[0]
    up = jnp.concatenate([u0_ref[0], u0_ref[1], u1_ref[0], u1_ref[1]], axis=0).astype(BF16)
    down = jnp.concatenate([d0_ref[0], d1_ref[0], d0_ref[1], d1_ref[1]], axis=0).astype(BF16)
    ub_ref[...] = up
    db_ref[...] = down
    bias = b_ref[1:2, 0 : up.shape[0]]
    for r, (s_ref, c_ref) in enumerate(((sec_ref, cot_ref), (secp_ref, cotp_ref))):
        rows = slice(r * share, (r + 1) * share)
        sec = s_ref[...].astype(BF16)
        cot = c_ref[...].astype(BF16)
        pre = mm_nt(sec, up) + bias
        cdf = 0.5 * (1.0 + lax.erf(pre * (1.0 / math.sqrt(2.0))))
        hid = (pre * cdf).astype(BF16)
        pdf = jnp.exp(-0.5 * pre * pre) * (1.0 / math.sqrt(2.0 * math.pi))
        gpre = (mm_nt(cot, down) * (cdf + pre * pdf)).astype(BF16)
        hid_ref[rows, :] = hid
        gp_ref[rows, :] = gpre
        gb_r = jnp.sum(gpre.astype(F32), axis=0, keepdims=True)
        gd_r = mm_tn(hid, cot)
        gu_r = mm_tn(gpre, sec)
        if r == 0:
            gb, gd, gu = gb_r, gd_r, gu_r
        else:
            gb, gd, gu = gb + gb_r, gd + gd_r, gu + gu_r
    gb_ref[...] = gb
    order = (0, 1, 2, 3) if kind == "a" else (0, 2, 1, 3)
    gu_at = [gu[i * part : (i + 1) * part] for i in order]
    gd_at = [gd[i * part : (i + 1) * part] for i in order]
    if keeps:
        gu_at[3] = gu_at[3] + p_ref[0:part, :]
        gu_at[2] = gu_at[2] + p_ref[part:, :]
        for i, ref in enumerate((k0_ref, k1_ref, s0_ref, s1_ref)):
            ref[0:part, :] = gu_at[i]
            ref[part:, :] = gd_at[i]
    else:
        up_ref[0:part, :] = gu_at[3]
        up_ref[part:, :] = gu_at[2]
        uq_ref[0:part, :] = gu_at[0]
        uq_ref[part:, :] = gu_at[1]
        k0_ref[...] = gd_at[0]
        k1_ref[...] = gd_at[1]
        sd_ref[0:part, :] = gd_at[3]
        sd_ref[part:, :] = gd_at[2]


def down_kernel(nslot, *refs):
    hids = refs[:nslot]
    gps = refs[nslot : 2 * nslot]
    ubs = refs[2 * nslot : 3 * nslot]
    dbs = refs[3 * nslot : 4 * nslot]
    outs = refs[4 * nslot :]
    cat = lambda refs, axis: jnp.concatenate([r[...] for r in refs], axis=axis)
    share = outs[0].shape[1]
    for i, (rows_of, w_of) in enumerate(((hids, dbs), (gps, ubs))):
        w = cat(w_of, 0)
        for r, out_ref in enumerate(outs):
            rows = slice(r * share, (r + 1) * share)
            out_ref[i] = mm(jnp.concatenate([a[rows, :] for a in rows_of], axis=1), w)


def mid_kernel(nslot, mid_ref, own_ref, got_ref, cot_ref, db_ref, g_ref, *refs):
    ows = refs[:nslot]
    gmts = refs[nslot : 2 * nslot]
    bo_ref, gm_ref, low_ref, st_ref = refs[2 * nslot :]
    mid = mid_ref[...]
    n, rstd = row_norm(mid)
    e = own_ref[1] + got_ref[1]
    cot = cot_ref[...].astype(F32)
    gm = cot + row_norm_back(e * g_ref[...], n, rstd)
    gm_ref[...] = gm
    gm_low = gm.astype(BF16)
    low_ref[...] = gm_low
    for k in range(nslot):
        gmts[k][...] = mm_nt(ows[k][...], gm_low).astype(gmts[k].dtype)
    bo_ref[...] = (mid + (own_ref[0] + got_ref[0]) + db_ref[...]).astype(BF16)
    st_ref[0:1, :] = jnp.sum(e * n, axis=0, keepdims=True)
    st_ref[1:2, :] = jnp.sum(e, axis=0, keepdims=True)
    st_ref[2:3, :] = jnp.sum(gm_low.astype(F32), axis=0, keepdims=True)
    st_ref[3:4, :] = jnp.sum(cot, axis=0, keepdims=True)
    st_ref[4:8, :] = jnp.zeros((4, mid.shape[1]), F32)


def out_grad_kernel(nslot, idx_ref, low_ref, *refs):
    mixts = refs[:nslot]
    gow_keep, gow_send = refs[nslot:]
    part = 24
    gm_low = low_ref[...]
    for k in range(nslot):
        g = mm(mix_of(mixts[k], gm_low.shape[0]), gm_low)
        for p in range(PIECES):
            at = idx_ref[p]
            rows = slice(k * part, (k + 1) * part)

            @pl.when(at < PIECES // 2)
            def _():
                gow_keep[at, rows, :] = g[p * part : (p + 1) * part, :]

            @pl.when(at >= PIECES // 2)
            def _():
                gow_send[at - PIECES // 2, rows, :] = g[p * part : (p + 1) * part, :]


def attn_bwd_kernel(
    ncuts, idx_ref, x_ref, qpre_ref, kpre_ref, vt_ref, wt_ref, gmt_ref, gmtp_ref, mixf_ref, l_ref,
    hv_ref, kmask_ref, qhot_ref, *refs
):
    if ncuts:
        gn_in, gk_ref, gs_ref, *gn_refs = refs[: 3 + ncuts]
    else:
        gk_ref, gs_ref, gn_ref = refs[:3]
    st_ref, gb_ref, qaug_ref, kaug_ref, gpt_ref = refs[-5:]
    part = 24
    e = PIECES * part
    full = x_ref.shape[0]
    heads = e // DH
    qaug_ref[2 * DH :, :] = qhot_ref[...]
    kaug_ref[:, 2 * DH :] = kmask_ref[...]
    qg, qs, kg = hv_ref[:, 0:1], hv_ref[:, 1:2], hv_ref[:, 2:3]
    qg_sum = jnp.zeros((DH, 128), F32)
    qs_sum = jnp.zeros((DH, 128), F32)
    kg_sum = jnp.zeros((DH, 128), F32)
    row_no = lax.broadcasted_iota(jnp.int32, (DH, full), 0)
    one_rows = (row_no < 3).astype(F32).astype(BF16)
    for h in range(heads):
        hs = slice(h * DH, (h + 1) * DH)
        qn, qr, q_low = build_q_aug(qpre_ref[hs, :], qg, qs, qaug_ref)
        kn, kr, k_low = build_k_aug(kpre_ref[hs, :], kg, kaug_ref)
        inv = 1.0 / l_ref[h : h + 1, :]
        gm = jnp.concatenate(
            [gmt_ref[hs, :].astype(F32), gmtp_ref[hs, :].astype(BF16).astype(F32)], axis=1
        )
        go_low = (gm * inv).astype(BF16)
        delta = -jnp.sum(go_low.astype(F32) * mixf_ref[hs, :], axis=0, keepdims=True)
        d0 = delta.astype(BF16).astype(F32)
        d1 = (delta - d0).astype(BF16).astype(F32)
        d2 = delta - d0 - d1
        extra = jnp.where(
            row_no == 0, d0, jnp.where(row_no == 1, d1, jnp.where(row_no == 2, d2, 0.0))
        ).astype(BF16)
        goaug = jnp.concatenate([go_low, extra], axis=0)
        vaug = jnp.concatenate([vt_ref[hs, :], one_rows], axis=0).T
        prob = jnp.exp2(mm(kaug_ref[...], qaug_ref[...]))
        ds = (prob * mm(vaug, goaug)).astype(BF16)
        gv = mm_nt(go_low, prob.astype(BF16))
        gk = mm_nt(q_low, ds) * SCALE
        gq = mm(k_low, ds) * SCALE
        qg_sum += lane_fold(gq * qn)
        qs_sum += lane_fold(gq)
        kg_sum += lane_fold(gk * kn)
        gpt_ref[h * DH : (h + 1) * DH, :] = col_norm_back(gq * qg, qn, qr).astype(BF16)
        gpt_ref[e + h * DH : e + (h + 1) * DH, :] = col_norm_back(gk * kg, kn, kr).astype(BF16)
        gpt_ref[2 * e + h * DH : 2 * e + (h + 1) * DH, :] = gv.astype(BF16)
    st_ref[0] = qg_sum
    st_ref[1] = qs_sum
    st_ref[2] = kg_sum
    gp = gpt_ref[...]
    gb_ref[...] = lane_fold(gp.astype(F32))
    gw = mm(gp, x_ref[...])

    def put(ref, at, p):
        for s in range(3):
            ref[at, s * part : (s + 1) * part, :] = gw[s * e + p * part : s * e + (p + 1) * part, :]

    for p in range(PIECES):
        at = idx_ref[p]

        @pl.when(at < PIECES // 2)
        def _():
            put(gk_ref, at, p)

        @pl.when(at >= PIECES // 2)
        def _():
            put(gs_ref, at - PIECES // 2, p)

    gn = mm_tn(gp, wt_ref[...])
    if not ncuts:
        gn_ref[...] = gn
    else:
        at = 0
        for ref in gn_refs:
            rows = slice(at, at + ref.shape[0])
            ref[...] = gn_in[rows, :] + gn[rows]
            at += ref.shape[0]


def sums_kernel(
    nslot, blk_ref, me_ref, x_ref, xf_ref, gn_ref, mst_ref, h0_ref, h2_ref, b0_ref, b2_ref, *refs
):
    ubs = refs[:nslot]
    fars = refs[nslot:-1]
    out_ref = refs[-1]

    def fill():
        out_ref[...] = jnp.zeros_like(out_ref)
        out_ref[0:4, :] = mst_ref[0:4, :]
        heads = jnp.concatenate([h0_ref[i] + h2_ref[i] for i in range(3)], axis=0).T
        out_ref[6:7, 0 : heads.shape[1]] = jnp.sum(heads, axis=0, keepdims=True)
        me = me_ref[0]
        upart = out_ref.shape[1] // PIECES
        for row, k in zip((8, 10, 12, 14), (0, 2, 1, 3)):
            if k % 2 == 0:
                cols = (b0_ref if k == 0 else b2_ref)[...].T
                out_ref[row : row + 1, 0 : cols.shape[1]] = jnp.sum(cols, axis=0, keepdims=True)
            mine = ubs[k][...]
            for p in range(PIECES):
                piece = jnp.zeros((1, upart), F32)
                for t in range(PIECES // 2):
                    here = (me ^ offset_of(t, BITS_A)) == p
                    piece = piece + jnp.where(here, mine[:, t * upart : (t + 1) * upart], 0.0)
                out_ref[row + 1 : row + 2, p * upart : (p + 1) * upart] = piece

    fill()

    def add(x, e):
        n, _ = row_norm(x.astype(F32))
        out_ref[4:5, :] += jnp.sum(e * n, axis=0, keepdims=True)
        out_ref[5:6, :] += jnp.sum(e, axis=0, keepdims=True)

    add(x_ref[...], gn_ref[...])
    at = 0
    for ref in fars:
        add(xf_ref[at : at + ref.shape[0], :], ref[...])
        at += ref.shape[0]


def small_out_kernel(a_ref, b_ref, qb_ref, h0_ref, h1_ref, h2_ref, *rows):
    total = a_ref[...] + b_ref[...]
    for row, ref in zip((0, 1, 2, 3, 4, 5, 9), rows):
        ref[...] = total[row]
    for i, ref in enumerate((h0_ref, h1_ref, h2_ref)):
        ref[...] = total[6, i * DH : (i + 1) * DH]
        n = qb_ref.shape[1]
        qb_ref[i : i + 1, :] = total[8:9, i * n : (i + 1) * n]


def final_kernel(blk_ref, x_ref, gn_ref, *refs):
    gots = refs[:-3]
    gm_ref, g_ref, out_ref = refs[-3:]
    at = 0
    for ref in gots:
        rows = slice(at, at + ref.shape[0])
        n, rstd = row_norm(x_ref[rows, :].astype(F32))
        f = (gn_ref[rows, :] + ref[...]) * g_ref[...]
        out_ref[rows, :] = (gm_ref[rows, :] + row_norm_back(f, n, rstd)).astype(BF16)
        at += ref.shape[0]


def unpack_mlp_kernel(ia_ref, ib_ref, a_ref, b_ref, up_ref, down_ref, s_ref):
    part = s_ref.shape[2]
    half = PIECES // 2
    for w in range(2):
        for j in range(half):
            rows = slice((w * half + j) * part, (w * half + j + 1) * part)
            s_ref[w, j] = a_ref[rows, :]
            s_ref[w, half + j] = b_ref[rows, :]
    up_ref[...] = jnp.concatenate([s_ref[0, ia_ref[p]] for p in range(PIECES)], axis=0).T
    for p in range(PIECES):
        down_ref[p * part : (p + 1) * part, :] = s_ref[1, ib_ref[p]]


def unpack_att_kernel(i_ref, a_ref, b_ref, qkv_ref, out_ref, s_ref):
    rows = s_ref.shape[1]
    part = rows // 4
    half = PIECES // 2
    for j in range(half):
        s_ref[j] = a_ref[j * rows : (j + 1) * rows, :]
        s_ref[half + j] = b_ref[j * rows : (j + 1) * rows, :]
    for s, ref in enumerate((qkv_ref.at[0], qkv_ref.at[1], qkv_ref.at[2], out_ref)):
        for p in range(PIECES):
            ref[p * part : (p + 1) * part, :] = s_ref[i_ref[p], s * part : (s + 1) * part, :]


def swap_mp(a, k, size):
    return lax.ppermute(a, "mp", [(s, s ^ k) for s in range(size)])


def swap_plane(a, bit, size):
    return lax.ppermute(a, "dp", [(d, d ^ bit) for d in range(size)])


def storage_of(r, bits):
    return sum(jnp.where((r & bit) != 0, 1 << t, 0) for t, bit in enumerate(bits))


class Stages:
    def __init__(self):
        self.live = {}

    def __setitem__(self, name, value):
        self.live[name] = value

    def __getitem__(self, name):
        return self.live[name]

    def pop(self, name):
        return self.live.pop(name)

    def fence(self, *still_flying):
        now = {n: a for n, a in self.live.items() if n not in still_flying}
        leaves, tree = jax.tree.flatten(now)
        self.live.update(jax.tree.unflatten(tree, lax.optimization_barrier(leaves)))


def shards(
    tokens,
    seg_ids,
    qkv_weight,
    qkv_bias,
    out_weight,
    out_bias,
    up_weight,
    up_bias,
    down_weight,
    down_bias,
    norm1_gain,
    norm1_shift,
    query_gain,
    query_shift,
    key_gain,
    norm2_gain,
    norm2_shift,
    cotangent,
):
    ndp = lax.axis_size("dp")
    nmp = lax.axis_size("mp")
    dp_no = lax.axis_index("dp")
    mp_no = lax.axis_index("mp")
    me = dp_no % PIECES
    row_count, width = tokens.shape
    share = row_count // nmp
    full = SEQ_LEN
    assert full == 2 * share and nmp == 4 and ndp % PIECES == 0
    e = qkv_weight.shape[2]
    part = e // PIECES
    units = up_weight.shape[1]
    upart = units // PIECES
    half = PIECES // 2
    mine = half * upart
    core, px, py = 1, 2, 4

    vmem = pl.BlockSpec(memory_space=pltpu.VMEM)
    smem = pl.BlockSpec(memory_space=pltpu.SMEM)
    row1 = lambda v: v.reshape(1, -1)
    col = lambda v: v.reshape(-1, 1)
    swap = lambda a, bit: swap_plane(a, bit, ndp)
    zswap = lambda a, k: swap_mp(a, k, nmp)
    v = Stages()

    me1 = me.astype(jnp.int32).reshape(1)
    qkv_t = jnp.swapaxes(qkv_weight, 1, 2)
    wt0 = qkv_t.reshape(3 * e, width)
    att_piece, ob_piece, bias0, mlp_piece, u0, u1, d0, d1 = call(
        prep_kernel,
        (
            sds((4 * part + 8, width), F32),
            sds((part + 8, width), F32),
            sds((8, width), F32),
            sds((2 * upart, width), F32),
            *[sds((2, upart, width), BF16)] * 4,
        ),
        bytes_accessed=9_000_000,
        vmem_limit=VMEM_LARGE,
        in_specs=[smem] + [vmem] * 6,
        out_specs=(vmem,) * 8,
        scratch_shapes=[pltpu.VMEM((units, width), F32), pltpu.VMEM((e, width), F32)],
    )(
        me1, qkv_t, out_weight, qkv_bias, up_bias, up_weight, down_weight
    )

    n_gn = (176, 136, 120, 80)
    n_q0 = 40
    numbers = jnp.arange(PIECES, dtype=jnp.int32)
    idx_a = storage_of(numbers ^ me, BITS_A).astype(jnp.int32)
    idx_b = storage_of(numbers ^ me, BITS_B).astype(jnp.int32)

    block = 256
    per = share // block
    steps = 2 * per
    tile_no = jnp.arange(steps, dtype=jnp.int32)
    blk = jnp.where(tile_no < per, mp_no * per + tile_no, (mp_no ^ 1) * per + tile_no - per).astype(
        jnp.int32
    )
    const2 = lambda t, b: (0, 0)
    tok_spec = pl.BlockSpec((block, width), lambda t, b: (b[t], 0))
    run_spec = pl.BlockSpec((block, width), lambda t, b: (t, 0))
    vec_spec = pl.BlockSpec((1, width), const2)

    def run_norm1():
        return call(
            norm1_kernel,
            sds((full, width), BF16),
            flops=full * width * 10,
            bytes_accessed=full * width * 4,
            grid_spec=pltpu.PrefetchScalarGridSpec(
                num_scalar_prefetch=1,
                grid=(steps,),
                in_specs=[tok_spec, vec_spec, vec_spec],
                out_specs=run_spec,
            ),
        )(blk, tokens, row1(norm1_gain), row1(norm1_shift))

    seg_own = lax.dynamic_slice_in_dim(seg_ids, mp_no * share, share, 0)
    seg_other = lax.dynamic_slice_in_dim(seg_ids, (mp_no ^ 1) * share, share, 0)
    seg_keys = jnp.concatenate([seg_own, seg_other])
    qhot = (
        lax.broadcasted_iota(jnp.int32, (SEG_COLS, full), 0) == seg_keys[None, :]
    ).astype(BF16)
    kmask = jnp.where(
        lax.broadcasted_iota(jnp.int32, (full, SEG_COLS), 1) == seg_keys[:, None], 0.0, -1e30
    ).astype(BF16)
    hv = jnp.stack([query_gain, query_shift, key_gain], axis=1)
    scratch = [
        pltpu.VMEM((2 * DH + SEG_COLS, full), BF16),
        pltpu.VMEM((full, 2 * DH + SEG_COLS), BF16),
    ]

    def whole(a):
        return pl.BlockSpec(a.shape, lambda t: (0,) * len(a.shape))

    def bias_at(block_no):
        return pl.BlockSpec((8, width), lambda t: (block_no, 0))

    att_names = ["qpre", "kpre", "vt", "mixt", "mixf", "mixs", "l"]
    att_shapes = [
        sds((e, full), F32),
        sds((e, full), F32),
        sds((e, full), BF16),
        sds((e, share), BF16),
        sds((e, full), F32),
        sds((e * share // width, width), F32),
        sds((8, full), F32),
    ]
    mix_rows = e * share // width

    def run_attn_own():
        outs = call(
            attn_fwd_own_kernel,
            tuple(att_shapes),
            flops=2 * (full * width * e * 3 + full * full * e * 8),
            bytes_accessed=10_000_000,
            in_specs=[vmem] * 6,
            out_specs=(vmem,) * 7,
            scratch_shapes=scratch,
        )(v["normed"], wt0, bias0, hv, kmask, qhot)
        v["st0"] = dict(zip(att_names, outs))
        v["st0"]["wt"] = wt0
        v["st0"]["ow"] = out_weight

    def run_attn_far():
        shapes = [sds((3 * e, width), BF16)] + [sds((e, width), BF16)] * 3 + att_shapes
        args = [
            *v.pop("ta"), *v.pop("tb"), v["normed"], v["t2"], hv, kmask, qhot,
        ]
        specs = [whole(a) for a in args]
        specs[5] = bias_at(4 * part // 8)
        outs = call(
            attn_fwd_kernel,
            tuple(shapes),
            flops=2 * (full * width * e * 3 + full * full * e * 8),
            bytes_accessed=10_000_000,
            grid=(1,),
            in_specs=[smem, smem] + specs,
            out_specs=tuple(whole(a) for a in shapes),
            scratch_shapes=scratch
            + [pltpu.VMEM((PIECES, 3 * part, width), F32)] * 2,
        )(idx_a, idx_b, *args)
        v["st2"] = dict(zip(["wt", "ow", "ow1", "ow3"] + att_names, outs))

    def by_slot():
        st0, st2 = v["st0"], v["st2"]
        mixes = [st0["mixt"], v["mix0"], st2["mixt"], v["mix2"]]
        ows = [st0["ow"], st2["ow1"], st2["ow"], st2["ow3"]]
        return mixes, ows

    def run_out():
        own_spec = pl.BlockSpec((share, width), lambda t, b: (b[0] // per, 0))
        whole2 = lambda shape: pl.BlockSpec(shape, lambda t, b: (0,) * len(shape))
        mixes, ows = by_slot()
        v["middle"], v["second"], v["sec_f"] = call(
            functools.partial(out_norm2_kernel, nmp),
            (sds((share, width), F32), sds((share, width), BF16), sds((share, width), F32)),
            flops=2 * share * width * e * nmp,
            bytes_accessed=8_000_000,
            grid_spec=pltpu.PrefetchScalarGridSpec(
                num_scalar_prefetch=1,
                grid=(1,),
                in_specs=[own_spec]
                + [whole2((e, share)), whole2((mix_rows, width))] * 2
                + [whole2((e, width))] * nmp
                + [whole2((1, width))] * 3,
                out_specs=(whole2((share, width)),) * 3,
            ),
        )(blk, tokens, *mixes, *ows, row1(out_bias), row1(norm2_gain), row1(norm2_shift))

    def run_mlp(k, up, down, bias, block_no):
        keeps = k % 2 == 0
        args = [
            v["second"], v["sec_p"], v["cot"], v["cot_p"], up[0], up[1], down[0], down[1], bias,
        ]
        if keeps:
            args.append(v.pop(f"p{k + 1}"))
        specs = [whole(a) for a in args]
        specs[8] = bias_at(block_no)
        piece = lambda n: sds((n * upart, width), F32)
        shapes = (
            *[sds((full, mine), BF16)] * 2,
            *[sds((mine, width), BF16)] * 2,
            *([piece(2)] * 4 if keeps else [piece(2), piece(2), piece(1), piece(1), piece(2)]),
            sds((1, mine), F32),
        )
        res = call(
            functools.partial(mlp_kernel, MLP_KIND[k], keeps),
            shapes,
            flops=2 * full * width * mine * 4,
            bytes_accessed=12_000_000,
            grid=(1,),
            in_specs=specs,
            out_specs=tuple(whole(a) for a in shapes),
        )(*args)
        v[f"h{k}"] = res[:4]
        v[f"ubg{k}"] = res[-1]
        if keeps:
            v[f"w{k}"] = res[4:8]
        else:
            v[f"p{k}"], v[f"q{k}u"] = res[4], res[5]
            v[f"w{k}"] = res[6:9]

    def run_down():
        return call(
            functools.partial(down_kernel, nmp),
            (sds((2, share, width), F32),) * 2,
            flops=4 * full * width * mine * nmp,
            bytes_accessed=17_000_000,
            vmem_limit=40 * 1024 * 1024,
            in_specs=[vmem] * (4 * nmp),
            out_specs=(vmem,) * 2,
        )(*[v[f"h{k}"][i] for i in range(4) for k in range(nmp)])

    def run_mid():
        mixes, ows = by_slot()
        shapes = (
            *[sds((e, share), F32 if k % 2 else BF16) for k in range(nmp)],
            sds((share, width), BF16),
            sds((share, width), F32),
            sds((share, width), BF16),
            sds((8, width), F32),
        )
        *gmts, bo, gm, low, mst = call(
            functools.partial(mid_kernel, nmp),
            shapes,
            flops=2 * share * width * e * nmp,
            bytes_accessed=12_000_000,
            in_specs=[vmem] * (6 + nmp),
            out_specs=(vmem,) * (4 + nmp),
        )(
            v["middle"], v.pop("acc_own"), v.pop("acc_got"), v["cot"], row1(down_bias),
            row1(norm2_gain), *ows,
        )
        v["block_out"], v["gm"], v["mst"] = bo, gm, mst
        for k in range(nmp):
            v[f"gmt{k}"] = gmts[k]
        return low

    def run_out_grad(low):
        mixes, ows = by_slot()
        args = [low, *mixes]
        specs = [whole(a) for a in args]
        for k in (1, 3):
            specs[1 + k] = pl.BlockSpec((mix_rows, width), lambda t: (0, 0))
        shapes = (sds((half, nmp * part, width), F32),) * 2
        v["o"] = call(
            functools.partial(out_grad_kernel, nmp),
            shapes,
            flops=2 * share * width * e * nmp,
            bytes_accessed=5_000_000,
            grid=(1,),
            in_specs=[smem] + specs,
            out_specs=tuple(whole(a) for a in shapes),
        )(idx_a, *args)

    def run_attn_bwd(k, got, idx, first):
        st = v.pop(f"st{k}")
        args = [
            idx, v["normed"], st["qpre"], st["kpre"], st["vt"], st["wt"], v.pop(f"gmt{k}"),
            v.pop(got), st["mixf"], st["l"], hv, kmask, qhot,
        ]
        cuts_now = (full,) if first else (share, *n_gn)
        if not first:
            args.append(v.pop("gn"))
        keep, send, *gn, hst, gb = call(
            functools.partial(attn_bwd_kernel, 0 if first else len(cuts_now)),
            (
                sds((half, 3 * part, width), F32),
                sds((half, 3 * part, width), F32),
                *[sds((n, width), F32) for n in cuts_now],
                sds((3, DH, 128), F32),
                sds((3 * e, 128), F32),
            ),
            flops=2 * (full * width * e * 6 + full * full * e * 20),
            bytes_accessed=14_000_000,
            in_specs=[smem] + [vmem] * (len(args) - 1),
            out_specs=(vmem,) * (4 + len(cuts_now)),
            scratch_shapes=scratch + [pltpu.VMEM((3 * e, full), BF16)],
        )(*args)
        v[f"q{k}"] = (keep, send)
        if first:
            v["gn"] = gn[0]
        else:
            v["gn_own"], v["gn_far"] = gn[0], tuple(gn[1:])
        v[f"hst{k}"] = hst
        v[f"qbg{k}"] = gb

    def g1(n):
        a, b = v[n + "a"], v[n + "b"]
        v[n + "a"] = (a, swap(a, px))
        v[n + "b"] = (b, swap(b, py))

    def g2(n):
        a, b = (jnp.stack(v[n + t]) for t in "ab")
        v[n + "a"] = (a, swap(a, py))
        v[n + "b"] = (b, swap(b, px))

    def g3(n):
        a, b = (jnp.concatenate(v[n + t], axis=0) for t in "ab")
        v[n + "a"] = (a, swap(a, core))
        v[n + "b"] = (b, swap(b, core))

    def r1(n):
        keep, send = v[n]
        v[n] = (keep, swap(send, core))

    def r2(n, kind):
        keep, got = v[n]
        keep_sum = keep[:2] + got[:2]
        v[n] = (keep_sum, swap(keep[2:] + got[2:], py if kind == "a" else px))

    def r3(n, kind):
        keep, got = v[n]
        v[n] = (keep[0] + got[0], swap(keep[1] + got[1], px if kind == "a" else py))

    def r4(n):
        keep, got = v[n]
        v[n] = keep + got

    def first_link(k):
        return py if MLP_KIND[k] == "a" else px

    def second_link(k):
        return px if MLP_KIND[k] == "a" else py

    def c1(k):
        k0, k1, s0, s1 = v[f"w{k}"]
        v[f"w{k}"] = (k0, k1, s0, swap(s1, first_link(k)))

    def c0(k):
        k0, k1, s0, g1 = v[f"w{k}"]
        v[f"w{k}"] = (k0, k1, g1, swap(s0, first_link(k)))

    def c2u(k):
        k0, k1, g1, g0 = v[f"w{k}"]
        q0, q1 = v.pop(f"q{k + 1}u")
        sent = k1[:upart] + q1 + g1[:upart]
        v[f"w{k}"] = (k0, k1, g1, g0, q0, swap(sent, second_link(k)))

    def c2d(k):
        k0, k1, g1, g0, q, gu = v[f"w{k}"]
        up_sum = k0[:upart] + g0[:upart] + q + gu
        sent = k1[upart:] + g1[upart:]
        v[f"w{k}"] = (up_sum, k0[upart:], g0[upart:], swap(sent, second_link(k)))

    def c3(k):
        up_sum, kd, g0, gd = v[f"w{k}"]
        v[f"w{k}"] = (up_sum, kd + g0 + gd + v.pop(f"d{k + 1}"))

    def e1(k):
        k0, k1, s = v[f"w{k}"]
        v[f"w{k}"] = (k0, k1, swap(s, first_link(k)))

    def e2(k):
        k0, k1, g = v[f"w{k}"]
        v[f"w{k}"] = (k0 + g[upart:], swap(k1 + g[:upart], second_link(k)))

    def e3(k):
        k0, g = v[f"w{k}"]
        v[f"w{k}"] = k0 + g

    inner = (mp_no == 1) | (mp_no == 2)

    def middle_swap(a):
        return lax.ppermute(a, "mp", [(1, 2), (2, 1)])

    def pass_out(a):
        return lax.ppermute(a, "mp", [(1, 0), (2, 3)])

    def high_bits(a):
        bit = PIECES
        while bit < ndp:
            a = a + swap(a, bit)
            bit *= 2
        return a

    cot_all, att_piece, ob_piece, mlp_piece = lax.optimization_barrier(
        (cotangent, att_piece, ob_piece, mlp_piece)
    )
    v["cot"] = lax.dynamic_slice_in_dim(cot_all, mp_no * share, share, 0)
    v["cot_f"] = v["cot"].astype(F32)
    v["piece"] = mlp_piece
    v["o3"] = zswap(ob_piece, 3)
    v["o1"] = zswap(ob_piece, 1)
    v["t2"] = zswap(att_piece, 2)
    v["normed"] = run_norm1()
    v.fence()
    hp = 2 * part
    t2, o1, o3 = v["t2"], v["o1"], v["o3"]
    v["ta"] = jnp.concatenate([t2[:hp], o1[:part]], axis=0)
    v["tb"] = jnp.concatenate([t2[hp : 2 * hp], o3[:part]], axis=0)
    g1("t")
    v["cot_p"] = swap(v.pop("cot_f"), core)
    v["m1"] = zswap(v["piece"], 1)
    v["mid_a"] = middle_swap(v.pop("piece"))
    run_attn_own()
    v.fence()
    m1 = v["m1"]
    to_y = jnp.concatenate([*v["ta"], m1[upart:]], axis=0)
    to_x = jnp.concatenate([*v["tb"], m1[:upart]], axis=0)
    v["ta"] = (to_y, swap(to_y, py))
    v["tb"] = (to_x, swap(to_x, px))
    v["mid_b"] = middle_swap(v.pop("m1"))
    v["mix0"] = zswap(jnp.concatenate([v["st0"].pop("mixs"), v["mid_a"]], axis=0), 1)
    v.fence()
    nt = 2 * 3 * part
    ya, yb = v.pop("ta")
    xa, xb = v.pop("tb")
    v["m1a"], v["m1b"] = (xa[nt:], xb[nt:]), (ya[nt:], yb[nt:])
    v["ta"], v["tb"] = (
        tuple(
            a.reshape(half, 3 * part, width) for a in (both_, swap(both_, core))
        )
        for both_ in (
            jnp.concatenate([ya[:nt], yb[:nt]], axis=0),
            jnp.concatenate([xa[:nt], xb[:nt]], axis=0),
        )
    )
    run_attn_far()
    g2("m1")
    v["end_b"] = pass_out(v["mid_b"])
    v.fence()
    v["mix2"] = zswap(v["st2"].pop("mixs"), 1)
    run_out()
    m3 = jnp.where(inner, v.pop("mid_a"), v.pop("end_b"))
    m2 = jnp.where(inner, v.pop("mid_b"), v["mix0"][mix_rows:])
    to_x = jnp.concatenate([m3[:upart], m2[:upart]], axis=0)
    to_y = jnp.concatenate([m3[upart:], m2[upart:]], axis=0)
    v["ma"], v["mb"] = (to_x, swap(to_x, px)), (to_y, swap(to_y, py))
    v.fence()
    for t in "ab":
        own, got = v.pop(f"m{t}")
        v[f"m3{t}"] = (own[:upart], got[:upart])
        v[f"m2{t}"] = (own[upart:], got[upart:])
    v["sec_p"] = swap(v.pop("sec_f"), core)
    run_mlp(1, v.pop("m1a"), v.pop("m1b"), v["o1"], part // 8)
    g2("m3")
    v.fence()
    v["p1"] = zswap(v["p1"], 1)
    run_mlp(3, v.pop("m3a"), v.pop("m3b"), v["o3"], part // 8)
    g2("m2")
    v.fence()
    v["p3"] = zswap(v["p3"], 1)
    run_mlp(0, (u0, u1), (d0, d1), bias0, 0)
    e1(1)
    e1(3)
    v.fence()
    run_mlp(2, v.pop("m2a"), v.pop("m2b"), v["t2"], 4 * part // 8)
    e2(1)
    e2(3)
    q1u = v.pop("q1u")
    v["q1x"] = zswap(q1u[:upart], 1)
    v["q1r"] = q1u[upart:]
    v.fence()
    e3(1)
    e3(3)
    q3u = v.pop("q3u")
    v["qm"] = zswap(jnp.concatenate([v.pop("q1r"), q3u[:upart]], axis=0), 1)
    v["q3r"] = q3u[upart:]
    c1(0)
    c1(2)
    v["acc_own"], v["acc_far"] = run_down()
    v.fence()
    c0(0)
    c0(2)
    v["q3y"] = zswap(jnp.concatenate([v.pop("q3r"), v.pop("w3")], axis=0), 1)
    v["acc_got"] = swap(v.pop("acc_far"), core)
    v["low"] = run_mid()
    v.fence()
    qm = v.pop("qm")
    q3y = v.pop("q3y")
    v["q1u"], v["q3u"] = (v.pop("q1x"), qm[:upart]), (qm[upart:], q3y[:upart])
    v["d3"] = q3y[upart:]
    c2u(0)
    c2u(2)
    v["gp2"] = zswap(v.pop("gmt3"), 1)
    run_out_grad(v.pop("low"))
    v.fence()
    c2d(0)
    c2d(2)
    v["gp0"] = zswap(v.pop("gmt1"), 1)
    v["z2x"] = zswap(v["w2"][0], 2)
    run_attn_bwd(2, "gp2", idx_b, True)
    v.fence()
    r1("q2")
    r1("o")
    v.fence()
    c3(2)
    v["d1"] = zswap(v.pop("w1"), 1)
    v["z2y"] = zswap(v.pop("w2")[1], 2)
    r2("q2", "b")
    r2("o", "a")
    run_attn_bwd(0, "gp0", idx_b, False)
    v.fence()
    c3(0)
    up_sum, down_sum = v.pop("w0")
    ma = high_bits(up_sum + v.pop("z2x"))
    mb = high_bits(down_sum + v.pop("z2y"))
    r1("q0")
    keep, got = v["o"]
    to_x = jnp.concatenate([ma, keep[1] + got[1]], axis=0)
    v["o"] = keep[0] + got[0]
    keep, got = v["q2"]
    to_y = jnp.concatenate([mb, keep[1] + got[1]], axis=0)
    v["q2"] = keep[0] + got[0]
    v["gx"], v["gy"] = (to_x, swap(to_x, px)), (to_y, swap(to_y, py))
    v["gn0"] = zswap(v["gn_far"][0], 1)
    v["small"] = call(
        functools.partial(sums_kernel, nmp),
        sds((16, width), F32),
        flops=full * width * 10,
        bytes_accessed=full * width * 6,
        grid_spec=pltpu.PrefetchScalarGridSpec(
            num_scalar_prefetch=2,
            grid=(1,),
            in_specs=[
                pl.BlockSpec((share, width), lambda t, b, m: (b[0] // per, 0)),
                pl.BlockSpec((share, width), lambda t, b, m: (b[per] // per, 0)),
                pl.BlockSpec((share, width), lambda t, b, m: (0, 0)),
                pl.BlockSpec((8, width), lambda t, b, m: (0, 0)),
                *[pl.BlockSpec((3, DH, 128), lambda t, b, m: (0, 0, 0))] * 2,
                *[pl.BlockSpec((3 * e, 128), lambda t, b, m: (0, 0))] * 2,
                *[pl.BlockSpec((1, mine), lambda t, b, m: (0, 0))] * nmp,
                *[pl.BlockSpec((n, width), lambda t, b, m: (0, 0)) for n in n_gn],
            ],
            out_specs=pl.BlockSpec((16, width), lambda t, b, m: (0, 0)),
        ),
    )(
        blk, me1, tokens, tokens, v["gn_own"], v.pop("mst"), v.pop("hst0"), v.pop("hst2"),
        v.pop("qbg0"), v.pop("qbg2"), *[v.pop(f"ubg{k}") for k in range(nmp)], *v["gn_far"],
    )
    v["small"] = v["small"] + swap(v["small"], core)
    v.fence()
    (xa, xb), (ya, yb) = v.pop("gx"), v.pop("gy")
    o = v.pop("o") + xb[upart:]
    v["q2"] = v["q2"] + yb[upart:]
    keep, got = v.pop("q0")
    q0 = keep + got
    v["q0b"], v["q0a"] = q0[:2, :n_q0], (q0[0, n_q0:], q0[2, n_q0:])
    to_y = jnp.concatenate([xa[:upart], xb[:upart], q0[1, n_q0:], q0[3, n_q0:]], axis=0)
    to_x = jnp.concatenate([ya[:upart], yb[:upart], q0[2, :n_q0], q0[3, :n_q0]], axis=0)
    v["gx"], v["gy"] = (to_x, swap(to_x, px)), (to_y, swap(to_y, py))
    v["o0"], v["o2"] = o[:part], o[2 * part : 3 * part]
    v["gn1"] = zswap(
        jnp.concatenate([v["gn_far"][1], o[part : 2 * part], o[3 * part :]], axis=0), 1
    )
    v["yq"] = zswap(v.pop("q2"), 2)
    v["small"] = v["small"] + swap(v["small"], px)
    v.fence()
    (xa, xb), (ya, yb) = v.pop("gx"), v.pop("gy")
    q0b = v.pop("q0b") + xb[2 * upart :].reshape(2, n_q0, width)
    n_rest = 3 * part - n_q0
    q0a = [
        a + yb[2 * upart + i * n_rest : 2 * upart + (i + 1) * n_rest]
        for i, a in enumerate(v.pop("q0a"))
    ]
    v["q0b"] = (q0b[0], swap(q0b[1], py))
    v["q0a"] = (q0a[0], swap(q0a[1], px))
    oz = v["gn1"][n_gn[1] :]
    v["o0"] = v["o0"] + oz[:part]
    v["yo"] = zswap(v.pop("o2") + oz[part:], 2)
    v["gn2"] = zswap(v["gn_far"][2], 1)
    v["small"] = v["small"] + swap(v["small"], py)
    n2 = 2 * upart
    v["mlp"] = jnp.concatenate([ya[:n2], yb[:n2], xa[:n2], xb[:n2]], axis=0)
    v.fence()
    q0 = jnp.concatenate([a + b for a, b in (v.pop("q0b"), v.pop("q0a"))], axis=0)
    att_sum = high_bits(
        jnp.concatenate([q0 + v.pop("yq"), v.pop("o0") + v.pop("yo")], axis=0)
    )
    v["w"] = (att_sum, swap(att_sum, px), swap(att_sum, py), swap(att_sum, px | py))
    small = high_bits(v.pop("small"))
    v["gn3"] = zswap(jnp.concatenate([v.pop("gn_far")[3], small[:8], small[12:]], axis=0), 1)
    v["small"] = small[:12] + v["gn3"][n_gn[3] :]

    mlp = v.pop("mlp")
    v["up_g"], v["down_g"] = call(
        unpack_mlp_kernel,
        (sds((width, units), F32), sds((units, width), F32)),
        bytes_accessed=10_000_000,
        in_specs=[smem, smem] + [vmem] * 2,
        out_specs=(vmem,) * 2,
        scratch_shapes=[pltpu.VMEM((2, PIECES, upart, width), F32)],
    )(idx_a, idx_b, mlp, swap(mlp, core))
    v.fence()
    input_grad = call(
        final_kernel,
        sds((share, width), BF16),
        flops=share * width * 20,
        bytes_accessed=share * width * 16,
        grid_spec=pltpu.PrefetchScalarGridSpec(
            num_scalar_prefetch=1,
            grid=(1,),
            in_specs=[
                pl.BlockSpec((share, width), lambda t, b: (b[0] // per, 0)),
                pl.BlockSpec((share, width), const2),
                *[pl.BlockSpec((n, width), const2) for n in n_gn],
                pl.BlockSpec((share, width), const2),
                vec_spec,
            ],
            out_specs=pl.BlockSpec((share, width), const2),
        ),
    )(blk, tokens, v["gn_own"], *[v[f"gn{i}"] for i in range(4)], v["gm"], row1(norm1_gain))
    w = jnp.concatenate(v.pop("w"), axis=0)
    small = v.pop("small")
    small_got = zswap(jnp.concatenate([small[:8], small[10:]], axis=0), 2)
    qkv_weight_grad, out_weight_grad = call(
        unpack_att_kernel,
        (sds((3, e, width), F32), sds((e, width), F32)),
        bytes_accessed=2 * 4 * 4 * width * e,
        in_specs=[smem] + [vmem] * 2,
        out_specs=(vmem, vmem),
        scratch_shapes=[pltpu.VMEM((PIECES, 4 * part, width), F32)],
    )(idx_a, w, swap(w, core))
    qkv_weight_grad = jnp.swapaxes(qkv_weight_grad, 1, 2)
    qkv_weight_grad, out_weight_grad, input_grad, small, small_got = lax.optimization_barrier(
        (qkv_weight_grad, out_weight_grad, input_grad, small, small_got)
    )
    qkv_bias_grad, *rows_of = call(
        small_out_kernel,
        (sds((3, e), F32), *[sds((DH,), F32)] * 3, *[sds((width,), F32)] * 7),
        bytes_accessed=100_000,
        in_specs=[vmem, vmem],
        out_specs=(vmem,) * 11,
    )(small[:10], small_got)
    heads_of, rows_of = rows_of[:3], rows_of[3:]
    return (
        v["block_out"],
        input_grad,
        qkv_weight_grad,
        qkv_bias_grad,
        out_weight_grad,
        rows_of[2],
        v["up_g"],
        rows_of[6],
        v["down_g"],
        rows_of[3],
        rows_of[4],
        rows_of[5],
        heads_of[0],
        heads_of[1],
        heads_of[2],
        rows_of[0],
        rows_of[1],
    )


def solution(mesh):
    in_specs = (
        P("dp", None),
        P("dp"),
        P(None, None, "mp"),
        P(None, "mp"),
        P("mp", None),
        P(),
        P(None, "mp"),
        P("mp"),
        P("mp", None),
        P(),
        P(),
        P(),
        P(),
        P(),
        P(),
        P(),
        P(),
        P("dp", None),
    )
    out_specs = (
        P(("dp", "mp"), None),
        P(("dp", "mp"), None),
        P(None, None, "mp"),
        P(None, "mp"),
        P("mp", None),
        P(),
        P(None, "mp"),
        P("mp"),
        P("mp", None),
        P(),
        P(),
        P(),
        P(),
        P(),
        P(),
        P(),
        P(),
    )
    return jax.shard_map(shards, mesh=mesh, in_specs=in_specs, out_specs=out_specs, check_vma=False)
```

```python
import functools
import math

import jax
import jax.numpy as jnp
from jax import lax
from jax.experimental import pallas as pl
from jax.experimental.pallas import tpu as pltpu
from jax.sharding import PartitionSpec as P

F32 = jnp.float32
BF16 = jnp.bfloat16
DH = 64
SEQ_LEN = 1024
NORM_EPS = 1e-06
PIECES = 8
SEG_COLS = 128
LOG2E = math.log2(math.e)
SCALE = DH ** (-0.5)
BITS_A = (2, 4, 1)
BITS_B = (4, 2, 1)
MLP_KIND = ("a", "a", "b", "b")
VMEM_LIMIT = 26 * 1024 * 1024
VMEM_LARGE = 56 * 1024 * 1024


def mm(a, b):
    return lax.dot_general(a, b, (((1,), (0,)), ((), ())), preferred_element_type=F32)


def mm_nt(a, b):
    return lax.dot_general(a, b, (((1,), (1,)), ((), ())), preferred_element_type=F32)


def mm_tn(a, b):
    return lax.dot_general(a, b, (((0,), (0,)), ((), ())), preferred_element_type=F32)


def call(kernel, out_shape, flops=0, bytes_accessed=0, vmem_limit=VMEM_LIMIT, **kw):
    return pl.pallas_call(
        kernel,
        out_shape=out_shape,
        compiler_params=pltpu.CompilerParams(vmem_limit_bytes=vmem_limit),
        cost_estimate=pl.CostEstimate(
            flops=flops, bytes_accessed=bytes_accessed, transcendentals=0
        ),
        **kw,
    )


def sds(shape, dtype):
    return jax.ShapeDtypeStruct(shape, dtype)


def row_norm(x):
    mean = jnp.mean(x, axis=-1, keepdims=True)
    cen = x - mean
    rstd = lax.rsqrt(jnp.mean(cen * cen, axis=-1, keepdims=True) + NORM_EPS)
    return cen * rstd, rstd


def row_norm_back(f, n, rstd):
    mean_f = jnp.mean(f, axis=-1, keepdims=True)
    mean_fn = jnp.mean(f * n, axis=-1, keepdims=True)
    return (f - mean_f - n * mean_fn) * rstd


def col_norm(x):
    mean = jnp.mean(x, axis=0, keepdims=True)
    cen = x - mean
    rstd = lax.rsqrt(jnp.mean(cen * cen, axis=0, keepdims=True) + NORM_EPS)
    return cen * rstd, rstd


def col_norm_back(f, n, rstd):
    mean_f = jnp.mean(f, axis=0, keepdims=True)
    mean_fn = jnp.mean(f * n, axis=0, keepdims=True)
    return (f - mean_f - n * mean_fn) * rstd


def lane_fold(x):
    out = x[:, :128]
    for t in range(1, x.shape[1] // 128):
        out = out + x[:, t * 128 : (t + 1) * 128]
    return out


def offset_of(s, bits):
    return sum(bit for t, bit in enumerate(bits) if (s >> t) & 1)


def build_q_aug(q_pre, qg, qs, qaug_ref):
    n, rstd = col_norm(q_pre)
    q_low = (n * qg + qs).astype(BF16)
    scaled = q_low.astype(F32) * (SCALE * LOG2E)
    hi = scaled.astype(BF16)
    lo = (scaled - hi.astype(F32)).astype(BF16)
    qaug_ref[0:DH, :] = hi
    qaug_ref[DH : 2 * DH, :] = lo
    return n, rstd, q_low


def build_k_aug(k_pre, kg, kaug_ref):
    n, rstd = col_norm(k_pre)
    k_low = (n * kg).astype(BF16)
    kaug_ref[:, 0 : 2 * DH] = jnp.concatenate([k_low, k_low], axis=0).T
    return n, rstd, k_low


def bias_col(b_ref, n):
    return b_ref[...].T[0:n, 0:1]


def prep_att_kernel(
    me_ref, w_ref, o_ref, qb_ref, ub_ref, att_ref, ob_ref, b_ref, wf_ref
):
    part = 24
    e = PIECES * part
    me = me_ref[0]
    b_ref[...] = jnp.zeros(b_ref.shape, F32)
    for s in range(3):
        wf_ref[...] = w_ref[s].astype(F32)
        rows = wf_ref[pl.ds(pl.multiple_of(me * part, 8), part), :]
        att_ref[s * part : (s + 1) * part, :] = rows
        b_ref[0:1, s * e : (s + 1) * e] = qb_ref[s : s + 1, :]
    upart = ub_ref.shape[0] // PIECES
    ub = ub_ref[...].reshape(1, PIECES * upart)
    for s in range(PIECES // 2):
        piece = jnp.zeros((1, upart), F32)
        for p in range(PIECES):
            here = (me ^ offset_of(s, BITS_A)) == p
            piece = piece + jnp.where(here, ub[:, p * upart : (p + 1) * upart], 0.0)
        b_ref[1:2, s * upart : (s + 1) * upart] = piece
    wf_ref[...] = o_ref[...].astype(F32)
    rows = wf_ref[pl.ds(pl.multiple_of(me * part, 8), part), :]
    att_ref[3 * part : 4 * part, :] = rows
    ob_ref[0:part, :] = rows
    att_ref[4 * part :, :] = b_ref[...]
    ob_ref[part:, :] = b_ref[...]


def prep_mlp_kernel(me_ref, up_ref, dn_ref, p_ref, u0_ref, u1_ref, d0_ref, d1_ref, t_ref):
    me = me_ref[0]
    upart = up_ref.shape[1] // PIECES
    t_ref[...] = up_ref[...].astype(F32).T

    def at_piece(r):
        return pl.ds(pl.multiple_of((me ^ r) * upart, 32), upart)

    p_ref[0:upart, :] = t_ref[at_piece(0), :]
    p_ref[upart:, :] = dn_ref[at_piece(0), :].astype(F32)
    for i, (u_ref, d_ref) in enumerate(((u0_ref, d0_ref), (u1_ref, d1_ref))):
        for j in range(2):
            u_ref[j] = t_ref[at_piece(offset_of(2 * i + j, BITS_A)), :].astype(BF16)
            d_ref[j] = dn_ref[at_piece(offset_of(2 * i + j, BITS_B)), :]


def attend(x_ref, wt_ref, b_ref, hv_ref, kmask_ref, qhot_ref, outs, qaug_ref, kaug_ref):
    qpre_ref, kpre_ref, vt_ref, mixt_ref, mixf_ref, mixs_ref, l_ref = outs
    e = qpre_ref.shape[0]
    full = x_ref.shape[0]
    share = full // 2
    heads = e // DH
    x = x_ref[...]
    bias = bias_col(b_ref, 3 * e)
    qpre_ref[...] = mm_nt(wt_ref[0:e, :], x) + bias[0:e]
    kpre_ref[...] = mm_nt(wt_ref[e : 2 * e, :], x) + bias[e : 2 * e]
    vt_ref[...] = (mm_nt(wt_ref[2 * e : 3 * e, :], x) + bias[2 * e :]).astype(BF16)
    qaug_ref[2 * DH :, :] = qhot_ref[...]
    kaug_ref[:, 2 * DH :] = kmask_ref[...]
    ones = jnp.ones((16, full), BF16)
    for h in range(heads):
        hs = slice(h * DH, (h + 1) * DH)
        build_q_aug(qpre_ref[hs, :], hv_ref[:, 0:1], hv_ref[:, 1:2], qaug_ref)
        build_k_aug(kpre_ref[hs, :], hv_ref[:, 2:3], kaug_ref)
        prob = jnp.exp2(mm(kaug_ref[...], qaug_ref[...])).astype(BF16)
        vaug = jnp.concatenate([vt_ref[hs, :], ones], axis=0)
        o = mm(vaug, prob)
        total = o[DH : DH + 1, :]
        l_ref[h : h + 1, :] = total
        mix = o[0:DH, :] / total
        mixf_ref[hs, :] = mix
        mixt_ref[hs, :] = mix[:, 0:share].astype(BF16)
        at = h * share
        for c in range(0, share, 256):
            block_no, lane = divmod(at + c, x.shape[1])
            mixs_ref[block_no * DH : (block_no + 1) * DH, lane : lane + 256] = mix[
                :, share + c : share + c + 256
            ]


def attn_fwd_own_kernel(
    blk_ref, x_ref, xf_ref, g_ref, s_ref, wt_ref, b_ref, hv_ref, kmask_ref, qhot_ref, n_ref, *refs
):
    share = x_ref.shape[0]
    for i, ref in enumerate((x_ref, xf_ref)):
        n, _ = row_norm(ref[...].astype(F32))
        n_ref[i * share : (i + 1) * share, :] = (n * g_ref[...] + s_ref[...]).astype(BF16)
    attend(n_ref, wt_ref, b_ref, hv_ref, kmask_ref, qhot_ref, refs[:7], *refs[7:])


def attn_fwd_kernel(
    ia_ref, ib_ref, a0_ref, a1_ref, b0_ref, b1_ref, x_ref, b_ref, hv_ref, kmask_ref, qhot_ref,
    wt_ref, ow_ref, ow1_ref, ow3_ref, *refs,
):
    wa_ref, wb_ref = refs[-2:]
    part = 24
    e = PIECES * part
    half = PIECES // 2
    wa_ref[0:half] = a0_ref[...]
    wa_ref[half:] = a1_ref[...]
    wb_ref[0:half] = b0_ref[...]
    wb_ref[half:] = b1_ref[...]

    def rows(w_ref, i_ref, at):
        return jnp.concatenate(
            [w_ref[i_ref[p], at * part : (at + 1) * part, :] for p in range(PIECES)], axis=0
        ).astype(BF16)

    wt_ref[0:e, :] = rows(wa_ref, ia_ref, 0)
    wt_ref[e : 2 * e, :] = rows(wa_ref, ia_ref, 1)
    wt_ref[2 * e : 3 * e, :] = rows(wb_ref, ib_ref, 0)
    ow_ref[...] = rows(wb_ref, ib_ref, 1)
    ow1_ref[...] = rows(wa_ref, ia_ref, 2)
    ow3_ref[...] = rows(wb_ref, ib_ref, 2)
    attend(x_ref, wt_ref, b_ref, hv_ref, kmask_ref, qhot_ref, refs[:7], *refs[7:9])


def unmix(ref, heads, share):
    width = ref.shape[1]
    rows = []
    for h in range(heads):
        cols = []
        for c in range(0, share, 256):
            block_no, lane = divmod(h * share + c, width)
            cols.append(ref[block_no * DH : (block_no + 1) * DH, lane : lane + 256])
        rows.append(jnp.concatenate(cols, axis=1))
    return jnp.concatenate(rows, axis=0).astype(BF16)


def mix_of(ref, share):
    if ref.dtype == BF16:
        return ref[...]
    return unmix(ref, ref.shape[0] * ref.shape[1] // (DH * share), share)


def out_norm2_kernel(nslot, blk_ref, x_ref, *refs):
    mixes = refs[:nslot]
    ws = refs[nslot : 2 * nslot]
    ob_ref, g_ref, s_ref, mid_ref, sec_ref, secf_ref = refs[2 * nslot :]
    acc = x_ref[...].astype(F32) + ob_ref[...]
    for k in range(nslot):
        acc = acc + mm_tn(mix_of(mixes[k], x_ref.shape[0]), ws[k][...])
    mid_ref[...] = acc
    n, _ = row_norm(acc)
    sec = (n * g_ref[...] + s_ref[...]).astype(BF16)
    sec_ref[...] = sec
    secf_ref[...] = sec.astype(F32)


def mlp_kernel(
    kind, keeps, sec_ref, secp_ref, cot_ref, cotp_ref, u0_ref, u1_ref, d0_ref, d1_ref, b_ref, *refs
):
    if keeps:
        p_ref, hid_ref, gp_ref, ub_ref, db_ref, k0_ref, k1_ref, s0_ref, s1_ref, gb_ref = refs
    else:
        hid_ref, gp_ref, ub_ref, db_ref, up_ref, uq_ref, k0_ref, k1_ref, sd_ref, gb_ref = refs
    part = u0_ref.shape[1]
    share = sec_ref.shape[0]
    up = jnp.concatenate([u0_ref[0], u0_ref[1], u1_ref[0], u1_ref[1]], axis=0).astype(BF16)
    down = jnp.concatenate([d0_ref[0], d1_ref[0], d0_ref[1], d1_ref[1]], axis=0).astype(BF16)
    ub_ref[...] = up
    db_ref[...] = down
    bias = b_ref[1:2, 0 : up.shape[0]]
    for r, (s_ref, c_ref) in enumerate(((sec_ref, cot_ref), (secp_ref, cotp_ref))):
        rows = slice(r * share, (r + 1) * share)
        sec = s_ref[...].astype(BF16)
        cot = c_ref[...].astype(BF16)
        pre = mm_nt(sec, up) + bias
        cdf = 0.5 * (1.0 + lax.erf(pre * (1.0 / math.sqrt(2.0))))
        hid = (pre * cdf).astype(BF16)
        pdf = jnp.exp(-0.5 * pre * pre) * (1.0 / math.sqrt(2.0 * math.pi))
        gpre = (mm_nt(cot, down) * (cdf + pre * pdf)).astype(BF16)
        hid_ref[rows, :] = hid
        gp_ref[rows, :] = gpre
        gb_r = jnp.sum(gpre.astype(F32), axis=0, keepdims=True)
        gd_r = mm_tn(hid, cot)
        gu_r = mm_tn(gpre, sec)
        if r == 0:
            gb, gd, gu = gb_r, gd_r, gu_r
        else:
            gb, gd, gu = gb + gb_r, gd + gd_r, gu + gu_r
    gb_ref[...] = gb
    order = (0, 1, 2, 3) if kind == "a" else (0, 2, 1, 3)
    gu_at = [gu[i * part : (i + 1) * part] for i in order]
    gd_at = [gd[i * part : (i + 1) * part] for i in order]
    if keeps:
        gu_at[3] = gu_at[3] + p_ref[0:part, :]
        gu_at[2] = gu_at[2] + p_ref[part:, :]
        for i, ref in enumerate((k0_ref, k1_ref, s0_ref, s1_ref)):
            ref[0:part, :] = gu_at[i]
            ref[part:, :] = gd_at[i]
    else:
        up_ref[0:part, :] = gu_at[3]
        up_ref[part:, :] = gu_at[2]
        uq_ref[0:part, :] = gu_at[0]
        uq_ref[part:, :] = gu_at[1]
        k0_ref[...] = gd_at[0]
        k1_ref[...] = gd_at[1]
        sd_ref[0:part, :] = gd_at[3]
        sd_ref[part:, :] = gd_at[2]


def down_kernel(nslot, *refs):
    hids = refs[:nslot]
    gps = refs[nslot : 2 * nslot]
    ubs = refs[2 * nslot : 3 * nslot]
    dbs = refs[3 * nslot : 4 * nslot]
    outs = refs[4 * nslot :]
    cat = lambda refs, axis: jnp.concatenate([r[...] for r in refs], axis=axis)
    share = outs[0].shape[1]
    for i, (rows_of, w_of) in enumerate(((hids, dbs), (gps, ubs))):
        w = cat(w_of, 0)
        for r, out_ref in enumerate(outs):
            rows = slice(r * share, (r + 1) * share)
            out_ref[i] = mm(jnp.concatenate([a[rows, :] for a in rows_of], axis=1), w)


def mid_kernel(nslot, mid_ref, own_ref, got_ref, cot_ref, db_ref, g_ref, *refs):
    ows = refs[:nslot]
    gmts = refs[nslot : 2 * nslot]
    bo_ref, gm_ref, low_ref, st_ref = refs[2 * nslot :]
    mid = mid_ref[...]
    n, rstd = row_norm(mid)
    e = own_ref[1] + got_ref[1]
    cot = cot_ref[...].astype(F32)
    gm = cot + row_norm_back(e * g_ref[...], n, rstd)
    gm_ref[...] = gm
    gm_low = gm.astype(BF16)
    low_ref[...] = gm_low
    for k in range(nslot):
        gmts[k][...] = mm_nt(ows[k][...], gm_low).astype(gmts[k].dtype)
    bo_ref[...] = (mid + (own_ref[0] + got_ref[0]) + db_ref[...]).astype(BF16)
    st_ref[0:1, :] = jnp.sum(e * n, axis=0, keepdims=True)
    st_ref[1:2, :] = jnp.sum(e, axis=0, keepdims=True)
    st_ref[2:3, :] = jnp.sum(gm_low.astype(F32), axis=0, keepdims=True)
    st_ref[3:4, :] = jnp.sum(cot, axis=0, keepdims=True)
    st_ref[4:8, :] = jnp.zeros((4, mid.shape[1]), F32)


def out_grad_kernel(nslot, idx_ref, low_ref, *refs):
    mixts = refs[:nslot]
    gow_keep, gow_send = refs[nslot:]
    part = 24
    gm_low = low_ref[...]
    for k in range(nslot):
        g = mm(mix_of(mixts[k], gm_low.shape[0]), gm_low)
        for p in range(PIECES):
            at = idx_ref[p]
            rows = slice(k * part, (k + 1) * part)

            @pl.when(at < PIECES // 2)
            def _():
                gow_keep[at, rows, :] = g[p * part : (p + 1) * part, :]

            @pl.when(at >= PIECES // 2)
            def _():
                gow_send[at - PIECES // 2, rows, :] = g[p * part : (p + 1) * part, :]


def attn_bwd_kernel(
    ncuts, idx_ref, x_ref, qpre_ref, kpre_ref, vt_ref, wt_ref, gmt_ref, gmtp_ref, mixf_ref, l_ref,
    hv_ref, kmask_ref, qhot_ref, *refs
):
    if ncuts:
        gn_in, gk_ref, gs_ref, *gn_refs = refs[: 3 + ncuts]
    else:
        gk_ref, gs_ref, gn_ref = refs[:3]
    st_ref, gb_ref, qaug_ref, kaug_ref, gpt_ref = refs[-5:]
    part = 24
    e = PIECES * part
    full = x_ref.shape[0]
    heads = e // DH
    qaug_ref[2 * DH :, :] = qhot_ref[...]
    kaug_ref[:, 2 * DH :] = kmask_ref[...]
    qg, qs, kg = hv_ref[:, 0:1], hv_ref[:, 1:2], hv_ref[:, 2:3]
    qg_sum = jnp.zeros((DH, 128), F32)
    qs_sum = jnp.zeros((DH, 128), F32)
    kg_sum = jnp.zeros((DH, 128), F32)
    row_no = lax.broadcasted_iota(jnp.int32, (DH, full), 0)
    one_rows = (row_no < 3).astype(F32).astype(BF16)
    for h in range(heads):
        hs = slice(h * DH, (h + 1) * DH)
        qn, qr, q_low = build_q_aug(qpre_ref[hs, :], qg, qs, qaug_ref)
        kn, kr, k_low = build_k_aug(kpre_ref[hs, :], kg, kaug_ref)
        inv = 1.0 / l_ref[h : h + 1, :]
        gm = jnp.concatenate(
            [gmt_ref[hs, :].astype(F32), gmtp_ref[hs, :].astype(BF16).astype(F32)], axis=1
        )
        go_low = (gm * inv).astype(BF16)
        delta = -jnp.sum(go_low.astype(F32) * mixf_ref[hs, :], axis=0, keepdims=True)
        d0 = delta.astype(BF16).astype(F32)
        d1 = (delta - d0).astype(BF16).astype(F32)
        d2 = delta - d0 - d1
        extra = jnp.where(
            row_no == 0, d0, jnp.where(row_no == 1, d1, jnp.where(row_no == 2, d2, 0.0))
        ).astype(BF16)
        goaug = jnp.concatenate([go_low, extra], axis=0)
        vaug = jnp.concatenate([vt_ref[hs, :], one_rows], axis=0).T
        prob = jnp.exp2(mm(kaug_ref[...], qaug_ref[...]))
        ds = (prob * mm(vaug, goaug)).astype(BF16)
        gv = mm_nt(go_low, prob.astype(BF16))
        gk = mm_nt(q_low, ds) * SCALE
        gq = mm(k_low, ds) * SCALE
        qg_sum += lane_fold(gq * qn)
        qs_sum += lane_fold(gq)
        kg_sum += lane_fold(gk * kn)
        gpt_ref[h * DH : (h + 1) * DH, :] = col_norm_back(gq * qg, qn, qr).astype(BF16)
        gpt_ref[e + h * DH : e + (h + 1) * DH, :] = col_norm_back(gk * kg, kn, kr).astype(BF16)
        gpt_ref[2 * e + h * DH : 2 * e + (h + 1) * DH, :] = gv.astype(BF16)
    st_ref[0] = qg_sum
    st_ref[1] = qs_sum
    st_ref[2] = kg_sum
    gp = gpt_ref[...]
    gb_ref[...] = lane_fold(gp.astype(F32))
    gw = mm(gp, x_ref[...])

    def put(ref, at, p):
        for s in range(3):
            ref[at, s * part : (s + 1) * part, :] = gw[s * e + p * part : s * e + (p + 1) * part, :]

    for p in range(PIECES):
        at = idx_ref[p]

        @pl.when(at < PIECES // 2)
        def _():
            put(gk_ref, at, p)

        @pl.when(at >= PIECES // 2)
        def _():
            put(gs_ref, at - PIECES // 2, p)

    gn = mm_tn(gp, wt_ref[...])
    if not ncuts:
        gn_ref[...] = gn
    else:
        at = 0
        for ref in gn_refs:
            rows = slice(at, at + ref.shape[0])
            ref[...] = gn_in[rows, :] + gn[rows]
            at += ref.shape[0]


def sums_kernel(
    nslot, blk_ref, me_ref, x_ref, xf_ref, gn_ref, mst_ref, h0_ref, h2_ref, b0_ref, b2_ref, *refs
):
    ubs = refs[:nslot]
    fars = refs[nslot:-1]
    out_ref = refs[-1]

    def fill():
        out_ref[...] = jnp.zeros_like(out_ref)
        out_ref[0:4, :] = mst_ref[0:4, :]
        heads = jnp.concatenate([h0_ref[i] + h2_ref[i] for i in range(3)], axis=0).T
        out_ref[6:7, 0 : heads.shape[1]] = jnp.sum(heads, axis=0, keepdims=True)
        me = me_ref[0]
        upart = out_ref.shape[1] // PIECES
        for row, k in zip((8, 10, 12, 14), (0, 2, 1, 3)):
            if k % 2 == 0:
                cols = (b0_ref if k == 0 else b2_ref)[...].T
                out_ref[row : row + 1, 0 : cols.shape[1]] = jnp.sum(cols, axis=0, keepdims=True)
            mine = ubs[k][...]
            for p in range(PIECES):
                piece = jnp.zeros((1, upart), F32)
                for t in range(PIECES // 2):
                    here = (me ^ offset_of(t, BITS_A)) == p
                    piece = piece + jnp.where(here, mine[:, t * upart : (t + 1) * upart], 0.0)
                out_ref[row + 1 : row + 2, p * upart : (p + 1) * upart] = piece

    fill()

    def add(x, e):
        n, _ = row_norm(x.astype(F32))
        out_ref[4:5, :] += jnp.sum(e * n, axis=0, keepdims=True)
        out_ref[5:6, :] += jnp.sum(e, axis=0, keepdims=True)

    add(x_ref[...], gn_ref[...])
    at = 0
    for ref in fars:
        add(xf_ref[at : at + ref.shape[0], :], ref[...])
        at += ref.shape[0]


def small_out_kernel(a_ref, b_ref, qb_ref, h0_ref, h1_ref, h2_ref, *rows):
    total = a_ref[...] + b_ref[...]
    for row, ref in zip((0, 1, 2, 3, 4, 5, 9), rows):
        ref[...] = total[row]
    for i, ref in enumerate((h0_ref, h1_ref, h2_ref)):
        ref[...] = total[6, i * DH : (i + 1) * DH]
        n = qb_ref.shape[1]
        qb_ref[i : i + 1, :] = total[8:9, i * n : (i + 1) * n]


def final_kernel(blk_ref, x_ref, gn_ref, *refs):
    gots = refs[:-3]
    gm_ref, g_ref, out_ref = refs[-3:]
    at = 0
    for ref in gots:
        rows = slice(at, at + ref.shape[0])
        n, rstd = row_norm(x_ref[rows, :].astype(F32))
        f = (gn_ref[rows, :] + ref[...]) * g_ref[...]
        out_ref[rows, :] = (gm_ref[rows, :] + row_norm_back(f, n, rstd)).astype(BF16)
        at += ref.shape[0]


def unpack_mlp_kernel(ia_ref, ib_ref, a_ref, b_ref, up_ref, down_ref, s_ref):
    part = s_ref.shape[2]
    half = PIECES // 2
    for w in range(2):
        for j in range(half):
            rows = slice((w * half + j) * part, (w * half + j + 1) * part)
            s_ref[w, j] = a_ref[rows, :]
            s_ref[w, half + j] = b_ref[rows, :]
    up_ref[...] = jnp.concatenate([s_ref[0, ia_ref[p]] for p in range(PIECES)], axis=0).T
    for p in range(PIECES):
        down_ref[p * part : (p + 1) * part, :] = s_ref[1, ib_ref[p]]


def unpack_att_kernel(i_ref, a_ref, b_ref, qkv_ref, out_ref, s_ref):
    rows = s_ref.shape[1]
    part = rows // 4
    half = PIECES // 2
    for j in range(half):
        s_ref[j] = a_ref[j * rows : (j + 1) * rows, :]
        s_ref[half + j] = b_ref[j * rows : (j + 1) * rows, :]
    for s, ref in enumerate((qkv_ref.at[0], qkv_ref.at[1], qkv_ref.at[2], out_ref)):
        for p in range(PIECES):
            ref[p * part : (p + 1) * part, :] = s_ref[i_ref[p], s * part : (s + 1) * part, :]


def swap_mp(a, k, size):
    return lax.ppermute(a, "mp", [(s, s ^ k) for s in range(size)])


def swap_plane(a, bit, size):
    return lax.ppermute(a, "dp", [(d, d ^ bit) for d in range(size)])


def storage_of(r, bits):
    return sum(jnp.where((r & bit) != 0, 1 << t, 0) for t, bit in enumerate(bits))


class Stages:
    def __init__(self):
        self.live = {}

    def __setitem__(self, name, value):
        self.live[name] = value

    def __getitem__(self, name):
        return self.live[name]

    def pop(self, name):
        return self.live.pop(name)

    def fence(self, *still_flying):
        now = {n: a for n, a in self.live.items() if n not in still_flying}
        leaves, tree = jax.tree.flatten(now)
        self.live.update(jax.tree.unflatten(tree, lax.optimization_barrier(leaves)))


def shards(
    tokens,
    seg_ids,
    qkv_weight,
    qkv_bias,
    out_weight,
    out_bias,
    up_weight,
    up_bias,
    down_weight,
    down_bias,
    norm1_gain,
    norm1_shift,
    query_gain,
    query_shift,
    key_gain,
    norm2_gain,
    norm2_shift,
    cotangent,
):
    ndp = lax.axis_size("dp")
    nmp = lax.axis_size("mp")
    dp_no = lax.axis_index("dp")
    mp_no = lax.axis_index("mp")
    me = dp_no % PIECES
    row_count, width = tokens.shape
    share = row_count // nmp
    full = SEQ_LEN
    assert full == 2 * share and nmp == 4 and ndp % PIECES == 0
    e = qkv_weight.shape[2]
    part = e // PIECES
    units = up_weight.shape[1]
    upart = units // PIECES
    half = PIECES // 2
    mine = half * upart
    core, px, py = 1, 2, 4

    vmem = pl.BlockSpec(memory_space=pltpu.VMEM)
    smem = pl.BlockSpec(memory_space=pltpu.SMEM)
    row1 = lambda v: v.reshape(1, -1)
    col = lambda v: v.reshape(-1, 1)
    swap = lambda a, bit: swap_plane(a, bit, ndp)
    zswap = lambda a, k: swap_mp(a, k, nmp)
    v = Stages()

    me1 = me.astype(jnp.int32).reshape(1)
    qkv_t = jnp.swapaxes(qkv_weight, 1, 2)
    wt0 = qkv_t.reshape(3 * e, width)
    att_piece, ob_piece, bias0 = call(
        prep_att_kernel,
        (
            sds((4 * part + 8, width), F32),
            sds((part + 8, width), F32),
            sds((8, width), F32),
        ),
        bytes_accessed=3_000_000,
        vmem_limit=VMEM_LARGE,
        in_specs=[smem] + [vmem] * 4,
        out_specs=(vmem,) * 3,
        scratch_shapes=[pltpu.VMEM((e, width), F32)],
    )(me1, qkv_t, out_weight, qkv_bias, up_bias)
    mlp_piece, u0, u1, d0, d1 = call(
        prep_mlp_kernel,
        (sds((2 * upart, width), F32), *[sds((2, upart, width), BF16)] * 4),
        bytes_accessed=6_000_000,
        vmem_limit=VMEM_LARGE,
        in_specs=[smem] + [vmem] * 2,
        out_specs=(vmem,) * 5,
        scratch_shapes=[pltpu.VMEM((units, width), F32)],
    )(me1, up_weight, down_weight)

    n_gn = (176, 136, 120, 80)
    n_q0 = 40
    numbers = jnp.arange(PIECES, dtype=jnp.int32)
    idx_a = storage_of(numbers ^ me, BITS_A).astype(jnp.int32)
    idx_b = storage_of(numbers ^ me, BITS_B).astype(jnp.int32)

    block = 256
    per = share // block
    steps = 2 * per
    tile_no = jnp.arange(steps, dtype=jnp.int32)
    blk = jnp.where(tile_no < per, mp_no * per + tile_no, (mp_no ^ 1) * per + tile_no - per).astype(
        jnp.int32
    )
    const2 = lambda t, b: (0, 0)
    tok_spec = pl.BlockSpec((block, width), lambda t, b: (b[t], 0))
    run_spec = pl.BlockSpec((block, width), lambda t, b: (t, 0))
    vec_spec = pl.BlockSpec((1, width), const2)

    seg_own = lax.dynamic_slice_in_dim(seg_ids, mp_no * share, share, 0)
    seg_other = lax.dynamic_slice_in_dim(seg_ids, (mp_no ^ 1) * share, share, 0)
    seg_keys = jnp.concatenate([seg_own, seg_other])
    qhot = (
        lax.broadcasted_iota(jnp.int32, (SEG_COLS, full), 0) == seg_keys[None, :]
    ).astype(BF16)
    kmask = jnp.where(
        lax.broadcasted_iota(jnp.int32, (full, SEG_COLS), 1) == seg_keys[:, None], 0.0, -1e30
    ).astype(BF16)
    hv = jnp.stack([query_gain, query_shift, key_gain], axis=1)
    scratch = [
        pltpu.VMEM((2 * DH + SEG_COLS, full), BF16),
        pltpu.VMEM((full, 2 * DH + SEG_COLS), BF16),
    ]

    def whole(a):
        return pl.BlockSpec(a.shape, lambda t: (0,) * len(a.shape))

    def bias_at(block_no):
        return pl.BlockSpec((8, width), lambda t: (block_no, 0))

    att_names = ["qpre", "kpre", "vt", "mixt", "mixf", "mixs", "l"]
    att_shapes = [
        sds((e, full), F32),
        sds((e, full), F32),
        sds((e, full), BF16),
        sds((e, share), BF16),
        sds((e, full), F32),
        sds((e * share // width, width), F32),
        sds((8, full), F32),
    ]
    mix_rows = e * share // width

    def run_attn_own():
        all_of = lambda a: pl.BlockSpec(a.shape, lambda t, b: (0,) * len(a.shape))
        rest = [wt0, bias0, hv, kmask, qhot]
        shapes = [sds((full, width), BF16)] + att_shapes
        v["normed"], *outs = call(
            attn_fwd_own_kernel,
            tuple(shapes),
            flops=2 * (full * width * e * 3 + full * full * e * 8),
            bytes_accessed=10_000_000,
            grid_spec=pltpu.PrefetchScalarGridSpec(
                num_scalar_prefetch=1,
                grid=(1,),
                in_specs=[
                    pl.BlockSpec((share, width), lambda t, b: (b[0] // per, 0)),
                    pl.BlockSpec((share, width), lambda t, b: (b[per] // per, 0)),
                    vec_spec,
                    vec_spec,
                    *[all_of(a) for a in rest],
                ],
                out_specs=tuple(all_of(a) for a in shapes),
                scratch_shapes=scratch,
            ),
        )(blk, tokens, tokens, row1(norm1_gain), row1(norm1_shift), *rest)
        v["st0"] = dict(zip(att_names, outs))
        v["st0"]["wt"] = wt0
        v["st0"]["ow"] = out_weight

    def run_attn_far():
        shapes = [sds((3 * e, width), BF16)] + [sds((e, width), BF16)] * 3 + att_shapes
        args = [
            *v.pop("ta"), *v.pop("tb"), v["normed"], v["t2"], hv, kmask, qhot,
        ]
        specs = [whole(a) for a in args]
        specs[5] = bias_at(4 * part // 8)
        outs = call(
            attn_fwd_kernel,
            tuple(shapes),
            flops=2 * (full * width * e * 3 + full * full * e * 8),
            bytes_accessed=10_000_000,
            grid=(1,),
            vmem_limit=VMEM_LARGE,
            in_specs=[smem, smem] + specs,
            out_specs=tuple(whole(a) for a in shapes),
            scratch_shapes=scratch
            + [pltpu.VMEM((PIECES, 3 * part, width), F32)] * 2,
        )(idx_a, idx_b, *args)
        v["st2"] = dict(zip(["wt", "ow", "ow1", "ow3"] + att_names, outs))

    def by_slot():
        st0, st2 = v["st0"], v["st2"]
        mixes = [st0["mixt"], v["mix0"], st2["mixt"], v["mix2"]]
        ows = [st0["ow"], st2["ow1"], st2["ow"], st2["ow3"]]
        return mixes, ows

    def run_out():
        own_spec = pl.BlockSpec((share, width), lambda t, b: (b[0] // per, 0))
        whole2 = lambda shape: pl.BlockSpec(shape, lambda t, b: (0,) * len(shape))
        mixes, ows = by_slot()
        v["middle"], v["second"], v["sec_f"] = call(
            functools.partial(out_norm2_kernel, nmp),
            (sds((share, width), F32), sds((share, width), BF16), sds((share, width), F32)),
            flops=2 * share * width * e * nmp,
            bytes_accessed=8_000_000,
            grid_spec=pltpu.PrefetchScalarGridSpec(
                num_scalar_prefetch=1,
                grid=(1,),
                in_specs=[own_spec]
                + [whole2((e, share)), whole2((mix_rows, width))] * 2
                + [whole2((e, width))] * nmp
                + [whole2((1, width))] * 3,
                out_specs=(whole2((share, width)),) * 3,
            ),
        )(blk, tokens, *mixes, *ows, row1(out_bias), row1(norm2_gain), row1(norm2_shift))

    def run_mlp(k, up, down, bias, block_no):
        keeps = k % 2 == 0
        args = [
            v["second"], v["sec_p"], v["cot"], v["cot_p"], up[0], up[1], down[0], down[1], bias,
        ]
        if keeps:
            args.append(v.pop(f"p{k + 1}"))
        specs = [whole(a) for a in args]
        specs[8] = bias_at(block_no)
        piece = lambda n: sds((n * upart, width), F32)
        shapes = (
            *[sds((full, mine), BF16)] * 2,
            *[sds((mine, width), BF16)] * 2,
            *([piece(2)] * 4 if keeps else [piece(2), piece(2), piece(1), piece(1), piece(2)]),
            sds((1, mine), F32),
        )
        res = call(
            functools.partial(mlp_kernel, MLP_KIND[k], keeps),
            shapes,
            flops=2 * full * width * mine * 4,
            bytes_accessed=12_000_000,
            grid=(1,),
            in_specs=specs,
            out_specs=tuple(whole(a) for a in shapes),
        )(*args)
        v[f"h{k}"] = res[:4]
        v[f"ubg{k}"] = res[-1]
        if keeps:
            v[f"w{k}"] = res[4:8]
        else:
            v[f"p{k}"], v[f"q{k}u"] = res[4], res[5]
            v[f"w{k}"] = res[6:9]

    def run_down():
        return call(
            functools.partial(down_kernel, nmp),
            (sds((2, share, width), F32),) * 2,
            flops=4 * full * width * mine * nmp,
            bytes_accessed=17_000_000,
            vmem_limit=40 * 1024 * 1024,
            in_specs=[vmem] * (4 * nmp),
            out_specs=(vmem,) * 2,
        )(*[v[f"h{k}"][i] for i in range(4) for k in range(nmp)])

    def run_mid():
        mixes, ows = by_slot()
        shapes = (
            *[sds((e, share), F32 if k % 2 else BF16) for k in range(nmp)],
            sds((share, width), BF16),
            sds((share, width), F32),
            sds((share, width), BF16),
            sds((8, width), F32),
        )
        *gmts, bo, gm, low, mst = call(
            functools.partial(mid_kernel, nmp),
            shapes,
            flops=2 * share * width * e * nmp,
            bytes_accessed=12_000_000,
            in_specs=[vmem] * (6 + nmp),
            out_specs=(vmem,) * (4 + nmp),
        )(
            v["middle"], v.pop("acc_own"), v.pop("acc_got"), v["cot"], row1(down_bias),
            row1(norm2_gain), *ows,
        )
        v["block_out"], v["gm"], v["mst"] = bo, gm, mst
        for k in range(nmp):
            v[f"gmt{k}"] = gmts[k]
        return low

    def run_out_grad(low):
        mixes, ows = by_slot()
        args = [low, *mixes]
        specs = [whole(a) for a in args]
        for k in (1, 3):
            specs[1 + k] = pl.BlockSpec((mix_rows, width), lambda t: (0, 0))
        shapes = (sds((half, nmp * part, width), F32),) * 2
        v["o"] = call(
            functools.partial(out_grad_kernel, nmp),
            shapes,
            flops=2 * share * width * e * nmp,
            bytes_accessed=5_000_000,
            grid=(1,),
            in_specs=[smem] + specs,
            out_specs=tuple(whole(a) for a in shapes),
        )(idx_a, *args)

    def run_attn_bwd(k, got, idx, first):
        st = v.pop(f"st{k}")
        args = [
            idx, v["normed"], st["qpre"], st["kpre"], st["vt"], st["wt"], v.pop(f"gmt{k}"),
            v.pop(got), st["mixf"], st["l"], hv, kmask, qhot,
        ]
        cuts_now = (full,) if first else (share, *n_gn)
        if not first:
            args.append(v.pop("gn"))
        keep, send, *gn, hst, gb = call(
            functools.partial(attn_bwd_kernel, 0 if first else len(cuts_now)),
            (
                sds((half, 3 * part, width), F32),
                sds((half, 3 * part, width), F32),
                *[sds((n, width), F32) for n in cuts_now],
                sds((3, DH, 128), F32),
                sds((3 * e, 128), F32),
            ),
            flops=2 * (full * width * e * 6 + full * full * e * 20),
            bytes_accessed=14_000_000,
            in_specs=[smem] + [vmem] * (len(args) - 1),
            out_specs=(vmem,) * (4 + len(cuts_now)),
            scratch_shapes=scratch + [pltpu.VMEM((3 * e, full), BF16)],
        )(*args)
        v[f"q{k}"] = (keep, send)
        if first:
            v["gn"] = gn[0]
        else:
            v["gn_own"], v["gn_far"] = gn[0], tuple(gn[1:])
        v[f"hst{k}"] = hst
        v[f"qbg{k}"] = gb

    def g1(n):
        a, b = v[n + "a"], v[n + "b"]
        v[n + "a"] = (a, swap(a, px))
        v[n + "b"] = (b, swap(b, py))

    def g2(n):
        a, b = (jnp.stack(v[n + t]) for t in "ab")
        v[n + "a"] = (a, swap(a, py))
        v[n + "b"] = (b, swap(b, px))

    def g3(n):
        a, b = (jnp.concatenate(v[n + t], axis=0) for t in "ab")
        v[n + "a"] = (a, swap(a, core))
        v[n + "b"] = (b, swap(b, core))

    def r1(n):
        keep, send = v[n]
        v[n] = (keep, swap(send, core))

    def r2(n, kind):
        keep, got = v[n]
        keep_sum = keep[:2] + got[:2]
        v[n] = (keep_sum, swap(keep[2:] + got[2:], py if kind == "a" else px))

    def r3(n, kind):
        keep, got = v[n]
        v[n] = (keep[0] + got[0], swap(keep[1] + got[1], px if kind == "a" else py))

    def r4(n):
        keep, got = v[n]
        v[n] = keep + got

    def first_link(k):
        return py if MLP_KIND[k] == "a" else px

    def second_link(k):
        return px if MLP_KIND[k] == "a" else py

    def c1(k):
        k0, k1, s0, s1 = v[f"w{k}"]
        v[f"w{k}"] = (k0, k1, s0, swap(s1, first_link(k)))

    def c0(k):
        k0, k1, s0, g1 = v[f"w{k}"]
        v[f"w{k}"] = (k0, k1, g1, swap(s0, first_link(k)))

    def c2u(k):
        k0, k1, g1, g0 = v[f"w{k}"]
        q0, q1 = v.pop(f"q{k + 1}u")
        sent = k1[:upart] + q1 + g1[:upart]
        v[f"w{k}"] = (k0, k1, g1, g0, q0, swap(sent, second_link(k)))

    def c2d(k):
        k0, k1, g1, g0, q, gu = v[f"w{k}"]
        up_sum = k0[:upart] + g0[:upart] + q + gu
        sent = k1[upart:] + g1[upart:]
        v[f"w{k}"] = (up_sum, k0[upart:], g0[upart:], swap(sent, second_link(k)))

    def c3(k):
        up_sum, kd, g0, gd = v[f"w{k}"]
        v[f"w{k}"] = (up_sum, kd + g0 + gd + v.pop(f"d{k + 1}"))

    def e1(k):
        k0, k1, s = v[f"w{k}"]
        v[f"w{k}"] = (k0, k1, swap(s, first_link(k)))

    def e2(k):
        k0, k1, g = v[f"w{k}"]
        v[f"w{k}"] = (k0 + g[upart:], swap(k1 + g[:upart], second_link(k)))

    def e3(k):
        k0, g = v[f"w{k}"]
        v[f"w{k}"] = k0 + g

    inner = (mp_no == 1) | (mp_no == 2)

    def middle_swap(a):
        return lax.ppermute(a, "mp", [(1, 2), (2, 1)])

    def pass_out(a):
        return lax.ppermute(a, "mp", [(1, 0), (2, 3)])

    def high_bits(a):
        bit = PIECES
        while bit < ndp:
            a = a + swap(a, bit)
            bit *= 2
        return a

    cot_all, mlp_piece = lax.optimization_barrier((cotangent, mlp_piece))
    v["cot"] = lax.dynamic_slice_in_dim(cot_all, mp_no * share, share, 0)
    v["cot_f"] = v["cot"].astype(F32)
    v["piece"] = mlp_piece
    v["o3"] = zswap(ob_piece, 3)
    v["o1"] = zswap(ob_piece, 1)
    v["t2"] = zswap(att_piece, 2)
    v.fence()
    hp = 2 * part
    t2, o1, o3 = v["t2"], v["o1"], v["o3"]
    v["ta"] = jnp.concatenate([t2[:hp], o1[:part]], axis=0)
    v["tb"] = jnp.concatenate([t2[hp : 2 * hp], o3[:part]], axis=0)
    g1("t")
    v["cot_p"] = swap(v.pop("cot_f"), core)
    v["m1"] = zswap(v["piece"], 1)
    v["mid_a"] = middle_swap(v.pop("piece"))
    run_attn_own()
    v.fence()
    m1 = v["m1"]
    to_y = jnp.concatenate([*v["ta"], m1[upart:]], axis=0)
    to_x = jnp.concatenate([*v["tb"], m1[:upart]], axis=0)
    v["ta"] = (to_y, swap(to_y, py))
    v["tb"] = (to_x, swap(to_x, px))
    v["mid_b"] = middle_swap(v.pop("m1"))
    v["mix0"] = zswap(jnp.concatenate([v["st0"].pop("mixs"), v["mid_a"]], axis=0), 1)
    v.fence()
    nt = 2 * 3 * part
    ya, yb = v.pop("ta")
    xa, xb = v.pop("tb")
    v["m1a"], v["m1b"] = (xa[nt:], xb[nt:]), (ya[nt:], yb[nt:])
    v["ta"], v["tb"] = (
        tuple(
            a.reshape(half, 3 * part, width) for a in (both_, swap(both_, core))
        )
        for both_ in (
            jnp.concatenate([ya[:nt], yb[:nt]], axis=0),
            jnp.concatenate([xa[:nt], xb[:nt]], axis=0),
        )
    )
    run_attn_far()
    g2("m1")
    v["end_b"] = pass_out(v["mid_b"])
    v.fence()
    v["mix2"] = zswap(v["st2"].pop("mixs"), 1)
    run_out()
    m3 = jnp.where(inner, v.pop("mid_a"), v.pop("end_b"))
    m2 = jnp.where(inner, v.pop("mid_b"), v["mix0"][mix_rows:])
    to_x = jnp.concatenate([m3[:upart], m2[:upart]], axis=0)
    to_y = jnp.concatenate([m3[upart:], m2[upart:]], axis=0)
    v["ma"], v["mb"] = (to_x, swap(to_x, px)), (to_y, swap(to_y, py))
    v.fence()
    for t in "ab":
        own, got = v.pop(f"m{t}")
        v[f"m3{t}"] = (own[:upart], got[:upart])
        v[f"m2{t}"] = (own[upart:], got[upart:])
    v["sec_p"] = swap(v.pop("sec_f"), core)
    run_mlp(1, v.pop("m1a"), v.pop("m1b"), v["o1"], part // 8)
    g2("m3")
    v.fence()
    v["p1"] = zswap(v["p1"], 1)
    run_mlp(3, v.pop("m3a"), v.pop("m3b"), v["o3"], part // 8)
    g2("m2")
    v.fence()
    v["p3"] = zswap(v["p3"], 1)
    run_mlp(0, (u0, u1), (d0, d1), bias0, 0)
    e1(1)
    e1(3)
    v.fence()
    run_mlp(2, v.pop("m2a"), v.pop("m2b"), v["t2"], 4 * part // 8)
    e2(1)
    e2(3)
    q1u = v.pop("q1u")
    v["q1x"] = zswap(q1u[:upart], 1)
    v["q1r"] = q1u[upart:]
    v.fence()
    e3(1)
    e3(3)
    q3u = v.pop("q3u")
    v["qm"] = zswap(jnp.concatenate([v.pop("q1r"), q3u[:upart]], axis=0), 1)
    v["q3r"] = q3u[upart:]
    c1(0)
    c1(2)
    v["acc_own"], v["acc_far"] = run_down()
    v.fence()
    c0(0)
    c0(2)
    v["q3y"] = zswap(jnp.concatenate([v.pop("q3r"), v.pop("w3")], axis=0), 1)
    v["acc_got"] = swap(v.pop("acc_far"), core)
    v["low"] = run_mid()
    v.fence()
    qm = v.pop("qm")
    q3y = v.pop("q3y")
    v["q1u"], v["q3u"] = (v.pop("q1x"), qm[:upart]), (qm[upart:], q3y[:upart])
    v["d3"] = q3y[upart:]
    c2u(0)
    c2u(2)
    v["gp2"] = zswap(v.pop("gmt3"), 1)
    run_out_grad(v.pop("low"))
    v.fence()
    c2d(0)
    c2d(2)
    v["gp0"] = zswap(v.pop("gmt1"), 1)
    v["z2x"] = zswap(v["w2"][0], 2)
    run_attn_bwd(2, "gp2", idx_b, True)
    v.fence()
    r1("q2")
    r1("o")
    v.fence()
    c3(2)
    v["d1"] = zswap(v.pop("w1"), 1)
    v["z2y"] = zswap(v.pop("w2")[1], 2)
    r2("q2", "b")
    r2("o", "a")
    run_attn_bwd(0, "gp0", idx_b, False)
    v.fence()
    c3(0)
    up_sum, down_sum = v.pop("w0")
    ma = high_bits(up_sum + v.pop("z2x"))
    mb = high_bits(down_sum + v.pop("z2y"))
    r1("q0")
    keep, got = v["o"]
    to_x = jnp.concatenate([ma, keep[1] + got[1]], axis=0)
    v["o"] = keep[0] + got[0]
    keep, got = v["q2"]
    to_y = jnp.concatenate([mb, keep[1] + got[1]], axis=0)
    v["q2"] = keep[0] + got[0]
    v["gx"], v["gy"] = (to_x, swap(to_x, px)), (to_y, swap(to_y, py))
    v["gn0"] = zswap(v["gn_far"][0], 1)
    v["small"] = call(
        functools.partial(sums_kernel, nmp),
        sds((16, width), F32),
        flops=full * width * 10,
        bytes_accessed=full * width * 6,
        grid_spec=pltpu.PrefetchScalarGridSpec(
            num_scalar_prefetch=2,
            grid=(1,),
            in_specs=[
                pl.BlockSpec((share, width), lambda t, b, m: (b[0] // per, 0)),
                pl.BlockSpec((share, width), lambda t, b, m: (b[per] // per, 0)),
                pl.BlockSpec((share, width), lambda t, b, m: (0, 0)),
                pl.BlockSpec((8, width), lambda t, b, m: (0, 0)),
                *[pl.BlockSpec((3, DH, 128), lambda t, b, m: (0, 0, 0))] * 2,
                *[pl.BlockSpec((3 * e, 128), lambda t, b, m: (0, 0))] * 2,
                *[pl.BlockSpec((1, mine), lambda t, b, m: (0, 0))] * nmp,
                *[pl.BlockSpec((n, width), lambda t, b, m: (0, 0)) for n in n_gn],
            ],
            out_specs=pl.BlockSpec((16, width), lambda t, b, m: (0, 0)),
        ),
    )(
        blk, me1, tokens, tokens, v["gn_own"], v.pop("mst"), v.pop("hst0"), v.pop("hst2"),
        v.pop("qbg0"), v.pop("qbg2"), *[v.pop(f"ubg{k}") for k in range(nmp)], *v["gn_far"],
    )
    v["small"] = v["small"] + swap(v["small"], core)
    v.fence()
    (xa, xb), (ya, yb) = v.pop("gx"), v.pop("gy")
    o = v.pop("o") + xb[upart:]
    v["q2"] = v["q2"] + yb[upart:]
    keep, got = v.pop("q0")
    q0 = keep + got
    v["q0b"], v["q0a"] = q0[:2, :n_q0], (q0[0, n_q0:], q0[2, n_q0:])
    to_y = jnp.concatenate([xa[:upart], xb[:upart], q0[1, n_q0:], q0[3, n_q0:]], axis=0)
    to_x = jnp.concatenate([ya[:upart], yb[:upart], q0[2, :n_q0], q0[3, :n_q0]], axis=0)
    v["gx"], v["gy"] = (to_x, swap(to_x, px)), (to_y, swap(to_y, py))
    v["o0"], v["o2"] = o[:part], o[2 * part : 3 * part]
    v["gn1"] = zswap(
        jnp.concatenate([v["gn_far"][1], o[part : 2 * part], o[3 * part :]], axis=0), 1
    )
    v["yq"] = zswap(v.pop("q2"), 2)
    v["small"] = v["small"] + swap(v["small"], px)
    v.fence()
    (xa, xb), (ya, yb) = v.pop("gx"), v.pop("gy")
    q0b = v.pop("q0b") + xb[2 * upart :].reshape(2, n_q0, width)
    n_rest = 3 * part - n_q0
    q0a = [
        a + yb[2 * upart + i * n_rest : 2 * upart + (i + 1) * n_rest]
        for i, a in enumerate(v.pop("q0a"))
    ]
    v["q0b"] = (q0b[0], swap(q0b[1], py))
    v["q0a"] = (q0a[0], swap(q0a[1], px))
    oz = v["gn1"][n_gn[1] :]
    v["o0"] = v["o0"] + oz[:part]
    v["yo"] = zswap(v.pop("o2") + oz[part:], 2)
    v["gn2"] = zswap(v["gn_far"][2], 1)
    v["small"] = v["small"] + swap(v["small"], py)
    n2 = 2 * upart
    v["mlp"] = jnp.concatenate([ya[:n2], yb[:n2], xa[:n2], xb[:n2]], axis=0)
    v.fence()
    q0 = jnp.concatenate([a + b for a, b in (v.pop("q0b"), v.pop("q0a"))], axis=0)
    att_sum = high_bits(
        jnp.concatenate([q0 + v.pop("yq"), v.pop("o0") + v.pop("yo")], axis=0)
    )
    v["w"] = (att_sum, swap(att_sum, px), swap(att_sum, py), swap(att_sum, px | py))
    small = high_bits(v.pop("small"))
    v["gn3"] = zswap(jnp.concatenate([v.pop("gn_far")[3], small[:8], small[12:]], axis=0), 1)
    v["small"] = small[:12] + v["gn3"][n_gn[3] :]

    mlp = v.pop("mlp")
    v["up_g"], v["down_g"] = call(
        unpack_mlp_kernel,
        (sds((width, units), F32), sds((units, width), F32)),
        bytes_accessed=10_000_000,
        in_specs=[smem, smem] + [vmem] * 2,
        out_specs=(vmem,) * 2,
        scratch_shapes=[pltpu.VMEM((2, PIECES, upart, width), F32)],
    )(idx_a, idx_b, mlp, swap(mlp, core))
    v.fence()
    input_grad = call(
        final_kernel,
        sds((share, width), BF16),
        flops=share * width * 20,
        bytes_accessed=share * width * 16,
        grid_spec=pltpu.PrefetchScalarGridSpec(
            num_scalar_prefetch=1,
            grid=(1,),
            in_specs=[
                pl.BlockSpec((share, width), lambda t, b: (b[0] // per, 0)),
                pl.BlockSpec((share, width), const2),
                *[pl.BlockSpec((n, width), const2) for n in n_gn],
                pl.BlockSpec((share, width), const2),
                vec_spec,
            ],
            out_specs=pl.BlockSpec((share, width), const2),
        ),
    )(blk, tokens, v["gn_own"], *[v[f"gn{i}"] for i in range(4)], v["gm"], row1(norm1_gain))
    w = jnp.concatenate(v.pop("w"), axis=0)
    small = v.pop("small")
    small_got = zswap(jnp.concatenate([small[:8], small[10:]], axis=0), 2)
    qkv_weight_grad, out_weight_grad = call(
        unpack_att_kernel,
        (sds((3, e, width), F32), sds((e, width), F32)),
        bytes_accessed=2 * 4 * 4 * width * e,
        in_specs=[smem] + [vmem] * 2,
        out_specs=(vmem, vmem),
        scratch_shapes=[pltpu.VMEM((PIECES, 4 * part, width), F32)],
    )(idx_a, w, swap(w, core))
    qkv_weight_grad = jnp.swapaxes(qkv_weight_grad, 1, 2)
    qkv_weight_grad, out_weight_grad, input_grad, small, small_got = lax.optimization_barrier(
        (qkv_weight_grad, out_weight_grad, input_grad, small, small_got)
    )
    qkv_bias_grad, *rows_of = call(
        small_out_kernel,
        (sds((3, e), F32), *[sds((DH,), F32)] * 3, *[sds((width,), F32)] * 7),
        bytes_accessed=100_000,
        in_specs=[vmem, vmem],
        out_specs=(vmem,) * 11,
    )(small[:10], small_got)
    heads_of, rows_of = rows_of[:3], rows_of[3:]
    return (
        v["block_out"],
        input_grad,
        qkv_weight_grad,
        qkv_bias_grad,
        out_weight_grad,
        rows_of[2],
        v["up_g"],
        rows_of[6],
        v["down_g"],
        rows_of[3],
        rows_of[4],
        rows_of[5],
        heads_of[0],
        heads_of[1],
        heads_of[2],
        rows_of[0],
        rows_of[1],
    )


def solution(mesh):
    in_specs = (
        P("dp", None),
        P("dp"),
        P(None, None, "mp"),
        P(None, "mp"),
        P("mp", None),
        P(),
        P(None, "mp"),
        P("mp"),
        P("mp", None),
        P(),
        P(),
        P(),
        P(),
        P(),
        P(),
        P(),
        P(),
        P("dp", None),
    )
    out_specs = (
        P(("dp", "mp"), None),
        P(("dp", "mp"), None),
        P(None, None, "mp"),
        P(None, "mp"),
        P("mp", None),
        P(),
        P(None, "mp"),
        P("mp"),
        P("mp", None),
        P(),
        P(),
        P(),
        P(),
        P(),
        P(),
        P(),
        P(),
    )
    return jax.shard_map(shards, mesh=mesh, in_specs=in_specs, out_specs=out_specs, check_vma=False)
```

```python
import functools
import math

import jax
import jax.numpy as jnp
from jax import lax
from jax.experimental import pallas as pl
from jax.experimental.pallas import tpu as pltpu
from jax.sharding import PartitionSpec as P

F32 = jnp.float32
BF16 = jnp.bfloat16
DH = 64
SEQ_LEN = 1024
NORM_EPS = 1e-06
PIECES = 8
SEG_COLS = 128
LOG2E = math.log2(math.e)
SCALE = DH ** (-0.5)
BITS_A = (2, 4, 1)
BITS_B = (4, 2, 1)
MLP_KIND = ("a", "a", "b", "b")
VMEM_LIMIT = 26 * 1024 * 1024
VMEM_LARGE = 56 * 1024 * 1024


def mm(a, b):
    return lax.dot_general(a, b, (((1,), (0,)), ((), ())), preferred_element_type=F32)


def mm_nt(a, b):
    return lax.dot_general(a, b, (((1,), (1,)), ((), ())), preferred_element_type=F32)


def mm_tn(a, b):
    return lax.dot_general(a, b, (((0,), (0,)), ((), ())), preferred_element_type=F32)


def call(kernel, out_shape, flops=0, bytes_accessed=0, vmem_limit=VMEM_LIMIT, **kw):
    return pl.pallas_call(
        kernel,
        out_shape=out_shape,
        compiler_params=pltpu.CompilerParams(vmem_limit_bytes=vmem_limit),
        cost_estimate=pl.CostEstimate(
            flops=flops, bytes_accessed=bytes_accessed, transcendentals=0
        ),
        **kw,
    )


def sds(shape, dtype):
    return jax.ShapeDtypeStruct(shape, dtype)


def row_norm(x):
    mean = jnp.mean(x, axis=-1, keepdims=True)
    cen = x - mean
    rstd = lax.rsqrt(jnp.mean(cen * cen, axis=-1, keepdims=True) + NORM_EPS)
    return cen * rstd, rstd


def row_norm_back(f, n, rstd):
    mean_f = jnp.mean(f, axis=-1, keepdims=True)
    mean_fn = jnp.mean(f * n, axis=-1, keepdims=True)
    return (f - mean_f - n * mean_fn) * rstd


def col_norm(x):
    mean = jnp.mean(x, axis=0, keepdims=True)
    cen = x - mean
    rstd = lax.rsqrt(jnp.mean(cen * cen, axis=0, keepdims=True) + NORM_EPS)
    return cen * rstd, rstd


def col_norm_back(f, n, rstd):
    mean_f = jnp.mean(f, axis=0, keepdims=True)
    mean_fn = jnp.mean(f * n, axis=0, keepdims=True)
    return (f - mean_f - n * mean_fn) * rstd


def lane_fold(x):
    out = x[:, :128]
    for t in range(1, x.shape[1] // 128):
        out = out + x[:, t * 128 : (t + 1) * 128]
    return out


def offset_of(s, bits):
    return sum(bit for t, bit in enumerate(bits) if (s >> t) & 1)


def build_q_aug(q_pre, qg, qs, qaug_ref):
    n, rstd = col_norm(q_pre)
    q_low = (n * qg + qs).astype(BF16)
    scaled = q_low.astype(F32) * (SCALE * LOG2E)
    hi = scaled.astype(BF16)
    lo = (scaled - hi.astype(F32)).astype(BF16)
    qaug_ref[0:DH, :] = hi
    qaug_ref[DH : 2 * DH, :] = lo
    return n, rstd, q_low


def build_k_aug(k_pre, kg, kaug_ref):
    n, rstd = col_norm(k_pre)
    k_low = (n * kg).astype(BF16)
    kaug_ref[:, 0 : 2 * DH] = jnp.concatenate([k_low, k_low], axis=0).T
    return n, rstd, k_low


def bias_col(b_ref, n):
    return b_ref[...].T[0:n, 0:1]


def prep_att_kernel(
    me_ref, w_ref, o_ref, qb_ref, ub_ref, att_ref, ob_ref, b_ref, wf_ref
):
    part = 24
    e = PIECES * part
    me = me_ref[0]
    b_ref[...] = jnp.zeros(b_ref.shape, F32)
    for s in range(3):
        wf_ref[...] = w_ref[s].astype(F32)
        rows = wf_ref[pl.ds(pl.multiple_of(me * part, 8), part), :]
        att_ref[s * part : (s + 1) * part, :] = rows
        b_ref[0:1, s * e : (s + 1) * e] = qb_ref[s : s + 1, :]
    upart = ub_ref.shape[0] // PIECES
    ub = ub_ref[...].reshape(1, PIECES * upart)
    for s in range(PIECES // 2):
        piece = jnp.zeros((1, upart), F32)
        for p in range(PIECES):
            here = (me ^ offset_of(s, BITS_A)) == p
            piece = piece + jnp.where(here, ub[:, p * upart : (p + 1) * upart], 0.0)
        b_ref[1:2, s * upart : (s + 1) * upart] = piece
    wf_ref[...] = o_ref[...].astype(F32)
    rows = wf_ref[pl.ds(pl.multiple_of(me * part, 8), part), :]
    att_ref[3 * part : 4 * part, :] = rows
    ob_ref[0:part, :] = rows
    att_ref[4 * part :, :] = b_ref[...]
    ob_ref[part:, :] = b_ref[...]


def prep_mlp_kernel(me_ref, up_ref, dn_ref, p_ref, u0_ref, u1_ref, d0_ref, d1_ref, t_ref):
    me = me_ref[0]
    upart = up_ref.shape[1] // PIECES
    t_ref[...] = up_ref[...].astype(F32).T

    def at_piece(r):
        return pl.ds(pl.multiple_of((me ^ r) * upart, 32), upart)

    p_ref[0:upart, :] = t_ref[at_piece(0), :]
    p_ref[upart:, :] = dn_ref[at_piece(0), :].astype(F32)
    for i, (u_ref, d_ref) in enumerate(((u0_ref, d0_ref), (u1_ref, d1_ref))):
        for j in range(2):
            u_ref[j] = t_ref[at_piece(offset_of(2 * i + j, BITS_A)), :].astype(BF16)
            d_ref[j] = dn_ref[at_piece(offset_of(2 * i + j, BITS_B)), :]


def attend(x_ref, wt_ref, b_ref, hv_ref, kmask_ref, qhot_ref, outs, qaug_ref, kaug_ref):
    qpre_ref, kpre_ref, vt_ref, mixt_ref, mixf_ref, mixs_ref, l_ref = outs
    e = qpre_ref.shape[0]
    full = x_ref.shape[0]
    share = full // 2
    heads = e // DH
    x = x_ref[...]
    bias = bias_col(b_ref, 3 * e)
    qpre_ref[...] = mm_nt(wt_ref[0:e, :], x) + bias[0:e]
    kpre_ref[...] = mm_nt(wt_ref[e : 2 * e, :], x) + bias[e : 2 * e]
    vt_ref[...] = (mm_nt(wt_ref[2 * e : 3 * e, :], x) + bias[2 * e :]).astype(BF16)
    qaug_ref[2 * DH :, :] = qhot_ref[...]
    kaug_ref[:, 2 * DH :] = kmask_ref[...]
    ones = jnp.ones((16, full), BF16)
    for h in range(heads):
        hs = slice(h * DH, (h + 1) * DH)
        build_q_aug(qpre_ref[hs, :], hv_ref[:, 0:1], hv_ref[:, 1:2], qaug_ref)
        build_k_aug(kpre_ref[hs, :], hv_ref[:, 2:3], kaug_ref)
        prob = jnp.exp2(mm(kaug_ref[...], qaug_ref[...])).astype(BF16)
        vaug = jnp.concatenate([vt_ref[hs, :], ones], axis=0)
        o = mm(vaug, prob)
        total = o[DH : DH + 1, :]
        l_ref[h : h + 1, :] = total
        mix = o[0:DH, :] / total
        mixf_ref[hs, :] = mix
        mixt_ref[hs, :] = mix[:, 0:share].astype(BF16)
        at = h * share
        for c in range(0, share, 256):
            block_no, lane = divmod(at + c, x.shape[1])
            mixs_ref[block_no * DH : (block_no + 1) * DH, lane : lane + 256] = mix[
                :, share + c : share + c + 256
            ]


def attn_fwd_own_kernel(
    blk_ref, x_ref, xf_ref, g_ref, s_ref, wt_ref, b_ref, hv_ref, kmask_ref, qhot_ref, n_ref, *refs
):
    share = x_ref.shape[0]
    for i, ref in enumerate((x_ref, xf_ref)):
        n, _ = row_norm(ref[...].astype(F32))
        n_ref[i * share : (i + 1) * share, :] = (n * g_ref[...] + s_ref[...]).astype(BF16)
    attend(n_ref, wt_ref, b_ref, hv_ref, kmask_ref, qhot_ref, refs[:7], *refs[7:])


def attn_fwd_kernel(
    ia_ref, ib_ref, a0_ref, a1_ref, b0_ref, b1_ref, x_ref, b_ref, hv_ref, kmask_ref, qhot_ref,
    wt_ref, ow_ref, ow1_ref, ow3_ref, *refs,
):
    wa_ref, wb_ref = refs[-2:]
    part = 24
    e = PIECES * part
    half = PIECES // 2
    wa_ref[0:half] = a0_ref[...]
    wa_ref[half:] = a1_ref[...]
    wb_ref[0:half] = b0_ref[...]
    wb_ref[half:] = b1_ref[...]

    def rows(w_ref, i_ref, at):
        return jnp.concatenate(
            [w_ref[i_ref[p], at * part : (at + 1) * part, :] for p in range(PIECES)], axis=0
        ).astype(BF16)

    wt_ref[0:e, :] = rows(wa_ref, ia_ref, 0)
    wt_ref[e : 2 * e, :] = rows(wa_ref, ia_ref, 1)
    wt_ref[2 * e : 3 * e, :] = rows(wb_ref, ib_ref, 0)
    ow_ref[...] = rows(wb_ref, ib_ref, 1)
    ow1_ref[...] = rows(wa_ref, ia_ref, 2)
    ow3_ref[...] = rows(wb_ref, ib_ref, 2)
    attend(x_ref, wt_ref, b_ref, hv_ref, kmask_ref, qhot_ref, refs[:7], *refs[7:9])


def unmix(ref, heads, share):
    width = ref.shape[1]
    rows = []
    for h in range(heads):
        cols = []
        for c in range(0, share, 256):
            block_no, lane = divmod(h * share + c, width)
            cols.append(ref[block_no * DH : (block_no + 1) * DH, lane : lane + 256])
        rows.append(jnp.concatenate(cols, axis=1))
    return jnp.concatenate(rows, axis=0).astype(BF16)


def mix_of(ref, share):
    if ref.dtype == BF16:
        return ref[...]
    return unmix(ref, ref.shape[0] * ref.shape[1] // (DH * share), share)


def out_norm2_kernel(nslot, blk_ref, x_ref, *refs):
    mixes = refs[:nslot]
    ws = refs[nslot : 2 * nslot]
    ob_ref, g_ref, s_ref, mid_ref, sec_ref, secf_ref = refs[2 * nslot :]
    acc = x_ref[...].astype(F32) + ob_ref[...]
    for k in range(nslot):
        acc = acc + mm_tn(mix_of(mixes[k], x_ref.shape[0]), ws[k][...])
    mid_ref[...] = acc
    n, _ = row_norm(acc)
    sec = (n * g_ref[...] + s_ref[...]).astype(BF16)
    sec_ref[...] = sec
    secf_ref[...] = sec.astype(F32)


def mlp_kernel(
    kind, keeps, sec_ref, secp_ref, cot_ref, cotp_ref, u0_ref, u1_ref, d0_ref, d1_ref, b_ref, *refs
):
    if keeps:
        p_ref, hid_ref, gp_ref, ub_ref, db_ref, k0_ref, k1_ref, s0_ref, s1_ref, gb_ref = refs
    else:
        hid_ref, gp_ref, ub_ref, db_ref, up_ref, uq_ref, k0_ref, k1_ref, sd_ref, gb_ref = refs
    part = u0_ref.shape[1]
    share = sec_ref.shape[0]
    up = jnp.concatenate([u0_ref[0], u0_ref[1], u1_ref[0], u1_ref[1]], axis=0).astype(BF16)
    down = jnp.concatenate([d0_ref[0], d1_ref[0], d0_ref[1], d1_ref[1]], axis=0).astype(BF16)
    ub_ref[...] = up
    db_ref[...] = down
    bias = b_ref[1:2, 0 : up.shape[0]]
    for r, (s_ref, c_ref) in enumerate(((sec_ref, cot_ref), (secp_ref, cotp_ref))):
        rows = slice(r * share, (r + 1) * share)
        sec = s_ref[...].astype(BF16)
        cot = c_ref[...].astype(BF16)
        pre = mm_nt(sec, up) + bias
        cdf = 0.5 * (1.0 + lax.erf(pre * (1.0 / math.sqrt(2.0))))
        hid = (pre * cdf).astype(BF16)
        pdf = jnp.exp(-0.5 * pre * pre) * (1.0 / math.sqrt(2.0 * math.pi))
        gpre = (mm_nt(cot, down) * (cdf + pre * pdf)).astype(BF16)
        hid_ref[rows, :] = hid
        gp_ref[rows, :] = gpre
        gb_r = jnp.sum(gpre.astype(F32), axis=0, keepdims=True)
        gd_r = mm_tn(hid, cot)
        gu_r = mm_tn(gpre, sec)
        if r == 0:
            gb, gd, gu = gb_r, gd_r, gu_r
        else:
            gb, gd, gu = gb + gb_r, gd + gd_r, gu + gu_r
    gb_ref[...] = gb
    order = (0, 1, 2, 3) if kind == "a" else (0, 2, 1, 3)
    gu_at = [gu[i * part : (i + 1) * part] for i in order]
    gd_at = [gd[i * part : (i + 1) * part] for i in order]
    if keeps:
        gu_at[3] = gu_at[3] + p_ref[0:part, :]
        gu_at[2] = gu_at[2] + p_ref[part:, :]
        for i, ref in enumerate((k0_ref, k1_ref, s0_ref, s1_ref)):
            ref[0:part, :] = gu_at[i]
            ref[part:, :] = gd_at[i]
    else:
        up_ref[0:part, :] = gu_at[3]
        up_ref[part:, :] = gu_at[2]
        uq_ref[0:part, :] = gu_at[0]
        uq_ref[part:, :] = gu_at[1]
        k0_ref[...] = gd_at[0]
        k1_ref[...] = gd_at[1]
        sd_ref[0:part, :] = gd_at[3]
        sd_ref[part:, :] = gd_at[2]


def down_kernel(nslot, *refs):
    hids = refs[:nslot]
    gps = refs[nslot : 2 * nslot]
    ubs = refs[2 * nslot : 3 * nslot]
    dbs = refs[3 * nslot : 4 * nslot]
    outs = refs[4 * nslot :]
    cat = lambda refs, axis: jnp.concatenate([r[...] for r in refs], axis=axis)
    share = outs[0].shape[1]
    for i, (rows_of, w_of) in enumerate(((hids, dbs), (gps, ubs))):
        w = cat(w_of, 0)
        for r, out_ref in enumerate(outs):
            rows = slice(r * share, (r + 1) * share)
            out_ref[i] = mm(jnp.concatenate([a[rows, :] for a in rows_of], axis=1), w)


def mid_kernel(nslot, mid_ref, own_ref, got_ref, cot_ref, db_ref, g_ref, *refs):
    ows = refs[:nslot]
    gmts = refs[nslot : 2 * nslot]
    bo_ref, gm_ref, low_ref, st_ref = refs[2 * nslot :]
    mid = mid_ref[...]
    n, rstd = row_norm(mid)
    e = own_ref[1] + got_ref[1]
    cot = cot_ref[...].astype(F32)
    gm = cot + row_norm_back(e * g_ref[...], n, rstd)
    gm_ref[...] = gm
    gm_low = gm.astype(BF16)
    low_ref[...] = gm_low
    for k in range(nslot):
        gmts[k][...] = mm_nt(ows[k][...], gm_low).astype(gmts[k].dtype)
    bo_ref[...] = (mid + (own_ref[0] + got_ref[0]) + db_ref[...]).astype(BF16)
    st_ref[0:1, :] = jnp.sum(e * n, axis=0, keepdims=True)
    st_ref[1:2, :] = jnp.sum(e, axis=0, keepdims=True)
    st_ref[2:3, :] = jnp.sum(gm_low.astype(F32), axis=0, keepdims=True)
    st_ref[3:4, :] = jnp.sum(cot, axis=0, keepdims=True)
    st_ref[4:8, :] = jnp.zeros((4, mid.shape[1]), F32)


def out_grad_kernel(nslot, idx_ref, low_ref, *refs):
    mixts = refs[:nslot]
    gow_keep, gow_send = refs[nslot:]
    part = 24
    gm_low = low_ref[...]
    for k in range(nslot):
        g = mm(mix_of(mixts[k], gm_low.shape[0]), gm_low)
        for p in range(PIECES):
            at = idx_ref[p]
            rows = slice(k * part, (k + 1) * part)

            @pl.when(at < PIECES // 2)
            def _():
                gow_keep[at, rows, :] = g[p * part : (p + 1) * part, :]

            @pl.when(at >= PIECES // 2)
            def _():
                gow_send[at - PIECES // 2, rows, :] = g[p * part : (p + 1) * part, :]


def attn_bwd_kernel(
    ncuts, idx_ref, x_ref, qpre_ref, kpre_ref, vt_ref, wt_ref, gmt_ref, gmtp_ref, mixf_ref, l_ref,
    hv_ref, kmask_ref, qhot_ref, *refs
):
    if ncuts:
        gn_in, gk_ref, gs_ref, *gn_refs = refs[: 3 + ncuts]
    else:
        gk_ref, gs_ref, gn_ref = refs[:3]
    st_ref, gb_ref, qaug_ref, kaug_ref, gpt_ref = refs[-5:]
    part = 24
    e = PIECES * part
    full = x_ref.shape[0]
    heads = e // DH
    qaug_ref[2 * DH :, :] = qhot_ref[...]
    kaug_ref[:, 2 * DH :] = kmask_ref[...]
    qg, qs, kg = hv_ref[:, 0:1], hv_ref[:, 1:2], hv_ref[:, 2:3]
    qg_sum = jnp.zeros((DH, 128), F32)
    qs_sum = jnp.zeros((DH, 128), F32)
    kg_sum = jnp.zeros((DH, 128), F32)
    row_no = lax.broadcasted_iota(jnp.int32, (DH, full), 0)
    one_rows = (row_no < 3).astype(F32).astype(BF16)
    for h in range(heads):
        hs = slice(h * DH, (h + 1) * DH)
        qn, qr, q_low = build_q_aug(qpre_ref[hs, :], qg, qs, qaug_ref)
        kn, kr, k_low = build_k_aug(kpre_ref[hs, :], kg, kaug_ref)
        inv = 1.0 / l_ref[h : h + 1, :]
        gm = jnp.concatenate(
            [gmt_ref[hs, :].astype(F32), gmtp_ref[hs, :].astype(BF16).astype(F32)], axis=1
        )
        go_low = (gm * inv).astype(BF16)
        delta = -jnp.sum(go_low.astype(F32) * mixf_ref[hs, :], axis=0, keepdims=True)
        d0 = delta.astype(BF16).astype(F32)
        d1 = (delta - d0).astype(BF16).astype(F32)
        d2 = delta - d0 - d1
        extra = jnp.where(
            row_no == 0, d0, jnp.where(row_no == 1, d1, jnp.where(row_no == 2, d2, 0.0))
        ).astype(BF16)
        goaug = jnp.concatenate([go_low, extra], axis=0)
        vaug = jnp.concatenate([vt_ref[hs, :], one_rows], axis=0).T
        prob = jnp.exp2(mm(kaug_ref[...], qaug_ref[...]))
        ds = (prob * mm(vaug, goaug)).astype(BF16)
        gv = mm_nt(go_low, prob.astype(BF16))
        gk = mm_nt(q_low, ds) * SCALE
        gq = mm(k_low, ds) * SCALE
        qg_sum += lane_fold(gq * qn)
        qs_sum += lane_fold(gq)
        kg_sum += lane_fold(gk * kn)
        gpt_ref[h * DH : (h + 1) * DH, :] = col_norm_back(gq * qg, qn, qr).astype(BF16)
        gpt_ref[e + h * DH : e + (h + 1) * DH, :] = col_norm_back(gk * kg, kn, kr).astype(BF16)
        gpt_ref[2 * e + h * DH : 2 * e + (h + 1) * DH, :] = gv.astype(BF16)
    st_ref[0] = qg_sum
    st_ref[1] = qs_sum
    st_ref[2] = kg_sum
    gp = gpt_ref[...]
    gb_ref[...] = lane_fold(gp.astype(F32))
    gw = mm(gp, x_ref[...])

    def put(ref, at, p):
        for s in range(3):
            ref[at, s * part : (s + 1) * part, :] = gw[s * e + p * part : s * e + (p + 1) * part, :]

    for p in range(PIECES):
        at = idx_ref[p]

        @pl.when(at < PIECES // 2)
        def _():
            put(gk_ref, at, p)

        @pl.when(at >= PIECES // 2)
        def _():
            put(gs_ref, at - PIECES // 2, p)

    gn = mm_tn(gp, wt_ref[...])
    if not ncuts:
        gn_ref[...] = gn
    else:
        at = 0
        for ref in gn_refs:
            rows = slice(at, at + ref.shape[0])
            ref[...] = gn_in[rows, :] + gn[rows]
            at += ref.shape[0]


def sums_kernel(
    nslot, blk_ref, me_ref, x_ref, xf_ref, gn_ref, mst_ref, h0_ref, h2_ref, b0_ref, b2_ref, *refs
):
    ubs = refs[:nslot]
    fars = refs[nslot:-1]
    out_ref = refs[-1]

    def fill():
        out_ref[...] = jnp.zeros_like(out_ref)
        out_ref[0:4, :] = mst_ref[0:4, :]
        heads = jnp.concatenate([h0_ref[i] + h2_ref[i] for i in range(3)], axis=0).T
        out_ref[6:7, 0 : heads.shape[1]] = jnp.sum(heads, axis=0, keepdims=True)
        me = me_ref[0]
        upart = out_ref.shape[1] // PIECES
        for row, k in zip((8, 10, 12, 14), (0, 2, 1, 3)):
            if k % 2 == 0:
                cols = (b0_ref if k == 0 else b2_ref)[...].T
                out_ref[row : row + 1, 0 : cols.shape[1]] = jnp.sum(cols, axis=0, keepdims=True)
            mine = ubs[k][...]
            for p in range(PIECES):
                piece = jnp.zeros((1, upart), F32)
                for t in range(PIECES // 2):
                    here = (me ^ offset_of(t, BITS_A)) == p
                    piece = piece + jnp.where(here, mine[:, t * upart : (t + 1) * upart], 0.0)
                out_ref[row + 1 : row + 2, p * upart : (p + 1) * upart] = piece

    fill()

    def add(x, e):
        n, _ = row_norm(x.astype(F32))
        out_ref[4:5, :] += jnp.sum(e * n, axis=0, keepdims=True)
        out_ref[5:6, :] += jnp.sum(e, axis=0, keepdims=True)

    add(x_ref[...], gn_ref[...])
    at = 0
    for ref in fars:
        add(xf_ref[at : at + ref.shape[0], :], ref[...])
        at += ref.shape[0]


def small_out_kernel(a_ref, b_ref, qb_ref, h0_ref, h1_ref, h2_ref, *rows):
    total = a_ref[...] + b_ref[...]
    for row, ref in zip((0, 1, 2, 3, 4, 5, 9), rows):
        ref[...] = total[row]
    for i, ref in enumerate((h0_ref, h1_ref, h2_ref)):
        ref[...] = total[6, i * DH : (i + 1) * DH]
        n = qb_ref.shape[1]
        qb_ref[i : i + 1, :] = total[8:9, i * n : (i + 1) * n]


def final_kernel(blk_ref, x_ref, gn_ref, *refs):
    gots = refs[:-3]
    gm_ref, g_ref, out_ref = refs[-3:]
    at = 0
    for ref in gots:
        rows = slice(at, at + ref.shape[0])
        n, rstd = row_norm(x_ref[rows, :].astype(F32))
        f = (gn_ref[rows, :] + ref[...]) * g_ref[...]
        out_ref[rows, :] = (gm_ref[rows, :] + row_norm_back(f, n, rstd)).astype(BF16)
        at += ref.shape[0]


def unpack_mlp_kernel(ia_ref, ib_ref, a_ref, b_ref, up_ref, down_ref, s_ref):
    part = s_ref.shape[2]
    half = PIECES // 2
    for w in range(2):
        for j in range(half):
            rows = slice((w * half + j) * part, (w * half + j + 1) * part)
            s_ref[w, j] = a_ref[rows, :]
            s_ref[w, half + j] = b_ref[rows, :]
    up_ref[...] = jnp.concatenate([s_ref[0, ia_ref[p]] for p in range(PIECES)], axis=0).T
    for p in range(PIECES):
        down_ref[p * part : (p + 1) * part, :] = s_ref[1, ib_ref[p]]


def unpack_att_kernel(i_ref, a_ref, b_ref, qkv_ref, out_ref, s_ref):
    rows = s_ref.shape[1]
    part = rows // 4
    half = PIECES // 2
    for j in range(half):
        s_ref[j] = a_ref[j * rows : (j + 1) * rows, :]
        s_ref[half + j] = b_ref[j * rows : (j + 1) * rows, :]
    for s, ref in enumerate((qkv_ref.at[0], qkv_ref.at[1], qkv_ref.at[2], out_ref)):
        for p in range(PIECES):
            ref[p * part : (p + 1) * part, :] = s_ref[i_ref[p], s * part : (s + 1) * part, :]


def swap_mp(a, k, size):
    return lax.ppermute(a, "mp", [(s, s ^ k) for s in range(size)])


def swap_plane(a, bit, size):
    return lax.ppermute(a, "dp", [(d, d ^ bit) for d in range(size)])


def storage_of(r, bits):
    return sum(jnp.where((r & bit) != 0, 1 << t, 0) for t, bit in enumerate(bits))


class Stages:
    def __init__(self):
        self.live = {}

    def __setitem__(self, name, value):
        self.live[name] = value

    def __getitem__(self, name):
        return self.live[name]

    def pop(self, name):
        return self.live.pop(name)

    def fence(self, *still_flying):
        now = {n: a for n, a in self.live.items() if n not in still_flying}
        leaves, tree = jax.tree.flatten(now)
        self.live.update(jax.tree.unflatten(tree, lax.optimization_barrier(leaves)))


def shards(
    tokens,
    seg_ids,
    qkv_weight,
    qkv_bias,
    out_weight,
    out_bias,
    up_weight,
    up_bias,
    down_weight,
    down_bias,
    norm1_gain,
    norm1_shift,
    query_gain,
    query_shift,
    key_gain,
    norm2_gain,
    norm2_shift,
    cotangent,
):
    ndp = lax.axis_size("dp")
    nmp = lax.axis_size("mp")
    dp_no = lax.axis_index("dp")
    mp_no = lax.axis_index("mp")
    me = dp_no % PIECES
    row_count, width = tokens.shape
    share = row_count // nmp
    full = SEQ_LEN
    assert full == 2 * share and nmp == 4 and ndp % PIECES == 0
    e = qkv_weight.shape[2]
    part = e // PIECES
    units = up_weight.shape[1]
    upart = units // PIECES
    half = PIECES // 2
    mine = half * upart
    core, px, py = 1, 2, 4

    vmem = pl.BlockSpec(memory_space=pltpu.VMEM)
    smem = pl.BlockSpec(memory_space=pltpu.SMEM)
    row1 = lambda v: v.reshape(1, -1)
    col = lambda v: v.reshape(-1, 1)
    swap = lambda a, bit: swap_plane(a, bit, ndp)
    zswap = lambda a, k: swap_mp(a, k, nmp)
    v = Stages()

    me1 = me.astype(jnp.int32).reshape(1)
    qkv_t = jnp.swapaxes(qkv_weight, 1, 2)
    wt0 = qkv_t.reshape(3 * e, width)
    att_piece, ob_piece, bias0 = call(
        prep_att_kernel,
        (
            sds((4 * part + 8, width), F32),
            sds((part + 8, width), F32),
            sds((8, width), F32),
        ),
        bytes_accessed=3_000_000,
        vmem_limit=VMEM_LARGE,
        in_specs=[smem] + [vmem] * 4,
        out_specs=(vmem,) * 3,
        scratch_shapes=[pltpu.VMEM((e, width), F32)],
    )(me1, qkv_t, out_weight, qkv_bias, up_bias)
    mlp_piece, u0, u1, d0, d1 = call(
        prep_mlp_kernel,
        (sds((2 * upart, width), F32), *[sds((2, upart, width), BF16)] * 4),
        bytes_accessed=6_000_000,
        vmem_limit=VMEM_LARGE,
        in_specs=[smem] + [vmem] * 2,
        out_specs=(vmem,) * 5,
        scratch_shapes=[pltpu.VMEM((units, width), F32)],
    )(me1, up_weight, down_weight)

    n_gn = (192, 176, 144)
    n_q0 = 56
    numbers = jnp.arange(PIECES, dtype=jnp.int32)
    idx_a = storage_of(numbers ^ me, BITS_A).astype(jnp.int32)
    idx_b = storage_of(numbers ^ me, BITS_B).astype(jnp.int32)

    block = 256
    per = share // block
    steps = 2 * per
    tile_no = jnp.arange(steps, dtype=jnp.int32)
    blk = jnp.where(tile_no < per, mp_no * per + tile_no, (mp_no ^ 1) * per + tile_no - per).astype(
        jnp.int32
    )
    const2 = lambda t, b: (0, 0)
    tok_spec = pl.BlockSpec((block, width), lambda t, b: (b[t], 0))
    run_spec = pl.BlockSpec((block, width), lambda t, b: (t, 0))
    vec_spec = pl.BlockSpec((1, width), const2)

    seg_own = lax.dynamic_slice_in_dim(seg_ids, mp_no * share, share, 0)
    seg_other = lax.dynamic_slice_in_dim(seg_ids, (mp_no ^ 1) * share, share, 0)
    seg_keys = jnp.concatenate([seg_own, seg_other])
    qhot = (
        lax.broadcasted_iota(jnp.int32, (SEG_COLS, full), 0) == seg_keys[None, :]
    ).astype(BF16)
    kmask = jnp.where(
        lax.broadcasted_iota(jnp.int32, (full, SEG_COLS), 1) == seg_keys[:, None], 0.0, -1e30
    ).astype(BF16)
    hv = jnp.stack([query_gain, query_shift, key_gain], axis=1)
    scratch = [
        pltpu.VMEM((2 * DH + SEG_COLS, full), BF16),
        pltpu.VMEM((full, 2 * DH + SEG_COLS), BF16),
    ]

    def whole(a):
        return pl.BlockSpec(a.shape, lambda t: (0,) * len(a.shape))

    def bias_at(block_no):
        return pl.BlockSpec((8, width), lambda t: (block_no, 0))

    att_names = ["qpre", "kpre", "vt", "mixt", "mixf", "mixs", "l"]
    att_shapes = [
        sds((e, full), F32),
        sds((e, full), F32),
        sds((e, full), BF16),
        sds((e, share), BF16),
        sds((e, full), F32),
        sds((e * share // width, width), F32),
        sds((8, full), F32),
    ]
    mix_rows = e * share // width

    def run_attn_own():
        all_of = lambda a: pl.BlockSpec(a.shape, lambda t, b: (0,) * len(a.shape))
        rest = [wt0, bias0, hv, kmask, qhot]
        shapes = [sds((full, width), BF16)] + att_shapes
        v["normed"], *outs = call(
            attn_fwd_own_kernel,
            tuple(shapes),
            flops=2 * (full * width * e * 3 + full * full * e * 8),
            bytes_accessed=10_000_000,
            grid_spec=pltpu.PrefetchScalarGridSpec(
                num_scalar_prefetch=1,
                grid=(1,),
                in_specs=[
                    pl.BlockSpec((share, width), lambda t, b: (b[0] // per, 0)),
                    pl.BlockSpec((share, width), lambda t, b: (b[per] // per, 0)),
                    vec_spec,
                    vec_spec,
                    *[all_of(a) for a in rest],
                ],
                out_specs=tuple(all_of(a) for a in shapes),
                scratch_shapes=scratch,
            ),
        )(blk, tokens, tokens, row1(norm1_gain), row1(norm1_shift), *rest)
        v["st0"] = dict(zip(att_names, outs))
        v["st0"]["wt"] = wt0
        v["st0"]["ow"] = out_weight

    def run_attn_far():
        shapes = [sds((3 * e, width), BF16)] + [sds((e, width), BF16)] * 3 + att_shapes
        args = [
            *v.pop("ta"), *v.pop("tb"), v["normed"], v["t2"], hv, kmask, qhot,
        ]
        specs = [whole(a) for a in args]
        specs[5] = bias_at(4 * part // 8)
        outs = call(
            attn_fwd_kernel,
            tuple(shapes),
            flops=2 * (full * width * e * 3 + full * full * e * 8),
            bytes_accessed=10_000_000,
            grid=(1,),
            vmem_limit=VMEM_LARGE,
            in_specs=[smem, smem] + specs,
            out_specs=tuple(whole(a) for a in shapes),
            scratch_shapes=scratch
            + [pltpu.VMEM((PIECES, 3 * part, width), F32)] * 2,
        )(idx_a, idx_b, *args)
        v["st2"] = dict(zip(["wt", "ow", "ow1", "ow3"] + att_names, outs))

    def by_slot():
        st0, st2 = v["st0"], v["st2"]
        mixes = [st0["mixt"], v["mix0"], st2["mixt"], v["mix2"]]
        ows = [st0["ow"], st2["ow1"], st2["ow"], st2["ow3"]]
        return mixes, ows

    def run_out():
        own_spec = pl.BlockSpec((share, width), lambda t, b: (b[0] // per, 0))
        whole2 = lambda shape: pl.BlockSpec(shape, lambda t, b: (0,) * len(shape))
        mixes, ows = by_slot()
        v["middle"], v["second"], v["sec_f"] = call(
            functools.partial(out_norm2_kernel, nmp),
            (sds((share, width), F32), sds((share, width), BF16), sds((share, width), F32)),
            flops=2 * share * width * e * nmp,
            bytes_accessed=8_000_000,
            grid_spec=pltpu.PrefetchScalarGridSpec(
                num_scalar_prefetch=1,
                grid=(1,),
                in_specs=[own_spec]
                + [whole2((e, share)), whole2((mix_rows, width))] * 2
                + [whole2((e, width))] * nmp
                + [whole2((1, width))] * 3,
                out_specs=(whole2((share, width)),) * 3,
            ),
        )(blk, tokens, *mixes, *ows, row1(out_bias), row1(norm2_gain), row1(norm2_shift))

    def run_mlp(k, up, down, bias, block_no):
        keeps = k % 2 == 0
        args = [
            v["second"], v["sec_p"], v["cot"], v["cot_p"], up[0], up[1], down[0], down[1], bias,
        ]
        if keeps:
            args.append(v.pop(f"p{k + 1}"))
        specs = [whole(a) for a in args]
        specs[8] = bias_at(block_no)
        piece = lambda n: sds((n * upart, width), F32)
        shapes = (
            *[sds((full, mine), BF16)] * 2,
            *[sds((mine, width), BF16)] * 2,
            *([piece(2)] * 4 if keeps else [piece(2), piece(2), piece(1), piece(1), piece(2)]),
            sds((1, mine), F32),
        )
        res = call(
            functools.partial(mlp_kernel, MLP_KIND[k], keeps),
            shapes,
            flops=2 * full * width * mine * 4,
            bytes_accessed=12_000_000,
            grid=(1,),
            in_specs=specs,
            out_specs=tuple(whole(a) for a in shapes),
        )(*args)
        v[f"h{k}"] = res[:4]
        v[f"ubg{k}"] = res[-1]
        if keeps:
            v[f"w{k}"] = res[4:8]
        else:
            v[f"p{k}"], v[f"q{k}u"] = res[4], res[5]
            v[f"w{k}"] = res[6:9]

    def run_down():
        return call(
            functools.partial(down_kernel, nmp),
            (sds((2, share, width), F32),) * 2,
            flops=4 * full * width * mine * nmp,
            bytes_accessed=17_000_000,
            vmem_limit=40 * 1024 * 1024,
            in_specs=[vmem] * (4 * nmp),
            out_specs=(vmem,) * 2,
        )(*[v[f"h{k}"][i] for i in range(4) for k in range(nmp)])

    def run_mid():
        mixes, ows = by_slot()
        shapes = (
            *[sds((e, share), F32 if k % 2 else BF16) for k in range(nmp)],
            sds((share, width), BF16),
            sds((share, width), F32),
            sds((share, width), BF16),
            sds((8, width), F32),
        )
        *gmts, bo, gm, low, mst = call(
            functools.partial(mid_kernel, nmp),
            shapes,
            flops=2 * share * width * e * nmp,
            bytes_accessed=12_000_000,
            in_specs=[vmem] * (6 + nmp),
            out_specs=(vmem,) * (4 + nmp),
        )(
            v["middle"], v.pop("acc_own"), v.pop("acc_got"), v["cot"], row1(down_bias),
            row1(norm2_gain), *ows,
        )
        v["block_out"], v["gm"], v["mst"] = bo, gm, mst
        for k in range(nmp):
            v[f"gmt{k}"] = gmts[k]
        return low

    def run_out_grad(low):
        mixes, ows = by_slot()
        args = [low, *mixes]
        specs = [whole(a) for a in args]
        for k in (1, 3):
            specs[1 + k] = pl.BlockSpec((mix_rows, width), lambda t: (0, 0))
        shapes = (sds((half, nmp * part, width), F32),) * 2
        v["o"] = call(
            functools.partial(out_grad_kernel, nmp),
            shapes,
            flops=2 * share * width * e * nmp,
            bytes_accessed=5_000_000,
            grid=(1,),
            in_specs=[smem] + specs,
            out_specs=tuple(whole(a) for a in shapes),
        )(idx_a, *args)

    def run_attn_bwd(k, got, idx, first):
        st = v.pop(f"st{k}")
        args = [
            idx, v["normed"], st["qpre"], st["kpre"], st["vt"], st["wt"], v.pop(f"gmt{k}"),
            v.pop(got), st["mixf"], st["l"], hv, kmask, qhot,
        ]
        cuts_now = (full,) if first else (share, *n_gn)
        if not first:
            args.append(v.pop("gn"))
        keep, send, *gn, hst, gb = call(
            functools.partial(attn_bwd_kernel, 0 if first else len(cuts_now)),
            (
                sds((half, 3 * part, width), F32),
                sds((half, 3 * part, width), F32),
                *[sds((n, width), F32) for n in cuts_now],
                sds((3, DH, 128), F32),
                sds((3 * e, 128), F32),
            ),
            flops=2 * (full * width * e * 6 + full * full * e * 20),
            bytes_accessed=14_000_000,
            in_specs=[smem] + [vmem] * (len(args) - 1),
            out_specs=(vmem,) * (4 + len(cuts_now)),
            scratch_shapes=scratch + [pltpu.VMEM((3 * e, full), BF16)],
        )(*args)
        v[f"q{k}"] = (keep, send)
        if first:
            v["gn"] = gn[0]
        else:
            v["gn_own"], v["gn_far"] = gn[0], tuple(gn[1:])
        v[f"hst{k}"] = hst
        v[f"qbg{k}"] = gb

    def g1(n):
        a, b = v[n + "a"], v[n + "b"]
        v[n + "a"] = (a, swap(a, px))
        v[n + "b"] = (b, swap(b, py))

    def g2(n):
        a, b = (jnp.stack(v[n + t]) for t in "ab")
        v[n + "a"] = (a, swap(a, py))
        v[n + "b"] = (b, swap(b, px))

    def g3(n):
        a, b = (jnp.concatenate(v[n + t], axis=0) for t in "ab")
        v[n + "a"] = (a, swap(a, core))
        v[n + "b"] = (b, swap(b, core))

    def r1(n):
        keep, send = v[n]
        v[n] = (keep, swap(send, core))

    def r2(n, kind):
        keep, got = v[n]
        keep_sum = keep[:2] + got[:2]
        v[n] = (keep_sum, swap(keep[2:] + got[2:], py if kind == "a" else px))

    def r3(n, kind):
        keep, got = v[n]
        v[n] = (keep[0] + got[0], swap(keep[1] + got[1], px if kind == "a" else py))

    def r4(n):
        keep, got = v[n]
        v[n] = keep + got

    def first_link(k):
        return py if MLP_KIND[k] == "a" else px

    def second_link(k):
        return px if MLP_KIND[k] == "a" else py

    def c1(k):
        k0, k1, s0, s1 = v[f"w{k}"]
        v[f"w{k}"] = (k0, k1, s0, swap(s1, first_link(k)))

    def c0(k):
        k0, k1, s0, g1 = v[f"w{k}"]
        v[f"w{k}"] = (k0, k1, g1, swap(s0, first_link(k)))

    def c2u(k):
        k0, k1, g1, g0 = v[f"w{k}"]
        q0, q1 = v.pop(f"q{k + 1}u")
        sent = k1[:upart] + q1 + g1[:upart]
        v[f"w{k}"] = (k0, k1, g1, g0, q0, swap(sent, second_link(k)))

    def c2d(k):
        k0, k1, g1, g0, q, gu = v.pop(f"w{k}")
        up_sum = k0[:upart] + g0[:upart] + q + gu
        return up_sum, k0[upart:] + g0[upart:], k1[upart:] + g1[upart:]

    def e1(k):
        k0, k1, s = v[f"w{k}"]
        v[f"w{k}"] = (k0, k1, swap(s, first_link(k)))

    def e2(k):
        k0, k1, g = v[f"w{k}"]
        v[f"w{k}"] = (k0 + g[upart:], swap(k1 + g[:upart], second_link(k)))

    def e3(k):
        k0, g = v[f"w{k}"]
        v[f"w{k}"] = k0 + g

    inner = (mp_no == 1) | (mp_no == 2)

    def middle_swap(a):
        return lax.ppermute(a, "mp", [(1, 2), (2, 1)])

    def pass_out(a):
        return lax.ppermute(a, "mp", [(1, 0), (2, 3)])

    def high_bits(a):
        bit = PIECES
        while bit < ndp:
            a = a + swap(a, bit)
            bit *= 2
        return a

    cot_all, mlp_piece = lax.optimization_barrier((cotangent, mlp_piece))
    v["cot"] = lax.dynamic_slice_in_dim(cot_all, mp_no * share, share, 0)
    v["cot_f"] = v["cot"].astype(F32)
    v["piece"] = mlp_piece
    v["o3"] = zswap(ob_piece, 3)
    v["o1"] = zswap(ob_piece, 1)
    v["t2"] = zswap(att_piece, 2)
    v.fence()
    hp = 2 * part
    t2, o1, o3 = v["t2"], v["o1"], v["o3"]
    v["ta"] = jnp.concatenate([t2[:hp], o1[:part]], axis=0)
    v["tb"] = jnp.concatenate([t2[hp : 2 * hp], o3[:part]], axis=0)
    g1("t")
    v["cot_p"] = swap(v.pop("cot_f"), core)
    v["m1"] = zswap(v["piece"], 1)
    v["mid_a"] = middle_swap(v.pop("piece"))
    run_attn_own()
    v.fence()
    m1 = v["m1"]
    to_y = jnp.concatenate([*v["ta"], m1[upart:]], axis=0)
    to_x = jnp.concatenate([*v["tb"], m1[:upart]], axis=0)
    v["ta"] = (to_y, swap(to_y, py))
    v["tb"] = (to_x, swap(to_x, px))
    v["mid_b"] = middle_swap(v.pop("m1"))
    v["mix0"] = zswap(jnp.concatenate([v["st0"].pop("mixs"), v["mid_a"]], axis=0), 1)
    v.fence()
    nt = 2 * 3 * part
    ya, yb = v.pop("ta")
    xa, xb = v.pop("tb")
    v["m1a"], v["m1b"] = (xa[nt:], xb[nt:]), (ya[nt:], yb[nt:])
    v["ta"], v["tb"] = (
        tuple(
            a.reshape(half, 3 * part, width) for a in (both_, swap(both_, core))
        )
        for both_ in (
            jnp.concatenate([ya[:nt], yb[:nt]], axis=0),
            jnp.concatenate([xa[:nt], xb[:nt]], axis=0),
        )
    )
    run_attn_far()
    g2("m1")
    v["end_b"] = pass_out(v["mid_b"])
    v.fence()
    v["mix2"] = zswap(v["st2"].pop("mixs"), 1)
    run_out()
    m3 = jnp.where(inner, v.pop("mid_a"), v.pop("end_b"))
    m2 = jnp.where(inner, v.pop("mid_b"), v["mix0"][mix_rows:])
    to_x = jnp.concatenate([m3[:upart], m2[:upart]], axis=0)
    to_y = jnp.concatenate([m3[upart:], m2[upart:]], axis=0)
    v["ma"], v["mb"] = (to_x, swap(to_x, px)), (to_y, swap(to_y, py))
    v.fence()
    for t in "ab":
        own, got = v.pop(f"m{t}")
        v[f"m3{t}"] = (own[:upart], got[:upart])
        v[f"m2{t}"] = (own[upart:], got[upart:])
    v["sec_p"] = swap(v.pop("sec_f"), core)
    run_mlp(1, v.pop("m1a"), v.pop("m1b"), v["o1"], part // 8)
    g2("m3")
    v.fence()
    v["p1"] = zswap(v["p1"], 1)
    run_mlp(3, v.pop("m3a"), v.pop("m3b"), v["o3"], part // 8)
    g2("m2")
    v.fence()
    v["p3"] = zswap(v["p3"], 1)
    run_mlp(0, (u0, u1), (d0, d1), bias0, 0)
    e1(1)
    e1(3)
    v.fence()
    run_mlp(2, v.pop("m2a"), v.pop("m2b"), v["t2"], 4 * part // 8)
    e2(1)
    e2(3)
    q1u = v.pop("q1u")
    v["q1x"] = zswap(q1u[:upart], 1)
    v["q1r"] = q1u[upart:]
    v.fence()
    e3(1)
    e3(3)
    q3u = v.pop("q3u")
    v["qm"] = zswap(jnp.concatenate([v.pop("q1r"), q3u[:upart]], axis=0), 1)
    v["q3r"] = q3u[upart:]
    c1(0)
    c1(2)
    v["acc_own"], v["acc_far"] = run_down()
    v.fence()
    c0(0)
    c0(2)
    v["q3y"] = zswap(jnp.concatenate([v.pop("q3r"), v.pop("w3")], axis=0), 1)
    v["acc_got"] = swap(v.pop("acc_far"), core)
    v["low"] = run_mid()
    v.fence()
    qm = v.pop("qm")
    q3y = v.pop("q3y")
    v["q1u"], v["q3u"] = (v.pop("q1x"), qm[:upart]), (qm[upart:], q3y[:upart])
    v["d3"] = q3y[upart:]
    c2u(0)
    c2u(2)
    v["gp2"] = zswap(v.pop("gmt3"), 1)
    run_out_grad(v.pop("low"))
    v.fence()
    up0, down0, send_x = c2d(0)
    up2, down2, send_y = c2d(2)
    v["gp0"] = zswap(v.pop("gmt1"), 1)
    v["z2x"] = zswap(up2, 2)
    r1("o")
    keep, got = v.pop("o")
    o4 = keep + got
    ho = 2 * part
    to_x = jnp.concatenate([send_x, o4[1, ho:], o4[3, ho:]], axis=0)
    to_y = jnp.concatenate([send_y, o4[2, :ho], o4[3, :ho]], axis=0)
    v["gx"], v["gy"] = swap(to_x, px), swap(to_y, py)
    v["op"], v["oq"] = (o4[0, :ho], o4[1, :ho]), (o4[0, ho:], o4[2, ho:])
    v["w0"], v["w2"] = (up0, down0), down2
    run_attn_bwd(2, "gp2", idx_b, True)
    v.fence()
    r1("q2")
    gx, gy = v.pop("gx"), v.pop("gy")
    v["d1"] = zswap(v.pop("w1"), 1)
    v["z2y"] = zswap(v.pop("w2") + gy[:upart] + v.pop("d3"), 2)
    up0, down0 = v["w0"]
    v["w0"] = (up0, down0 + gx[:upart])
    op = [a + gy[upart + i * ho : upart + (i + 1) * ho] for i, a in enumerate(v["op"])]
    oq = [a + gx[upart + i * ho : upart + (i + 1) * ho] for i, a in enumerate(v["oq"])]
    v["op"], v["oq"] = op[0], oq[0]
    keep, got = v["q2"]
    to_x = jnp.concatenate([(keep[2:] + got[2:]).reshape(-1, width), op[1]], axis=0)
    v["q2"] = keep[:2] + got[:2]
    v["gx"], v["gy"] = swap(to_x, px), swap(oq[1], py)
    run_attn_bwd(0, "gp0", idx_b, False)
    v.fence()
    nq = 3 * part
    gx, gy = v.pop("gx"), v.pop("gy")
    up_sum, down_sum = v.pop("w0")
    ma = high_bits(up_sum + v.pop("z2x"))
    mb = high_bits(down_sum + v.pop("d1") + v.pop("z2y"))
    q2 = v["q2"] + gx[: 2 * nq].reshape(2, nq, width)
    v["q2"] = q2[0]
    o = jnp.concatenate([v.pop("op") + gx[2 * nq :], v.pop("oq") + gy], axis=0)
    v["o0"], v["o2"] = o[:part], o[2 * part : 3 * part]
    v["gn0"] = zswap(
        jnp.concatenate([v["gn_far"][0], o[part : 2 * part], o[3 * part :]], axis=0), 1
    )
    keep, send = v.pop("q0")
    q4 = keep + swap(send, core)
    v["q0b"], v["q0a"] = q4[:2, :n_q0], (q4[0, n_q0:], q4[2, n_q0:])
    to_x = jnp.concatenate([ma, q4[2, :n_q0], q4[3, :n_q0]], axis=0)
    to_y = jnp.concatenate([mb, q2[1], q4[1, n_q0:], q4[3, n_q0:]], axis=0)
    v["gx"], v["gy"] = (ma, swap(to_x, px)), (mb, swap(to_y, py))
    v["small"] = call(
        functools.partial(sums_kernel, nmp),
        sds((16, width), F32),
        flops=full * width * 10,
        bytes_accessed=full * width * 6,
        grid_spec=pltpu.PrefetchScalarGridSpec(
            num_scalar_prefetch=2,
            grid=(1,),
            in_specs=[
                pl.BlockSpec((share, width), lambda t, b, m: (b[0] // per, 0)),
                pl.BlockSpec((share, width), lambda t, b, m: (b[per] // per, 0)),
                pl.BlockSpec((share, width), lambda t, b, m: (0, 0)),
                pl.BlockSpec((8, width), lambda t, b, m: (0, 0)),
                *[pl.BlockSpec((3, DH, 128), lambda t, b, m: (0, 0, 0))] * 2,
                *[pl.BlockSpec((3 * e, 128), lambda t, b, m: (0, 0))] * 2,
                *[pl.BlockSpec((1, mine), lambda t, b, m: (0, 0))] * nmp,
                *[pl.BlockSpec((n, width), lambda t, b, m: (0, 0)) for n in n_gn],
            ],
            out_specs=pl.BlockSpec((16, width), lambda t, b, m: (0, 0)),
        ),
    )(
        blk, me1, tokens, tokens, v["gn_own"], v.pop("mst"), v.pop("hst0"), v.pop("hst2"),
        v.pop("qbg0"), v.pop("qbg2"), *[v.pop(f"ubg{k}") for k in range(nmp)], *v["gn_far"],
    )
    v["small"] = v["small"] + swap(v["small"], core)
    v.fence()
    (ma, gx), (mb, gy) = v.pop("gx"), v.pop("gy")
    q0b = v.pop("q0b") + gx[upart:].reshape(2, n_q0, width)
    n_rest = nq - n_q0
    at = upart + nq
    q0a = [
        a + gy[at + i * n_rest : at + (i + 1) * n_rest] for i, a in enumerate(v.pop("q0a"))
    ]
    v["q0"] = (q0b[0], q0a[0])
    to_y = jnp.concatenate([ma, gx[:upart], q0b[1]], axis=0)
    to_x = jnp.concatenate([mb, gy[:upart], q0a[1]], axis=0)
    v["gx"], v["gy"] = (to_x, swap(to_x, px)), (to_y, swap(to_y, py))
    oz = v["gn0"][n_gn[0] :]
    v["o0"] = v["o0"] + oz[:part]
    q2 = v.pop("q2") + gy[upart:at]
    v["y2"] = zswap(jnp.concatenate([q2, v.pop("o2") + oz[part:]], axis=0), 2)
    v["gn1"] = zswap(v["gn_far"][1], 1)
    v["small"] = v["small"] + swap(v["small"], px)
    v.fence()
    (xa, xb), (ya, yb) = v.pop("gx"), v.pop("gy")
    n2 = 2 * upart
    mlp = jnp.concatenate([ya[:n2], yb[:n2], xa[:n2], xb[:n2]], axis=0)
    q0b, q0a = v.pop("q0")
    q0 = jnp.concatenate([q0b + yb[n2:], q0a + xb[n2:]], axis=0)
    att_sum = high_bits(jnp.concatenate([q0, v.pop("o0")], axis=0) + v.pop("y2"))
    v["w"] = (att_sum, swap(att_sum, px), swap(att_sum, py), swap(att_sum, px | py))
    small = high_bits(v["small"] + swap(v["small"], py))
    v["gn2"] = zswap(jnp.concatenate([v.pop("gn_far")[2], small[:8], small[12:]], axis=0), 1)
    v["small"] = small[:12] + v["gn2"][n_gn[2] :]

    v["up_g"], v["down_g"] = call(
        unpack_mlp_kernel,
        (sds((width, units), F32), sds((units, width), F32)),
        bytes_accessed=10_000_000,
        in_specs=[smem, smem] + [vmem] * 2,
        out_specs=(vmem,) * 2,
        scratch_shapes=[pltpu.VMEM((2, PIECES, upart, width), F32)],
    )(idx_a, idx_b, mlp, swap(mlp, core))
    v.fence()
    input_grad = call(
        final_kernel,
        sds((share, width), BF16),
        flops=share * width * 20,
        bytes_accessed=share * width * 16,
        grid_spec=pltpu.PrefetchScalarGridSpec(
            num_scalar_prefetch=1,
            grid=(1,),
            in_specs=[
                pl.BlockSpec((share, width), lambda t, b: (b[0] // per, 0)),
                pl.BlockSpec((share, width), const2),
                *[pl.BlockSpec((n, width), const2) for n in n_gn],
                pl.BlockSpec((share, width), const2),
                vec_spec,
            ],
            out_specs=pl.BlockSpec((share, width), const2),
        ),
    )(blk, tokens, v["gn_own"], *[v[f"gn{i}"] for i in range(3)], v["gm"], row1(norm1_gain))
    w = jnp.concatenate(v.pop("w"), axis=0)
    small = v.pop("small")
    small_got = zswap(jnp.concatenate([small[:8], small[10:]], axis=0), 2)
    qkv_weight_grad, out_weight_grad = call(
        unpack_att_kernel,
        (sds((3, e, width), F32), sds((e, width), F32)),
        bytes_accessed=2 * 4 * 4 * width * e,
        in_specs=[smem] + [vmem] * 2,
        out_specs=(vmem, vmem),
        scratch_shapes=[pltpu.VMEM((PIECES, 4 * part, width), F32)],
    )(idx_a, w, swap(w, core))
    qkv_weight_grad = jnp.swapaxes(qkv_weight_grad, 1, 2)
    qkv_weight_grad, out_weight_grad, input_grad, small, small_got = lax.optimization_barrier(
        (qkv_weight_grad, out_weight_grad, input_grad, small, small_got)
    )
    qkv_bias_grad, *rows_of = call(
        small_out_kernel,
        (sds((3, e), F32), *[sds((DH,), F32)] * 3, *[sds((width,), F32)] * 7),
        bytes_accessed=100_000,
        in_specs=[vmem, vmem],
        out_specs=(vmem,) * 11,
    )(small[:10], small_got)
    heads_of, rows_of = rows_of[:3], rows_of[3:]
    return (
        v["block_out"],
        input_grad,
        qkv_weight_grad,
        qkv_bias_grad,
        out_weight_grad,
        rows_of[2],
        v["up_g"],
        rows_of[6],
        v["down_g"],
        rows_of[3],
        rows_of[4],
        rows_of[5],
        heads_of[0],
        heads_of[1],
        heads_of[2],
        rows_of[0],
        rows_of[1],
    )


def solution(mesh):
    in_specs = (
        P("dp", None),
        P("dp"),
        P(None, None, "mp"),
        P(None, "mp"),
        P("mp", None),
        P(),
        P(None, "mp"),
        P("mp"),
        P("mp", None),
        P(),
        P(),
        P(),
        P(),
        P(),
        P(),
        P(),
        P(),
        P("dp", None),
    )
    out_specs = (
        P(("dp", "mp"), None),
        P(("dp", "mp"), None),
        P(None, None, "mp"),
        P(None, "mp"),
        P("mp", None),
        P(),
        P(None, "mp"),
        P("mp"),
        P("mp", None),
        P(),
        P(),
        P(),
        P(),
        P(),
        P(),
        P(),
        P(),
    )
    return jax.shard_map(shards, mesh=mesh, in_specs=in_specs, out_specs=out_specs, check_vma=False)
```

```python
import functools
import math

import jax
import jax.numpy as jnp
from jax import lax
from jax.experimental import pallas as pl
from jax.experimental.pallas import tpu as pltpu
from jax.sharding import PartitionSpec as P

F32 = jnp.float32
BF16 = jnp.bfloat16
DH = 64
SEQ_LEN = 1024
NORM_EPS = 1e-06
PIECES = 8
SEG_COLS = 128
LOG2E = math.log2(math.e)
SCALE = DH ** (-0.5)
BITS_A = (2, 4, 1)
BITS_B = (4, 2, 1)
MLP_KIND = ("a", "a", "b", "b")
VMEM_LIMIT = 26 * 1024 * 1024
VMEM_LARGE = 56 * 1024 * 1024


def mm(a, b):
    return lax.dot_general(a, b, (((1,), (0,)), ((), ())), preferred_element_type=F32)


def mm_nt(a, b):
    return lax.dot_general(a, b, (((1,), (1,)), ((), ())), preferred_element_type=F32)


def mm_tn(a, b):
    return lax.dot_general(a, b, (((0,), (0,)), ((), ())), preferred_element_type=F32)


def call(kernel, out_shape, flops=0, bytes_accessed=0, vmem_limit=VMEM_LIMIT, **kw):
    return pl.pallas_call(
        kernel,
        out_shape=out_shape,
        compiler_params=pltpu.CompilerParams(vmem_limit_bytes=vmem_limit),
        cost_estimate=pl.CostEstimate(
            flops=flops, bytes_accessed=bytes_accessed, transcendentals=0
        ),
        **kw,
    )


def sds(shape, dtype):
    return jax.ShapeDtypeStruct(shape, dtype)


def row_norm(x):
    mean = jnp.mean(x, axis=-1, keepdims=True)
    cen = x - mean
    rstd = lax.rsqrt(jnp.mean(cen * cen, axis=-1, keepdims=True) + NORM_EPS)
    return cen * rstd, rstd


def row_norm_back(f, n, rstd):
    mean_f = jnp.mean(f, axis=-1, keepdims=True)
    mean_fn = jnp.mean(f * n, axis=-1, keepdims=True)
    return (f - mean_f - n * mean_fn) * rstd


def col_norm(x):
    mean = jnp.mean(x, axis=0, keepdims=True)
    cen = x - mean
    rstd = lax.rsqrt(jnp.mean(cen * cen, axis=0, keepdims=True) + NORM_EPS)
    return cen * rstd, rstd


def col_norm_back(f, n, rstd):
    mean_f = jnp.mean(f, axis=0, keepdims=True)
    mean_fn = jnp.mean(f * n, axis=0, keepdims=True)
    return (f - mean_f - n * mean_fn) * rstd


def lane_fold(x):
    out = x[:, :128]
    for t in range(1, x.shape[1] // 128):
        out = out + x[:, t * 128 : (t + 1) * 128]
    return out


def offset_of(s, bits):
    return sum(bit for t, bit in enumerate(bits) if (s >> t) & 1)


def build_q_aug(q_pre, qg, qs, qaug_ref):
    n, rstd = col_norm(q_pre)
    q_low = (n * qg + qs).astype(BF16)
    scaled = q_low.astype(F32) * (SCALE * LOG2E)
    hi = scaled.astype(BF16)
    lo = (scaled - hi.astype(F32)).astype(BF16)
    qaug_ref[0:DH, :] = hi
    qaug_ref[DH : 2 * DH, :] = lo
    return n, rstd, q_low


def build_k_aug(k_pre, kg, kaug_ref):
    n, rstd = col_norm(k_pre)
    k_low = (n * kg).astype(BF16)
    kaug_ref[:, 0 : 2 * DH] = jnp.concatenate([k_low, k_low], axis=0).T
    return n, rstd, k_low


def bias_col(b_ref, n):
    return b_ref[...].T[0:n, 0:1]


def prep_att_kernel(
    me_ref, w_ref, o_ref, qb_ref, ub_ref, att_ref, ob_ref, b_ref, wf_ref
):
    part = 24
    e = PIECES * part
    me = me_ref[0]
    b_ref[...] = jnp.zeros(b_ref.shape, F32)
    for s in range(3):
        wf_ref[...] = w_ref[s].astype(F32)
        rows = wf_ref[pl.ds(pl.multiple_of(me * part, 8), part), :]
        att_ref[s * part : (s + 1) * part, :] = rows
        b_ref[0:1, s * e : (s + 1) * e] = qb_ref[s : s + 1, :]
    upart = ub_ref.shape[0] // PIECES
    ub = ub_ref[...].reshape(1, PIECES * upart)
    for s in range(PIECES // 2):
        piece = jnp.zeros((1, upart), F32)
        for p in range(PIECES):
            here = (me ^ offset_of(s, BITS_A)) == p
            piece = piece + jnp.where(here, ub[:, p * upart : (p + 1) * upart], 0.0)
        b_ref[1:2, s * upart : (s + 1) * upart] = piece
    wf_ref[...] = o_ref[...].astype(F32)
    rows = wf_ref[pl.ds(pl.multiple_of(me * part, 8), part), :]
    att_ref[3 * part : 4 * part, :] = rows
    ob_ref[0:part, :] = rows
    att_ref[4 * part :, :] = b_ref[...]
    ob_ref[part:, :] = b_ref[...]


def prep_mlp_kernel(me_ref, up_ref, dn_ref, p_ref, u0_ref, u1_ref, d0_ref, d1_ref, t_ref):
    me = me_ref[0]
    upart = up_ref.shape[1] // PIECES
    t_ref[...] = up_ref[...].astype(F32).T

    def at_piece(r):
        return pl.ds(pl.multiple_of((me ^ r) * upart, 32), upart)

    p_ref[0:upart, :] = t_ref[at_piece(0), :]
    p_ref[upart:, :] = dn_ref[at_piece(0), :].astype(F32)
    for i, (u_ref, d_ref) in enumerate(((u0_ref, d0_ref), (u1_ref, d1_ref))):
        for j in range(2):
            u_ref[j] = t_ref[at_piece(offset_of(2 * i + j, BITS_A)), :].astype(BF16)
            d_ref[j] = dn_ref[at_piece(offset_of(2 * i + j, BITS_B)), :]


def attend(x_ref, wt_ref, b_ref, hv_ref, kmask_ref, qhot_ref, outs, qaug_ref, kaug_ref):
    qpre_ref, kpre_ref, vt_ref, mixt_ref, mixf_ref, mixs_ref, l_ref = outs
    e = qpre_ref.shape[0]
    full = x_ref.shape[0]
    share = full // 2
    heads = e // DH
    x = x_ref[...]
    bias = bias_col(b_ref, 3 * e)
    qpre_ref[...] = mm_nt(wt_ref[0:e, :], x) + bias[0:e]
    kpre_ref[...] = mm_nt(wt_ref[e : 2 * e, :], x) + bias[e : 2 * e]
    vt_ref[...] = (mm_nt(wt_ref[2 * e : 3 * e, :], x) + bias[2 * e :]).astype(BF16)
    qaug_ref[2 * DH :, :] = qhot_ref[...]
    kaug_ref[:, 2 * DH :] = kmask_ref[...]
    ones = jnp.ones((16, full), BF16)
    for h in range(heads):
        hs = slice(h * DH, (h + 1) * DH)
        build_q_aug(qpre_ref[hs, :], hv_ref[:, 0:1], hv_ref[:, 1:2], qaug_ref)
        build_k_aug(kpre_ref[hs, :], hv_ref[:, 2:3], kaug_ref)
        prob = jnp.exp2(mm(kaug_ref[...], qaug_ref[...])).astype(BF16)
        vaug = jnp.concatenate([vt_ref[hs, :], ones], axis=0)
        o = mm(vaug, prob)
        total = o[DH : DH + 1, :]
        l_ref[h : h + 1, :] = total
        mix = o[0:DH, :] / total
        mixf_ref[hs, :] = mix
        mixt_ref[hs, :] = mix[:, 0:share].astype(BF16)
        at = h * share
        for c in range(0, share, 256):
            block_no, lane = divmod(at + c, x.shape[1])
            mixs_ref[block_no * DH : (block_no + 1) * DH, lane : lane + 256] = mix[
                :, share + c : share + c + 256
            ]


def attn_fwd_own_kernel(
    blk_ref, x_ref, xf_ref, g_ref, s_ref, wt_ref, b_ref, hv_ref, kmask_ref, qhot_ref, n_ref, *refs
):
    share = x_ref.shape[0]
    for i, ref in enumerate((x_ref, xf_ref)):
        n, _ = row_norm(ref[...].astype(F32))
        n_ref[i * share : (i + 1) * share, :] = (n * g_ref[...] + s_ref[...]).astype(BF16)
    attend(n_ref, wt_ref, b_ref, hv_ref, kmask_ref, qhot_ref, refs[:7], *refs[7:])


def attn_fwd_kernel(
    ia_ref, ib_ref, a0_ref, a1_ref, b0_ref, b1_ref, x_ref, b_ref, hv_ref, kmask_ref, qhot_ref,
    wt_ref, ow_ref, ow1_ref, ow3_ref, *refs,
):
    wa_ref, wb_ref = refs[-2:]
    part = 24
    e = PIECES * part
    half = PIECES // 2
    wa_ref[0:half] = a0_ref[...]
    wa_ref[half:] = a1_ref[...]
    wb_ref[0:half] = b0_ref[...]
    wb_ref[half:] = b1_ref[...]

    def rows(w_ref, i_ref, at):
        return jnp.concatenate(
            [w_ref[i_ref[p], at * part : (at + 1) * part, :] for p in range(PIECES)], axis=0
        ).astype(BF16)

    wt_ref[0:e, :] = rows(wa_ref, ia_ref, 0)
    wt_ref[e : 2 * e, :] = rows(wa_ref, ia_ref, 1)
    wt_ref[2 * e : 3 * e, :] = rows(wb_ref, ib_ref, 0)
    ow_ref[...] = rows(wb_ref, ib_ref, 1)
    ow1_ref[...] = rows(wa_ref, ia_ref, 2)
    ow3_ref[...] = rows(wb_ref, ib_ref, 2)
    attend(x_ref, wt_ref, b_ref, hv_ref, kmask_ref, qhot_ref, refs[:7], *refs[7:9])


def unmix(ref, heads, share):
    width = ref.shape[1]
    rows = []
    for h in range(heads):
        cols = []
        for c in range(0, share, 256):
            block_no, lane = divmod(h * share + c, width)
            cols.append(ref[block_no * DH : (block_no + 1) * DH, lane : lane + 256])
        rows.append(jnp.concatenate(cols, axis=1))
    return jnp.concatenate(rows, axis=0).astype(BF16)


def mix_of(ref, share):
    if ref.dtype == BF16:
        return ref[...]
    return unmix(ref, ref.shape[0] * ref.shape[1] // (DH * share), share)


def out_norm2_kernel(nslot, blk_ref, x_ref, *refs):
    mixes = refs[:nslot]
    ws = refs[nslot : 2 * nslot]
    ob_ref, g_ref, s_ref, mid_ref, sec_ref, secf_ref = refs[2 * nslot :]
    acc = x_ref[...].astype(F32) + ob_ref[...]
    for k in range(nslot):
        acc = acc + mm_tn(mix_of(mixes[k], x_ref.shape[0]), ws[k][...])
    mid_ref[...] = acc
    n, _ = row_norm(acc)
    sec = (n * g_ref[...] + s_ref[...]).astype(BF16)
    sec_ref[...] = sec
    secf_ref[...] = sec.astype(F32)


def mlp_kernel(
    kind, keeps, sec_ref, secp_ref, cot_ref, cotp_ref, u0_ref, u1_ref, d0_ref, d1_ref, b_ref, *refs
):
    if keeps:
        p_ref, hid_ref, gp_ref, ub_ref, db_ref, k0_ref, k1_ref, s0_ref, s1_ref, gb_ref = refs
    else:
        hid_ref, gp_ref, ub_ref, db_ref, up_ref, uq_ref, k0_ref, k1_ref, sd_ref, gb_ref = refs
    part = u0_ref.shape[1]
    share = sec_ref.shape[0]
    up = jnp.concatenate([u0_ref[0], u0_ref[1], u1_ref[0], u1_ref[1]], axis=0).astype(BF16)
    down = jnp.concatenate([d0_ref[0], d1_ref[0], d0_ref[1], d1_ref[1]], axis=0).astype(BF16)
    ub_ref[...] = up
    db_ref[...] = down
    bias = b_ref[1:2, 0 : up.shape[0]]
    for r, (s_ref, c_ref) in enumerate(((sec_ref, cot_ref), (secp_ref, cotp_ref))):
        rows = slice(r * share, (r + 1) * share)
        sec = s_ref[...].astype(BF16)
        cot = c_ref[...].astype(BF16)
        pre = mm_nt(sec, up) + bias
        cdf = 0.5 * (1.0 + lax.erf(pre * (1.0 / math.sqrt(2.0))))
        hid = (pre * cdf).astype(BF16)
        pdf = jnp.exp(-0.5 * pre * pre) * (1.0 / math.sqrt(2.0 * math.pi))
        gpre = (mm_nt(cot, down) * (cdf + pre * pdf)).astype(BF16)
        hid_ref[rows, :] = hid
        gp_ref[rows, :] = gpre
        gb_r = jnp.sum(gpre.astype(F32), axis=0, keepdims=True)
        gd_r = mm_tn(hid, cot)
        gu_r = mm_tn(gpre, sec)
        if r == 0:
            gb, gd, gu = gb_r, gd_r, gu_r
        else:
            gb, gd, gu = gb + gb_r, gd + gd_r, gu + gu_r
    gb_ref[...] = gb
    order = (0, 1, 2, 3) if kind == "a" else (0, 2, 1, 3)
    gu_at = [gu[i * part : (i + 1) * part] for i in order]
    gd_at = [gd[i * part : (i + 1) * part] for i in order]
    if keeps:
        gu_at[3] = gu_at[3] + p_ref[0:part, :]
        gu_at[2] = gu_at[2] + p_ref[part:, :]
        for i, ref in enumerate((k0_ref, k1_ref, s0_ref, s1_ref)):
            ref[0:part, :] = gu_at[i]
            ref[part:, :] = gd_at[i]
    else:
        up_ref[0:part, :] = gu_at[3]
        up_ref[part:, :] = gu_at[2]
        uq_ref[0:part, :] = gu_at[0]
        uq_ref[part:, :] = gu_at[1]
        k0_ref[...] = gd_at[0]
        k1_ref[...] = gd_at[1]
        sd_ref[0:part, :] = gd_at[3]
        sd_ref[part:, :] = gd_at[2]


def down_kernel(nslot, *refs):
    hids = refs[:nslot]
    gps = refs[nslot : 2 * nslot]
    ubs = refs[2 * nslot : 3 * nslot]
    dbs = refs[3 * nslot : 4 * nslot]
    outs = refs[4 * nslot :]
    cat = lambda refs, axis: jnp.concatenate([r[...] for r in refs], axis=axis)
    share = outs[0].shape[1]
    for i, (rows_of, w_of) in enumerate(((hids, dbs), (gps, ubs))):
        w = cat(w_of, 0)
        for r, out_ref in enumerate(outs):
            rows = slice(r * share, (r + 1) * share)
            out_ref[i] = mm(jnp.concatenate([a[rows, :] for a in rows_of], axis=1), w)


def mid_kernel(nslot, mid_ref, own_ref, got_ref, cot_ref, db_ref, g_ref, *refs):
    ows = refs[:nslot]
    gmts = refs[nslot : 2 * nslot]
    bo_ref, gm_ref, low_ref, st_ref = refs[2 * nslot :]
    mid = mid_ref[...]
    n, rstd = row_norm(mid)
    e = own_ref[1] + got_ref[1]
    cot = cot_ref[...].astype(F32)
    gm = cot + row_norm_back(e * g_ref[...], n, rstd)
    gm_ref[...] = gm
    gm_low = gm.astype(BF16)
    low_ref[...] = gm_low
    for k in range(nslot):
        gmts[k][...] = mm_nt(ows[k][...], gm_low).astype(gmts[k].dtype)
    bo_ref[...] = (mid + (own_ref[0] + got_ref[0]) + db_ref[...]).astype(BF16)
    st_ref[0:1, :] = jnp.sum(e * n, axis=0, keepdims=True)
    st_ref[1:2, :] = jnp.sum(e, axis=0, keepdims=True)
    st_ref[2:3, :] = jnp.sum(gm_low.astype(F32), axis=0, keepdims=True)
    st_ref[3:4, :] = jnp.sum(cot, axis=0, keepdims=True)
    st_ref[4:8, :] = jnp.zeros((4, mid.shape[1]), F32)


def out_grad_kernel(nslot, idx_ref, low_ref, *refs):
    mixts = refs[:nslot]
    gow_keep, gow_send = refs[nslot:]
    part = 24
    gm_low = low_ref[...]
    for k in range(nslot):
        g = mm(mix_of(mixts[k], gm_low.shape[0]), gm_low)
        for p in range(PIECES):
            at = idx_ref[p]
            rows = slice(k * part, (k + 1) * part)

            @pl.when(at < PIECES // 2)
            def _():
                gow_keep[at, rows, :] = g[p * part : (p + 1) * part, :]

            @pl.when(at >= PIECES // 2)
            def _():
                gow_send[at - PIECES // 2, rows, :] = g[p * part : (p + 1) * part, :]


def attn_bwd_kernel(
    ncuts, idx_ref, x_ref, qpre_ref, kpre_ref, vt_ref, wt_ref, gmt_ref, gmtp_ref, mixf_ref, l_ref,
    hv_ref, kmask_ref, qhot_ref, *refs
):
    if ncuts:
        gn_in, gk_ref, gs_ref, *gn_refs = refs[: 3 + ncuts]
    else:
        gk_ref, gs_ref, gn_ref = refs[:3]
    st_ref, gb_ref, qaug_ref, kaug_ref, gpt_ref = refs[-5:]
    part = 24
    e = PIECES * part
    full = x_ref.shape[0]
    heads = e // DH
    qaug_ref[2 * DH :, :] = qhot_ref[...]
    kaug_ref[:, 2 * DH :] = kmask_ref[...]
    qg, qs, kg = hv_ref[:, 0:1], hv_ref[:, 1:2], hv_ref[:, 2:3]
    qg_sum = jnp.zeros((DH, 128), F32)
    qs_sum = jnp.zeros((DH, 128), F32)
    kg_sum = jnp.zeros((DH, 128), F32)
    row_no = lax.broadcasted_iota(jnp.int32, (DH, full), 0)
    one_rows = (row_no < 3).astype(F32).astype(BF16)
    for h in range(heads):
        hs = slice(h * DH, (h + 1) * DH)
        qn, qr, q_low = build_q_aug(qpre_ref[hs, :], qg, qs, qaug_ref)
        kn, kr, k_low = build_k_aug(kpre_ref[hs, :], kg, kaug_ref)
        inv = 1.0 / l_ref[h : h + 1, :]
        gm = jnp.concatenate(
            [gmt_ref[hs, :].astype(F32), gmtp_ref[hs, :].astype(BF16).astype(F32)], axis=1
        )
        go_low = (gm * inv).astype(BF16)
        delta = -jnp.sum(go_low.astype(F32) * mixf_ref[hs, :], axis=0, keepdims=True)
        d0 = delta.astype(BF16).astype(F32)
        d1 = (delta - d0).astype(BF16).astype(F32)
        d2 = delta - d0 - d1
        extra = jnp.where(
            row_no == 0, d0, jnp.where(row_no == 1, d1, jnp.where(row_no == 2, d2, 0.0))
        ).astype(BF16)
        goaug = jnp.concatenate([go_low, extra], axis=0)
        vaug = jnp.concatenate([vt_ref[hs, :], one_rows], axis=0).T
        prob = jnp.exp2(mm(kaug_ref[...], qaug_ref[...]))
        ds = (prob * mm(vaug, goaug)).astype(BF16)
        gv = mm_nt(go_low, prob.astype(BF16))
        gk = mm_nt(q_low, ds) * SCALE
        gq = mm(k_low, ds) * SCALE
        qg_sum += lane_fold(gq * qn)
        qs_sum += lane_fold(gq)
        kg_sum += lane_fold(gk * kn)
        gpt_ref[h * DH : (h + 1) * DH, :] = col_norm_back(gq * qg, qn, qr).astype(BF16)
        gpt_ref[e + h * DH : e + (h + 1) * DH, :] = col_norm_back(gk * kg, kn, kr).astype(BF16)
        gpt_ref[2 * e + h * DH : 2 * e + (h + 1) * DH, :] = gv.astype(BF16)
    st_ref[0] = qg_sum
    st_ref[1] = qs_sum
    st_ref[2] = kg_sum
    gp = gpt_ref[...]
    gb_ref[...] = lane_fold(gp.astype(F32))
    gw = mm(gp, x_ref[...])

    def put(ref, at, p):
        for s in range(3):
            ref[at, s * part : (s + 1) * part, :] = gw[s * e + p * part : s * e + (p + 1) * part, :]

    for p in range(PIECES):
        at = idx_ref[p]

        @pl.when(at < PIECES // 2)
        def _():
            put(gk_ref, at, p)

        @pl.when(at >= PIECES // 2)
        def _():
            put(gs_ref, at - PIECES // 2, p)

    gn = mm_tn(gp, wt_ref[...])
    if not ncuts:
        gn_ref[...] = gn
    else:
        at = 0
        for ref in gn_refs:
            rows = slice(at, at + ref.shape[0])
            ref[...] = gn_in[rows, :] + gn[rows]
            at += ref.shape[0]


def sums_kernel(
    nslot, blk_ref, me_ref, x_ref, xf_ref, gn_ref, mst_ref, h0_ref, h2_ref, b0_ref, b2_ref, *refs
):
    ubs = refs[:nslot]
    fars = refs[nslot:-1]
    out_ref = refs[-1]

    def fill():
        out_ref[...] = jnp.zeros_like(out_ref)
        out_ref[0:4, :] = mst_ref[0:4, :]
        heads = jnp.concatenate([h0_ref[i] + h2_ref[i] for i in range(3)], axis=0).T
        out_ref[6:7, 0 : heads.shape[1]] = jnp.sum(heads, axis=0, keepdims=True)
        me = me_ref[0]
        upart = out_ref.shape[1] // PIECES
        for row, k in zip((8, 10, 12, 14), (0, 2, 1, 3)):
            if k % 2 == 0:
                cols = (b0_ref if k == 0 else b2_ref)[...].T
                out_ref[row : row + 1, 0 : cols.shape[1]] = jnp.sum(cols, axis=0, keepdims=True)
            mine = ubs[k][...]
            for p in range(PIECES):
                piece = jnp.zeros((1, upart), F32)
                for t in range(PIECES // 2):
                    here = (me ^ offset_of(t, BITS_A)) == p
                    piece = piece + jnp.where(here, mine[:, t * upart : (t + 1) * upart], 0.0)
                out_ref[row + 1 : row + 2, p * upart : (p + 1) * upart] = piece

    fill()

    def add(x, e):
        n, _ = row_norm(x.astype(F32))
        out_ref[4:5, :] += jnp.sum(e * n, axis=0, keepdims=True)
        out_ref[5:6, :] += jnp.sum(e, axis=0, keepdims=True)

    add(x_ref[...], gn_ref[...])
    at = 0
    for ref in fars:
        add(xf_ref[at : at + ref.shape[0], :], ref[...])
        at += ref.shape[0]


def small_out_kernel(a_ref, b_ref, qb_ref, h0_ref, h1_ref, h2_ref, *rows):
    total = a_ref[...] + b_ref[...]
    for row, ref in zip((0, 1, 2, 3, 4, 5, 9), rows):
        ref[...] = total[row]
    for i, ref in enumerate((h0_ref, h1_ref, h2_ref)):
        ref[...] = total[6, i * DH : (i + 1) * DH]
        n = qb_ref.shape[1]
        qb_ref[i : i + 1, :] = total[8:9, i * n : (i + 1) * n]


def final_kernel(blk_ref, x_ref, gn_ref, *refs):
    gots = refs[:-3]
    gm_ref, g_ref, out_ref = refs[-3:]
    at = 0
    for ref in gots:
        rows = slice(at, at + ref.shape[0])
        n, rstd = row_norm(x_ref[rows, :].astype(F32))
        f = (gn_ref[rows, :] + ref[...]) * g_ref[...]
        out_ref[rows, :] = (gm_ref[rows, :] + row_norm_back(f, n, rstd)).astype(BF16)
        at += ref.shape[0]


def unpack_mlp_kernel(ia_ref, ib_ref, a_ref, b_ref, up_ref, down_ref, s_ref):
    part = s_ref.shape[2]
    half = PIECES // 2
    for w in range(2):
        for j in range(half):
            rows = slice((w * half + j) * part, (w * half + j + 1) * part)
            s_ref[w, j] = a_ref[rows, :]
            s_ref[w, half + j] = b_ref[rows, :]
    up_ref[...] = jnp.concatenate([s_ref[0, ia_ref[p]] for p in range(PIECES)], axis=0).T
    for p in range(PIECES):
        down_ref[p * part : (p + 1) * part, :] = s_ref[1, ib_ref[p]]


def unpack_att_kernel(i_ref, a_ref, b_ref, qkv_ref, out_ref, s_ref):
    rows = s_ref.shape[1]
    part = rows // 4
    half = PIECES // 2
    for j in range(half):
        s_ref[j] = a_ref[j * rows : (j + 1) * rows, :]
        s_ref[half + j] = b_ref[j * rows : (j + 1) * rows, :]
    for s, ref in enumerate((qkv_ref.at[0], qkv_ref.at[1], qkv_ref.at[2], out_ref)):
        for p in range(PIECES):
            ref[p * part : (p + 1) * part, :] = s_ref[i_ref[p], s * part : (s + 1) * part, :]


def swap_mp(a, k, size):
    return lax.ppermute(a, "mp", [(s, s ^ k) for s in range(size)])


def swap_plane(a, bit, size):
    return lax.ppermute(a, "dp", [(d, d ^ bit) for d in range(size)])


def storage_of(r, bits):
    return sum(jnp.where((r & bit) != 0, 1 << t, 0) for t, bit in enumerate(bits))


class Stages:
    def __init__(self):
        self.live = {}

    def __setitem__(self, name, value):
        self.live[name] = value

    def __getitem__(self, name):
        return self.live[name]

    def pop(self, name):
        return self.live.pop(name)

    def fence(self, *still_flying):
        now = {n: a for n, a in self.live.items() if n not in still_flying}
        leaves, tree = jax.tree.flatten(now)
        self.live.update(jax.tree.unflatten(tree, lax.optimization_barrier(leaves)))


def shards(
    tokens,
    seg_ids,
    qkv_weight,
    qkv_bias,
    out_weight,
    out_bias,
    up_weight,
    up_bias,
    down_weight,
    down_bias,
    norm1_gain,
    norm1_shift,
    query_gain,
    query_shift,
    key_gain,
    norm2_gain,
    norm2_shift,
    cotangent,
):
    ndp = lax.axis_size("dp")
    nmp = lax.axis_size("mp")
    dp_no = lax.axis_index("dp")
    mp_no = lax.axis_index("mp")
    me = dp_no % PIECES
    row_count, width = tokens.shape
    share = row_count // nmp
    full = SEQ_LEN
    assert full == 2 * share and nmp == 4 and ndp % PIECES == 0
    e = qkv_weight.shape[2]
    part = e // PIECES
    units = up_weight.shape[1]
    upart = units // PIECES
    half = PIECES // 2
    mine = half * upart
    core, px, py = 1, 2, 4

    vmem = pl.BlockSpec(memory_space=pltpu.VMEM)
    smem = pl.BlockSpec(memory_space=pltpu.SMEM)
    row1 = lambda v: v.reshape(1, -1)
    col = lambda v: v.reshape(-1, 1)
    swap = lambda a, bit: swap_plane(a, bit, ndp)
    zswap = lambda a, k: swap_mp(a, k, nmp)
    v = Stages()

    me1 = me.astype(jnp.int32).reshape(1)
    qkv_t = jnp.swapaxes(qkv_weight, 1, 2)
    wt0 = qkv_t.reshape(3 * e, width)
    att_piece, ob_piece, bias0 = call(
        prep_att_kernel,
        (
            sds((4 * part + 8, width), F32),
            sds((part + 8, width), F32),
            sds((8, width), F32),
        ),
        bytes_accessed=3_000_000,
        vmem_limit=VMEM_LARGE,
        in_specs=[smem] + [vmem] * 4,
        out_specs=(vmem,) * 3,
        scratch_shapes=[pltpu.VMEM((e, width), F32)],
    )(me1, qkv_t, out_weight, qkv_bias, up_bias)
    mlp_piece, u0, u1, d0, d1 = call(
        prep_mlp_kernel,
        (sds((2 * upart, width), F32), *[sds((2, upart, width), BF16)] * 4),
        bytes_accessed=6_000_000,
        vmem_limit=VMEM_LARGE,
        in_specs=[smem] + [vmem] * 2,
        out_specs=(vmem,) * 5,
        scratch_shapes=[pltpu.VMEM((units, width), F32)],
    )(me1, up_weight, down_weight)

    n_gn = (192, 176, 144)
    n_q0 = 56
    numbers = jnp.arange(PIECES, dtype=jnp.int32)
    idx_a = storage_of(numbers ^ me, BITS_A).astype(jnp.int32)
    idx_b = storage_of(numbers ^ me, BITS_B).astype(jnp.int32)

    block = 256
    per = share // block
    steps = 2 * per
    tile_no = jnp.arange(steps, dtype=jnp.int32)
    blk = jnp.where(tile_no < per, mp_no * per + tile_no, (mp_no ^ 1) * per + tile_no - per).astype(
        jnp.int32
    )
    const2 = lambda t, b: (0, 0)
    tok_spec = pl.BlockSpec((block, width), lambda t, b: (b[t], 0))
    run_spec = pl.BlockSpec((block, width), lambda t, b: (t, 0))
    vec_spec = pl.BlockSpec((1, width), const2)

    seg_own = lax.dynamic_slice_in_dim(seg_ids, mp_no * share, share, 0)
    seg_other = lax.dynamic_slice_in_dim(seg_ids, (mp_no ^ 1) * share, share, 0)
    seg_keys = jnp.concatenate([seg_own, seg_other])
    qhot = (
        lax.broadcasted_iota(jnp.int32, (SEG_COLS, full), 0) == seg_keys[None, :]
    ).astype(BF16)
    kmask = jnp.where(
        lax.broadcasted_iota(jnp.int32, (full, SEG_COLS), 1) == seg_keys[:, None], 0.0, -1e30
    ).astype(BF16)
    hv = jnp.stack([query_gain, query_shift, key_gain], axis=1)
    scratch = [
        pltpu.VMEM((2 * DH + SEG_COLS, full), BF16),
        pltpu.VMEM((full, 2 * DH + SEG_COLS), BF16),
    ]

    def whole(a):
        return pl.BlockSpec(a.shape, lambda t: (0,) * len(a.shape))

    def bias_at(block_no):
        return pl.BlockSpec((8, width), lambda t: (block_no, 0))

    att_names = ["qpre", "kpre", "vt", "mixt", "mixf", "mixs", "l"]
    att_shapes = [
        sds((e, full), F32),
        sds((e, full), F32),
        sds((e, full), BF16),
        sds((e, share), BF16),
        sds((e, full), F32),
        sds((e * share // width, width), F32),
        sds((8, full), F32),
    ]
    mix_rows = e * share // width

    def run_attn_own():
        all_of = lambda a: pl.BlockSpec(a.shape, lambda t, b: (0,) * len(a.shape))
        rest = [wt0, bias0, hv, kmask, qhot]
        shapes = [sds((full, width), BF16)] + att_shapes
        v["normed"], *outs = call(
            attn_fwd_own_kernel,
            tuple(shapes),
            flops=2 * (full * width * e * 3 + full * full * e * 8),
            bytes_accessed=10_000_000,
            grid_spec=pltpu.PrefetchScalarGridSpec(
                num_scalar_prefetch=1,
                grid=(1,),
                in_specs=[
                    pl.BlockSpec((share, width), lambda t, b: (b[0] // per, 0)),
                    pl.BlockSpec((share, width), lambda t, b: (b[per] // per, 0)),
                    vec_spec,
                    vec_spec,
                    *[all_of(a) for a in rest],
                ],
                out_specs=tuple(all_of(a) for a in shapes),
                scratch_shapes=scratch,
            ),
        )(blk, tokens, tokens, row1(norm1_gain), row1(norm1_shift), *rest)
        v["st0"] = dict(zip(att_names, outs))
        v["st0"]["wt"] = wt0
        v["st0"]["ow"] = out_weight

    def run_attn_far():
        shapes = [sds((3 * e, width), BF16)] + [sds((e, width), BF16)] * 3 + att_shapes
        args = [
            *v.pop("ta"), *v.pop("tb"), v["normed"], v["t2"], hv, kmask, qhot,
        ]
        specs = [whole(a) for a in args]
        specs[5] = bias_at(4 * part // 8)
        outs = call(
            attn_fwd_kernel,
            tuple(shapes),
            flops=2 * (full * width * e * 3 + full * full * e * 8),
            bytes_accessed=10_000_000,
            grid=(1,),
            vmem_limit=VMEM_LARGE,
            in_specs=[smem, smem] + specs,
            out_specs=tuple(whole(a) for a in shapes),
            scratch_shapes=scratch
            + [pltpu.VMEM((PIECES, 3 * part, width), F32)] * 2,
        )(idx_a, idx_b, *args)
        v["st2"] = dict(zip(["wt", "ow", "ow1", "ow3"] + att_names, outs))

    def by_slot():
        st0, st2 = v["st0"], v["st2"]
        mixes = [st0["mixt"], v["mix0"], st2["mixt"], v["mix2"]]
        ows = [st0["ow"], st2["ow1"], st2["ow"], st2["ow3"]]
        return mixes, ows

    def run_out():
        own_spec = pl.BlockSpec((share, width), lambda t, b: (b[0] // per, 0))
        whole2 = lambda shape: pl.BlockSpec(shape, lambda t, b: (0,) * len(shape))
        mixes, ows = by_slot()
        v["middle"], v["second"], v["sec_f"] = call(
            functools.partial(out_norm2_kernel, nmp),
            (sds((share, width), F32), sds((share, width), BF16), sds((share, width), F32)),
            flops=2 * share * width * e * nmp,
            bytes_accessed=8_000_000,
            grid_spec=pltpu.PrefetchScalarGridSpec(
                num_scalar_prefetch=1,
                grid=(1,),
                in_specs=[own_spec]
                + [whole2((e, share)), whole2((mix_rows, width))] * 2
                + [whole2((e, width))] * nmp
                + [whole2((1, width))] * 3,
                out_specs=(whole2((share, width)),) * 3,
            ),
        )(blk, tokens, *mixes, *ows, row1(out_bias), row1(norm2_gain), row1(norm2_shift))

    def run_mlp(k, up, down, bias, block_no):
        keeps = k % 2 == 0
        args = [
            v["second"], v["sec_p"], v["cot"], v["cot_p"], up[0], up[1], down[0], down[1], bias,
        ]
        if keeps:
            args.append(v.pop(f"p{k + 1}"))
        specs = [whole(a) for a in args]
        specs[8] = bias_at(block_no)
        piece = lambda n: sds((n * upart, width), F32)
        shapes = (
            *[sds((full, mine), BF16)] * 2,
            *[sds((mine, width), BF16)] * 2,
            *([piece(2)] * 4 if keeps else [piece(2), piece(2), piece(1), piece(1), piece(2)]),
            sds((1, mine), F32),
        )
        res = call(
            functools.partial(mlp_kernel, MLP_KIND[k], keeps),
            shapes,
            flops=2 * full * width * mine * 4,
            bytes_accessed=12_000_000,
            grid=(1,),
            in_specs=specs,
            out_specs=tuple(whole(a) for a in shapes),
        )(*args)
        v[f"h{k}"] = res[:4]
        v[f"ubg{k}"] = res[-1]
        if keeps:
            v[f"w{k}"] = res[4:8]
        else:
            v[f"p{k}"], v[f"q{k}u"] = res[4], res[5]
            v[f"w{k}"] = res[6:9]

    def run_down():
        return call(
            functools.partial(down_kernel, nmp),
            (sds((2, share, width), F32),) * 2,
            flops=4 * full * width * mine * nmp,
            bytes_accessed=17_000_000,
            vmem_limit=40 * 1024 * 1024,
            in_specs=[vmem] * (4 * nmp),
            out_specs=(vmem,) * 2,
        )(*[v[f"h{k}"][i] for i in range(4) for k in range(nmp)])

    def run_mid():
        mixes, ows = by_slot()
        shapes = (
            *[sds((e, share), F32 if k % 2 else BF16) for k in range(nmp)],
            sds((share, width), BF16),
            sds((share, width), F32),
            sds((share, width), BF16),
            sds((8, width), F32),
        )
        *gmts, bo, gm, low, mst = call(
            functools.partial(mid_kernel, nmp),
            shapes,
            flops=2 * share * width * e * nmp,
            bytes_accessed=12_000_000,
            in_specs=[vmem] * (6 + nmp),
            out_specs=(vmem,) * (4 + nmp),
        )(
            v["middle"], v.pop("acc_own"), v.pop("acc_got"), v["cot"], row1(down_bias),
            row1(norm2_gain), *ows,
        )
        v["block_out"], v["gm"], v["mst"] = bo, gm, mst
        for k in range(nmp):
            v[f"gmt{k}"] = gmts[k]
        return low

    def run_out_grad(low):
        mixes, ows = by_slot()
        args = [low, *mixes]
        specs = [whole(a) for a in args]
        for k in (1, 3):
            specs[1 + k] = pl.BlockSpec((mix_rows, width), lambda t: (0, 0))
        shapes = (sds((half, nmp * part, width), F32),) * 2
        v["o"] = call(
            functools.partial(out_grad_kernel, nmp),
            shapes,
            flops=2 * share * width * e * nmp,
            bytes_accessed=5_000_000,
            grid=(1,),
            in_specs=[smem] + specs,
            out_specs=tuple(whole(a) for a in shapes),
        )(idx_a, *args)

    def run_attn_bwd(k, got, idx, first):
        st = v.pop(f"st{k}")
        args = [
            idx, v["normed"], st["qpre"], st["kpre"], st["vt"], st["wt"], v.pop(f"gmt{k}"),
            v.pop(got), st["mixf"], st["l"], hv, kmask, qhot,
        ]
        cuts_now = (full,) if first else (share, *n_gn)
        if not first:
            args.append(v.pop("gn"))
        keep, send, *gn, hst, gb = call(
            functools.partial(attn_bwd_kernel, 0 if first else len(cuts_now)),
            (
                sds((half, 3 * part, width), F32),
                sds((half, 3 * part, width), F32),
                *[sds((n, width), F32) for n in cuts_now],
                sds((3, DH, 128), F32),
                sds((3 * e, 128), F32),
            ),
            flops=2 * (full * width * e * 6 + full * full * e * 20),
            bytes_accessed=14_000_000,
            in_specs=[smem] + [vmem] * (len(args) - 1),
            out_specs=(vmem,) * (4 + len(cuts_now)),
            scratch_shapes=scratch + [pltpu.VMEM((3 * e, full), BF16)],
        )(*args)
        v[f"q{k}"] = (keep, send)
        if first:
            v["gn"] = gn[0]
        else:
            v["gn_own"], v["gn_far"] = gn[0], tuple(gn[1:])
        v[f"hst{k}"] = hst
        v[f"qbg{k}"] = gb

    def g1(n):
        a, b = v[n + "a"], v[n + "b"]
        v[n + "a"] = (a, swap(a, px))
        v[n + "b"] = (b, swap(b, py))

    def g2(n):
        a, b = (jnp.stack(v[n + t]) for t in "ab")
        v[n + "a"] = (a, swap(a, py))
        v[n + "b"] = (b, swap(b, px))

    def g3(n):
        a, b = (jnp.concatenate(v[n + t], axis=0) for t in "ab")
        v[n + "a"] = (a, swap(a, core))
        v[n + "b"] = (b, swap(b, core))

    def r1(n):
        keep, send = v[n]
        v[n] = (keep, swap(send, core))

    def r2(n, kind):
        keep, got = v[n]
        keep_sum = keep[:2] + got[:2]
        v[n] = (keep_sum, swap(keep[2:] + got[2:], py if kind == "a" else px))

    def r3(n, kind):
        keep, got = v[n]
        v[n] = (keep[0] + got[0], swap(keep[1] + got[1], px if kind == "a" else py))

    def r4(n):
        keep, got = v[n]
        v[n] = keep + got

    def first_link(k):
        return py if MLP_KIND[k] == "a" else px

    def second_link(k):
        return px if MLP_KIND[k] == "a" else py

    def c1(k):
        k0, k1, s0, s1 = v[f"w{k}"]
        v[f"w{k}"] = (k0, k1, s0, swap(s1, first_link(k)))

    def c0(k):
        k0, k1, s0, g1 = v[f"w{k}"]
        v[f"w{k}"] = (k0, k1, g1, swap(s0, first_link(k)))

    def c2u(k):
        k0, k1, g1, g0 = v[f"w{k}"]
        q0, q1 = v.pop(f"q{k + 1}u")
        sent = k1[:upart] + q1 + g1[:upart]
        v[f"w{k}"] = (k0, k1, g1, g0, q0, swap(sent, second_link(k)))

    def c2d(k):
        k0, k1, g1, g0, q, gu = v.pop(f"w{k}")
        up_sum = k0[:upart] + g0[:upart] + q + gu
        return up_sum, k0[upart:] + g0[upart:], k1[upart:] + g1[upart:]

    def e1(k):
        k0, k1, s = v[f"w{k}"]
        v[f"w{k}"] = (k0, k1, swap(s, first_link(k)))

    def e2(k):
        k0, k1, g = v[f"w{k}"]
        v[f"w{k}"] = (k0 + g[upart:], swap(k1 + g[:upart], second_link(k)))

    def e3(k):
        k0, g = v[f"w{k}"]
        v[f"w{k}"] = k0 + g

    inner = (mp_no == 1) | (mp_no == 2)

    def middle_swap(a):
        return lax.ppermute(a, "mp", [(1, 2), (2, 1)])

    def pass_out(a):
        return lax.ppermute(a, "mp", [(1, 0), (2, 3)])

    def high_bits(a):
        bit = PIECES
        while bit < ndp:
            a = a + swap(a, bit)
            bit *= 2
        return a

    cot_all, mlp_piece = lax.optimization_barrier((cotangent, mlp_piece))
    v["cot"] = lax.dynamic_slice_in_dim(cot_all, mp_no * share, share, 0)
    v["cot_f"] = v["cot"].astype(F32)
    v["piece"] = mlp_piece
    v["o3"] = zswap(ob_piece, 3)
    v["o1"] = zswap(ob_piece, 1)
    v["t2"] = zswap(att_piece, 2)
    v.fence()
    hp = 2 * part
    t2, o1, o3 = v["t2"], v["o1"], v["o3"]
    v["ta"] = jnp.concatenate([t2[:hp], o1[:part]], axis=0)
    v["tb"] = jnp.concatenate([t2[hp : 2 * hp], o3[:part]], axis=0)
    g1("t")
    v["cot_p"] = swap(v.pop("cot_f"), core)
    v["m1"] = zswap(v["piece"], 1)
    v["mid_a"] = middle_swap(v.pop("piece"))
    run_attn_own()
    v.fence()
    m1 = v["m1"]
    to_y = jnp.concatenate([*v["ta"], m1[upart:]], axis=0)
    to_x = jnp.concatenate([*v["tb"], m1[:upart]], axis=0)
    v["ta"] = (to_y, swap(to_y, py))
    v["tb"] = (to_x, swap(to_x, px))
    v["mid_b"] = middle_swap(v.pop("m1"))
    v["mix0"] = zswap(jnp.concatenate([v["st0"].pop("mixs"), v["mid_a"]], axis=0), 1)
    v.fence()
    nt = 2 * 3 * part
    ya, yb = v.pop("ta")
    xa, xb = v.pop("tb")
    v["m1a"], v["m1b"] = (xa[nt:], xb[nt:]), (ya[nt:], yb[nt:])
    v["ta"], v["tb"] = (
        tuple(
            a.reshape(half, 3 * part, width) for a in (both_, swap(both_, core))
        )
        for both_ in (
            jnp.concatenate([ya[:nt], yb[:nt]], axis=0),
            jnp.concatenate([xa[:nt], xb[:nt]], axis=0),
        )
    )
    run_attn_far()
    g2("m1")
    v["end_b"] = pass_out(v["mid_b"])
    v.fence()
    v["mix2"] = zswap(v["st2"].pop("mixs"), 1)
    run_out()
    m3 = jnp.where(inner, v.pop("mid_a"), v.pop("end_b"))
    m2 = jnp.where(inner, v.pop("mid_b"), v["mix0"][mix_rows:])
    to_x = jnp.concatenate([m3[:upart], m2[:upart]], axis=0)
    to_y = jnp.concatenate([m3[upart:], m2[upart:]], axis=0)
    v["ma"], v["mb"] = (to_x, swap(to_x, px)), (to_y, swap(to_y, py))
    v.fence()
    for t in "ab":
        own, got = v.pop(f"m{t}")
        v[f"m3{t}"] = (own[:upart], got[:upart])
        v[f"m2{t}"] = (own[upart:], got[upart:])
    v["sec_p"] = swap(v.pop("sec_f"), core)
    run_mlp(1, v.pop("m1a"), v.pop("m1b"), v["o1"], part // 8)
    g2("m3")
    v.fence()
    v["p1"] = zswap(v["p1"], 1)
    run_mlp(3, v.pop("m3a"), v.pop("m3b"), v["o3"], part // 8)
    g2("m2")
    v.fence()
    v["p3"] = zswap(v["p3"], 1)
    run_mlp(0, (u0, u1), (d0, d1), bias0, 0)
    e1(1)
    e1(3)
    v.fence()
    run_mlp(2, v.pop("m2a"), v.pop("m2b"), v["t2"], 4 * part // 8)
    e2(1)
    e2(3)
    q1u = v.pop("q1u")
    v["q1x"] = zswap(q1u[:upart], 1)
    v["q1r"] = q1u[upart:]
    v.fence()
    e3(1)
    e3(3)
    q3u = v.pop("q3u")
    v["qm"] = zswap(jnp.concatenate([v.pop("q1r"), q3u[:upart]], axis=0), 1)
    v["q3r"] = q3u[upart:]
    c1(0)
    c1(2)
    v["acc_own"], v["acc_far"] = run_down()
    v.fence()
    c0(0)
    c0(2)
    v["q3y"] = zswap(jnp.concatenate([v.pop("q3r"), v.pop("w3")], axis=0), 1)
    v["acc_got"] = swap(v.pop("acc_far"), core)
    v["low"] = run_mid()
    v.fence()
    qm = v.pop("qm")
    q3y = v.pop("q3y")
    v["q1u"], v["q3u"] = (v.pop("q1x"), qm[:upart]), (qm[upart:], q3y[:upart])
    v["d3"] = q3y[upart:]
    c2u(0)
    c2u(2)
    v["gp2"] = zswap(v.pop("gmt3"), 1)
    run_out_grad(v.pop("low"))
    v.fence()
    up0, down0, send_x = c2d(0)
    up2, down2, send_y = c2d(2)
    v["gp0"] = zswap(v.pop("gmt1"), 1)
    v["z2x"] = zswap(up2, 2)
    r1("o")
    keep, got = v.pop("o")
    o4 = keep + got
    ho = 2 * part
    to_x = jnp.concatenate([send_x, o4[1, ho:], o4[3, ho:]], axis=0)
    to_y = jnp.concatenate([send_y, o4[2, :ho], o4[3, :ho]], axis=0)
    v["gx"], v["gy"] = swap(to_x, px), swap(to_y, py)
    v["op"], v["oq"] = (o4[0, :ho], o4[1, :ho]), (o4[0, ho:], o4[2, ho:])
    v["w0"], v["w2"] = (up0, down0), down2
    run_attn_bwd(2, "gp2", idx_b, True)
    v.fence()
    r1("q2")
    gx, gy = v.pop("gx"), v.pop("gy")
    v["d1"] = zswap(v.pop("w1"), 1)
    v["z2y"] = zswap(v.pop("w2") + gy[:upart] + v.pop("d3"), 2)
    up0, down0 = v["w0"]
    v["w0"] = (up0, down0 + gx[:upart])
    op = [a + gy[upart + i * ho : upart + (i + 1) * ho] for i, a in enumerate(v["op"])]
    oq = [a + gx[upart + i * ho : upart + (i + 1) * ho] for i, a in enumerate(v["oq"])]
    v["op"], v["oq"] = op[0], oq[0]
    keep, got = v["q2"]
    to_x = jnp.concatenate([(keep[2:] + got[2:]).reshape(-1, width), op[1]], axis=0)
    v["q2"] = keep[:2] + got[:2]
    v["gx"], v["gy"] = swap(to_x, px), swap(oq[1], py)
    run_attn_bwd(0, "gp0", idx_b, False)
    v.fence()
    nq = 3 * part
    gx, gy = v.pop("gx"), v.pop("gy")
    up_sum, down_sum = v.pop("w0")
    ma = high_bits(up_sum + v.pop("z2x"))
    mb = high_bits(down_sum + v.pop("d1") + v.pop("z2y"))
    q2 = v["q2"] + gx[: 2 * nq].reshape(2, nq, width)
    v["q2"] = q2[0]
    o = jnp.concatenate([v.pop("op") + gx[2 * nq :], v.pop("oq") + gy], axis=0)
    v["o0"], v["o2"] = o[:part], o[2 * part : 3 * part]
    v["gn0"] = zswap(
        jnp.concatenate([v["gn_far"][0], o[part : 2 * part], o[3 * part :]], axis=0), 1
    )
    keep, send = v.pop("q0")
    q4 = keep + swap(send, core)
    v["q0b"], v["q0a"] = q4[:2, :n_q0], (q4[0, n_q0:], q4[2, n_q0:])
    to_x = jnp.concatenate([ma, q4[2, :n_q0], q4[3, :n_q0]], axis=0)
    to_y = jnp.concatenate([mb, q2[1], q4[1, n_q0:], q4[3, n_q0:]], axis=0)
    v["gx"], v["gy"] = (ma, swap(to_x, px)), (mb, swap(to_y, py))
    v["small"] = call(
        functools.partial(sums_kernel, nmp),
        sds((16, width), F32),
        flops=full * width * 10,
        bytes_accessed=full * width * 6,
        grid_spec=pltpu.PrefetchScalarGridSpec(
            num_scalar_prefetch=2,
            grid=(1,),
            in_specs=[
                pl.BlockSpec((share, width), lambda t, b, m: (b[0] // per, 0)),
                pl.BlockSpec((share, width), lambda t, b, m: (b[per] // per, 0)),
                pl.BlockSpec((share, width), lambda t, b, m: (0, 0)),
                pl.BlockSpec((8, width), lambda t, b, m: (0, 0)),
                *[pl.BlockSpec((3, DH, 128), lambda t, b, m: (0, 0, 0))] * 2,
                *[pl.BlockSpec((3 * e, 128), lambda t, b, m: (0, 0))] * 2,
                *[pl.BlockSpec((1, mine), lambda t, b, m: (0, 0))] * nmp,
                *[pl.BlockSpec((n, width), lambda t, b, m: (0, 0)) for n in n_gn],
            ],
            out_specs=pl.BlockSpec((16, width), lambda t, b, m: (0, 0)),
        ),
    )(
        blk, me1, tokens, tokens, v["gn_own"], v.pop("mst"), v.pop("hst0"), v.pop("hst2"),
        v.pop("qbg0"), v.pop("qbg2"), *[v.pop(f"ubg{k}") for k in range(nmp)], *v["gn_far"],
    )
    v["small"] = v["small"] + swap(v["small"], core)
    v.fence()
    (ma, gx), (mb, gy) = v.pop("gx"), v.pop("gy")
    q0b = v.pop("q0b") + gx[upart:].reshape(2, n_q0, width)
    n_rest = nq - n_q0
    at = upart + nq
    q0a = [
        a + gy[at + i * n_rest : at + (i + 1) * n_rest] for i, a in enumerate(v.pop("q0a"))
    ]
    v["q0"] = (q0b[0], q0a[0])
    to_y = jnp.concatenate([ma, gx[:upart], q0b[1]], axis=0)
    to_x = jnp.concatenate([mb, gy[:upart], q0a[1]], axis=0)
    v["gx"], v["gy"] = (to_x, swap(to_x, px)), (to_y, swap(to_y, py))
    oz = v["gn0"][n_gn[0] :]
    v["o0"] = v["o0"] + oz[:part]
    q2 = v.pop("q2") + gy[upart:at]
    v["y2"] = zswap(jnp.concatenate([q2, v.pop("o2") + oz[part:]], axis=0), 2)
    v["gn1"] = zswap(v["gn_far"][1], 1)
    small = v["small"] + swap(v["small"], px)
    v["small"] = small + swap(small, py)
    v.fence()
    (xa, xb), (ya, yb) = v.pop("gx"), v.pop("gy")
    n2 = 2 * upart
    mlp = jnp.concatenate([ya[:n2], yb[:n2], xa[:n2], xb[:n2]], axis=0)
    q0b, q0a = v.pop("q0")
    q0 = jnp.concatenate([q0b + yb[n2:], q0a + xb[n2:]], axis=0)
    att_sum = high_bits(jnp.concatenate([q0, v.pop("o0")], axis=0) + v.pop("y2"))
    v["w"] = (att_sum, swap(att_sum, px), swap(att_sum, py), swap(att_sum, px | py))
    small = high_bits(v["small"])
    v["gn2"] = zswap(jnp.concatenate([v.pop("gn_far")[2], small[:8], small[12:]], axis=0), 1)
    v["small"] = small[:12] + v["gn2"][n_gn[2] :]

    v["up_g"], v["down_g"] = call(
        unpack_mlp_kernel,
        (sds((width, units), F32), sds((units, width), F32)),
        bytes_accessed=10_000_000,
        in_specs=[smem, smem] + [vmem] * 2,
        out_specs=(vmem,) * 2,
        scratch_shapes=[pltpu.VMEM((2, PIECES, upart, width), F32)],
    )(idx_a, idx_b, mlp, swap(mlp, core))
    v.fence()
    input_grad = call(
        final_kernel,
        sds((share, width), BF16),
        flops=share * width * 20,
        bytes_accessed=share * width * 16,
        grid_spec=pltpu.PrefetchScalarGridSpec(
            num_scalar_prefetch=1,
            grid=(1,),
            in_specs=[
                pl.BlockSpec((share, width), lambda t, b: (b[0] // per, 0)),
                pl.BlockSpec((share, width), const2),
                *[pl.BlockSpec((n, width), const2) for n in n_gn],
                pl.BlockSpec((share, width), const2),
                vec_spec,
            ],
            out_specs=pl.BlockSpec((share, width), const2),
        ),
    )(blk, tokens, v["gn_own"], *[v[f"gn{i}"] for i in range(3)], v["gm"], row1(norm1_gain))
    w = jnp.concatenate(v.pop("w"), axis=0)
    small = v.pop("small")
    small_got = zswap(jnp.concatenate([small[:8], small[10:]], axis=0), 2)
    qkv_weight_grad, out_weight_grad = call(
        unpack_att_kernel,
        (sds((3, e, width), F32), sds((e, width), F32)),
        bytes_accessed=2 * 4 * 4 * width * e,
        in_specs=[smem] + [vmem] * 2,
        out_specs=(vmem, vmem),
        scratch_shapes=[pltpu.VMEM((PIECES, 4 * part, width), F32)],
    )(idx_a, w, swap(w, core))
    qkv_weight_grad = jnp.swapaxes(qkv_weight_grad, 1, 2)
    qkv_weight_grad, out_weight_grad, input_grad, small, small_got = lax.optimization_barrier(
        (qkv_weight_grad, out_weight_grad, input_grad, small, small_got)
    )
    qkv_bias_grad, *rows_of = call(
        small_out_kernel,
        (sds((3, e), F32), *[sds((DH,), F32)] * 3, *[sds((width,), F32)] * 7),
        bytes_accessed=100_000,
        in_specs=[vmem, vmem],
        out_specs=(vmem,) * 11,
    )(small[:10], small_got)
    heads_of, rows_of = rows_of[:3], rows_of[3:]
    return (
        v["block_out"],
        input_grad,
        qkv_weight_grad,
        qkv_bias_grad,
        out_weight_grad,
        rows_of[2],
        v["up_g"],
        rows_of[6],
        v["down_g"],
        rows_of[3],
        rows_of[4],
        rows_of[5],
        heads_of[0],
        heads_of[1],
        heads_of[2],
        rows_of[0],
        rows_of[1],
    )


def solution(mesh):
    in_specs = (
        P("dp", None),
        P("dp"),
        P(None, None, "mp"),
        P(None, "mp"),
        P("mp", None),
        P(),
        P(None, "mp"),
        P("mp"),
        P("mp", None),
        P(),
        P(),
        P(),
        P(),
        P(),
        P(),
        P(),
        P(),
        P("dp", None),
    )
    out_specs = (
        P(("dp", "mp"), None),
        P(("dp", "mp"), None),
        P(None, None, "mp"),
        P(None, "mp"),
        P("mp", None),
        P(),
        P(None, "mp"),
        P("mp"),
        P("mp", None),
        P(),
        P(),
        P(),
        P(),
        P(),
        P(),
        P(),
        P(),
    )
    return jax.shard_map(shards, mesh=mesh, in_specs=in_specs, out_specs=out_specs, check_vma=False)
```

```python
import functools
import math

import jax
import jax.numpy as jnp
from jax import lax
from jax.experimental import pallas as pl
from jax.experimental.pallas import tpu as pltpu
from jax.sharding import PartitionSpec as P

F32 = jnp.float32
BF16 = jnp.bfloat16
DH = 64
SEQ_LEN = 1024
NORM_EPS = 1e-06
PIECES = 8
SEG_COLS = 128
LOG2E = math.log2(math.e)
SCALE = DH ** (-0.5)
BITS_A = (2, 4, 1)
BITS_B = (4, 2, 1)
MLP_KIND = ("a", "a", "b", "b")
VMEM_LIMIT = 26 * 1024 * 1024
VMEM_LARGE = 56 * 1024 * 1024


def mm(a, b):
    return lax.dot_general(a, b, (((1,), (0,)), ((), ())), preferred_element_type=F32)


def mm_nt(a, b):
    return lax.dot_general(a, b, (((1,), (1,)), ((), ())), preferred_element_type=F32)


def mm_tn(a, b):
    return lax.dot_general(a, b, (((0,), (0,)), ((), ())), preferred_element_type=F32)


def call(kernel, out_shape, flops=0, bytes_accessed=0, vmem_limit=VMEM_LIMIT, **kw):
    return pl.pallas_call(
        kernel,
        out_shape=out_shape,
        compiler_params=pltpu.CompilerParams(vmem_limit_bytes=vmem_limit),
        cost_estimate=pl.CostEstimate(
            flops=flops, bytes_accessed=bytes_accessed, transcendentals=0
        ),
        **kw,
    )


def sds(shape, dtype):
    return jax.ShapeDtypeStruct(shape, dtype)


def row_norm(x):
    mean = jnp.mean(x, axis=-1, keepdims=True)
    cen = x - mean
    rstd = lax.rsqrt(jnp.mean(cen * cen, axis=-1, keepdims=True) + NORM_EPS)
    return cen * rstd, rstd


def row_norm_back(f, n, rstd):
    mean_f = jnp.mean(f, axis=-1, keepdims=True)
    mean_fn = jnp.mean(f * n, axis=-1, keepdims=True)
    return (f - mean_f - n * mean_fn) * rstd


def col_norm(x):
    mean = jnp.mean(x, axis=0, keepdims=True)
    cen = x - mean
    rstd = lax.rsqrt(jnp.mean(cen * cen, axis=0, keepdims=True) + NORM_EPS)
    return cen * rstd, rstd


def col_norm_back(f, n, rstd):
    mean_f = jnp.mean(f, axis=0, keepdims=True)
    mean_fn = jnp.mean(f * n, axis=0, keepdims=True)
    return (f - mean_f - n * mean_fn) * rstd


def lane_fold(x):
    out = x[:, :128]
    for t in range(1, x.shape[1] // 128):
        out = out + x[:, t * 128 : (t + 1) * 128]
    return out


def offset_of(s, bits):
    return sum(bit for t, bit in enumerate(bits) if (s >> t) & 1)


def build_q_aug(q_pre, qg, qs, qaug_ref):
    n, rstd = col_norm(q_pre)
    q_low = (n * qg + qs).astype(BF16)
    scaled = q_low.astype(F32) * (SCALE * LOG2E)
    hi = scaled.astype(BF16)
    lo = (scaled - hi.astype(F32)).astype(BF16)
    qaug_ref[0:DH, :] = hi
    qaug_ref[DH : 2 * DH, :] = lo
    return n, rstd, q_low


def build_k_aug(k_pre, kg, kaug_ref):
    n, rstd = col_norm(k_pre)
    k_low = (n * kg).astype(BF16)
    kaug_ref[:, 0 : 2 * DH] = jnp.concatenate([k_low, k_low], axis=0).T
    return n, rstd, k_low


def bias_col(b_ref, n):
    return b_ref[...].T[0:n, 0:1]


def prep_att_kernel(
    me_ref, w_ref, o_ref, qb_ref, ub_ref, att_ref, ob_ref, b_ref, wf_ref
):
    part = 24
    e = PIECES * part
    me = me_ref[0]
    b_ref[...] = jnp.zeros(b_ref.shape, F32)
    for s in range(3):
        wf_ref[...] = w_ref[s].astype(F32)
        rows = wf_ref[pl.ds(pl.multiple_of(me * part, 8), part), :]
        att_ref[s * part : (s + 1) * part, :] = rows
        b_ref[0:1, s * e : (s + 1) * e] = qb_ref[s : s + 1, :]
    upart = ub_ref.shape[0] // PIECES
    ub = ub_ref[...].reshape(1, PIECES * upart)
    for s in range(PIECES // 2):
        piece = jnp.zeros((1, upart), F32)
        for p in range(PIECES):
            here = (me ^ offset_of(s, BITS_A)) == p
            piece = piece + jnp.where(here, ub[:, p * upart : (p + 1) * upart], 0.0)
        b_ref[1:2, s * upart : (s + 1) * upart] = piece
    wf_ref[...] = o_ref[...].astype(F32)
    rows = wf_ref[pl.ds(pl.multiple_of(me * part, 8), part), :]
    att_ref[3 * part : 4 * part, :] = rows
    ob_ref[0:part, :] = rows
    att_ref[4 * part :, :] = b_ref[...]
    ob_ref[part:, :] = b_ref[...]


def prep_mlp_kernel(me_ref, up_ref, dn_ref, p_ref, u0_ref, u1_ref, d0_ref, d1_ref, t_ref):
    me = me_ref[0]
    upart = up_ref.shape[1] // PIECES
    t_ref[...] = up_ref[...].astype(F32).T

    def at_piece(r):
        return pl.ds(pl.multiple_of((me ^ r) * upart, 32), upart)

    p_ref[0:upart, :] = t_ref[at_piece(0), :]
    p_ref[upart:, :] = dn_ref[at_piece(0), :].astype(F32)
    for i, (u_ref, d_ref) in enumerate(((u0_ref, d0_ref), (u1_ref, d1_ref))):
        for j in range(2):
            u_ref[j] = t_ref[at_piece(offset_of(2 * i + j, BITS_A)), :].astype(BF16)
            d_ref[j] = dn_ref[at_piece(offset_of(2 * i + j, BITS_B)), :]


def attend(x_ref, wt_ref, b_ref, hv_ref, kmask_ref, qhot_ref, outs, qaug_ref, kaug_ref):
    qpre_ref, kpre_ref, vt_ref, mixt_ref, mixf_ref, mixs_ref, l_ref = outs
    e = qpre_ref.shape[0]
    full = x_ref.shape[0]
    share = full // 2
    heads = e // DH
    x = x_ref[...]
    bias = bias_col(b_ref, 3 * e)
    qpre_ref[...] = mm_nt(wt_ref[0:e, :], x) + bias[0:e]
    kpre_ref[...] = mm_nt(wt_ref[e : 2 * e, :], x) + bias[e : 2 * e]
    vt_ref[...] = (mm_nt(wt_ref[2 * e : 3 * e, :], x) + bias[2 * e :]).astype(BF16)
    qaug_ref[2 * DH :, :] = qhot_ref[...]
    kaug_ref[:, 2 * DH :] = kmask_ref[...]
    ones = jnp.ones((16, full), BF16)
    for h in range(heads):
        hs = slice(h * DH, (h + 1) * DH)
        build_q_aug(qpre_ref[hs, :], hv_ref[:, 0:1], hv_ref[:, 1:2], qaug_ref)
        build_k_aug(kpre_ref[hs, :], hv_ref[:, 2:3], kaug_ref)
        prob = jnp.exp2(mm(kaug_ref[...], qaug_ref[...])).astype(BF16)
        vaug = jnp.concatenate([vt_ref[hs, :], ones], axis=0)
        o = mm(vaug, prob)
        total = o[DH : DH + 1, :]
        l_ref[h : h + 1, :] = total
        mix = o[0:DH, :] / total
        mixf_ref[hs, :] = mix
        mixt_ref[hs, :] = mix[:, 0:share].astype(BF16)
        at = h * share
        for c in range(0, share, 256):
            block_no, lane = divmod(at + c, x.shape[1])
            mixs_ref[block_no * DH : (block_no + 1) * DH, lane : lane + 256] = mix[
                :, share + c : share + c + 256
            ]


def attn_fwd_own_kernel(
    blk_ref, x_ref, xf_ref, g_ref, s_ref, wt_ref, b_ref, hv_ref, kmask_ref, qhot_ref, n_ref, *refs
):
    share = x_ref.shape[0]
    for i, ref in enumerate((x_ref, xf_ref)):
        n, _ = row_norm(ref[...].astype(F32))
        n_ref[i * share : (i + 1) * share, :] = (n * g_ref[...] + s_ref[...]).astype(BF16)
    attend(n_ref, wt_ref, b_ref, hv_ref, kmask_ref, qhot_ref, refs[:7], *refs[7:])


def attn_fwd_kernel(
    ia_ref, ib_ref, a0_ref, a1_ref, b0_ref, b1_ref, x_ref, b_ref, hv_ref, kmask_ref, qhot_ref,
    wt_ref, ow_ref, ow1_ref, ow3_ref, *refs,
):
    wa_ref, wb_ref = refs[-2:]
    part = 24
    e = PIECES * part
    half = PIECES // 2
    wa_ref[0:half] = a0_ref[...]
    wa_ref[half:] = a1_ref[...]
    wb_ref[0:half] = b0_ref[...]
    wb_ref[half:] = b1_ref[...]

    def rows(w_ref, i_ref, at):
        return jnp.concatenate(
            [w_ref[i_ref[p], at * part : (at + 1) * part, :] for p in range(PIECES)], axis=0
        ).astype(BF16)

    wt_ref[0:e, :] = rows(wa_ref, ia_ref, 0)
    wt_ref[e : 2 * e, :] = rows(wa_ref, ia_ref, 1)
    wt_ref[2 * e : 3 * e, :] = rows(wb_ref, ib_ref, 0)
    ow_ref[...] = rows(wb_ref, ib_ref, 1)
    ow1_ref[...] = rows(wa_ref, ia_ref, 2)
    ow3_ref[...] = rows(wb_ref, ib_ref, 2)
    attend(x_ref, wt_ref, b_ref, hv_ref, kmask_ref, qhot_ref, refs[:7], *refs[7:9])


def unmix(ref, heads, share):
    width = ref.shape[1]
    rows = []
    for h in range(heads):
        cols = []
        for c in range(0, share, 256):
            block_no, lane = divmod(h * share + c, width)
            cols.append(ref[block_no * DH : (block_no + 1) * DH, lane : lane + 256])
        rows.append(jnp.concatenate(cols, axis=1))
    return jnp.concatenate(rows, axis=0).astype(BF16)


def mix_of(ref, share):
    if ref.dtype == BF16:
        return ref[...]
    return unmix(ref, ref.shape[0] * ref.shape[1] // (DH * share), share)


def out_norm2_kernel(nslot, blk_ref, x_ref, *refs):
    mixes = refs[:nslot]
    ws = refs[nslot : 2 * nslot]
    ob_ref, g_ref, s_ref, mid_ref, sec_ref, secf_ref = refs[2 * nslot :]
    acc = x_ref[...].astype(F32) + ob_ref[...]
    for k in range(nslot):
        acc = acc + mm_tn(mix_of(mixes[k], x_ref.shape[0]), ws[k][...])
    mid_ref[...] = acc
    n, _ = row_norm(acc)
    sec = (n * g_ref[...] + s_ref[...]).astype(BF16)
    sec_ref[...] = sec
    secf_ref[...] = sec.astype(F32)


def mlp_kernel(
    kind, keeps, sec_ref, secp_ref, cot_ref, cotp_ref, u0_ref, u1_ref, d0_ref, d1_ref, b_ref, *refs
):
    if keeps:
        p_ref, hid_ref, gp_ref, ub_ref, db_ref, k0_ref, k1_ref, s0_ref, s1_ref, gb_ref = refs
    else:
        hid_ref, gp_ref, ub_ref, db_ref, up_ref, uq_ref, k0_ref, k1_ref, sd_ref, gb_ref = refs
    part = u0_ref.shape[1]
    share = sec_ref.shape[0]
    up = jnp.concatenate([u0_ref[0], u0_ref[1], u1_ref[0], u1_ref[1]], axis=0).astype(BF16)
    down = jnp.concatenate([d0_ref[0], d1_ref[0], d0_ref[1], d1_ref[1]], axis=0).astype(BF16)
    ub_ref[...] = up
    db_ref[...] = down
    bias = b_ref[1:2, 0 : up.shape[0]]
    for r, (s_ref, c_ref) in enumerate(((sec_ref, cot_ref), (secp_ref, cotp_ref))):
        rows = slice(r * share, (r + 1) * share)
        sec = s_ref[...].astype(BF16)
        cot = c_ref[...].astype(BF16)
        pre = mm_nt(sec, up) + bias
        cdf = 0.5 * (1.0 + lax.erf(pre * (1.0 / math.sqrt(2.0))))
        hid = (pre * cdf).astype(BF16)
        pdf = jnp.exp(-0.5 * pre * pre) * (1.0 / math.sqrt(2.0 * math.pi))
        gpre = (mm_nt(cot, down) * (cdf + pre * pdf)).astype(BF16)
        hid_ref[rows, :] = hid
        gp_ref[rows, :] = gpre
        gb_r = jnp.sum(gpre.astype(F32), axis=0, keepdims=True)
        gd_r = mm_tn(hid, cot)
        gu_r = mm_tn(gpre, sec)
        if r == 0:
            gb, gd, gu = gb_r, gd_r, gu_r
        else:
            gb, gd, gu = gb + gb_r, gd + gd_r, gu + gu_r
    gb_ref[...] = gb
    order = (0, 1, 2, 3) if kind == "a" else (0, 2, 1, 3)
    gu_at = [gu[i * part : (i + 1) * part] for i in order]
    gd_at = [gd[i * part : (i + 1) * part] for i in order]
    if keeps:
        gu_at[3] = gu_at[3] + p_ref[0:part, :]
        gu_at[2] = gu_at[2] + p_ref[part:, :]
        for i, ref in enumerate((k0_ref, k1_ref, s0_ref, s1_ref)):
            ref[0:part, :] = gu_at[i]
            ref[part:, :] = gd_at[i]
    else:
        up_ref[0:part, :] = gu_at[3]
        up_ref[part:, :] = gu_at[2]
        uq_ref[0:part, :] = gu_at[0]
        uq_ref[part:, :] = gu_at[1]
        k0_ref[...] = gd_at[0]
        k1_ref[...] = gd_at[1]
        sd_ref[0:part, :] = gd_at[3]
        sd_ref[part:, :] = gd_at[2]


def down_kernel(nslot, *refs):
    hids = refs[:nslot]
    gps = refs[nslot : 2 * nslot]
    ubs = refs[2 * nslot : 3 * nslot]
    dbs = refs[3 * nslot : 4 * nslot]
    outs = refs[4 * nslot :]
    cat = lambda refs, axis: jnp.concatenate([r[...] for r in refs], axis=axis)
    share = outs[0].shape[1]
    for i, (rows_of, w_of) in enumerate(((hids, dbs), (gps, ubs))):
        w = cat(w_of, 0)
        for r, out_ref in enumerate(outs):
            rows = slice(r * share, (r + 1) * share)
            out_ref[i] = mm(jnp.concatenate([a[rows, :] for a in rows_of], axis=1), w)


def mid_kernel(nslot, mid_ref, own_ref, got_ref, cot_ref, db_ref, g_ref, *refs):
    ows = refs[:nslot]
    gmts = refs[nslot : 2 * nslot]
    bo_ref, gm_ref, low_ref, st_ref = refs[2 * nslot :]
    mid = mid_ref[...]
    n, rstd = row_norm(mid)
    e = own_ref[1] + got_ref[1]
    cot = cot_ref[...].astype(F32)
    gm = cot + row_norm_back(e * g_ref[...], n, rstd)
    gm_ref[...] = gm
    gm_low = gm.astype(BF16)
    low_ref[...] = gm_low
    for k in range(nslot):
        gmts[k][...] = mm_nt(ows[k][...], gm_low).astype(gmts[k].dtype)
    bo_ref[...] = (mid + (own_ref[0] + got_ref[0]) + db_ref[...]).astype(BF16)
    st_ref[0:1, :] = jnp.sum(e * n, axis=0, keepdims=True)
    st_ref[1:2, :] = jnp.sum(e, axis=0, keepdims=True)
    st_ref[2:3, :] = jnp.sum(gm_low.astype(F32), axis=0, keepdims=True)
    st_ref[3:4, :] = jnp.sum(cot, axis=0, keepdims=True)
    st_ref[4:8, :] = jnp.zeros((4, mid.shape[1]), F32)


def out_grad_kernel(nslot, idx_ref, low_ref, *refs):
    mixts = refs[:nslot]
    gow_keep, gow_send = refs[nslot:]
    part = 24
    gm_low = low_ref[...]
    for k in range(nslot):
        g = mm(mix_of(mixts[k], gm_low.shape[0]), gm_low)
        for p in range(PIECES):
            at = idx_ref[p]
            rows = slice(k * part, (k + 1) * part)

            @pl.when(at < PIECES // 2)
            def _():
                gow_keep[at, rows, :] = g[p * part : (p + 1) * part, :]

            @pl.when(at >= PIECES // 2)
            def _():
                gow_send[at - PIECES // 2, rows, :] = g[p * part : (p + 1) * part, :]


def attn_bwd_kernel(
    ncuts, idx_ref, x_ref, qpre_ref, kpre_ref, vt_ref, wt_ref, gmt_ref, gmtp_ref, mixf_ref, l_ref,
    hv_ref, kmask_ref, qhot_ref, *refs
):
    if ncuts:
        gn_in, gk_ref, gs_ref, *gn_refs = refs[: 3 + ncuts]
    else:
        gk_ref, gs_ref, gn_ref = refs[:3]
    st_ref, gb_ref, qaug_ref, kaug_ref, gpt_ref = refs[-5:]
    part = 24
    e = PIECES * part
    full = x_ref.shape[0]
    heads = e // DH
    qaug_ref[2 * DH :, :] = qhot_ref[...]
    kaug_ref[:, 2 * DH :] = kmask_ref[...]
    qg, qs, kg = hv_ref[:, 0:1], hv_ref[:, 1:2], hv_ref[:, 2:3]
    qg_sum = jnp.zeros((DH, 128), F32)
    qs_sum = jnp.zeros((DH, 128), F32)
    kg_sum = jnp.zeros((DH, 128), F32)
    row_no = lax.broadcasted_iota(jnp.int32, (DH, full), 0)
    one_rows = (row_no < 3).astype(F32).astype(BF16)
    for h in range(heads):
        hs = slice(h * DH, (h + 1) * DH)
        qn, qr, q_low = build_q_aug(qpre_ref[hs, :], qg, qs, qaug_ref)
        kn, kr, k_low = build_k_aug(kpre_ref[hs, :], kg, kaug_ref)
        inv = 1.0 / l_ref[h : h + 1, :]
        gm = jnp.concatenate(
            [gmt_ref[hs, :].astype(F32), gmtp_ref[hs, :].astype(BF16).astype(F32)], axis=1
        )
        go_low = (gm * inv).astype(BF16)
        delta = -jnp.sum(go_low.astype(F32) * mixf_ref[hs, :], axis=0, keepdims=True)
        d0 = delta.astype(BF16).astype(F32)
        d1 = (delta - d0).astype(BF16).astype(F32)
        d2 = delta - d0 - d1
        extra = jnp.where(
            row_no == 0, d0, jnp.where(row_no == 1, d1, jnp.where(row_no == 2, d2, 0.0))
        ).astype(BF16)
        goaug = jnp.concatenate([go_low, extra], axis=0)
        vaug = jnp.concatenate([vt_ref[hs, :], one_rows], axis=0).T
        prob = jnp.exp2(mm(kaug_ref[...], qaug_ref[...]))
        ds = (prob * mm(vaug, goaug)).astype(BF16)
        gv = mm_nt(go_low, prob.astype(BF16))
        gk = mm_nt(q_low, ds) * SCALE
        gq = mm(k_low, ds) * SCALE
        qg_sum += lane_fold(gq * qn)
        qs_sum += lane_fold(gq)
        kg_sum += lane_fold(gk * kn)
        gpt_ref[h * DH : (h + 1) * DH, :] = col_norm_back(gq * qg, qn, qr).astype(BF16)
        gpt_ref[e + h * DH : e + (h + 1) * DH, :] = col_norm_back(gk * kg, kn, kr).astype(BF16)
        gpt_ref[2 * e + h * DH : 2 * e + (h + 1) * DH, :] = gv.astype(BF16)
    st_ref[0] = qg_sum
    st_ref[1] = qs_sum
    st_ref[2] = kg_sum
    gp = gpt_ref[...]
    gb_ref[...] = lane_fold(gp.astype(F32))
    gw = mm(gp, x_ref[...])

    def put(ref, at, p):
        for s in range(3):
            ref[at, s * part : (s + 1) * part, :] = gw[s * e + p * part : s * e + (p + 1) * part, :]

    for p in range(PIECES):
        at = idx_ref[p]

        @pl.when(at < PIECES // 2)
        def _():
            put(gk_ref, at, p)

        @pl.when(at >= PIECES // 2)
        def _():
            put(gs_ref, at - PIECES // 2, p)

    gn = mm_tn(gp, wt_ref[...])
    if not ncuts:
        gn_ref[...] = gn
    else:
        at = 0
        for ref in gn_refs:
            rows = slice(at, at + ref.shape[0])
            ref[...] = gn_in[rows, :] + gn[rows]
            at += ref.shape[0]


def sums_kernel(
    nslot, blk_ref, me_ref, x_ref, xf_ref, gn_ref, mst_ref, h0_ref, h2_ref, b0_ref, b2_ref, *refs
):
    ubs = refs[:nslot]
    fars = refs[nslot:-1]
    out_ref = refs[-1]

    def fill():
        out_ref[...] = jnp.zeros_like(out_ref)
        out_ref[0:4, :] = mst_ref[0:4, :]
        heads = jnp.concatenate([h0_ref[i] + h2_ref[i] for i in range(3)], axis=0).T
        out_ref[6:7, 0 : heads.shape[1]] = jnp.sum(heads, axis=0, keepdims=True)
        me = me_ref[0]
        upart = out_ref.shape[1] // PIECES
        for row, k in zip((8, 10, 12, 14), (0, 2, 1, 3)):
            if k % 2 == 0:
                cols = (b0_ref if k == 0 else b2_ref)[...].T
                out_ref[row : row + 1, 0 : cols.shape[1]] = jnp.sum(cols, axis=0, keepdims=True)
            mine = ubs[k][...]
            for p in range(PIECES):
                piece = jnp.zeros((1, upart), F32)
                for t in range(PIECES // 2):
                    here = (me ^ offset_of(t, BITS_A)) == p
                    piece = piece + jnp.where(here, mine[:, t * upart : (t + 1) * upart], 0.0)
                out_ref[row + 1 : row + 2, p * upart : (p + 1) * upart] = piece

    fill()

    def add(x, e):
        n, _ = row_norm(x.astype(F32))
        out_ref[4:5, :] += jnp.sum(e * n, axis=0, keepdims=True)
        out_ref[5:6, :] += jnp.sum(e, axis=0, keepdims=True)

    add(x_ref[...], gn_ref[...])
    at = 0
    for ref in fars:
        add(xf_ref[at : at + ref.shape[0], :], ref[...])
        at += ref.shape[0]


def small_out_kernel(a_ref, b_ref, qb_ref, h0_ref, h1_ref, h2_ref, *rows):
    total = a_ref[...] + b_ref[...]
    for row, ref in zip((0, 1, 2, 3, 4, 5, 9), rows):
        ref[...] = total[row]
    for i, ref in enumerate((h0_ref, h1_ref, h2_ref)):
        ref[...] = total[6, i * DH : (i + 1) * DH]
        n = qb_ref.shape[1]
        qb_ref[i : i + 1, :] = total[8:9, i * n : (i + 1) * n]


def final_kernel(blk_ref, x_ref, gn_ref, *refs):
    gots = refs[:-3]
    gm_ref, g_ref, out_ref = refs[-3:]
    at = 0
    for ref in gots:
        rows = slice(at, at + ref.shape[0])
        n, rstd = row_norm(x_ref[rows, :].astype(F32))
        f = (gn_ref[rows, :] + ref[...]) * g_ref[...]
        out_ref[rows, :] = (gm_ref[rows, :] + row_norm_back(f, n, rstd)).astype(BF16)
        at += ref.shape[0]


def unpack_mlp_kernel(ia_ref, ib_ref, a_ref, b_ref, up_ref, down_ref, s_ref):
    part = s_ref.shape[2]
    half = PIECES // 2
    for w in range(2):
        for j in range(half):
            rows = slice((w * half + j) * part, (w * half + j + 1) * part)
            s_ref[w, j] = a_ref[rows, :]
            s_ref[w, half + j] = b_ref[rows, :]
    up_ref[...] = jnp.concatenate([s_ref[0, ia_ref[p]] for p in range(PIECES)], axis=0).T
    for p in range(PIECES):
        down_ref[p * part : (p + 1) * part, :] = s_ref[1, ib_ref[p]]


def unpack_att_kernel(i_ref, a_ref, b_ref, qkv_ref, out_ref, s_ref):
    rows = s_ref.shape[1]
    part = rows // 4
    half = PIECES // 2
    for j in range(half):
        s_ref[j] = a_ref[j * rows : (j + 1) * rows, :]
        s_ref[half + j] = b_ref[j * rows : (j + 1) * rows, :]
    for s, ref in enumerate((qkv_ref.at[0], qkv_ref.at[1], qkv_ref.at[2], out_ref)):
        for p in range(PIECES):
            ref[p * part : (p + 1) * part, :] = s_ref[i_ref[p], s * part : (s + 1) * part, :]


def swap_mp(a, k, size):
    return lax.ppermute(a, "mp", [(s, s ^ k) for s in range(size)])


def swap_plane(a, bit, size):
    return lax.ppermute(a, "dp", [(d, d ^ bit) for d in range(size)])


def storage_of(r, bits):
    return sum(jnp.where((r & bit) != 0, 1 << t, 0) for t, bit in enumerate(bits))


class Stages:
    def __init__(self):
        self.live = {}

    def __setitem__(self, name, value):
        self.live[name] = value

    def __getitem__(self, name):
        return self.live[name]

    def pop(self, name):
        return self.live.pop(name)

    def fence(self, *still_flying):
        now = {n: a for n, a in self.live.items() if n not in still_flying}
        leaves, tree = jax.tree.flatten(now)
        self.live.update(jax.tree.unflatten(tree, lax.optimization_barrier(leaves)))


def shards(
    tokens,
    seg_ids,
    qkv_weight,
    qkv_bias,
    out_weight,
    out_bias,
    up_weight,
    up_bias,
    down_weight,
    down_bias,
    norm1_gain,
    norm1_shift,
    query_gain,
    query_shift,
    key_gain,
    norm2_gain,
    norm2_shift,
    cotangent,
):
    ndp = lax.axis_size("dp")
    nmp = lax.axis_size("mp")
    dp_no = lax.axis_index("dp")
    mp_no = lax.axis_index("mp")
    me = dp_no % PIECES
    row_count, width = tokens.shape
    share = row_count // nmp
    full = SEQ_LEN
    assert full == 2 * share and nmp == 4 and ndp % PIECES == 0
    e = qkv_weight.shape[2]
    part = e // PIECES
    units = up_weight.shape[1]
    upart = units // PIECES
    half = PIECES // 2
    mine = half * upart
    core, px, py = 1, 2, 4

    vmem = pl.BlockSpec(memory_space=pltpu.VMEM)
    smem = pl.BlockSpec(memory_space=pltpu.SMEM)
    row1 = lambda v: v.reshape(1, -1)
    col = lambda v: v.reshape(-1, 1)
    swap = lambda a, bit: swap_plane(a, bit, ndp)
    zswap = lambda a, k: swap_mp(a, k, nmp)
    v = Stages()

    me1 = me.astype(jnp.int32).reshape(1)
    qkv_t = jnp.swapaxes(qkv_weight, 1, 2)
    wt0 = qkv_t.reshape(3 * e, width)
    att_piece, ob_piece, bias0 = call(
        prep_att_kernel,
        (
            sds((4 * part + 8, width), F32),
            sds((part + 8, width), F32),
            sds((8, width), F32),
        ),
        bytes_accessed=3_000_000,
        vmem_limit=VMEM_LARGE,
        in_specs=[smem] + [vmem] * 4,
        out_specs=(vmem,) * 3,
        scratch_shapes=[pltpu.VMEM((e, width), F32)],
    )(me1, qkv_t, out_weight, qkv_bias, up_bias)
    mlp_piece, u0, u1, d0, d1 = call(
        prep_mlp_kernel,
        (sds((2 * upart, width), F32), *[sds((2, upart, width), BF16)] * 4),
        bytes_accessed=6_000_000,
        vmem_limit=VMEM_LARGE,
        in_specs=[smem] + [vmem] * 2,
        out_specs=(vmem,) * 5,
        scratch_shapes=[pltpu.VMEM((units, width), F32)],
    )(me1, up_weight, down_weight)

    n_gn = (176, 176, 160)
    n_q0 = 56
    numbers = jnp.arange(PIECES, dtype=jnp.int32)
    idx_a = storage_of(numbers ^ me, BITS_A).astype(jnp.int32)
    idx_b = storage_of(numbers ^ me, BITS_B).astype(jnp.int32)

    block = 256
    per = share // block
    steps = 2 * per
    tile_no = jnp.arange(steps, dtype=jnp.int32)
    blk = jnp.where(tile_no < per, mp_no * per + tile_no, (mp_no ^ 1) * per + tile_no - per).astype(
        jnp.int32
    )
    const2 = lambda t, b: (0, 0)
    tok_spec = pl.BlockSpec((block, width), lambda t, b: (b[t], 0))
    run_spec = pl.BlockSpec((block, width), lambda t, b: (t, 0))
    vec_spec = pl.BlockSpec((1, width), const2)

    seg_own = lax.dynamic_slice_in_dim(seg_ids, mp_no * share, share, 0)
    seg_other = lax.dynamic_slice_in_dim(seg_ids, (mp_no ^ 1) * share, share, 0)
    seg_keys = jnp.concatenate([seg_own, seg_other])
    qhot = (
        lax.broadcasted_iota(jnp.int32, (SEG_COLS, full), 0) == seg_keys[None, :]
    ).astype(BF16)
    kmask = jnp.where(
        lax.broadcasted_iota(jnp.int32, (full, SEG_COLS), 1) == seg_keys[:, None], 0.0, -1e30
    ).astype(BF16)
    hv = jnp.stack([query_gain, query_shift, key_gain], axis=1)
    scratch = [
        pltpu.VMEM((2 * DH + SEG_COLS, full), BF16),
        pltpu.VMEM((full, 2 * DH + SEG_COLS), BF16),
    ]

    def whole(a):
        return pl.BlockSpec(a.shape, lambda t: (0,) * len(a.shape))

    def bias_at(block_no):
        return pl.BlockSpec((8, width), lambda t: (block_no, 0))

    att_names = ["qpre", "kpre", "vt", "mixt", "mixf", "mixs", "l"]
    att_shapes = [
        sds((e, full), F32),
        sds((e, full), F32),
        sds((e, full), BF16),
        sds((e, share), BF16),
        sds((e, full), F32),
        sds((e * share // width, width), F32),
        sds((8, full), F32),
    ]
    mix_rows = e * share // width

    def run_attn_own():
        all_of = lambda a: pl.BlockSpec(a.shape, lambda t, b: (0,) * len(a.shape))
        rest = [wt0, bias0, hv, kmask, qhot]
        shapes = [sds((full, width), BF16)] + att_shapes
        v["normed"], *outs = call(
            attn_fwd_own_kernel,
            tuple(shapes),
            flops=2 * (full * width * e * 3 + full * full * e * 8),
            bytes_accessed=10_000_000,
            grid_spec=pltpu.PrefetchScalarGridSpec(
                num_scalar_prefetch=1,
                grid=(1,),
                in_specs=[
                    pl.BlockSpec((share, width), lambda t, b: (b[0] // per, 0)),
                    pl.BlockSpec((share, width), lambda t, b: (b[per] // per, 0)),
                    vec_spec,
                    vec_spec,
                    *[all_of(a) for a in rest],
                ],
                out_specs=tuple(all_of(a) for a in shapes),
                scratch_shapes=scratch,
            ),
        )(blk, tokens, tokens, row1(norm1_gain), row1(norm1_shift), *rest)
        v["st0"] = dict(zip(att_names, outs))
        v["st0"]["wt"] = wt0
        v["st0"]["ow"] = out_weight

    def run_attn_far():
        shapes = [sds((3 * e, width), BF16)] + [sds((e, width), BF16)] * 3 + att_shapes
        args = [
            *v.pop("ta"), *v.pop("tb"), v["normed"], v["t2"], hv, kmask, qhot,
        ]
        specs = [whole(a) for a in args]
        specs[5] = bias_at(4 * part // 8)
        outs = call(
            attn_fwd_kernel,
            tuple(shapes),
            flops=2 * (full * width * e * 3 + full * full * e * 8),
            bytes_accessed=10_000_000,
            grid=(1,),
            vmem_limit=VMEM_LARGE,
            in_specs=[smem, smem] + specs,
            out_specs=tuple(whole(a) for a in shapes),
            scratch_shapes=scratch
            + [pltpu.VMEM((PIECES, 3 * part, width), F32)] * 2,
        )(idx_a, idx_b, *args)
        v["st2"] = dict(zip(["wt", "ow", "ow1", "ow3"] + att_names, outs))

    def by_slot():
        st0, st2 = v["st0"], v["st2"]
        mixes = [st0["mixt"], v["mix0"], st2["mixt"], v["mix2"]]
        ows = [st0["ow"], st2["ow1"], st2["ow"], st2["ow3"]]
        return mixes, ows

    def run_out():
        own_spec = pl.BlockSpec((share, width), lambda t, b: (b[0] // per, 0))
        whole2 = lambda shape: pl.BlockSpec(shape, lambda t, b: (0,) * len(shape))
        mixes, ows = by_slot()
        v["middle"], v["second"], v["sec_f"] = call(
            functools.partial(out_norm2_kernel, nmp),
            (sds((share, width), F32), sds((share, width), BF16), sds((share, width), F32)),
            flops=2 * share * width * e * nmp,
            bytes_accessed=8_000_000,
            grid_spec=pltpu.PrefetchScalarGridSpec(
                num_scalar_prefetch=1,
                grid=(1,),
                in_specs=[own_spec]
                + [whole2((e, share)), whole2((mix_rows, width))] * 2
                + [whole2((e, width))] * nmp
                + [whole2((1, width))] * 3,
                out_specs=(whole2((share, width)),) * 3,
            ),
        )(blk, tokens, *mixes, *ows, row1(out_bias), row1(norm2_gain), row1(norm2_shift))

    def run_mlp(k, up, down, bias, block_no):
        keeps = k % 2 == 0
        args = [
            v["second"], v["sec_p"], v["cot"], v["cot_p"], up[0], up[1], down[0], down[1], bias,
        ]
        if keeps:
            args.append(v.pop(f"p{k + 1}"))
        specs = [whole(a) for a in args]
        specs[8] = bias_at(block_no)
        piece = lambda n: sds((n * upart, width), F32)
        shapes = (
            *[sds((full, mine), BF16)] * 2,
            *[sds((mine, width), BF16)] * 2,
            *([piece(2)] * 4 if keeps else [piece(2), piece(2), piece(1), piece(1), piece(2)]),
            sds((1, mine), F32),
        )
        res = call(
            functools.partial(mlp_kernel, MLP_KIND[k], keeps),
            shapes,
            flops=2 * full * width * mine * 4,
            bytes_accessed=12_000_000,
            grid=(1,),
            in_specs=specs,
            out_specs=tuple(whole(a) for a in shapes),
        )(*args)
        v[f"h{k}"] = res[:4]
        v[f"ubg{k}"] = res[-1]
        if keeps:
            v[f"w{k}"] = res[4:8]
        else:
            v[f"p{k}"], v[f"q{k}u"] = res[4], res[5]
            v[f"w{k}"] = res[6:9]

    def run_down():
        return call(
            functools.partial(down_kernel, nmp),
            (sds((2, share, width), F32),) * 2,
            flops=4 * full * width * mine * nmp,
            bytes_accessed=17_000_000,
            vmem_limit=40 * 1024 * 1024,
            in_specs=[vmem] * (4 * nmp),
            out_specs=(vmem,) * 2,
        )(*[v[f"h{k}"][i] for i in range(4) for k in range(nmp)])

    def run_mid():
        mixes, ows = by_slot()
        shapes = (
            *[sds((e, share), F32 if k % 2 else BF16) for k in range(nmp)],
            sds((share, width), BF16),
            sds((share, width), F32),
            sds((share, width), BF16),
            sds((8, width), F32),
        )
        *gmts, bo, gm, low, mst = call(
            functools.partial(mid_kernel, nmp),
            shapes,
            flops=2 * share * width * e * nmp,
            bytes_accessed=12_000_000,
            in_specs=[vmem] * (6 + nmp),
            out_specs=(vmem,) * (4 + nmp),
        )(
            v["middle"], v.pop("acc_own"), v.pop("acc_got"), v["cot"], row1(down_bias),
            row1(norm2_gain), *ows,
        )
        v["block_out"], v["gm"], v["mst"] = bo, gm, mst
        for k in range(nmp):
            v[f"gmt{k}"] = gmts[k]
        return low

    def run_out_grad(low):
        mixes, ows = by_slot()
        args = [low, *mixes]
        specs = [whole(a) for a in args]
        for k in (1, 3):
            specs[1 + k] = pl.BlockSpec((mix_rows, width), lambda t: (0, 0))
        shapes = (sds((half, nmp * part, width), F32),) * 2
        v["o"] = call(
            functools.partial(out_grad_kernel, nmp),
            shapes,
            flops=2 * share * width * e * nmp,
            bytes_accessed=5_000_000,
            grid=(1,),
            in_specs=[smem] + specs,
            out_specs=tuple(whole(a) for a in shapes),
        )(idx_a, *args)

    def run_attn_bwd(k, got, idx, first):
        st = v.pop(f"st{k}")
        args = [
            idx, v["normed"], st["qpre"], st["kpre"], st["vt"], st["wt"], v.pop(f"gmt{k}"),
            v.pop(got), st["mixf"], st["l"], hv, kmask, qhot,
        ]
        cuts_now = (full,) if first else (share, *n_gn)
        if not first:
            args.append(v.pop("gn"))
        keep, send, *gn, hst, gb = call(
            functools.partial(attn_bwd_kernel, 0 if first else len(cuts_now)),
            (
                sds((half, 3 * part, width), F32),
                sds((half, 3 * part, width), F32),
                *[sds((n, width), F32) for n in cuts_now],
                sds((3, DH, 128), F32),
                sds((3 * e, 128), F32),
            ),
            flops=2 * (full * width * e * 6 + full * full * e * 20),
            bytes_accessed=14_000_000,
            in_specs=[smem] + [vmem] * (len(args) - 1),
            out_specs=(vmem,) * (4 + len(cuts_now)),
            scratch_shapes=scratch + [pltpu.VMEM((3 * e, full), BF16)],
        )(*args)
        v[f"q{k}"] = (keep, send)
        if first:
            v["gn"] = gn[0]
        else:
            v["gn_own"], v["gn_far"] = gn[0], tuple(gn[1:])
        v[f"hst{k}"] = hst
        v[f"qbg{k}"] = gb

    def g1(n):
        a, b = v[n + "a"], v[n + "b"]
        v[n + "a"] = (a, swap(a, px))
        v[n + "b"] = (b, swap(b, py))

    def g2(n):
        a, b = (jnp.stack(v[n + t]) for t in "ab")
        v[n + "a"] = (a, swap(a, py))
        v[n + "b"] = (b, swap(b, px))

    def g3(n):
        a, b = (jnp.concatenate(v[n + t], axis=0) for t in "ab")
        v[n + "a"] = (a, swap(a, core))
        v[n + "b"] = (b, swap(b, core))

    def r1(n):
        keep, send = v[n]
        v[n] = (keep, swap(send, core))

    def r2(n, kind):
        keep, got = v[n]
        keep_sum = keep[:2] + got[:2]
        v[n] = (keep_sum, swap(keep[2:] + got[2:], py if kind == "a" else px))

    def r3(n, kind):
        keep, got = v[n]
        v[n] = (keep[0] + got[0], swap(keep[1] + got[1], px if kind == "a" else py))

    def r4(n):
        keep, got = v[n]
        v[n] = keep + got

    def first_link(k):
        return py if MLP_KIND[k] == "a" else px

    def second_link(k):
        return px if MLP_KIND[k] == "a" else py

    def c1(k):
        k0, k1, s0, s1 = v[f"w{k}"]
        v[f"w{k}"] = (k0, k1, s0, swap(s1, first_link(k)))

    def c0(k):
        k0, k1, s0, g1 = v[f"w{k}"]
        v[f"w{k}"] = (k0, k1, g1, swap(s0, first_link(k)))

    def c2u(k):
        k0, k1, g1, g0 = v[f"w{k}"]
        q0, q1 = v.pop(f"q{k + 1}u")
        sent = k1[:upart] + q1 + g1[:upart]
        v[f"w{k}"] = (k0, k1, g1, g0, q0, swap(sent, second_link(k)))

    def c2d(k):
        k0, k1, g1, g0, q, gu = v.pop(f"w{k}")
        up_sum = k0[:upart] + g0[:upart] + q + gu
        return up_sum, k0[upart:] + g0[upart:], k1[upart:] + g1[upart:]

    def e1(k):
        k0, k1, s = v[f"w{k}"]
        v[f"w{k}"] = (k0, k1, swap(s, first_link(k)))

    def e2(k):
        k0, k1, g = v[f"w{k}"]
        v[f"w{k}"] = (k0 + g[upart:], swap(k1 + g[:upart], second_link(k)))

    def e3(k):
        k0, g = v[f"w{k}"]
        v[f"w{k}"] = k0 + g

    inner = (mp_no == 1) | (mp_no == 2)

    def middle_swap(a):
        return lax.ppermute(a, "mp", [(1, 2), (2, 1)])

    def pass_out(a):
        return lax.ppermute(a, "mp", [(1, 0), (2, 3)])

    def high_bits(a):
        bit = PIECES
        while bit < ndp:
            a = a + swap(a, bit)
            bit *= 2
        return a

    cot_all, mlp_piece = lax.optimization_barrier((cotangent, mlp_piece))
    v["cot"] = lax.dynamic_slice_in_dim(cot_all, mp_no * share, share, 0)
    v["cot_f"] = v["cot"].astype(F32)
    v["piece"] = mlp_piece
    v["o3"] = zswap(ob_piece, 3)
    v["o1"] = zswap(ob_piece, 1)
    v["t2"] = zswap(att_piece, 2)
    v.fence()
    hp = 2 * part
    t2, o1, o3 = v["t2"], v["o1"], v["o3"]
    v["ta"] = jnp.concatenate([t2[:hp], o1[:part]], axis=0)
    v["tb"] = jnp.concatenate([t2[hp : 2 * hp], o3[:part]], axis=0)
    g1("t")
    v["cot_p"] = swap(v.pop("cot_f"), core)
    v["m1"] = zswap(v["piece"], 1)
    v["mid_a"] = middle_swap(v.pop("piece"))
    run_attn_own()
    v.fence()
    m1 = v["m1"]
    to_y = jnp.concatenate([*v["ta"], m1[upart:]], axis=0)
    to_x = jnp.concatenate([*v["tb"], m1[:upart]], axis=0)
    v["ta"] = (to_y, swap(to_y, py))
    v["tb"] = (to_x, swap(to_x, px))
    v["mid_b"] = middle_swap(v.pop("m1"))
    v["mix0"] = zswap(jnp.concatenate([v["st0"].pop("mixs"), v["mid_a"]], axis=0), 1)
    v.fence()
    nt = 2 * 3 * part
    ya, yb = v.pop("ta")
    xa, xb = v.pop("tb")
    v["m1a"], v["m1b"] = (xa[nt:], xb[nt:]), (ya[nt:], yb[nt:])
    v["ta"], v["tb"] = (
        tuple(
            a.reshape(half, 3 * part, width) for a in (both_, swap(both_, core))
        )
        for both_ in (
            jnp.concatenate([ya[:nt], yb[:nt]], axis=0),
            jnp.concatenate([xa[:nt], xb[:nt]], axis=0),
        )
    )
    run_attn_far()
    g2("m1")
    v["end_b"] = pass_out(v["mid_b"])
    v.fence()
    v["mix2"] = zswap(v["st2"].pop("mixs"), 1)
    run_out()
    m3 = jnp.where(inner, v.pop("mid_a"), v.pop("end_b"))
    m2 = jnp.where(inner, v.pop("mid_b"), v["mix0"][mix_rows:])
    to_x = jnp.concatenate([m3[:upart], m2[:upart]], axis=0)
    to_y = jnp.concatenate([m3[upart:], m2[upart:]], axis=0)
    v["ma"], v["mb"] = (to_x, swap(to_x, px)), (to_y, swap(to_y, py))
    v.fence()
    for t in "ab":
        own, got = v.pop(f"m{t}")
        v[f"m3{t}"] = (own[:upart], got[:upart])
        v[f"m2{t}"] = (own[upart:], got[upart:])
    v["sec_p"] = swap(v.pop("sec_f"), core)
    run_mlp(1, v.pop("m1a"), v.pop("m1b"), v["o1"], part // 8)
    g2("m3")
    v.fence()
    v["p1"] = zswap(v["p1"], 1)
    run_mlp(3, v.pop("m3a"), v.pop("m3b"), v["o3"], part // 8)
    g2("m2")
    v.fence()
    v["p3"] = zswap(v["p3"], 1)
    run_mlp(0, (u0, u1), (d0, d1), bias0, 0)
    e1(1)
    e1(3)
    v.fence()
    run_mlp(2, v.pop("m2a"), v.pop("m2b"), v["t2"], 4 * part // 8)
    e2(1)
    e2(3)
    q1u = v.pop("q1u")
    v["q1x"] = zswap(q1u[:upart], 1)
    v["q1r"] = q1u[upart:]
    v.fence()
    e3(1)
    e3(3)
    q3u = v.pop("q3u")
    v["qm"] = zswap(jnp.concatenate([v.pop("q1r"), q3u[:upart]], axis=0), 1)
    v["q3r"] = q3u[upart:]
    c1(0)
    c1(2)
    v["acc_own"], v["acc_far"] = run_down()
    v.fence()
    c0(0)
    c0(2)
    v["q3y"] = zswap(jnp.concatenate([v.pop("q3r"), v.pop("w3")], axis=0), 1)
    v["acc_got"] = swap(v.pop("acc_far"), core)
    v["low"] = run_mid()
    v.fence()
    qm = v.pop("qm")
    q3y = v.pop("q3y")
    v["q1u"], v["q3u"] = (v.pop("q1x"), qm[:upart]), (qm[upart:], q3y[:upart])
    v["d3"] = q3y[upart:]
    c2u(0)
    c2u(2)
    v["gp2"] = zswap(v.pop("gmt3"), 1)
    run_out_grad(v.pop("low"))
    v.fence()
    up0, down0, send_x = c2d(0)
    up2, down2, send_y = c2d(2)
    v["gp0"] = zswap(v.pop("gmt1"), 1)
    v["z2x"] = zswap(up2, 2)
    r1("o")
    keep, got = v.pop("o")
    o4 = keep + got
    ho = 2 * part
    to_x = jnp.concatenate([send_x, o4[1, ho:], o4[3, ho:]], axis=0)
    to_y = jnp.concatenate([send_y, o4[2, :ho], o4[3, :ho]], axis=0)
    v["gx"], v["gy"] = swap(to_x, px), swap(to_y, py)
    v["op"], v["oq"] = (o4[0, :ho], o4[1, :ho]), (o4[0, ho:], o4[2, ho:])
    v["w0"], v["w2"] = (up0, down0), down2
    run_attn_bwd(2, "gp2", idx_b, True)
    v.fence()
    r1("q2")
    gx, gy = v.pop("gx"), v.pop("gy")
    v["d1"] = zswap(v.pop("w1"), 1)
    v["z2y"] = zswap(v.pop("w2") + gy[:upart] + v.pop("d3"), 2)
    up0, down0 = v["w0"]
    v["w0"] = (up0, down0 + gx[:upart])
    op = [a + gy[upart + i * ho : upart + (i + 1) * ho] for i, a in enumerate(v["op"])]
    oq = [a + gx[upart + i * ho : upart + (i + 1) * ho] for i, a in enumerate(v["oq"])]
    v["op"], v["oq"] = op[0], oq[0]
    keep, got = v["q2"]
    to_x = jnp.concatenate([(keep[2:] + got[2:]).reshape(-1, width), op[1]], axis=0)
    v["q2"] = keep[:2] + got[:2]
    v["gx"], v["gy"] = swap(to_x, px), swap(oq[1], py)
    run_attn_bwd(0, "gp0", idx_b, False)
    v.fence()
    nq = 3 * part
    gx, gy = v.pop("gx"), v.pop("gy")
    up_sum, down_sum = v.pop("w0")
    ma = high_bits(up_sum + v.pop("z2x"))
    mb = high_bits(down_sum + v.pop("d1") + v.pop("z2y"))
    q2 = v["q2"] + gx[: 2 * nq].reshape(2, nq, width)
    v["q2"] = q2[0]
    o = jnp.concatenate([v.pop("op") + gx[2 * nq :], v.pop("oq") + gy], axis=0)
    v["o0"], v["o2"] = o[:part], o[2 * part : 3 * part]
    v["gn0"] = zswap(
        jnp.concatenate([v["gn_far"][0], o[part : 2 * part], o[3 * part :]], axis=0), 1
    )
    keep, send = v.pop("q0")
    q4 = keep + swap(send, core)
    v["q0b"], v["q0a"] = q4[:2, :n_q0], (q4[0, n_q0:], q4[2, n_q0:])
    to_x = jnp.concatenate([ma, q4[2, :n_q0], q4[3, :n_q0]], axis=0)
    to_y = jnp.concatenate([mb, q2[1], q4[1, n_q0:], q4[3, n_q0:]], axis=0)
    v["gx"], v["gy"] = (ma, swap(to_x, px)), (mb, swap(to_y, py))
    v["small"] = call(
        functools.partial(sums_kernel, nmp),
        sds((16, width), F32),
        flops=full * width * 10,
        bytes_accessed=full * width * 6,
        grid_spec=pltpu.PrefetchScalarGridSpec(
            num_scalar_prefetch=2,
            grid=(1,),
            in_specs=[
                pl.BlockSpec((share, width), lambda t, b, m: (b[0] // per, 0)),
                pl.BlockSpec((share, width), lambda t, b, m: (b[per] // per, 0)),
                pl.BlockSpec((share, width), lambda t, b, m: (0, 0)),
                pl.BlockSpec((8, width), lambda t, b, m: (0, 0)),
                *[pl.BlockSpec((3, DH, 128), lambda t, b, m: (0, 0, 0))] * 2,
                *[pl.BlockSpec((3 * e, 128), lambda t, b, m: (0, 0))] * 2,
                *[pl.BlockSpec((1, mine), lambda t, b, m: (0, 0))] * nmp,
                *[pl.BlockSpec((n, width), lambda t, b, m: (0, 0)) for n in n_gn],
            ],
            out_specs=pl.BlockSpec((16, width), lambda t, b, m: (0, 0)),
        ),
    )(
        blk, me1, tokens, tokens, v["gn_own"], v.pop("mst"), v.pop("hst0"), v.pop("hst2"),
        v.pop("qbg0"), v.pop("qbg2"), *[v.pop(f"ubg{k}") for k in range(nmp)], *v["gn_far"],
    )
    v["small"] = v["small"] + swap(v["small"], core)
    v.fence()
    (ma, gx), (mb, gy) = v.pop("gx"), v.pop("gy")
    q0b = v.pop("q0b") + gx[upart:].reshape(2, n_q0, width)
    n_rest = nq - n_q0
    at = upart + nq
    q0a = [
        a + gy[at + i * n_rest : at + (i + 1) * n_rest] for i, a in enumerate(v.pop("q0a"))
    ]
    v["q0"] = (q0b[0], q0a[0])
    to_y = jnp.concatenate([ma, gx[:upart], q0b[1]], axis=0)
    to_x = jnp.concatenate([mb, gy[:upart], q0a[1]], axis=0)
    v["gx"], v["gy"] = (to_x, swap(to_x, px)), (to_y, swap(to_y, py))
    oz = v["gn0"][n_gn[0] :]
    v["o0"] = v["o0"] + oz[:part]
    q2 = v.pop("q2") + gy[upart:at]
    v["y2"] = zswap(jnp.concatenate([q2, v.pop("o2") + oz[part:]], axis=0), 2)
    v["gn1"] = zswap(v["gn_far"][1], 1)
    small = v["small"] + swap(v["small"], px)
    v["small"] = small + swap(small, py)
    v.fence()
    (xa, xb), (ya, yb) = v.pop("gx"), v.pop("gy")
    n2 = 2 * upart
    mlp = jnp.concatenate([ya[:n2], yb[:n2], xa[:n2], xb[:n2]], axis=0)
    q0b, q0a = v.pop("q0")
    q0 = jnp.concatenate([q0b + yb[n2:], q0a + xb[n2:]], axis=0)
    att_sum = high_bits(jnp.concatenate([q0, v.pop("o0")], axis=0) + v.pop("y2"))
    v["w"] = (att_sum, swap(att_sum, px), swap(att_sum, py), swap(att_sum, px | py))
    small = high_bits(v["small"])
    v["gn2"] = zswap(jnp.concatenate([v.pop("gn_far")[2], small[:8], small[12:]], axis=0), 1)
    v["small"] = small[:12] + v["gn2"][n_gn[2] :]

    v["up_g"], v["down_g"] = call(
        unpack_mlp_kernel,
        (sds((width, units), F32), sds((units, width), F32)),
        bytes_accessed=10_000_000,
        in_specs=[smem, smem] + [vmem] * 2,
        out_specs=(vmem,) * 2,
        scratch_shapes=[pltpu.VMEM((2, PIECES, upart, width), F32)],
    )(idx_a, idx_b, mlp, swap(mlp, core))
    v.fence()
    input_grad = call(
        final_kernel,
        sds((share, width), BF16),
        flops=share * width * 20,
        bytes_accessed=share * width * 16,
        grid_spec=pltpu.PrefetchScalarGridSpec(
            num_scalar_prefetch=1,
            grid=(1,),
            in_specs=[
                pl.BlockSpec((share, width), lambda t, b: (b[0] // per, 0)),
                pl.BlockSpec((share, width), const2),
                *[pl.BlockSpec((n, width), const2) for n in n_gn],
                pl.BlockSpec((share, width), const2),
                vec_spec,
            ],
            out_specs=pl.BlockSpec((share, width), const2),
        ),
    )(blk, tokens, v["gn_own"], *[v[f"gn{i}"] for i in range(3)], v["gm"], row1(norm1_gain))
    w = jnp.concatenate(v.pop("w"), axis=0)
    small = v.pop("small")
    small_got = zswap(jnp.concatenate([small[:8], small[10:]], axis=0), 2)
    qkv_weight_grad, out_weight_grad = call(
        unpack_att_kernel,
        (sds((3, e, width), F32), sds((e, width), F32)),
        bytes_accessed=2 * 4 * 4 * width * e,
        in_specs=[smem] + [vmem] * 2,
        out_specs=(vmem, vmem),
        scratch_shapes=[pltpu.VMEM((PIECES, 4 * part, width), F32)],
    )(idx_a, w, swap(w, core))
    qkv_weight_grad = jnp.swapaxes(qkv_weight_grad, 1, 2)
    qkv_weight_grad, out_weight_grad, input_grad, small, small_got = lax.optimization_barrier(
        (qkv_weight_grad, out_weight_grad, input_grad, small, small_got)
    )
    qkv_bias_grad, *rows_of = call(
        small_out_kernel,
        (sds((3, e), F32), *[sds((DH,), F32)] * 3, *[sds((width,), F32)] * 7),
        bytes_accessed=100_000,
        in_specs=[vmem, vmem],
        out_specs=(vmem,) * 11,
    )(small[:10], small_got)
    heads_of, rows_of = rows_of[:3], rows_of[3:]
    return (
        v["block_out"],
        input_grad,
        qkv_weight_grad,
        qkv_bias_grad,
        out_weight_grad,
        rows_of[2],
        v["up_g"],
        rows_of[6],
        v["down_g"],
        rows_of[3],
        rows_of[4],
        rows_of[5],
        heads_of[0],
        heads_of[1],
        heads_of[2],
        rows_of[0],
        rows_of[1],
    )


def solution(mesh):
    in_specs = (
        P("dp", None),
        P("dp"),
        P(None, None, "mp"),
        P(None, "mp"),
        P("mp", None),
        P(),
        P(None, "mp"),
        P("mp"),
        P("mp", None),
        P(),
        P(),
        P(),
        P(),
        P(),
        P(),
        P(),
        P(),
        P("dp", None),
    )
    out_specs = (
        P(("dp", "mp"), None),
        P(("dp", "mp"), None),
        P(None, None, "mp"),
        P(None, "mp"),
        P("mp", None),
        P(),
        P(None, "mp"),
        P("mp"),
        P("mp", None),
        P(),
        P(),
        P(),
        P(),
        P(),
        P(),
        P(),
        P(),
    )
    return jax.shard_map(shards, mesh=mesh, in_specs=in_specs, out_specs=out_specs, check_vma=False)
```
